32 devices in a mesh: row: 16 (over z, y, core), col: 2 (over x).
Axes of the slice: x: 2, y: 2, z: 4, core: 2. Of those that a mesh axis runs over, the one named last changes fastest.
Arguments:
- object_field: float32 [2, 4096, 512], P(None, 'row', 'col'), may hold values from -6 to 6
- probe_field: float32 [2, 256, 256], replicated, may hold values from -6 to 6
- intensity: float32 [16, 2, 4, 256, 256], P('row', 'col'), may hold values from 0.25 to 16
- view_offsets: int32 [16, 2, 4, 2], P('row', 'col'), may hold values from 0 to 128
- view_counts: int32 [16, 2], P('row', 'col'), may hold values from 1 to 4, as said below
Outputs:
- updated_object: float32 [2, 4096, 512], P(None, 'row', 'col')
The draws below stay inside these ranges and needn't reach their ends.
Inputs may be any that keep to these rules, and one draw needn't show every extreme that they name: `view_counts`: every draw has some tile with 4 valid views. `view_offsets`: each view lies inside its tile's padded window.
All inputs are finite; a program needn't handle non-finite values.
Results may differ from the reference program's by a relative error of at most 0.0003.
Values sent between devices are 32-bit elements; how exact they have to be, the bound alone decides.
No kernel may reach another device: no remote copies, remote signals or barrier semaphores. Data moves between devices by JAX's collectives and lax.ppermute only.
A program may use at most 64 MiB of HBM per device.

```python
import math
import jax
import jax.numpy as jnp
from jax import lax

CORE = 256
MARGIN = 64
PROBE = 256
VIEWS = 4
NR = 4096
NC = 512
N_ROW = 16
N_COL = 2


def draw_view_counts(key, part):
    drawn_counts = jax.random.randint(key, (N_ROW * N_COL,), 1, VIEWS + 1)
    chosen_tile = jax.random.randint(jax.random.fold_in(key, 7), (), 0, N_ROW * N_COL)
    flattened = jnp.where(jnp.arange(N_ROW * N_COL) == chosen_tile, VIEWS, drawn_counts)
    return flattened.reshape(N_ROW, N_COL).astype(jnp.int32)


def plant(drawn, rng, least, largest):
    longest = drawn.shape.index(max(drawn.shape))
    spots = []
    for shift in (0, 1):
        where = [jax.random.randint(jax.random.fold_in(rng, axis), (), 0, length) for axis, length in enumerate(drawn.shape)]
        where[longest] = (where[longest] + shift) % drawn.shape[longest]
        spots.append(tuple(where))
    return drawn.at[spots[0]].set(least).at[spots[1]].set(largest)


def steps_of(stream_key, extent, pieces, low, top_value):
    gain = 1.0
    for axis_at, parts in pieces:
        draws = jax.random.uniform(jax.random.fold_in(jax.random.fold_in(stream_key, 6), axis_at), (parts,), jnp.float32, low / len(pieces), top_value / len(pieces))
        gain = gain * jnp.repeat(jnp.exp(draws), extent[axis_at] // parts).reshape((-1,) + (1,) * (len(extent) - 1 - axis_at))
    return gain


def gaussian(stream_key, shape, width, reach, pieces=(), held_as=jnp.bfloat16):
    factor_of = steps_of(stream_key, shape, pieces, -0.22, 0.18) if pieces else 1.0
    result = jax.random.normal(stream_key, shape, jnp.float32) * width * factor_of
    return jnp.minimum(jnp.maximum(result, -reach), reach).astype(held_as)


def setup_inputs(seed: int = 0) -> dict:
    arg_keys = jax.random.split(jax.random.key(seed), 6)
    return {
        "object_field": gaussian(arg_keys[0], (2, NR, NC), 1.0, 6.0, ((1, 16), (2, 2)), jnp.float32),
        "probe_field": gaussian(arg_keys[1], (2, PROBE, PROBE), 1.0, 6.0, (), jnp.float32),
        "intensity": jnp.clip(jnp.exp(math.log(16.0) - 4.158883 * jax.random.uniform(arg_keys[2], (N_ROW, N_COL, VIEWS, PROBE, PROBE), jnp.float32) ** steps_of(arg_keys[2], (N_ROW, N_COL, VIEWS, PROBE, PROBE), ((0, 16), (1, 2)), -0.2, 0.2)), 0.25, 16.0),
        "view_offsets": plant(jax.random.randint(arg_keys[3], (N_ROW, N_COL, VIEWS, 2), 0, CORE + 2 * MARGIN - PROBE + 1), jax.random.fold_in(arg_keys[3], 1), 0, CORE + 2 * MARGIN - PROBE).astype(jnp.int32),
        "view_counts": draw_view_counts(jax.random.fold_in(arg_keys[5], 71), 0),
    }


smooth_eps = 0.1
step_size = 0.2

def tile_gradient(window, probe_field, measured, offsets, active):
    probe_len = probe_field.shape[-1]
    wave_probe = lax.complex(probe_field[0], probe_field[1])
    gradient = jnp.zeros_like(window)
    for number in range(VIEWS):
        anchor = (jnp.int32(0), offsets[number, 0], offsets[number, 1])
        patch_field = lax.dynamic_slice(window, anchor, (2, probe_len, probe_len))
        exit_wave = wave_probe * lax.complex(patch_field[0], patch_field[1])
        farfield = jnp.fft.fft2(exit_wave, norm='ortho')
        modulus = jnp.sqrt(farfield.real * farfield.real + farfield.imag * farfield.imag + smooth_eps)
        scaling = 1.0 - jnp.sqrt(measured[number] + smooth_eps) / modulus
        backward = jnp.fft.ifft2(farfield * scaling, norm='ortho')
        contrib = jnp.conj(wave_probe) * backward
        stacked = jnp.stack([contrib.real, contrib.imag])
        stacked = jnp.where(number < active, stacked, jnp.zeros_like(stacked))
        current = lax.dynamic_slice(gradient, anchor, (2, probe_len, probe_len))
        gradient = lax.dynamic_update_slice(gradient, current + stacked, anchor)
    return gradient

def reference(object_field, probe_field, intensity, view_offsets, view_counts):
    core_len = CORE
    margin_len = MARGIN
    side_len = core_len + 2 * margin_len
    padded_image = jnp.pad(object_field, ((0, 0), (margin_len, margin_len), (margin_len, margin_len)))

    def one_tile(flat_index):
        tile_row = flat_index // N_COL
        tile_col = flat_index % N_COL
        window = lax.dynamic_slice(padded_image, (jnp.int32(0), tile_row * core_len, tile_col * core_len), (2, side_len, side_len))
        return tile_gradient(window, probe_field, intensity[tile_row, tile_col], view_offsets[tile_row, tile_col], view_counts[tile_row, tile_col])
    tile_grads = lax.map(one_tile, jnp.arange(N_ROW * N_COL, dtype=jnp.int32))
    tile_grads = tile_grads.reshape(N_ROW, N_COL, 2, side_len, side_len)
    zero_pad = (0, 0)
    from_above = jnp.pad(tile_grads[:-1, :, :, core_len + margin_len:, :], ((1, 0), zero_pad, zero_pad, zero_pad, zero_pad))
    from_below = jnp.pad(tile_grads[1:, :, :, :margin_len, :], ((0, 1), zero_pad, zero_pad, zero_pad, zero_pad))
    banded = tile_grads[:, :, :, margin_len:margin_len + core_len, :]
    banded = banded.at[:, :, :, :margin_len, :].add(from_above)
    banded = banded.at[:, :, :, core_len - margin_len:, :].add(from_below)
    from_left = jnp.pad(banded[:, :-1, :, :, core_len + margin_len:], (zero_pad, (1, 0), zero_pad, zero_pad, zero_pad))
    from_right = jnp.pad(banded[:, 1:, :, :, :margin_len], (zero_pad, (0, 1), zero_pad, zero_pad, zero_pad))
    folded = banded[:, :, :, :, margin_len:margin_len + core_len]
    folded = folded.at[:, :, :, :, :margin_len].add(from_left)
    folded = folded.at[:, :, :, :, core_len - margin_len:].add(from_right)
    assembled = jnp.transpose(folded, (2, 0, 3, 1, 4)).reshape(2, N_ROW * core_len, N_COL * core_len)
    return object_field - step_size * assembled
```

```python
import functools
import math

import jax
import jax.numpy as jnp
import ml_dtypes
import numpy as np
from jax import lax
from jax.experimental import pallas as pl
from jax.experimental.pallas import tpu as pltpu
from jax.sharding import PartitionSpec as P

MARGIN = 64
LANES = 128
CHUNK = 64

smooth_eps = 0.1
step_size = 0.2

F32 = jnp.float32
BF16 = jnp.bfloat16


def dft_tables(length):
    half = length // 2
    counter = np.arange(half)
    factor = 1.0 / math.sqrt(length)
    product = np.outer(counter, counter)
    even = np.exp(-2j * np.pi * (product % half) / half) * factor
    odd = np.exp(-2j * np.pi * ((2 * product + counter[:, None]) % length) / length) * factor

    def as_real(table):
        return np.block([[table.real, table.imag], [-table.imag, table.real]])

    def parts(table):
        high = table.astype(ml_dtypes.bfloat16)
        low = (table - high.astype(np.float64)).astype(ml_dtypes.bfloat16)
        return high, low

    even, odd = as_real(even), as_real(odd)
    by_right = [np.concatenate(parts(t), 0) for t in (even, odd, even.T, odd.T)]
    by_left = [np.concatenate(parts(t), 1) for t in (even.T, odd.T, even, odd)]
    order = np.zeros((length, length))
    order[np.arange(length), (np.arange(length) % 2) * half + np.arange(length) // 2] = 1.0
    return np.stack(by_right), np.stack(by_left), order.astype(ml_dtypes.bfloat16)


def channels(mesh_cols):
    if mesh_cols == 1:
        return []
    if mesh_cols == 2:
        return [([(0, 1), (1, 0)], None, None)]
    forward = [(i, i + 1) for i in range(mesh_cols - 1)]
    return [(forward, True, False), ([(j, i) for i, j in forward], False, True)]


def row_pairs(count, first):
    pairs = [(i, i + 1) for i in range(first, count - 1, 2)]
    return pairs + [(j, i) for i, j in pairs]


def sends_right(channel):
    return lax.axis_index("col") == 0 if channel[1] is None else channel[1]


def takes_right(channel):
    return lax.axis_index("col") == 0 if channel[2] is None else channel[2]


def lower_partner():
    return lax.rem(lax.axis_index("row"), 2) == 0


def lane_ids():
    return lax.broadcasted_iota(jnp.int32, (1, LANES), 1)


def half_lanes(right):
    low = lane_ids() < LANES // 2
    if isinstance(right, bool):
        return low if right else ~low
    return lane_ids() // (LANES // 2) == jnp.where(right, 0, 1)


def split(value):
    high = value.astype(BF16)
    return high, (value - high.astype(F32)).astype(BF16)


def dot(first, second):
    return jnp.dot(first, second, preferred_element_type=F32)


def swap_halves(block):
    return pltpu.roll(block, LANES // 2, 1)


def pack_kernel(chans, object_ref, a_ref, b_ref, *edge_refs):
    size = object_ref.shape[1]
    top, bottom = pl.ds(0, MARGIN), pl.ds(size - MARGIN, MARGIN)
    lower = lower_partner()
    for part in range(2):
        head, tail = object_ref[part, top, :], object_ref[part, bottom, :]
        a_ref[part] = jnp.where(lower, tail, head)
        b_ref[part] = jnp.where(lower, head, tail)
    for number, channel in enumerate(chans):
        right = sends_right(channel)
        x_ref, k_ref = edge_refs[2 * number : 2 * number + 2]
        low = lane_ids() < LANES // 2
        for start in range(0, size, CHUNK):
            rows = slice(start, start + CHUNK)
            left_edge = jnp.where(
                low, object_ref[0, rows, :LANES], swap_halves(object_ref[1, rows, :LANES])
            )
            right_edge = jnp.where(
                low,
                swap_halves(object_ref[1, rows, size - LANES :]),
                object_ref[0, rows, size - LANES :],
            )
            x_ref[rows] = jnp.where(right, right_edge, left_edge)
        k_ref[...] = jnp.where(lower, x_ref[:MARGIN], x_ref[size - MARGIN :])


def pack_call(object_field, chans):
    size = object_field.shape[1]
    shapes = [(2, MARGIN, size)] * 2 + [(size, LANES), (MARGIN, LANES)] * len(chans)
    vmem = pl.BlockSpec(memory_space=pltpu.VMEM)
    return pl.pallas_call(
        functools.partial(pack_kernel, chans),
        out_shape=[jax.ShapeDtypeStruct(shape, F32) for shape in shapes],
        in_specs=[vmem],
        out_specs=[vmem] * len(shapes),
    )(object_field)


def prepare_kernel(offsets, counts, probe, intensity, order, placed, amplitude, doubled):
    views, size = intensity.shape[2], probe.shape[1]
    half = size // 2
    for part in range(2):
        doubled[part, :size] = probe[part]
        doubled[part, size : 2 * size] = probe[part]
    sublane = lax.broadcasted_iota(jnp.int32, (1, 8, 1), 1)
    for view in range(views):
        valid = (view < counts[0, 0]).astype(F32)
        high, low = split(jnp.sqrt(intensity[0, 0, view] + smooth_eps) * valid)
        ordered = dot(high, order[...]) + dot(low, order[...])
        amplitude[view, 0] = ordered[:, :half]
        amplitude[view, 1] = ordered[:, half:]
        shift_row = lax.rem(offsets[0, 0, view, 0] - MARGIN + size, size)
        shift_col = lax.rem(offsets[0, 0, view, 1] - MARGIN + size, size)
        start = lax.rem(size - shift_row, size)
        whole = pl.multiple_of((start // 8) * 8, 8)
        rest = start - whole
        for part in range(2):
            for row in range(0, size, CHUNK):
                block = doubled[part, pl.ds(whole + row, CHUNK + 8), :]
                block = pltpu.roll(block, shift_col, 1).reshape(CHUNK // 8 + 1, 8, size)
                block = pltpu.roll(block, lax.rem(8 - rest, 8), 1)
                block = jnp.where(sublane < 8 - rest, block[:-1], block[1:])
                placed[view, part, row : row + CHUNK] = block.reshape(CHUNK, size)


def prepare_call(offsets, counts, probe, intensity, order):
    views, size = intensity.shape[2], probe.shape[1]
    vmem = pl.BlockSpec(memory_space=pltpu.VMEM)
    smem = pl.BlockSpec(memory_space=pltpu.SMEM)
    return pl.pallas_call(
        prepare_kernel,
        out_shape=[
            jax.ShapeDtypeStruct((views, 2, size, size), F32),
            jax.ShapeDtypeStruct((views, 2, size, size // 2), F32),
        ],
        in_specs=[smem, smem, vmem, vmem, vmem],
        out_specs=[vmem] * 2,
        scratch_shapes=[pltpu.VMEM((2, 2 * size + 8, size), F32)],
        compiler_params=pltpu.CompilerParams(vmem_limit_bytes=20 * 1024 * 1024),
        cost_estimate=pl.CostEstimate(flops=2 * 10**9, bytes_accessed=6 * 10**6, transcendentals=0),
    )(offsets, counts, probe, intensity, order)


def views_kernel(chans, offsets, counts, core, placed, amplitude, right, left, a_in, b_in, *rest):
    count = len(chans)
    x_in, ka_in, kb_in = rest[:count], rest[count : 2 * count], rest[2 * count : 3 * count]
    rest = rest[3 * count :]
    g_core, g_a, g_b = rest[:3]
    g_x, g_kb = rest[3 : 3 + count], rest[3 + count : 3 + 2 * count]
    cols_m, rows_m, corner_m, s1, y, s2, z, s3, u, s4, g = rest[3 + 2 * count :]
    views, size = placed.shape[0], core.shape[1]
    half, m = size // 2, MARGIN
    lower = lower_partner()
    low_lanes = lane_ids() < LANES // 2
    zero = jnp.zeros((CHUNK, LANES), F32)

    def unpack(blocks):
        re = im = None
        for channel, block in zip(chans, blocks):
            mine = half_lanes(takes_right(channel))
            re = jnp.where(mine, block, 0.0 if re is None else re)
            im = jnp.where(mine, swap_halves(block), 0.0 if im is None else im)
        return (re, im) if blocks else (zero, zero)

    for row in range(0, size, CHUNK):
        rows = slice(row, row + CHUNK)
        cols_m[0, rows], cols_m[1, rows] = unpack([ref[rows] for ref in x_in])
    corner_a = unpack([ref[...] for ref in ka_in])
    corner_b = unpack([ref[...] for ref in kb_in])
    for part in range(2):
        a_rows, b_rows = a_in[part], b_in[part]
        rows_m[part, :m] = jnp.where(lower, a_rows, b_rows)
        rows_m[part, m:] = jnp.where(lower, b_rows, a_rows)
        corner_m[part, :m] = jnp.where(lower, corner_a[part], corner_b[part])
        corner_m[part, m:] = jnp.where(lower, corner_b[part], corner_a[part])

    def by_right(lhs, t):
        out = dot(lhs[:, :size], right[t, :size]) + dot(lhs[:, size:], right[t, :size])
        return out + dot(lhs[:, :size], right[t, size:])

    def by_left(t, rhs):
        out = dot(left[t, :, :size], rhs[:size]) + dot(left[t, :, :size], rhs[size:])
        return out + dot(left[t, :, size:], rhs[:size])

    def put_below(ref, row, col, value):
        high, low = split(value)
        rows, cols = value.shape
        ref[row : row + rows, col : col + cols] = high
        ref[size + row : size + row + rows, col : col + cols] = low

    def put_beside(ref, row, col, value):
        high, low = split(value)
        rows, cols = value.shape
        ref[row : row + rows, col : col + cols] = high
        ref[row : row + rows, size + col : size + col + cols] = low

    def row_mask(view, row):
        ids = row + lax.broadcasted_iota(jnp.int32, (CHUNK, LANES), 0)
        if row < m:
            return ids < offsets[0, 0, view, 0] - m, row
        if row >= size - m:
            return ids >= size - m + offsets[0, 0, view, 0], row - size + 2 * m
        return None, None

    def col_mask(view, block):
        if block == 0:
            return lane_ids() < offsets[0, 0, view, 1] - m
        return lane_ids() >= m + offsets[0, 0, view, 1]

    def patch(view, row, block):
        cols = slice(block * LANES, (block + 1) * LANES)
        rows = slice(row, row + CHUNK)
        beside = col_mask(view, block)
        beyond, place = row_mask(view, row)
        found = []
        for part in range(2):
            value = jnp.where(beside, cols_m[part, rows], core[part, rows, cols])
            if beyond is not None:
                there = slice(place, place + CHUNK)
                outer = jnp.where(beside, corner_m[part, there], rows_m[part, there, cols])
                value = jnp.where(beyond, outer, value)
            found.append(value)
        return found

    for view in range(views):
        for row in range(0, size, CHUNK):
            rows = slice(row, row + CHUNK)
            waves = []
            for block in range(2):
                cols = slice(block * LANES, (block + 1) * LANES)
                o_re, o_im = patch(view, row, block)
                p_re, p_im = placed[view, 0, rows, cols], placed[view, 1, rows, cols]
                waves.append((p_re * o_re - p_im * o_im, p_re * o_im + p_im * o_re))
            for part in range(2):
                put_beside(s1.at[view, 0], row, part * half, waves[0][part] + waves[1][part])
                put_beside(s1.at[view, 1], row, part * half, waves[0][part] - waves[1][part])
        for odd in range(2):
            y[view, odd] = by_right(s1.at[view, odd], odd)
        for odd in range(2):
            for part in range(2):
                cols = slice(part * half, (part + 1) * half)
                for row in range(0, half, CHUNK):
                    above = y[view, odd, row : row + CHUNK, cols]
                    below = y[view, odd, half + row : half + row + CHUNK, cols]
                    put_below(s2.at[view, 0], part * half + row, odd * half, above + below)
                    put_below(s2.at[view, 1], part * half + row, odd * half, above - below)
        for odd in range(2):
            z[view, odd] = by_left(odd, s2.at[view, odd])
        valid = (view < counts[0, 0]).astype(F32)
        for odd in range(2):
            for row in range(0, half, CHUNK):
                re, im = z[view, odd, row : row + CHUNK], z[view, odd, half + row : half + row + CHUNK]
                taken = pl.ds(2 * row + odd, CHUNK, stride=2)
                wanted = jnp.concatenate([amplitude[view, 0, taken], amplitude[view, 1, taken]], 1)
                scaling = valid - wanted * lax.rsqrt(re * re + im * im + smooth_eps)
                put_below(s3.at[view, odd], row, 0, re * scaling)
                put_below(s3.at[view, odd], half + row, 0, im * scaling)
        for odd in range(2):
            u[view, odd] = by_left(2 + odd, s3.at[view, odd])
        for part in range(2):
            for row in range(0, half, CHUNK):
                rows = slice(part * half + row, part * half + row + CHUNK)
                even_rows, odd_rows = u[view, 0, rows], u[view, 1, rows]
                for value, place in ((even_rows + odd_rows, row), (even_rows - odd_rows, half + row)):
                    put_beside(s4.at[view, 0], place, part * half, value[:, :half])
                    put_beside(s4.at[view, 1], place, part * half, value[:, half:])
        for odd in range(2):
            g[view, odd] = by_right(s4.at[view, odd], 2 + odd)

    for row in range(0, size, CHUNK):
        rows = slice(row, row + CHUNK)
        sums = {}

        def add(key, value):
            sums[key] = sums[key] + value if key in sums else value

        for view in range(views):
            beyond, place = row_mask(view, row)
            halves = []
            for part in range(2):
                cols = slice(part * half, (part + 1) * half)
                even_cols, odd_cols = g[view, 0, rows, cols], g[view, 1, rows, cols]
                halves.append((even_cols + odd_cols, even_cols - odd_cols))
            for block in range(2):
                cols = slice(block * LANES, (block + 1) * LANES)
                beside = col_mask(view, block)
                b_re, b_im = halves[0][block], halves[1][block]
                p_re, p_im = placed[view, 0, rows, cols], placed[view, 1, rows, cols]
                for part, value in enumerate((p_re * b_re + p_im * b_im, p_re * b_im - p_im * b_re)):
                    if beyond is not None:
                        outer, value = jnp.where(beyond, value, zero), jnp.where(beyond, zero, value)
                        add(("corner", part), jnp.where(beside, outer, zero))
                        add(("row", part, block), jnp.where(beside, zero, outer))
                    add(("col", part), jnp.where(beside, value, zero))
                    add(("core", part, block), jnp.where(beside, zero, value))
        for part in range(2):
            cols_m[part, rows] = sums["col", part]
            if place is not None:
                corner_m[part, place : place + CHUNK] = sums["corner", part]
            for block in range(2):
                cols = slice(block * LANES, (block + 1) * LANES)
                g_core[part, rows, cols] = sums["core", part, block]
                if place is not None:
                    rows_m[part, place : place + CHUNK, cols] = sums["row", part, block]

    def packed(channel, re, im):
        to_right = jnp.where(low_lanes, re, swap_halves(im))
        to_left = jnp.where(low_lanes, swap_halves(im), re)
        return jnp.where(sends_right(channel), to_right, to_left)

    for part in range(2):
        bottom, top = rows_m[part, :m], rows_m[part, m:]
        cols = slice(part * size, (part + 1) * size)
        g_a[:, cols] = jnp.where(lower, bottom, top)
        g_b[:, cols] = jnp.where(lower, top, bottom)
    bottom = (corner_m[0, :m], corner_m[1, :m])
    top = (corner_m[0, m:], corner_m[1, m:])
    for number, channel in enumerate(chans):
        for row in range(0, size, CHUNK):
            rows = slice(row, row + CHUNK)
            g_x[number][rows] = packed(channel, cols_m[0, rows], cols_m[1, rows])
        below, above = packed(channel, *bottom), packed(channel, *top)
        place = 2 * size + number * LANES
        g_a[:, place : place + LANES] = jnp.where(lower, below, above)
        g_kb[number][...] = jnp.where(lower, above, below)


def views_call(chans, offsets, counts, core, placed, amplitude, tables, a_in, b_in, x_in, ka_in, kb_in):
    views, size = placed.shape[0], core.shape[1]
    count = len(chans)
    vmem = pl.BlockSpec(memory_space=pltpu.VMEM)
    smem = pl.BlockSpec(memory_space=pltpu.SMEM)
    shapes = [(2, size, size), (MARGIN, 2 * size + count * LANES), (MARGIN, 2 * size)]
    shapes += [(size, LANES)] * count + [(MARGIN, LANES)] * count
    full = pltpu.VMEM((views, 2, size, size), F32)
    tall = pltpu.VMEM((views, 2, 2 * size, size), BF16)
    wide = pltpu.VMEM((views, 2, size, 2 * size), BF16)
    outs = pl.pallas_call(
        functools.partial(views_kernel, chans),
        out_shape=[jax.ShapeDtypeStruct(shape, F32) for shape in shapes],
        in_specs=[smem] * 2 + [vmem] * (7 + 3 * count),
        out_specs=[vmem] * len(shapes),
        scratch_shapes=[
            pltpu.VMEM((2, size, LANES), F32),
            pltpu.VMEM((2, 2 * MARGIN, size), F32),
            pltpu.VMEM((2, 2 * MARGIN, LANES), F32),
            wide, full, tall, full, tall, full, wide, full,
        ],
        compiler_params=pltpu.CompilerParams(vmem_limit_bytes=40 * 1024 * 1024),
    )(offsets, counts, core, placed, amplitude, *tables, a_in, b_in, *x_in, *ka_in, *kb_in)
    return outs[0], outs[1], outs[2], outs[3 : 3 + count], outs[3 + count :]


def finish_kernel(chans, object_ref, g_core, a_in, b_in, *rest):
    count = len(chans)
    x_in, kb_in, out = rest[:count], rest[count : 2 * count], rest[-1]
    size = object_ref.shape[1]
    lower = lower_partner()
    a_start = pl.multiple_of(jnp.where(lower, size - MARGIN, 0), MARGIN)
    b_start = pl.multiple_of(jnp.where(lower, 0, size - MARGIN), MARGIN)
    for part in range(2):
        out[part] = object_ref[part] - step_size * g_core[part]
        cols = slice(part * size, (part + 1) * size)
        out[part, pl.ds(a_start, MARGIN)] -= step_size * a_in[:, cols]
        out[part, pl.ds(b_start, MARGIN)] -= step_size * b_in[:, cols]
    for number, channel in enumerate(chans):
        right = takes_right(channel)
        block = pl.multiple_of(jnp.where(right, size - LANES, 0), LANES)
        mine = ~half_lanes(right) if isinstance(right, bool) else (
            lane_ids() // (LANES // 2) == jnp.where(right, 1, 0)
        )
        edge, corner = x_in[number][...], kb_in[number][...]
        for part in range(2):
            value = edge if part == 0 else swap_halves(edge)
            out[part, :, pl.ds(block, LANES)] -= step_size * jnp.where(mine, value, 0.0)
            value = corner if part == 0 else swap_halves(corner)
            out[part, pl.ds(b_start, MARGIN), pl.ds(block, LANES)] -= step_size * jnp.where(
                mine, value, 0.0
            )


def finish_call(chans, object_field, g_core, a_in, b_in, x_in, kb_in):
    vmem = pl.BlockSpec(memory_space=pltpu.VMEM)
    return pl.pallas_call(
        functools.partial(finish_kernel, chans),
        out_shape=jax.ShapeDtypeStruct(object_field.shape, F32),
        in_specs=[vmem] * (4 + 2 * len(chans)),
        out_specs=vmem,
    )(object_field, g_core, a_in, b_in, *x_in, *kb_in)


def per_device(object_field, probe_field, intensity, view_offsets, view_counts):
    size = object_field.shape[1]
    mesh_rows, mesh_cols = lax.axis_size("row"), lax.axis_size("col")
    chans = channels(mesh_cols)
    by_right, by_left, order = dft_tables(size)
    a_pairs, b_pairs = row_pairs(mesh_rows, 0), row_pairs(mesh_rows, 1)
    lower = lower_partner()

    def swap_a(block):
        return lax.ppermute(block, "row", a_pairs)

    def swap_b(block):
        return lax.ppermute(block, "row", b_pairs)

    def swap_x(block, channel):
        return lax.ppermute(block, "col", channel[0])

    def swap_diagonal(block, channel):
        route = [
            (i * mesh_cols + k, j * mesh_cols + l) for i, j in b_pairs for k, l in channel[0]
        ]
        return lax.ppermute(block, ("row", "col"), route)

    def edge(block):
        return jnp.where(lower, block[size - MARGIN :], block[:MARGIN])

    packs = pack_call(object_field, chans)
    a_send, b_send, x_send, k_send = packs[0], packs[1], packs[2::2], packs[3::2]
    x_in = [swap_x(block, channel) for block, channel in zip(x_send, chans)]
    b_in = swap_b(b_send)
    kb_in = [swap_diagonal(block, channel) for block, channel in zip(k_send, chans)]
    a_in = swap_a(a_send)
    placed, amplitude = prepare_call(view_offsets, view_counts, probe_field, intensity, order)
    ka_in = [swap_a(edge(block)) for block in x_in]
    g_core, g_a, g_b, g_x, g_kb = views_call(
        chans, view_offsets, view_counts, object_field, placed, amplitude,
        (by_right, by_left), a_in, b_in, x_in, ka_in, kb_in,
    )
    a_in = swap_a(g_a)
    b_in = swap_b(g_b)
    x_send = []
    for number, block in enumerate(g_x):
        start = 2 * size + number * LANES
        corner = a_in[:, start : start + LANES]
        none = jnp.zeros((size - MARGIN, LANES), F32)
        placed_corner = jnp.where(
            lower, jnp.concatenate([none, corner]), jnp.concatenate([corner, none])
        )
        x_send.append(block + placed_corner)
    x_in = [swap_x(block, channel) for block, channel in zip(x_send, chans)]
    kb_in = [swap_diagonal(block, channel) for block, channel in zip(g_kb, chans)]
    return finish_call(chans, object_field, g_core, a_in, b_in, x_in, kb_in)


def solution(mesh):
    in_specs = (
        P(None, "row", "col"),
        P(),
        P("row", "col", None, None, None),
        P("row", "col", None, None),
        P("row", "col"),
    )
    out_specs = P(None, "row", "col")
    return jax.shard_map(
        per_device, mesh=mesh, in_specs=in_specs, out_specs=out_specs, check_vma=False
    )
```

```python
import functools
import math

import jax
import jax.numpy as jnp
import ml_dtypes
import numpy as np
from jax import lax
from jax.experimental import pallas as pl
from jax.experimental.pallas import tpu as pltpu
from jax.sharding import PartitionSpec as P

MARGIN = 64
LANES = 128
CHUNK = 64

smooth_eps = 0.1
step_size = 0.2

F32 = jnp.float32
BF16 = jnp.bfloat16


def dft_tables(length):
    half = length // 2
    counter = np.arange(half)
    factor = 1.0 / math.sqrt(length)
    product = np.outer(counter, counter)
    even = np.exp(-2j * np.pi * (product % half) / half) * factor
    odd = np.exp(-2j * np.pi * ((2 * product + counter[:, None]) % length) / length) * factor

    def as_real(table):
        return np.block([[table.real, table.imag], [-table.imag, table.real]])

    def parts(table):
        high = table.astype(ml_dtypes.bfloat16)
        low = (table - high.astype(np.float64)).astype(ml_dtypes.bfloat16)
        return high, low

    even, odd = as_real(even), as_real(odd)
    by_right = [np.concatenate(parts(t), 0) for t in (even, odd, even.T, odd.T)]
    by_left = [np.concatenate(parts(t), 1) for t in (even.T, odd.T, even, odd)]
    return np.stack(by_right), np.stack(by_left)


def channels(mesh_cols):
    if mesh_cols == 1:
        return []
    if mesh_cols == 2:
        return [([(0, 1), (1, 0)], None, None)]
    forward = [(i, i + 1) for i in range(mesh_cols - 1)]
    return [(forward, True, False), ([(j, i) for i, j in forward], False, True)]


def row_pairs(count, first):
    pairs = [(i, i + 1) for i in range(first, count - 1, 2)]
    return pairs + [(j, i) for i, j in pairs]


def spare_route(pairs, mesh_rows, mesh_cols):
    rows = [i for i in range(mesh_rows) if i not in dict(pairs)]
    if mesh_cols % 2:
        return []
    return [(i * mesh_cols + k, i * mesh_cols + (k ^ 1)) for i in rows for k in range(mesh_cols)]


def b_partner():
    row = lax.axis_index("row")
    return jnp.where(lower_partner(), row > 0, row < lax.axis_size("row") - 1)


def sends_right(channel):
    return lax.axis_index("col") == 0 if channel[1] is None else channel[1]


def takes_right(channel):
    return lax.axis_index("col") == 0 if channel[2] is None else channel[2]


def lower_partner():
    return lax.rem(lax.axis_index("row"), 2) == 0


def lane_ids():
    return lax.broadcasted_iota(jnp.int32, (1, LANES), 1)


def half_lanes(right):
    low = lane_ids() < LANES // 2
    if isinstance(right, bool):
        return low if right else ~low
    return lane_ids() // (LANES // 2) == jnp.where(right, 0, 1)


def split(value):
    high = value.astype(BF16)
    return high, (value - high.astype(F32)).astype(BF16)


def dot(first, second):
    return jnp.dot(first, second, preferred_element_type=F32)


def swap_halves(block):
    return pltpu.roll(block, LANES // 2, 1)


def pack_kernel(chans, object_ref, a_ref, b_ref, *edge_refs):
    size = object_ref.shape[1]
    top, bottom = pl.ds(0, MARGIN), pl.ds(size - MARGIN, MARGIN)
    lower = lower_partner()
    for part in range(2):
        head, tail = object_ref[part, top, :], object_ref[part, bottom, :]
        a_ref[part] = jnp.where(lower, tail, head)
        b_ref[part] = jnp.where(lower, head, tail)
    for number, channel in enumerate(chans):
        right = sends_right(channel)
        x_ref, ka_ref, kb_ref = edge_refs[3 * number : 3 * number + 3]
        low = lane_ids() < LANES // 2
        for start in range(0, size, CHUNK):
            rows = slice(start, start + CHUNK)
            left_edge = jnp.where(
                low, object_ref[0, rows, :LANES], swap_halves(object_ref[1, rows, :LANES])
            )
            right_edge = jnp.where(
                low,
                swap_halves(object_ref[1, rows, size - LANES :]),
                object_ref[0, rows, size - LANES :],
            )
            x_ref[rows] = jnp.where(right, right_edge, left_edge)
        ka_ref[...] = jnp.where(lower, x_ref[size - MARGIN :], x_ref[:MARGIN])
        kb_ref[...] = jnp.where(lower, x_ref[:MARGIN], x_ref[size - MARGIN :])


def pack_call(object_field, chans):
    size = object_field.shape[1]
    shapes = [(2, MARGIN, size)] * 2 + [(size, LANES), (MARGIN, LANES), (MARGIN, LANES)] * len(chans)
    vmem = pl.BlockSpec(memory_space=pltpu.VMEM)
    return pl.pallas_call(
        functools.partial(pack_kernel, chans),
        out_shape=[jax.ShapeDtypeStruct(shape, F32) for shape in shapes],
        in_specs=[vmem],
        out_specs=[vmem] * len(shapes),
        compiler_params=pltpu.CompilerParams(vmem_limit_bytes=4 * 1024 * 1024),
    )(object_field)


def prepare_kernel(offsets, counts, probe, intensity, placed, amplitude, doubled, measured, sems):
    views, size = measured.shape[0], probe.shape[1]
    half = size // 2
    copies = [
        pltpu.make_async_copy(probe, doubled.at[:, pl.ds(size * i, size)], sems.at[i]) for i in range(2)
    ]
    copies += [
        pltpu.make_async_copy(intensity.at[0, 0, view], measured.at[view], sems.at[2 + view])
        for view in range(views)
    ]
    for copy in copies:
        copy.start()
    source = lax.broadcasted_iota(jnp.int32, (size, size), 0)
    target = lax.broadcasted_iota(jnp.int32, (size, size), 1)
    order = (target == (source % 2) * half + source // 2).astype(F32).astype(BF16)
    sublane = lax.broadcasted_iota(jnp.int32, (1, 8, 1), 1)
    copies[0].wait()
    copies[1].wait()
    for view in range(views):
        shift_row = lax.rem(offsets[0, 0, 0, view] - MARGIN + size, size)
        shift_col = lax.rem(offsets[0, 0, 1, view] - MARGIN + size, size)
        start = lax.rem(size - shift_row, size)
        whole = pl.multiple_of((start // 8) * 8, 8)
        rest = start - whole
        for part in range(2):
            for row in range(0, size, CHUNK):
                block = doubled[part, pl.ds(whole + row, CHUNK + 8), :]
                block = pltpu.roll(block, shift_col, 1).reshape(CHUNK // 8 + 1, 8, size)
                block = pltpu.roll(block, lax.rem(8 - rest, 8), 1)
                block = jnp.where(sublane < 8 - rest, block[:-1], block[1:])
                placed[view, part, row : row + CHUNK] = block.reshape(CHUNK, size)
    for view in range(views):
        copies[2 + view].wait()
        valid = (view < counts[0, 0]).astype(F32)
        power = measured[view] + smooth_eps
        high, low = split(power * lax.rsqrt(power) * valid)
        ordered = dot(high, order) + dot(low, order)
        amplitude[view, 0] = ordered[:, :half]
        amplitude[view, 1] = ordered[:, half:]


def prepare_call(offsets, counts, probe, intensity):
    views, size = intensity.shape[2], probe.shape[1]
    vmem = pl.BlockSpec(memory_space=pltpu.VMEM)
    smem = pl.BlockSpec(memory_space=pltpu.SMEM)
    return pl.pallas_call(
        prepare_kernel,
        out_shape=[
            jax.ShapeDtypeStruct((views, 2, size, size), F32),
            jax.ShapeDtypeStruct((views, 2, size, size // 2), F32),
        ],
        in_specs=[smem, smem] + [pl.BlockSpec(memory_space=pl.ANY)] * 2,
        out_specs=[vmem] * 2,
        scratch_shapes=[
            pltpu.VMEM((2, 2 * size, size), F32),
            pltpu.VMEM((views, size, size), F32),
            pltpu.SemaphoreType.DMA((2 + views,)),
        ],
        compiler_params=pltpu.CompilerParams(vmem_limit_bytes=16 * 1024 * 1024),
        cost_estimate=pl.CostEstimate(flops=2 * 10**9, bytes_accessed=6 * 10**6, transcendentals=0),
    )(offsets, counts, probe, intensity)


def views_kernel(chans, offsets, counts, core, placed, amplitude, right, left, a_in, b_in, *rest):
    count = len(chans)
    x_in, ka_in, kb_in = rest[:count], rest[count : 2 * count], rest[2 * count : 3 * count]
    rest = rest[3 * count :]
    g_core, g_a, g_b = rest[:3]
    g_x, g_ka = rest[3 : 3 + count], rest[3 + count : 3 + 2 * count]
    g_kb = rest[3 + 2 * count : 3 + 3 * count]
    cols_m, rows_m, corner_m, s1, y, s2, z, s3, u, s4, g = rest[3 + 3 * count :]
    views, size = placed.shape[0], core.shape[1]
    half, m = size // 2, MARGIN
    lower, partner = lower_partner(), b_partner()
    low_lanes = lane_ids() < LANES // 2
    zero = jnp.zeros((CHUNK, LANES), F32)

    def unpack(blocks):
        re = im = None
        for channel, block in zip(chans, blocks):
            mine = half_lanes(takes_right(channel))
            re = jnp.where(mine, block, 0.0 if re is None else re)
            im = jnp.where(mine, swap_halves(block), 0.0 if im is None else im)
        return (re, im) if blocks else (zero, zero)

    for row in range(0, size, CHUNK):
        rows = slice(row, row + CHUNK)
        cols_m[0, rows], cols_m[1, rows] = unpack([ref[rows] for ref in x_in])
    corner_a = unpack([ref[...] for ref in ka_in])
    corner_b = [jnp.where(partner, part, 0.0) for part in unpack([ref[...] for ref in kb_in])]
    for part in range(2):
        a_rows, b_rows = a_in[part], jnp.where(partner, b_in[part], 0.0)
        rows_m[part, :m] = jnp.where(lower, a_rows, b_rows)
        rows_m[part, m:] = jnp.where(lower, b_rows, a_rows)
        corner_m[part, :m] = jnp.where(lower, corner_a[part], corner_b[part])
        corner_m[part, m:] = jnp.where(lower, corner_b[part], corner_a[part])

    def by_right(lhs, t):
        out = dot(lhs[:, :size], right[t, :size]) + dot(lhs[:, size:], right[t, :size])
        return out + dot(lhs[:, :size], right[t, size:])

    def by_left(t, rhs):
        out = dot(left[t, :, :size], rhs[:size]) + dot(left[t, :, :size], rhs[size:])
        return out + dot(left[t, :, size:], rhs[:size])

    def put_below(ref, row, col, value):
        high, low = split(value)
        rows, cols = value.shape
        ref[row : row + rows, col : col + cols] = high
        ref[size + row : size + row + rows, col : col + cols] = low

    def put_beside(ref, row, col, value):
        high, low = split(value)
        rows, cols = value.shape
        ref[row : row + rows, col : col + cols] = high
        ref[row : row + rows, size + col : size + col + cols] = low

    def row_mask(view, row):
        ids = row + lax.broadcasted_iota(jnp.int32, (CHUNK, LANES), 0)
        if row < m:
            return ids < offsets[0, 0, 0, view] - m, row
        if row >= size - m:
            return ids >= size - m + offsets[0, 0, 0, view], row - size + 2 * m
        return None, None

    def col_mask(view, block):
        if block == 0:
            return lane_ids() < offsets[0, 0, 1, view] - m
        return lane_ids() >= m + offsets[0, 0, 1, view]

    def patch(view, row, block):
        cols = slice(block * LANES, (block + 1) * LANES)
        rows = slice(row, row + CHUNK)
        beside = col_mask(view, block)
        beyond, place = row_mask(view, row)
        found = []
        for part in range(2):
            value = jnp.where(beside, cols_m[part, rows], core[part, rows, cols])
            if beyond is not None:
                there = slice(place, place + CHUNK)
                outer = jnp.where(beside, corner_m[part, there], rows_m[part, there, cols])
                value = jnp.where(beyond, outer, value)
            found.append(value)
        return found

    for view in range(views):
        for row in range(0, size, CHUNK):
            rows = slice(row, row + CHUNK)
            waves = []
            for block in range(2):
                cols = slice(block * LANES, (block + 1) * LANES)
                o_re, o_im = patch(view, row, block)
                p_re, p_im = placed[view, 0, rows, cols], placed[view, 1, rows, cols]
                waves.append((p_re * o_re - p_im * o_im, p_re * o_im + p_im * o_re))
            for part in range(2):
                put_beside(s1.at[view, 0], row, part * half, waves[0][part] + waves[1][part])
                put_beside(s1.at[view, 1], row, part * half, waves[0][part] - waves[1][part])
        for odd in range(2):
            y[view, odd] = by_right(s1.at[view, odd], odd)
        for odd in range(2):
            for part in range(2):
                cols = slice(part * half, (part + 1) * half)
                for row in range(0, half, CHUNK):
                    above = y[view, odd, row : row + CHUNK, cols]
                    below = y[view, odd, half + row : half + row + CHUNK, cols]
                    put_below(s2.at[view, 0], part * half + row, odd * half, above + below)
                    put_below(s2.at[view, 1], part * half + row, odd * half, above - below)
        for odd in range(2):
            z[view, odd] = by_left(odd, s2.at[view, odd])
        valid = (view < counts[0, 0]).astype(F32)
        for odd in range(2):
            for row in range(0, half, CHUNK):
                re, im = z[view, odd, row : row + CHUNK], z[view, odd, half + row : half + row + CHUNK]
                taken = pl.ds(2 * row + odd, CHUNK, stride=2)
                wanted = jnp.concatenate([amplitude[view, 0, taken], amplitude[view, 1, taken]], 1)
                scaling = valid - wanted * lax.rsqrt(re * re + im * im + smooth_eps)
                put_below(s3.at[view, odd], row, 0, re * scaling)
                put_below(s3.at[view, odd], half + row, 0, im * scaling)
        for odd in range(2):
            u[view, odd] = by_left(2 + odd, s3.at[view, odd])
        for part in range(2):
            for row in range(0, half, CHUNK):
                rows = slice(part * half + row, part * half + row + CHUNK)
                even_rows, odd_rows = u[view, 0, rows], u[view, 1, rows]
                for value, place in ((even_rows + odd_rows, row), (even_rows - odd_rows, half + row)):
                    put_beside(s4.at[view, 0], place, part * half, value[:, :half])
                    put_beside(s4.at[view, 1], place, part * half, value[:, half:])
        for odd in range(2):
            g[view, odd] = by_right(s4.at[view, odd], 2 + odd)

    for row in range(0, size, CHUNK):
        rows = slice(row, row + CHUNK)
        sums = {}

        def add(key, value):
            sums[key] = sums[key] + value if key in sums else value

        for view in range(views):
            beyond, place = row_mask(view, row)
            halves = []
            for part in range(2):
                cols = slice(part * half, (part + 1) * half)
                even_cols, odd_cols = g[view, 0, rows, cols], g[view, 1, rows, cols]
                halves.append((even_cols + odd_cols, even_cols - odd_cols))
            for block in range(2):
                cols = slice(block * LANES, (block + 1) * LANES)
                beside = col_mask(view, block)
                b_re, b_im = halves[0][block], halves[1][block]
                p_re, p_im = placed[view, 0, rows, cols], placed[view, 1, rows, cols]
                for part, value in enumerate((p_re * b_re + p_im * b_im, p_re * b_im - p_im * b_re)):
                    if beyond is not None:
                        outer, value = jnp.where(beyond, value, zero), jnp.where(beyond, zero, value)
                        add(("corner", part), jnp.where(beside, outer, zero))
                        add(("row", part, block), jnp.where(beside, zero, outer))
                    add(("col", part), jnp.where(beside, value, zero))
                    add(("core", part, block), jnp.where(beside, zero, value))
        for part in range(2):
            cols_m[part, rows] = sums["col", part]
            if place is not None:
                corner_m[part, place : place + CHUNK] = sums["corner", part]
            for block in range(2):
                cols = slice(block * LANES, (block + 1) * LANES)
                g_core[part, rows, cols] = sums["core", part, block]
                if place is not None:
                    rows_m[part, place : place + CHUNK, cols] = sums["row", part, block]

    def packed(channel, re, im):
        to_right = jnp.where(low_lanes, re, swap_halves(im))
        to_left = jnp.where(low_lanes, swap_halves(im), re)
        return jnp.where(sends_right(channel), to_right, to_left)

    for part in range(2):
        bottom, top = rows_m[part, :m], rows_m[part, m:]
        g_a[part] = jnp.where(lower, bottom, top)
        g_b[part] = jnp.where(lower, top, bottom)
    bottom = (corner_m[0, :m], corner_m[1, :m])
    top = (corner_m[0, m:], corner_m[1, m:])
    for number, channel in enumerate(chans):
        for row in range(0, size, CHUNK):
            rows = slice(row, row + CHUNK)
            g_x[number][rows] = packed(channel, cols_m[0, rows], cols_m[1, rows])
        below, above = packed(channel, *bottom), packed(channel, *top)
        g_ka[number][...] = jnp.where(lower, below, above)
        g_kb[number][...] = jnp.where(lower, above, below)


def views_call(chans, offsets, counts, core, placed, amplitude, tables, a_in, b_in, x_in, ka_in, kb_in):
    views, size = placed.shape[0], core.shape[1]
    count = len(chans)
    vmem = pl.BlockSpec(memory_space=pltpu.VMEM)
    smem = pl.BlockSpec(memory_space=pltpu.SMEM)
    shapes = [(2, size, size), (2, MARGIN, size), (2, MARGIN, size)]
    shapes += [(size, LANES)] * count + [(MARGIN, LANES)] * (2 * count)
    full = pltpu.VMEM((views, 2, size, size), F32)
    tall = pltpu.VMEM((views, 2, 2 * size, size), BF16)
    wide = pltpu.VMEM((views, 2, size, 2 * size), BF16)
    outs = pl.pallas_call(
        functools.partial(views_kernel, chans),
        out_shape=[jax.ShapeDtypeStruct(shape, F32) for shape in shapes],
        in_specs=[smem] * 2 + [vmem] * (7 + 3 * count),
        out_specs=[vmem] * len(shapes),
        scratch_shapes=[
            pltpu.VMEM((2, size, LANES), F32),
            pltpu.VMEM((2, 2 * MARGIN, size), F32),
            pltpu.VMEM((2, 2 * MARGIN, LANES), F32),
            wide, full, tall, full, tall, full, wide, full,
        ],
        compiler_params=pltpu.CompilerParams(vmem_limit_bytes=40 * 1024 * 1024),
    )(offsets, counts, core, placed, amplitude, *tables, a_in, b_in, *x_in, *ka_in, *kb_in)
    return (*outs[:3], outs[3 : 3 + count], outs[3 + count : 3 + 2 * count], outs[3 + 2 * count :])


def finish_kernel(chans, object_ref, g_core, a_in, b_in, *rest):
    count = len(chans)
    x_in, ka_in, kb_in = rest[:count], rest[count : 2 * count], rest[2 * count : 3 * count]
    out = rest[-1]
    size = object_ref.shape[1]
    lower = lower_partner()
    a_rows = pl.ds(pl.multiple_of(jnp.where(lower, size - MARGIN, 0), MARGIN), MARGIN)
    b_rows = pl.ds(pl.multiple_of(jnp.where(lower, 0, size - MARGIN), MARGIN), MARGIN)
    columns = []
    for channel in chans:
        right = takes_right(channel)
        mine = lane_ids() // (LANES // 2) == jnp.where(right, 1, 0)
        block = pl.multiple_of(jnp.where(right, size - LANES, 0), LANES)
        columns.append((mine, pl.ds(block, LANES)))

    def take(place, value):
        out[place] -= step_size * value

    def take_packed(rows, column, block):
        mine, lanes = column
        take((0, rows, lanes), jnp.where(mine, block, 0.0))
        take((1, rows, lanes), jnp.where(mine, swap_halves(block), 0.0))

    for part in range(2):
        out[part] = object_ref[part] - step_size * g_core[part]
        take((part, a_rows), a_in[part])
    for number, column in enumerate(columns):
        take_packed(slice(None), column, x_in[number][...])
        take_packed(a_rows, column, ka_in[number][...])

    @pl.when(b_partner())
    def _():
        for part in range(2):
            take((part, b_rows), b_in[part])
        for number, column in enumerate(columns):
            take_packed(b_rows, column, kb_in[number][...])


def finish_call(chans, object_field, g_core, a_in, b_in, x_in, ka_in, kb_in):
    vmem = pl.BlockSpec(memory_space=pltpu.VMEM)
    return pl.pallas_call(
        functools.partial(finish_kernel, chans),
        out_shape=jax.ShapeDtypeStruct(object_field.shape, F32),
        in_specs=[vmem] * (4 + 3 * len(chans)),
        out_specs=vmem,
        compiler_params=pltpu.CompilerParams(vmem_limit_bytes=6 * 1024 * 1024),
    )(object_field, g_core, a_in, b_in, *x_in, *ka_in, *kb_in)


def per_device(object_field, probe_field, intensity, view_offsets, view_counts):
    size = object_field.shape[1]
    mesh_rows, mesh_cols = lax.axis_size("row"), lax.axis_size("col")
    chans = channels(mesh_cols)
    tables = dft_tables(size)
    a_pairs, b_pairs = row_pairs(mesh_rows, 0), row_pairs(mesh_rows, 1)
    spare = spare_route(b_pairs, mesh_rows, mesh_cols)

    def over_rows(block, pairs, extra):
        route = [(i * mesh_cols + k, j * mesh_cols + k) for i, j in pairs for k in range(mesh_cols)]
        return lax.ppermute(block, ("row", "col"), route + extra)

    def across(block, pairs, extra, channel):
        route = [(i * mesh_cols + k, j * mesh_cols + l) for i, j in pairs for k, l in channel[0]]
        return lax.ppermute(block, ("row", "col"), route + (extra if mesh_cols == 2 else []))

    def exchange(a_send, b_send, x_send, ka_send, kb_send):
        x_in = [lax.ppermute(block, "col", channel[0]) for block, channel in zip(x_send, chans)]
        b_in = over_rows(b_send, b_pairs, spare)
        kb_in = [across(block, b_pairs, spare, channel) for block, channel in zip(kb_send, chans)]
        ka_in = [across(block, a_pairs, [], channel) for block, channel in zip(ka_send, chans)]
        a_in = over_rows(a_send, a_pairs, [])
        return a_in, b_in, x_in, ka_in, kb_in

    packs = pack_call(object_field, chans)
    offsets = jnp.swapaxes(view_offsets, 2, 3)
    margins = exchange(packs[0], packs[1], packs[2::3], packs[3::3], packs[4::3])
    placed, amplitude = prepare_call(offsets, view_counts, probe_field, intensity)
    g_core, *sends = views_call(
        chans, offsets, view_counts, object_field, placed, amplitude, tables, *margins
    )
    return finish_call(chans, object_field, g_core, *exchange(*sends))


def solution(mesh):
    in_specs = (
        P(None, "row", "col"),
        P(),
        P("row", "col", None, None, None),
        P("row", "col", None, None),
        P("row", "col"),
    )
    out_specs = P(None, "row", "col")
    return jax.shard_map(
        per_device, mesh=mesh, in_specs=in_specs, out_specs=out_specs, check_vma=False
    )
```

```python
import functools
import itertools
import math

import jax
import jax.numpy as jnp
import ml_dtypes
import numpy as np
from jax import lax
from jax.experimental import pallas as pl
from jax.experimental.pallas import tpu as pltpu
from jax.sharding import PartitionSpec as P

MARGIN = 64
LANES = 128
CHUNK = 64
STAGGER = 4

smooth_eps = 0.1
step_size = 0.2

F32 = jnp.float32
BF16 = jnp.bfloat16


def dft_tables(length):
    half = length // 2
    counter = np.arange(half)
    factor = 1.0 / math.sqrt(length)
    product = np.outer(counter, counter)
    even = np.exp(-2j * np.pi * (product % half) / half) * factor
    odd = np.exp(-2j * np.pi * ((2 * product + counter[:, None]) % length) / length) * factor

    def as_real(table):
        return np.block([[table.real, table.imag], [-table.imag, table.real]])

    def parts(table):
        high = table.astype(ml_dtypes.bfloat16)
        low = (table - high.astype(np.float64)).astype(ml_dtypes.bfloat16)
        return high, low

    even, odd = as_real(even), as_real(odd)
    by_right = [np.concatenate(parts(t), 0) for t in (even, odd, even.T, odd.T)]
    by_left = [np.concatenate(parts(t), 1) for t in (even.T, odd.T, even, odd)]
    return np.stack(by_right), np.stack(by_left)


def channels(mesh_cols):
    if mesh_cols == 1:
        return []
    if mesh_cols == 2:
        return [([(0, 1), (1, 0)], None, None)]
    forward = [(i, i + 1) for i in range(mesh_cols - 1)]
    return [(forward, True, False), ([(j, i) for i, j in forward], False, True)]


def row_pairs(count, first):
    pairs = [(i, i + 1) for i in range(first, count - 1, 2)]
    return pairs + [(j, i) for i, j in pairs]


def spare_route(pairs, mesh_rows, mesh_cols):
    rows = [i for i in range(mesh_rows) if i not in dict(pairs)]
    if mesh_cols % 2:
        return []
    return [(i * mesh_cols + k, i * mesh_cols + (k ^ 1)) for i in rows for k in range(mesh_cols)]


def b_partner():
    row = lax.axis_index("row")
    return jnp.where(lower_partner(), row > 0, row < lax.axis_size("row") - 1)


def sends_right(channel):
    return lax.axis_index("col") == 0 if channel[1] is None else channel[1]


def takes_right(channel):
    return lax.axis_index("col") == 0 if channel[2] is None else channel[2]


def lower_partner():
    return lax.rem(lax.axis_index("row"), 2) == 0


def lane_ids():
    return lax.broadcasted_iota(jnp.int32, (1, LANES), 1)


def half_lanes(right):
    low = lane_ids() < LANES // 2
    if isinstance(right, bool):
        return low if right else ~low
    return lane_ids() // (LANES // 2) == jnp.where(right, 0, 1)


def split(value):
    high = value.astype(BF16)
    return high, (value - high.astype(F32)).astype(BF16)


def dot(first, second):
    return jnp.dot(first, second, preferred_element_type=F32)


def swap_halves(block):
    return pltpu.roll(block, LANES // 2, 1)


def fetch(pairs, sems):
    copies = [pltpu.make_async_copy(source, target, sems.at[i]) for i, (source, target) in enumerate(pairs)]
    for copy in copies:
        copy.start()
    return copies


def pack_kernel(chans, object_ref, a_ref, b_ref, *edge_refs):
    size = object_ref.shape[1]
    top, bottom = pl.ds(0, MARGIN), pl.ds(size - MARGIN, MARGIN)
    lower = lower_partner()
    for part in range(2):
        head, tail = object_ref[part, top, :], object_ref[part, bottom, :]
        a_ref[part] = jnp.where(lower, tail, head)
        b_ref[part] = jnp.where(lower, head, tail)
    for number, channel in enumerate(chans):
        right = sends_right(channel)
        x_ref, ka_ref, kb_ref = edge_refs[3 * number : 3 * number + 3]
        low = lane_ids() < LANES // 2
        for start in range(0, size, CHUNK):
            rows = slice(start, start + CHUNK)
            left_edge = jnp.where(
                low, object_ref[0, rows, :LANES], swap_halves(object_ref[1, rows, :LANES])
            )
            right_edge = jnp.where(
                low,
                swap_halves(object_ref[1, rows, size - LANES :]),
                object_ref[0, rows, size - LANES :],
            )
            x_ref[rows] = jnp.where(right, right_edge, left_edge)
        ka_ref[...] = jnp.where(lower, x_ref[size - MARGIN :], x_ref[:MARGIN])
        kb_ref[...] = jnp.where(lower, x_ref[:MARGIN], x_ref[size - MARGIN :])


def pack_call(object_field, chans):
    size = object_field.shape[1]
    shapes = [(2, MARGIN, size)] * 2 + [(size, LANES), (MARGIN, LANES), (MARGIN, LANES)] * len(chans)
    vmem = pl.BlockSpec(memory_space=pltpu.VMEM)
    return pl.pallas_call(
        functools.partial(pack_kernel, chans),
        out_shape=[jax.ShapeDtypeStruct(shape, F32) for shape in shapes],
        in_specs=[vmem],
        out_specs=[vmem] * len(shapes),
        compiler_params=pltpu.CompilerParams(vmem_limit_bytes=4 * 1024 * 1024),
    )(object_field)


def prepare_kernel(
    offsets_in, counts_in, probe, intensity, placed, amplitude, offsets, counts, doubled, measured, sems
):
    views, size = measured.shape[0], probe.shape[1]
    half = size // 2
    copies = fetch(
        [(offsets_in, offsets), (counts_in, counts)]
        + [(probe, doubled.at[:, pl.ds(size * i, size)]) for i in range(2)]
        + [(intensity.at[0, 0, view], measured.at[view]) for view in range(views)],
        sems,
    )
    source = lax.broadcasted_iota(jnp.int32, (size, size), 0)
    target = lax.broadcasted_iota(jnp.int32, (size, size), 1)
    order = (target == (source % 2) * half + source // 2).astype(F32).astype(BF16)
    sublane = lax.broadcasted_iota(jnp.int32, (1, 8, 1), 1)
    for copy in copies[:4]:
        copy.wait()
    for view in range(views):
        shift_row = lax.rem(offsets[0, 0, 0, view] - MARGIN + size, size)
        shift_col = lax.rem(offsets[0, 0, 1, view] - MARGIN + size, size)
        start = lax.rem(size - shift_row, size)
        whole = pl.multiple_of((start // 8) * 8, 8)
        rest = start - whole
        for part in range(2):
            for row in range(0, size, CHUNK):
                block = doubled[part, pl.ds(whole + row, CHUNK + 8), :]
                block = pltpu.roll(block, shift_col, 1).reshape(CHUNK // 8 + 1, 8, size)
                block = pltpu.roll(block, lax.rem(8 - rest, 8), 1)
                block = jnp.where(sublane < 8 - rest, block[:-1], block[1:])
                placed[view, part, row : row + CHUNK] = block.reshape(CHUNK, size)
    for view in range(views):
        copies[4 + view].wait()
        valid = (view < counts[0, 0]).astype(F32)
        power = measured[view] + smooth_eps
        high, low = split(power * lax.rsqrt(power) * valid)
        ordered = dot(high, order) + dot(low, order)
        amplitude[view, 0] = ordered[:, :half]
        amplitude[view, 1] = ordered[:, half:]


def prepare_call(offsets, counts, probe, intensity):
    views, size = intensity.shape[2], probe.shape[1]
    vmem = pl.BlockSpec(memory_space=pltpu.VMEM)
    return pl.pallas_call(
        prepare_kernel,
        out_shape=[
            jax.ShapeDtypeStruct((views, 2, size, size), F32),
            jax.ShapeDtypeStruct((views, 2, size, size // 2), F32),
        ],
        in_specs=[pl.BlockSpec(memory_space=pltpu.HBM)] * 4,
        out_specs=[vmem] * 2,
        scratch_shapes=[
            pltpu.SMEM(offsets.shape, jnp.int32),
            pltpu.SMEM(counts.shape, jnp.int32),
            pltpu.VMEM((2, 2 * size, size), F32),
            pltpu.VMEM((views, size, size), F32),
            pltpu.SemaphoreType.DMA((4 + views,)),
        ],
        compiler_params=pltpu.CompilerParams(vmem_limit_bytes=16 * 1024 * 1024),
        cost_estimate=pl.CostEstimate(flops=2 * 10**9, bytes_accessed=6 * 10**6, transcendentals=0),
    )(offsets, counts, probe, intensity)


def views_kernel(chans, offsets_in, counts_in, core, placed, amplitude, right, left, a_in, b_in, *rest):
    count = len(chans)
    x_in, ka_in, kb_in = rest[:count], rest[count : 2 * count], rest[2 * count : 3 * count]
    rest = rest[3 * count :]
    g_core, g_a, g_b = rest[:3]
    g_x, g_ka = rest[3 : 3 + count], rest[3 + count : 3 + 2 * count]
    g_kb = rest[3 + 2 * count : 3 + 3 * count]
    offsets, counts, sems, cols_m, rows_m, corner_m, s1, y, s2, z, s3, u, s4, g = rest[3 + 3 * count :]
    copies = fetch([(offsets_in, offsets), (counts_in, counts)], sems)
    views, size = placed.shape[0], core.shape[1]
    half, m = size // 2, MARGIN
    lower, partner = lower_partner(), b_partner()
    low_lanes = lane_ids() < LANES // 2
    zero = jnp.zeros((CHUNK, LANES), F32)

    def unpack(blocks):
        re = im = None
        for channel, block in zip(chans, blocks):
            mine = half_lanes(takes_right(channel))
            re = jnp.where(mine, block, 0.0 if re is None else re)
            im = jnp.where(mine, swap_halves(block), 0.0 if im is None else im)
        return (re, im) if blocks else (jnp.zeros((MARGIN, LANES), F32),) * 2

    for row in range(0, size, CHUNK):
        rows = slice(row, row + CHUNK)
        cols_m[0, rows], cols_m[1, rows] = unpack([ref[rows] for ref in x_in]) if chans else (zero, zero)
    corner_a = unpack([ref[...] for ref in ka_in])
    corner_b = [jnp.where(partner, part, 0.0) for part in unpack([ref[...] for ref in kb_in])]
    for part in range(2):
        a_rows, b_rows = a_in[part], jnp.where(partner, b_in[part], 0.0)
        rows_m[part, :m] = jnp.where(lower, a_rows, b_rows)
        rows_m[part, m:] = jnp.where(lower, b_rows, a_rows)
        corner_m[part, :m] = jnp.where(lower, corner_a[part], corner_b[part])
        corner_m[part, m:] = jnp.where(lower, corner_b[part], corner_a[part])

    for copy in copies:
        copy.wait()

    def by_right(lhs, t):
        out = dot(lhs[:, :size], right[t, :size]) + dot(lhs[:, size:], right[t, :size])
        return out + dot(lhs[:, :size], right[t, size:])

    def by_left(t, rhs):
        out = dot(left[t, :, :size], rhs[:size]) + dot(left[t, :, :size], rhs[size:])
        return out + dot(left[t, :, size:], rhs[:size])

    def put_below(ref, row, col, value):
        high, low = split(value)
        rows, cols = value.shape
        ref[row : row + rows, col : col + cols] = high
        ref[size + row : size + row + rows, col : col + cols] = low

    def put_beside(ref, row, col, value):
        high, low = split(value)
        rows, cols = value.shape
        ref[row : row + rows, col : col + cols] = high
        ref[row : row + rows, size + col : size + col + cols] = low

    def row_mask(view, row):
        ids = row + lax.broadcasted_iota(jnp.int32, (CHUNK, LANES), 0)
        if row < m:
            return ids < offsets[0, 0, 0, view] - m, row
        if row >= size - m:
            return ids >= size - m + offsets[0, 0, 0, view], row - size + 2 * m
        return None, None

    def col_mask(view, block):
        if block == 0:
            return lane_ids() < offsets[0, 0, 1, view] - m
        return lane_ids() >= m + offsets[0, 0, 1, view]

    def patch(view, row, block):
        cols = slice(block * LANES, (block + 1) * LANES)
        rows = slice(row, row + CHUNK)
        beside = col_mask(view, block)
        beyond, place = row_mask(view, row)
        found = []
        for part in range(2):
            value = jnp.where(beside, cols_m[part, rows], core[part, rows, cols])
            if beyond is not None:
                there = slice(place, place + CHUNK)
                outer = jnp.where(beside, corner_m[part, there], rows_m[part, there, cols])
                value = jnp.where(beyond, outer, value)
            found.append(value)
        return found

    def steps(view):
        for row in range(0, size, CHUNK):
            rows = slice(row, row + CHUNK)
            waves = []
            for block in range(2):
                cols = slice(block * LANES, (block + 1) * LANES)
                o_re, o_im = patch(view, row, block)
                p_re, p_im = placed[view, 0, rows, cols], placed[view, 1, rows, cols]
                waves.append((p_re * o_re - p_im * o_im, p_re * o_im + p_im * o_re))
            for part in range(2):
                put_beside(s1.at[view, 0], row, part * half, waves[0][part] + waves[1][part])
                put_beside(s1.at[view, 1], row, part * half, waves[0][part] - waves[1][part])
            yield
        for odd in range(2):
            y[view, odd] = by_right(s1.at[view, odd], odd)
            yield
        for odd in range(2):
            for row in range(0, half, CHUNK):
                for part in range(2):
                    cols = slice(part * half, (part + 1) * half)
                    above = y[view, odd, row : row + CHUNK, cols]
                    below = y[view, odd, half + row : half + row + CHUNK, cols]
                    put_below(s2.at[view, 0], part * half + row, odd * half, above + below)
                    put_below(s2.at[view, 1], part * half + row, odd * half, above - below)
                yield
        for odd in range(2):
            z[view, odd] = by_left(odd, s2.at[view, odd])
            yield
        valid = (view < counts[0, 0]).astype(F32)
        for odd in range(2):
            for row in range(0, half, CHUNK):
                re, im = z[view, odd, row : row + CHUNK], z[view, odd, half + row : half + row + CHUNK]
                taken = pl.ds(2 * row + odd, CHUNK, stride=2)
                wanted = jnp.concatenate([amplitude[view, 0, taken], amplitude[view, 1, taken]], 1)
                scaling = valid - wanted * lax.rsqrt(re * re + im * im + smooth_eps)
                put_below(s3.at[view, odd], row, 0, re * scaling)
                put_below(s3.at[view, odd], half + row, 0, im * scaling)
                yield
        for odd in range(2):
            u[view, odd] = by_left(2 + odd, s3.at[view, odd])
            yield
        for row in range(0, half, CHUNK):
            for part in range(2):
                rows = slice(part * half + row, part * half + row + CHUNK)
                even_rows, odd_rows = u[view, 0, rows], u[view, 1, rows]
                for value, place in ((even_rows + odd_rows, row), (even_rows - odd_rows, half + row)):
                    put_beside(s4.at[view, 0], place, part * half, value[:, :half])
                    put_beside(s4.at[view, 1], place, part * half, value[:, half:])
                yield
        for odd in range(2):
            g[view, odd] = by_right(s4.at[view, odd], 2 + odd)
            yield

    work = [steps(view) for view in range(views)]
    for view in range(views):
        for _ in range(view * STAGGER):
            work[view] = itertools.chain([None], work[view])
    for _ in itertools.zip_longest(*work):
        pass

    for row in range(0, size, CHUNK):
        rows = slice(row, row + CHUNK)
        sums = {}

        def add(key, value):
            sums[key] = sums[key] + value if key in sums else value

        for view in range(views):
            beyond, place = row_mask(view, row)
            halves = []
            for part in range(2):
                cols = slice(part * half, (part + 1) * half)
                even_cols, odd_cols = g[view, 0, rows, cols], g[view, 1, rows, cols]
                halves.append((even_cols + odd_cols, even_cols - odd_cols))
            for block in range(2):
                cols = slice(block * LANES, (block + 1) * LANES)
                beside = col_mask(view, block)
                b_re, b_im = halves[0][block], halves[1][block]
                p_re, p_im = placed[view, 0, rows, cols], placed[view, 1, rows, cols]
                for part, value in enumerate((p_re * b_re + p_im * b_im, p_re * b_im - p_im * b_re)):
                    if beyond is not None:
                        outer, value = jnp.where(beyond, value, zero), jnp.where(beyond, zero, value)
                        add(("corner", part), jnp.where(beside, outer, zero))
                        add(("row", part, block), jnp.where(beside, zero, outer))
                    add(("col", part), jnp.where(beside, value, zero))
                    add(("core", part, block), jnp.where(beside, zero, value))
        for part in range(2):
            cols_m[part, rows] = sums["col", part]
            if place is not None:
                corner_m[part, place : place + CHUNK] = sums["corner", part]
            for block in range(2):
                cols = slice(block * LANES, (block + 1) * LANES)
                g_core[part, rows, cols] = sums["core", part, block]
                if place is not None:
                    rows_m[part, place : place + CHUNK, cols] = sums["row", part, block]

    def packed(channel, re, im):
        to_right = jnp.where(low_lanes, re, swap_halves(im))
        to_left = jnp.where(low_lanes, swap_halves(im), re)
        return jnp.where(sends_right(channel), to_right, to_left)

    for part in range(2):
        bottom, top = rows_m[part, :m], rows_m[part, m:]
        g_a[part] = jnp.where(lower, bottom, top)
        g_b[part] = jnp.where(lower, top, bottom)
    bottom = (corner_m[0, :m], corner_m[1, :m])
    top = (corner_m[0, m:], corner_m[1, m:])
    for number, channel in enumerate(chans):
        for row in range(0, size, CHUNK):
            rows = slice(row, row + CHUNK)
            g_x[number][rows] = packed(channel, cols_m[0, rows], cols_m[1, rows])
        below, above = packed(channel, *bottom), packed(channel, *top)
        g_ka[number][...] = jnp.where(lower, below, above)
        g_kb[number][...] = jnp.where(lower, above, below)


def views_call(chans, offsets, counts, core, placed, amplitude, tables, a_in, b_in, x_in, ka_in, kb_in):
    views, size = placed.shape[0], core.shape[1]
    count = len(chans)
    vmem = pl.BlockSpec(memory_space=pltpu.VMEM)
    shapes = [(2, size, size), (2, MARGIN, size), (2, MARGIN, size)]
    shapes += [(size, LANES)] * count + [(MARGIN, LANES)] * (2 * count)
    full = pltpu.VMEM((views, 2, size, size), F32)
    tall = pltpu.VMEM((views, 2, 2 * size, size), BF16)
    wide = pltpu.VMEM((views, 2, size, 2 * size), BF16)
    outs = pl.pallas_call(
        functools.partial(views_kernel, chans),
        out_shape=[jax.ShapeDtypeStruct(shape, F32) for shape in shapes],
        in_specs=[pl.BlockSpec(memory_space=pltpu.HBM)] * 2 + [vmem] * (7 + 3 * count),
        out_specs=[vmem] * len(shapes),
        scratch_shapes=[
            pltpu.SMEM(offsets.shape, jnp.int32),
            pltpu.SMEM(counts.shape, jnp.int32),
            pltpu.SemaphoreType.DMA((2,)),
            pltpu.VMEM((2, size, LANES), F32),
            pltpu.VMEM((2, 2 * MARGIN, size), F32),
            pltpu.VMEM((2, 2 * MARGIN, LANES), F32),
            wide, full, tall, full, tall, full, wide, full,
        ],
        compiler_params=pltpu.CompilerParams(vmem_limit_bytes=40 * 1024 * 1024),
    )(offsets, counts, core, placed, amplitude, *tables, a_in, b_in, *x_in, *ka_in, *kb_in)
    return (*outs[:3], outs[3 : 3 + count], outs[3 + count : 3 + 2 * count], outs[3 + 2 * count :])


def finish_kernel(chans, object_ref, g_core, a_in, b_in, *rest):
    count = len(chans)
    x_in, ka_in, kb_in = rest[:count], rest[count : 2 * count], rest[2 * count : 3 * count]
    out = rest[-1]
    size = object_ref.shape[1]
    lower = lower_partner()
    a_rows = pl.ds(pl.multiple_of(jnp.where(lower, size - MARGIN, 0), MARGIN), MARGIN)
    b_rows = pl.ds(pl.multiple_of(jnp.where(lower, 0, size - MARGIN), MARGIN), MARGIN)
    columns = []
    for channel in chans:
        right = takes_right(channel)
        mine = lane_ids() // (LANES // 2) == jnp.where(right, 1, 0)
        block = pl.multiple_of(jnp.where(right, size - LANES, 0), LANES)
        columns.append((mine, pl.ds(block, LANES)))

    def take(place, value):
        out[place] -= step_size * value

    def take_packed(rows, column, block):
        mine, lanes = column
        take((0, rows, lanes), jnp.where(mine, block, 0.0))
        take((1, rows, lanes), jnp.where(mine, swap_halves(block), 0.0))

    for part in range(2):
        out[part] = object_ref[part] - step_size * g_core[part]
        take((part, a_rows), a_in[part])
    for number, column in enumerate(columns):
        take_packed(slice(None), column, x_in[number][...])
        take_packed(a_rows, column, ka_in[number][...])

    @pl.when(b_partner())
    def _():
        for part in range(2):
            take((part, b_rows), b_in[part])
        for number, column in enumerate(columns):
            take_packed(b_rows, column, kb_in[number][...])


def finish_call(chans, object_field, g_core, a_in, b_in, x_in, ka_in, kb_in):
    vmem = pl.BlockSpec(memory_space=pltpu.VMEM)
    return pl.pallas_call(
        functools.partial(finish_kernel, chans),
        out_shape=jax.ShapeDtypeStruct(object_field.shape, F32),
        in_specs=[vmem] * (4 + 3 * len(chans)),
        out_specs=vmem,
        compiler_params=pltpu.CompilerParams(vmem_limit_bytes=6 * 1024 * 1024),
    )(object_field, g_core, a_in, b_in, *x_in, *ka_in, *kb_in)


def per_device(object_field, probe_field, intensity, view_offsets, view_counts):
    size = object_field.shape[1]
    mesh_rows, mesh_cols = lax.axis_size("row"), lax.axis_size("col")
    chans = channels(mesh_cols)
    tables = dft_tables(size)
    a_pairs, b_pairs = row_pairs(mesh_rows, 0), row_pairs(mesh_rows, 1)
    spare = spare_route(b_pairs, mesh_rows, mesh_cols)

    def over_rows(block, pairs, extra):
        route = [(i * mesh_cols + k, j * mesh_cols + k) for i, j in pairs for k in range(mesh_cols)]
        return lax.ppermute(block, ("row", "col"), route + extra)

    def across(block, pairs, extra, channel):
        route = [(i * mesh_cols + k, j * mesh_cols + l) for i, j in pairs for k, l in channel[0]]
        return lax.ppermute(block, ("row", "col"), route + (extra if mesh_cols == 2 else []))

    def exchange(a_send, b_send, x_send, ka_send, kb_send):
        x_in = [lax.ppermute(block, "col", channel[0]) for block, channel in zip(x_send, chans)]
        b_in = over_rows(b_send, b_pairs, spare)
        kb_in = [across(block, b_pairs, spare, channel) for block, channel in zip(kb_send, chans)]
        ka_in = [across(block, a_pairs, [], channel) for block, channel in zip(ka_send, chans)]
        a_in = over_rows(a_send, a_pairs, [])
        return a_in, b_in, x_in, ka_in, kb_in

    packs = pack_call(object_field, chans)
    offsets = jnp.swapaxes(view_offsets, 2, 3)
    margins = exchange(packs[0], packs[1], packs[2::3], packs[3::3], packs[4::3])
    placed, amplitude = prepare_call(offsets, view_counts, probe_field, intensity)
    g_core, *sends = views_call(
        chans, offsets, view_counts, object_field, placed, amplitude, tables, *margins
    )
    return finish_call(chans, object_field, g_core, *exchange(*sends))


def solution(mesh):
    in_specs = (
        P(None, "row", "col"),
        P(),
        P("row", "col", None, None, None),
        P("row", "col", None, None),
        P("row", "col"),
    )
    out_specs = P(None, "row", "col")
    return jax.shard_map(
        per_device, mesh=mesh, in_specs=in_specs, out_specs=out_specs, check_vma=False
    )
```

```python
import functools
import itertools
import math

import jax
import jax.numpy as jnp
import ml_dtypes
import numpy as np
from jax import lax
from jax.experimental import pallas as pl
from jax.experimental.pallas import tpu as pltpu
from jax.sharding import PartitionSpec as P

MARGIN = 64
LANES = 128
CHUNK = 64
STAGGER = 4

smooth_eps = 0.1
step_size = 0.2

F32 = jnp.float32
BF16 = jnp.bfloat16


def dft_tables(length):
    half = length // 2
    counter = np.arange(half)
    factor = 1.0 / math.sqrt(length)
    product = np.outer(counter, counter)
    even = np.exp(-2j * np.pi * (product % half) / half) * factor
    odd = np.exp(-2j * np.pi * ((2 * product + counter[:, None]) % length) / length) * factor

    def as_real(table):
        return np.block([[table.real, table.imag], [-table.imag, table.real]])

    def parts(table):
        high = table.astype(ml_dtypes.bfloat16)
        low = (table - high.astype(np.float64)).astype(ml_dtypes.bfloat16)
        return high, low

    even, odd = as_real(even), as_real(odd)
    by_right = [np.concatenate(parts(t), 0) for t in (even, odd, even.T, odd.T)]
    by_left = [np.concatenate(parts(t), 1) for t in (even.T, odd.T, even, odd)]
    return np.stack(by_right), np.stack(by_left)


def channels(mesh_cols):
    if mesh_cols == 1:
        return []
    if mesh_cols == 2:
        return [([(0, 1), (1, 0)], None, None)]
    forward = [(i, i + 1) for i in range(mesh_cols - 1)]
    return [(forward, True, False), ([(j, i) for i, j in forward], False, True)]


def row_pairs(count, first):
    pairs = [(i, i + 1) for i in range(first, count - 1, 2)]
    return pairs + [(j, i) for i, j in pairs]


def spare_route(pairs, mesh_rows, mesh_cols):
    rows = [i for i in range(mesh_rows) if i not in dict(pairs)]
    if mesh_cols % 2:
        return []
    return [(i * mesh_cols + k, i * mesh_cols + (k ^ 1)) for i in rows for k in range(mesh_cols)]


def b_partner():
    row = lax.axis_index("row")
    return jnp.where(lower_partner(), row > 0, row < lax.axis_size("row") - 1)


def sends_right(channel):
    return lax.axis_index("col") == 0 if channel[1] is None else channel[1]


def takes_right(channel):
    return lax.axis_index("col") == 0 if channel[2] is None else channel[2]


def lower_partner():
    return lax.rem(lax.axis_index("row"), 2) == 0


def lane_ids():
    return lax.broadcasted_iota(jnp.int32, (1, LANES), 1)


def half_lanes(right):
    low = lane_ids() < LANES // 2
    if isinstance(right, bool):
        return low if right else ~low
    return lane_ids() // (LANES // 2) == jnp.where(right, 0, 1)


def split(value):
    high = value.astype(BF16)
    return high, (value - high.astype(F32)).astype(BF16)


def dot(first, second):
    return jnp.dot(first, second, preferred_element_type=F32)


def swap_halves(block):
    return pltpu.roll(block, LANES // 2, 1)


def fetch(pairs, sems):
    copies = [pltpu.make_async_copy(source, target, sems.at[i]) for i, (source, target) in enumerate(pairs)]
    for copy in copies:
        copy.start()
    return copies


def pack_kernel(chans, object_ref, a_ref, b_ref, *edge_refs):
    size = object_ref.shape[1]
    top, bottom = pl.ds(0, MARGIN), pl.ds(size - MARGIN, MARGIN)
    lower = lower_partner()
    for part in range(2):
        head, tail = object_ref[part, top, :], object_ref[part, bottom, :]
        a_ref[part] = jnp.where(lower, tail, head)
        b_ref[part] = jnp.where(lower, head, tail)
    for number, channel in enumerate(chans):
        right = sends_right(channel)
        x_ref, ka_ref, kb_ref = edge_refs[3 * number : 3 * number + 3]
        low = lane_ids() < LANES // 2
        for start in range(0, size, CHUNK):
            rows = slice(start, start + CHUNK)
            left_edge = jnp.where(
                low, object_ref[0, rows, :LANES], swap_halves(object_ref[1, rows, :LANES])
            )
            right_edge = jnp.where(
                low,
                swap_halves(object_ref[1, rows, size - LANES :]),
                object_ref[0, rows, size - LANES :],
            )
            x_ref[rows] = jnp.where(right, right_edge, left_edge)
        ka_ref[...] = jnp.where(lower, x_ref[size - MARGIN :], x_ref[:MARGIN])
        kb_ref[...] = jnp.where(lower, x_ref[:MARGIN], x_ref[size - MARGIN :])


def pack_call(object_field, chans):
    size = object_field.shape[1]
    shapes = [(2, MARGIN, size)] * 2 + [(size, LANES), (MARGIN, LANES), (MARGIN, LANES)] * len(chans)
    vmem = pl.BlockSpec(memory_space=pltpu.VMEM)
    return pl.pallas_call(
        functools.partial(pack_kernel, chans),
        out_shape=[jax.ShapeDtypeStruct(shape, F32) for shape in shapes],
        in_specs=[vmem],
        out_specs=[vmem] * len(shapes),
        compiler_params=pltpu.CompilerParams(vmem_limit_bytes=4 * 1024 * 1024),
    )(object_field)


def prepare_kernel(
    offsets_in, counts, probe, intensity, placed, amplitude, offsets, doubled, measured, sems
):
    views, size = measured.shape[0], probe.shape[1]
    half = size // 2
    copies = fetch(
        [(offsets_in, offsets)]
        + [(probe, doubled.at[:, pl.ds(size * i, size)]) for i in range(2)]
        + [(intensity.at[0, 0, view], measured.at[view]) for view in range(views)],
        sems,
    )
    source = lax.broadcasted_iota(jnp.int32, (size, size), 0)
    target = lax.broadcasted_iota(jnp.int32, (size, size), 1)
    order = (target == (source % 2) * half + source // 2).astype(F32).astype(BF16)
    sublane = lax.broadcasted_iota(jnp.int32, (1, 8, 1), 1)
    for copy in copies[:3]:
        copy.wait()
    for view in range(views):
        shift_row = lax.rem(offsets[0, 0, 0, view] - MARGIN + size, size)
        shift_col = lax.rem(offsets[0, 0, 1, view] - MARGIN + size, size)
        start = lax.rem(size - shift_row, size)
        whole = pl.multiple_of((start // 8) * 8, 8)
        rest = start - whole
        for part in range(2):
            for row in range(0, size, CHUNK):
                block = doubled[part, pl.ds(whole + row, CHUNK + 8), :]
                block = pltpu.roll(block, shift_col, 1).reshape(CHUNK // 8 + 1, 8, size)
                block = pltpu.roll(block, lax.rem(8 - rest, 8), 1)
                block = jnp.where(sublane < 8 - rest, block[:-1], block[1:])
                placed[view, part, row : row + CHUNK] = block.reshape(CHUNK, size)
    for view in range(views):
        copies[3 + view].wait()
        valid = (view < counts[0, 0]).astype(F32)
        power = measured[view] + smooth_eps
        high, low = split(power * lax.rsqrt(power) * valid)
        ordered = dot(high, order) + dot(low, order)
        amplitude[view, 0] = ordered[:, :half]
        amplitude[view, 1] = ordered[:, half:]


def prepare_call(offsets, counts, probe, intensity):
    views, size = intensity.shape[2], probe.shape[1]
    vmem, hbm = pl.BlockSpec(memory_space=pltpu.VMEM), pl.BlockSpec(memory_space=pltpu.HBM)
    return pl.pallas_call(
        prepare_kernel,
        out_shape=[
            jax.ShapeDtypeStruct((views, 2, size, size), F32),
            jax.ShapeDtypeStruct((views, 2, size, size // 2), F32),
        ],
        in_specs=[hbm, pl.BlockSpec(memory_space=pltpu.SMEM), hbm, hbm],
        out_specs=[vmem] * 2,
        scratch_shapes=[
            pltpu.SMEM(offsets.shape, jnp.int32),
            pltpu.VMEM((2, 2 * size, size), F32),
            pltpu.VMEM((views, size, size), F32),
            pltpu.SemaphoreType.DMA((3 + views,)),
        ],
        compiler_params=pltpu.CompilerParams(vmem_limit_bytes=16 * 1024 * 1024),
        cost_estimate=pl.CostEstimate(flops=2 * 10**9, bytes_accessed=6 * 10**6, transcendentals=0),
    )(offsets, counts, probe, intensity)


def views_kernel(chans, offsets_in, counts, core, placed, amplitude, right, left, a_in, b_in, *rest):
    count = len(chans)
    x_in, ka_in, kb_in = rest[:count], rest[count : 2 * count], rest[2 * count : 3 * count]
    rest = rest[3 * count :]
    g_core, g_a, g_b = rest[:3]
    g_x, g_ka = rest[3 : 3 + count], rest[3 + count : 3 + 2 * count]
    g_kb = rest[3 + 2 * count : 3 + 3 * count]
    offsets, sem, cols_m, rows_m, corner_m, s1, y, s2, z, s3, u, s4, g = rest[3 + 3 * count :]
    (offsets_copy,) = fetch([(offsets_in, offsets)], sem)
    views, size = placed.shape[0], core.shape[1]
    half, m = size // 2, MARGIN
    lower, partner = lower_partner(), b_partner()
    low_lanes = lane_ids() < LANES // 2
    zero = jnp.zeros((CHUNK, LANES), F32)

    def unpack(blocks):
        re = im = None
        for channel, block in zip(chans, blocks):
            mine = half_lanes(takes_right(channel))
            re = jnp.where(mine, block, 0.0 if re is None else re)
            im = jnp.where(mine, swap_halves(block), 0.0 if im is None else im)
        return (re, im) if blocks else (jnp.zeros((MARGIN, LANES), F32),) * 2

    for row in range(0, size, CHUNK):
        rows = slice(row, row + CHUNK)
        cols_m[0, rows], cols_m[1, rows] = unpack([ref[rows] for ref in x_in]) if chans else (zero, zero)
    corner_a = unpack([ref[...] for ref in ka_in])
    corner_b = [jnp.where(partner, part, 0.0) for part in unpack([ref[...] for ref in kb_in])]
    for part in range(2):
        a_rows, b_rows = a_in[part], jnp.where(partner, b_in[part], 0.0)
        rows_m[part, :m] = jnp.where(lower, a_rows, b_rows)
        rows_m[part, m:] = jnp.where(lower, b_rows, a_rows)
        corner_m[part, :m] = jnp.where(lower, corner_a[part], corner_b[part])
        corner_m[part, m:] = jnp.where(lower, corner_b[part], corner_a[part])

    offsets_copy.wait()

    def by_right(lhs, t):
        out = dot(lhs[:, :size], right[t, :size]) + dot(lhs[:, size:], right[t, :size])
        return out + dot(lhs[:, :size], right[t, size:])

    def by_left(t, rhs):
        out = dot(left[t, :, :size], rhs[:size]) + dot(left[t, :, :size], rhs[size:])
        return out + dot(left[t, :, size:], rhs[:size])

    def put_below(ref, row, col, value):
        high, low = split(value)
        rows, cols = value.shape
        ref[row : row + rows, col : col + cols] = high
        ref[size + row : size + row + rows, col : col + cols] = low

    def put_beside(ref, row, col, value):
        high, low = split(value)
        rows, cols = value.shape
        ref[row : row + rows, col : col + cols] = high
        ref[row : row + rows, size + col : size + col + cols] = low

    def row_mask(view, row):
        ids = row + lax.broadcasted_iota(jnp.int32, (CHUNK, LANES), 0)
        if row < m:
            return ids < offsets[0, 0, 0, view] - m, row
        if row >= size - m:
            return ids >= size - m + offsets[0, 0, 0, view], row - size + 2 * m
        return None, None

    def col_mask(view, block):
        if block == 0:
            return lane_ids() < offsets[0, 0, 1, view] - m
        return lane_ids() >= m + offsets[0, 0, 1, view]

    def patch(view, row, block):
        cols = slice(block * LANES, (block + 1) * LANES)
        rows = slice(row, row + CHUNK)
        beside = col_mask(view, block)
        beyond, place = row_mask(view, row)
        found = []
        for part in range(2):
            value = jnp.where(beside, cols_m[part, rows], core[part, rows, cols])
            if beyond is not None:
                there = slice(place, place + CHUNK)
                outer = jnp.where(beside, corner_m[part, there], rows_m[part, there, cols])
                value = jnp.where(beyond, outer, value)
            found.append(value)
        return found

    def steps(view):
        for row in range(0, size, CHUNK):
            rows = slice(row, row + CHUNK)
            waves = []
            for block in range(2):
                cols = slice(block * LANES, (block + 1) * LANES)
                o_re, o_im = patch(view, row, block)
                p_re, p_im = placed[view, 0, rows, cols], placed[view, 1, rows, cols]
                waves.append((p_re * o_re - p_im * o_im, p_re * o_im + p_im * o_re))
            for part in range(2):
                put_beside(s1.at[view, 0], row, part * half, waves[0][part] + waves[1][part])
                put_beside(s1.at[view, 1], row, part * half, waves[0][part] - waves[1][part])
            yield
        for odd in range(2):
            y[view, odd] = by_right(s1.at[view, odd], odd)
            yield
        for odd in range(2):
            for row in range(0, half, CHUNK):
                for part in range(2):
                    cols = slice(part * half, (part + 1) * half)
                    above = y[view, odd, row : row + CHUNK, cols]
                    below = y[view, odd, half + row : half + row + CHUNK, cols]
                    put_below(s2.at[view, 0], part * half + row, odd * half, above + below)
                    put_below(s2.at[view, 1], part * half + row, odd * half, above - below)
                yield
        for odd in range(2):
            z[view, odd] = by_left(odd, s2.at[view, odd])
            yield
        valid = (view < counts[0, 0]).astype(F32)
        for odd in range(2):
            for row in range(0, half, CHUNK):
                re, im = z[view, odd, row : row + CHUNK], z[view, odd, half + row : half + row + CHUNK]
                taken = pl.ds(2 * row + odd, CHUNK, stride=2)
                wanted = jnp.concatenate([amplitude[view, 0, taken], amplitude[view, 1, taken]], 1)
                scaling = valid - wanted * lax.rsqrt(re * re + im * im + smooth_eps)
                put_below(s3.at[view, odd], row, 0, re * scaling)
                put_below(s3.at[view, odd], half + row, 0, im * scaling)
                yield
        for odd in range(2):
            u[view, odd] = by_left(2 + odd, s3.at[view, odd])
            yield
        for row in range(0, half, CHUNK):
            for part in range(2):
                rows = slice(part * half + row, part * half + row + CHUNK)
                even_rows, odd_rows = u[view, 0, rows], u[view, 1, rows]
                for value, place in ((even_rows + odd_rows, row), (even_rows - odd_rows, half + row)):
                    put_beside(s4.at[view, 0], place, part * half, value[:, :half])
                    put_beside(s4.at[view, 1], place, part * half, value[:, half:])
                yield
        for odd in range(2):
            g[view, odd] = by_right(s4.at[view, odd], 2 + odd)
            yield

    work = [steps(view) for view in range(views)]
    for view in range(views):
        for _ in range(view * STAGGER):
            work[view] = itertools.chain([None], work[view])
    for _ in itertools.zip_longest(*work):
        pass

    for row in range(0, size, CHUNK):
        rows = slice(row, row + CHUNK)
        sums = {}

        def add(key, value):
            sums[key] = sums[key] + value if key in sums else value

        for view in range(views):
            beyond, place = row_mask(view, row)
            halves = []
            for part in range(2):
                cols = slice(part * half, (part + 1) * half)
                even_cols, odd_cols = g[view, 0, rows, cols], g[view, 1, rows, cols]
                halves.append((even_cols + odd_cols, even_cols - odd_cols))
            for block in range(2):
                cols = slice(block * LANES, (block + 1) * LANES)
                beside = col_mask(view, block)
                b_re, b_im = halves[0][block], halves[1][block]
                p_re, p_im = placed[view, 0, rows, cols], placed[view, 1, rows, cols]
                for part, value in enumerate((p_re * b_re + p_im * b_im, p_re * b_im - p_im * b_re)):
                    if beyond is not None:
                        outer, value = jnp.where(beyond, value, zero), jnp.where(beyond, zero, value)
                        add(("corner", part), jnp.where(beside, outer, zero))
                        add(("row", part, block), jnp.where(beside, zero, outer))
                    add(("col", part), jnp.where(beside, value, zero))
                    add(("core", part, block), jnp.where(beside, zero, value))
        for part in range(2):
            cols_m[part, rows] = sums["col", part]
            if place is not None:
                corner_m[part, place : place + CHUNK] = sums["corner", part]
            for block in range(2):
                cols = slice(block * LANES, (block + 1) * LANES)
                g_core[part, rows, cols] = sums["core", part, block]
                if place is not None:
                    rows_m[part, place : place + CHUNK, cols] = sums["row", part, block]

    def packed(channel, re, im):
        to_right = jnp.where(low_lanes, re, swap_halves(im))
        to_left = jnp.where(low_lanes, swap_halves(im), re)
        return jnp.where(sends_right(channel), to_right, to_left)

    for part in range(2):
        bottom, top = rows_m[part, :m], rows_m[part, m:]
        g_a[part] = jnp.where(lower, bottom, top)
        g_b[part] = jnp.where(lower, top, bottom)
    bottom = (corner_m[0, :m], corner_m[1, :m])
    top = (corner_m[0, m:], corner_m[1, m:])
    for number, channel in enumerate(chans):
        for row in range(0, size, CHUNK):
            rows = slice(row, row + CHUNK)
            g_x[number][rows] = packed(channel, cols_m[0, rows], cols_m[1, rows])
        below, above = packed(channel, *bottom), packed(channel, *top)
        g_ka[number][...] = jnp.where(lower, below, above)
        g_kb[number][...] = jnp.where(lower, above, below)


def views_call(chans, offsets, counts, core, placed, amplitude, tables, a_in, b_in, x_in, ka_in, kb_in):
    views, size = placed.shape[0], core.shape[1]
    count = len(chans)
    vmem = pl.BlockSpec(memory_space=pltpu.VMEM)
    shapes = [(2, size, size), (2, MARGIN, size), (2, MARGIN, size)]
    shapes += [(size, LANES)] * count + [(MARGIN, LANES)] * (2 * count)
    full = pltpu.VMEM((views, 2, size, size), F32)
    tall = pltpu.VMEM((views, 2, 2 * size, size), BF16)
    wide = pltpu.VMEM((views, 2, size, 2 * size), BF16)
    outs = pl.pallas_call(
        functools.partial(views_kernel, chans),
        out_shape=[jax.ShapeDtypeStruct(shape, F32) for shape in shapes],
        in_specs=[
            pl.BlockSpec(memory_space=pltpu.HBM),
            pl.BlockSpec(memory_space=pltpu.SMEM),
            *[vmem] * (7 + 3 * count),
        ],
        out_specs=[vmem] * len(shapes),
        scratch_shapes=[
            pltpu.SMEM(offsets.shape, jnp.int32),
            pltpu.SemaphoreType.DMA((1,)),
            pltpu.VMEM((2, size, LANES), F32),
            pltpu.VMEM((2, 2 * MARGIN, size), F32),
            pltpu.VMEM((2, 2 * MARGIN, LANES), F32),
            wide, full, tall, full, tall, full, wide, full,
        ],
        compiler_params=pltpu.CompilerParams(vmem_limit_bytes=40 * 1024 * 1024),
    )(offsets, counts, core, placed, amplitude, *tables, a_in, b_in, *x_in, *ka_in, *kb_in)
    return (*outs[:3], outs[3 : 3 + count], outs[3 + count : 3 + 2 * count], outs[3 + 2 * count :])


def finish_kernel(chans, object_ref, g_core, a_in, b_in, *rest):
    count = len(chans)
    x_in, ka_in, kb_in = rest[:count], rest[count : 2 * count], rest[2 * count : 3 * count]
    out = rest[-1]
    size = object_ref.shape[1]
    lower = lower_partner()
    a_rows = pl.ds(pl.multiple_of(jnp.where(lower, size - MARGIN, 0), MARGIN), MARGIN)
    b_rows = pl.ds(pl.multiple_of(jnp.where(lower, 0, size - MARGIN), MARGIN), MARGIN)
    columns = []
    for channel in chans:
        right = takes_right(channel)
        mine = lane_ids() // (LANES // 2) == jnp.where(right, 1, 0)
        block = pl.multiple_of(jnp.where(right, size - LANES, 0), LANES)
        columns.append((mine, pl.ds(block, LANES)))

    def take(place, value):
        out[place] -= step_size * value

    def take_packed(rows, column, block):
        mine, lanes = column
        take((0, rows, lanes), jnp.where(mine, block, 0.0))
        take((1, rows, lanes), jnp.where(mine, swap_halves(block), 0.0))

    for part in range(2):
        out[part] = object_ref[part] - step_size * g_core[part]
        take((part, a_rows), a_in[part])
    for number, column in enumerate(columns):
        take_packed(slice(None), column, x_in[number][...])
        take_packed(a_rows, column, ka_in[number][...])

    @pl.when(b_partner())
    def _():
        for part in range(2):
            take((part, b_rows), b_in[part])
        for number, column in enumerate(columns):
            take_packed(b_rows, column, kb_in[number][...])


def finish_call(chans, object_field, g_core, a_in, b_in, x_in, ka_in, kb_in):
    vmem = pl.BlockSpec(memory_space=pltpu.VMEM)
    return pl.pallas_call(
        functools.partial(finish_kernel, chans),
        out_shape=jax.ShapeDtypeStruct(object_field.shape, F32),
        in_specs=[vmem] * (4 + 3 * len(chans)),
        out_specs=vmem,
        compiler_params=pltpu.CompilerParams(vmem_limit_bytes=6 * 1024 * 1024),
    )(object_field, g_core, a_in, b_in, *x_in, *ka_in, *kb_in)


def per_device(object_field, probe_field, intensity, view_offsets, view_counts):
    size = object_field.shape[1]
    mesh_rows, mesh_cols = lax.axis_size("row"), lax.axis_size("col")
    chans = channels(mesh_cols)
    tables = dft_tables(size)
    a_pairs, b_pairs = row_pairs(mesh_rows, 0), row_pairs(mesh_rows, 1)
    spare = spare_route(b_pairs, mesh_rows, mesh_cols)

    def over_rows(block, pairs, extra):
        route = [(i * mesh_cols + k, j * mesh_cols + k) for i, j in pairs for k in range(mesh_cols)]
        return lax.ppermute(block, ("row", "col"), route + extra)

    def across(block, pairs, extra, channel):
        route = [(i * mesh_cols + k, j * mesh_cols + l) for i, j in pairs for k, l in channel[0]]
        return lax.ppermute(block, ("row", "col"), route + (extra if mesh_cols == 2 else []))

    def exchange(a_send, b_send, x_send, ka_send, kb_send):
        x_in = [lax.ppermute(block, "col", channel[0]) for block, channel in zip(x_send, chans)]
        b_in = over_rows(b_send, b_pairs, spare)
        kb_in = [across(block, b_pairs, spare, channel) for block, channel in zip(kb_send, chans)]
        ka_in = [across(block, a_pairs, [], channel) for block, channel in zip(ka_send, chans)]
        a_in = over_rows(a_send, a_pairs, [])
        return a_in, b_in, x_in, ka_in, kb_in

    packs = pack_call(object_field, chans)
    offsets, probe, measured = (
        pltpu.with_memory_space_constraint(array, pltpu.HBM)
        for array in (jnp.swapaxes(view_offsets, 2, 3), probe_field, intensity)
    )
    margins = exchange(packs[0], packs[1], packs[2::3], packs[3::3], packs[4::3])
    placed, amplitude = prepare_call(offsets, view_counts, probe, measured)
    g_core, *sends = views_call(
        chans, offsets, view_counts, object_field, placed, amplitude, tables, *margins
    )
    return finish_call(chans, object_field, g_core, *exchange(*sends))


def solution(mesh):
    in_specs = (
        P(None, "row", "col"),
        P(),
        P("row", "col", None, None, None),
        P("row", "col", None, None),
        P("row", "col"),
    )
    out_specs = P(None, "row", "col")
    return jax.shard_map(
        per_device, mesh=mesh, in_specs=in_specs, out_specs=out_specs, check_vma=False
    )
```

```python
import functools
import itertools
import math

import jax
import jax.numpy as jnp
import ml_dtypes
import numpy as np
from jax import lax
from jax.experimental import pallas as pl
from jax.experimental.pallas import tpu as pltpu
from jax.sharding import PartitionSpec as P

MARGIN = 64
LANES = 128
CHUNK = 64
STAGGER = 4

smooth_eps = 0.1
step_size = 0.2

F32 = jnp.float32
BF16 = jnp.bfloat16


def dft_tables(length):
    half = length // 2
    counter = np.arange(half)
    factor = 1.0 / math.sqrt(length)
    product = np.outer(counter, counter)
    even = np.exp(-2j * np.pi * (product % half) / half) * factor
    odd = np.exp(-2j * np.pi * ((2 * product + counter[:, None]) % length) / length) * factor

    def as_real(table):
        return np.block([[table.real, table.imag], [-table.imag, table.real]])

    def parts(table):
        high = table.astype(ml_dtypes.bfloat16)
        low = (table - high.astype(np.float64)).astype(ml_dtypes.bfloat16)
        return high, low

    even, odd = as_real(even), as_real(odd)
    by_right = [np.concatenate(parts(t), 0) for t in (even, odd, even.T, odd.T)]
    by_left = [np.concatenate(parts(t), 1) for t in (even.T, odd.T, even, odd)]
    return np.stack(by_right), np.stack(by_left)


def channels(mesh_cols):
    if mesh_cols == 1:
        return []
    if mesh_cols == 2:
        return [([(0, 1), (1, 0)], None, None)]
    forward = [(i, i + 1) for i in range(mesh_cols - 1)]
    return [(forward, True, False), ([(j, i) for i, j in forward], False, True)]


def row_pairs(count, first):
    pairs = [(i, i + 1) for i in range(first, count - 1, 2)]
    return pairs + [(j, i) for i, j in pairs]


def spare_route(pairs, mesh_rows, mesh_cols):
    rows = [i for i in range(mesh_rows) if i not in dict(pairs)]
    if mesh_cols % 2:
        return []
    return [(i * mesh_cols + k, i * mesh_cols + (k ^ 1)) for i in rows for k in range(mesh_cols)]


def b_partner():
    row = lax.axis_index("row")
    return jnp.where(lower_partner(), row > 0, row < lax.axis_size("row") - 1)


def sends_right(channel):
    return lax.axis_index("col") == 0 if channel[1] is None else channel[1]


def takes_right(channel):
    return lax.axis_index("col") == 0 if channel[2] is None else channel[2]


def lower_partner():
    return lax.rem(lax.axis_index("row"), 2) == 0


def lane_ids():
    return lax.broadcasted_iota(jnp.int32, (1, LANES), 1)


def half_lanes(right):
    low = lane_ids() < LANES // 2
    if isinstance(right, bool):
        return low if right else ~low
    return lane_ids() // (LANES // 2) == jnp.where(right, 0, 1)


def split(value):
    high = value.astype(BF16)
    return high, (value - high.astype(F32)).astype(BF16)


def dot(first, second):
    return jnp.dot(first, second, preferred_element_type=F32)


def swap_halves(block):
    return pltpu.roll(block, LANES // 2, 1)


def fetch(pairs, sems):
    copies = [pltpu.make_async_copy(source, target, sems.at[i]) for i, (source, target) in enumerate(pairs)]
    for copy in copies:
        copy.start()
    return copies


def pack_kernel(chans, object_ref, a_ref, b_ref, *edge_refs):
    size = object_ref.shape[1]
    top, bottom = pl.ds(0, MARGIN), pl.ds(size - MARGIN, MARGIN)
    lower = lower_partner()
    for part in range(2):
        head, tail = object_ref[part, top, :], object_ref[part, bottom, :]
        a_ref[part] = jnp.where(lower, tail, head)
        b_ref[part] = jnp.where(lower, head, tail)
    for number, channel in enumerate(chans):
        right = sends_right(channel)
        x_ref, ka_ref, kb_ref = edge_refs[3 * number : 3 * number + 3]
        low = lane_ids() < LANES // 2
        for start in range(0, size, CHUNK):
            rows = slice(start, start + CHUNK)
            left_edge = jnp.where(
                low, object_ref[0, rows, :LANES], swap_halves(object_ref[1, rows, :LANES])
            )
            right_edge = jnp.where(
                low,
                swap_halves(object_ref[1, rows, size - LANES :]),
                object_ref[0, rows, size - LANES :],
            )
            x_ref[rows] = jnp.where(right, right_edge, left_edge)
        ka_ref[...] = jnp.where(lower, x_ref[size - MARGIN :], x_ref[:MARGIN])
        kb_ref[...] = jnp.where(lower, x_ref[:MARGIN], x_ref[size - MARGIN :])


def pack_call(object_field, chans):
    size = object_field.shape[1]
    shapes = [(2, MARGIN, size)] * 2 + [(size, LANES), (MARGIN, LANES), (MARGIN, LANES)] * len(chans)
    vmem = pl.BlockSpec(memory_space=pltpu.VMEM)
    return pl.pallas_call(
        functools.partial(pack_kernel, chans),
        out_shape=[jax.ShapeDtypeStruct(shape, F32) for shape in shapes],
        in_specs=[vmem],
        out_specs=[vmem] * len(shapes),
        compiler_params=pltpu.CompilerParams(vmem_limit_bytes=4 * 1024 * 1024),
    )(object_field)


def prepare_kernel(
    offsets_in, counts, probe, intensity, placed, amplitude, offsets, doubled, measured, sems
):
    views, size = measured.shape[0], probe.shape[1]
    half = size // 2
    copies = fetch(
        [(offsets_in, offsets)]
        + [(probe, doubled.at[:, pl.ds(size * i, size)]) for i in range(2)]
        + [(intensity.at[0, 0, view], measured.at[view]) for view in range(views)],
        sems,
    )
    source = lax.broadcasted_iota(jnp.int32, (size, size), 0)
    target = lax.broadcasted_iota(jnp.int32, (size, size), 1)
    order = (target == (source % 2) * half + source // 2).astype(F32).astype(BF16)
    sublane = lax.broadcasted_iota(jnp.int32, (1, 8, 1), 1)
    for copy in copies[:3]:
        copy.wait()
    for view in range(views):
        shift_row = lax.rem(offsets[0, 0, 0, view] - MARGIN + size, size)
        shift_col = lax.rem(offsets[0, 0, 1, view] - MARGIN + size, size)
        start = lax.rem(size - shift_row, size)
        whole = pl.multiple_of((start // 8) * 8, 8)
        rest = start - whole
        for part in range(2):
            for row in range(0, size, CHUNK):
                block = doubled[part, pl.ds(whole + row, CHUNK + 8), :]
                block = pltpu.roll(block, shift_col, 1).reshape(CHUNK // 8 + 1, 8, size)
                block = pltpu.roll(block, lax.rem(8 - rest, 8), 1)
                block = jnp.where(sublane < 8 - rest, block[:-1], block[1:])
                placed[view, part, row : row + CHUNK] = block.reshape(CHUNK, size)
    for view in range(views):
        copies[3 + view].wait()
        valid = (view < counts[0, 0]).astype(F32)
        power = measured[view] + smooth_eps
        high, low = split(power * lax.rsqrt(power) * valid)
        ordered = dot(high, order) + dot(low, order)
        amplitude[view, 0] = ordered[:, :half]
        amplitude[view, 1] = ordered[:, half:]


def prepare_call(offsets, counts, probe, intensity):
    views, size = intensity.shape[2], probe.shape[1]
    vmem, hbm = pl.BlockSpec(memory_space=pltpu.VMEM), pl.BlockSpec(memory_space=pltpu.HBM)
    return pl.pallas_call(
        prepare_kernel,
        out_shape=[
            jax.ShapeDtypeStruct((views, 2, size, size), F32),
            jax.ShapeDtypeStruct((views, 2, size, size // 2), F32),
        ],
        in_specs=[hbm, pl.BlockSpec(memory_space=pltpu.SMEM), hbm, hbm],
        out_specs=[vmem] * 2,
        scratch_shapes=[
            pltpu.SMEM(offsets.shape, jnp.int32),
            pltpu.VMEM((2, 2 * size, size), F32),
            pltpu.VMEM((views, size, size), F32),
            pltpu.SemaphoreType.DMA((3 + views,)),
        ],
        compiler_params=pltpu.CompilerParams(vmem_limit_bytes=16 * 1024 * 1024),
        cost_estimate=pl.CostEstimate(flops=2 * 10**9, bytes_accessed=6 * 10**6, transcendentals=0),
    )(offsets, counts, probe, intensity)


def views_kernel(chans, offsets_in, counts, core, placed, amplitude, b_in, *rest):
    count = len(chans)
    x_in, kb_in, ka_in = rest[:count], rest[count : 2 * count], rest[2 * count : 3 * count]
    a_in, right, left, *rest = rest[3 * count :]
    g_core, g_a, g_b = rest[:3]
    g_x, g_ka = rest[3 : 3 + count], rest[3 + count : 3 + 2 * count]
    g_kb = rest[3 + 2 * count : 3 + 3 * count]
    offsets, sem, cols_m, rows_m, corner_m, s1, y, s2, z, s3, u, s4, g = rest[3 + 3 * count :]
    (offsets_copy,) = fetch([(offsets_in, offsets)], sem)
    views, size = placed.shape[0], core.shape[1]
    half, m = size // 2, MARGIN
    lower, partner = lower_partner(), b_partner()
    low_lanes = lane_ids() < LANES // 2
    zero = jnp.zeros((CHUNK, LANES), F32)

    def unpack(blocks):
        re = im = None
        for channel, block in zip(chans, blocks):
            mine = half_lanes(takes_right(channel))
            re = jnp.where(mine, block, 0.0 if re is None else re)
            im = jnp.where(mine, swap_halves(block), 0.0 if im is None else im)
        return (re, im) if blocks else (jnp.zeros((MARGIN, LANES), F32),) * 2

    for row in range(0, size, CHUNK):
        rows = slice(row, row + CHUNK)
        cols_m[0, rows], cols_m[1, rows] = unpack([ref[rows] for ref in x_in]) if chans else (zero, zero)
    corner_a = unpack([ref[...] for ref in ka_in])
    corner_b = [jnp.where(partner, part, 0.0) for part in unpack([ref[...] for ref in kb_in])]
    for part in range(2):
        a_rows, b_rows = a_in[part], jnp.where(partner, b_in[part], 0.0)
        rows_m[part, :m] = jnp.where(lower, a_rows, b_rows)
        rows_m[part, m:] = jnp.where(lower, b_rows, a_rows)
        corner_m[part, :m] = jnp.where(lower, corner_a[part], corner_b[part])
        corner_m[part, m:] = jnp.where(lower, corner_b[part], corner_a[part])

    offsets_copy.wait()

    def by_right(lhs, t):
        out = dot(lhs[:, :size], right[t, :size]) + dot(lhs[:, size:], right[t, :size])
        return out + dot(lhs[:, :size], right[t, size:])

    def by_left(t, rhs):
        out = dot(left[t, :, :size], rhs[:size]) + dot(left[t, :, :size], rhs[size:])
        return out + dot(left[t, :, size:], rhs[:size])

    def put_below(ref, row, col, value):
        high, low = split(value)
        rows, cols = value.shape
        ref[row : row + rows, col : col + cols] = high
        ref[size + row : size + row + rows, col : col + cols] = low

    def put_beside(ref, row, col, value):
        high, low = split(value)
        rows, cols = value.shape
        ref[row : row + rows, col : col + cols] = high
        ref[row : row + rows, size + col : size + col + cols] = low

    def row_mask(view, row):
        ids = row + lax.broadcasted_iota(jnp.int32, (CHUNK, LANES), 0)
        if row < m:
            return ids < offsets[0, 0, 0, view] - m, row
        if row >= size - m:
            return ids >= size - m + offsets[0, 0, 0, view], row - size + 2 * m
        return None, None

    def col_mask(view, block):
        if block == 0:
            return lane_ids() < offsets[0, 0, 1, view] - m
        return lane_ids() >= m + offsets[0, 0, 1, view]

    def patch(view, row, block):
        cols = slice(block * LANES, (block + 1) * LANES)
        rows = slice(row, row + CHUNK)
        beside = col_mask(view, block)
        beyond, place = row_mask(view, row)
        found = []
        for part in range(2):
            value = jnp.where(beside, cols_m[part, rows], core[part, rows, cols])
            if beyond is not None:
                there = slice(place, place + CHUNK)
                outer = jnp.where(beside, corner_m[part, there], rows_m[part, there, cols])
                value = jnp.where(beyond, outer, value)
            found.append(value)
        return found

    def steps(view):
        for row in range(0, size, CHUNK):
            rows = slice(row, row + CHUNK)
            waves = []
            for block in range(2):
                cols = slice(block * LANES, (block + 1) * LANES)
                o_re, o_im = patch(view, row, block)
                p_re, p_im = placed[view, 0, rows, cols], placed[view, 1, rows, cols]
                waves.append((p_re * o_re - p_im * o_im, p_re * o_im + p_im * o_re))
            for part in range(2):
                put_beside(s1.at[view, 0], row, part * half, waves[0][part] + waves[1][part])
                put_beside(s1.at[view, 1], row, part * half, waves[0][part] - waves[1][part])
            yield
        for odd in range(2):
            y[view, odd] = by_right(s1.at[view, odd], odd)
            yield
        for odd in range(2):
            for row in range(0, half, CHUNK):
                for part in range(2):
                    cols = slice(part * half, (part + 1) * half)
                    above = y[view, odd, row : row + CHUNK, cols]
                    below = y[view, odd, half + row : half + row + CHUNK, cols]
                    put_below(s2.at[view, 0], part * half + row, odd * half, above + below)
                    put_below(s2.at[view, 1], part * half + row, odd * half, above - below)
                yield
        for odd in range(2):
            z[view, odd] = by_left(odd, s2.at[view, odd])
            yield
        valid = (view < counts[0, 0]).astype(F32)
        for odd in range(2):
            for row in range(0, half, CHUNK):
                re, im = z[view, odd, row : row + CHUNK], z[view, odd, half + row : half + row + CHUNK]
                taken = pl.ds(2 * row + odd, CHUNK, stride=2)
                wanted = jnp.concatenate([amplitude[view, 0, taken], amplitude[view, 1, taken]], 1)
                scaling = valid - wanted * lax.rsqrt(re * re + im * im + smooth_eps)
                put_below(s3.at[view, odd], row, 0, re * scaling)
                put_below(s3.at[view, odd], half + row, 0, im * scaling)
                yield
        for odd in range(2):
            u[view, odd] = by_left(2 + odd, s3.at[view, odd])
            yield
        for row in range(0, half, CHUNK):
            for part in range(2):
                rows = slice(part * half + row, part * half + row + CHUNK)
                even_rows, odd_rows = u[view, 0, rows], u[view, 1, rows]
                for value, place in ((even_rows + odd_rows, row), (even_rows - odd_rows, half + row)):
                    put_beside(s4.at[view, 0], place, part * half, value[:, :half])
                    put_beside(s4.at[view, 1], place, part * half, value[:, half:])
                yield
        for odd in range(2):
            g[view, odd] = by_right(s4.at[view, odd], 2 + odd)
            yield

    work = [steps(view) for view in range(views)]
    for view in range(views):
        for _ in range(view * STAGGER):
            work[view] = itertools.chain([None], work[view])
    for _ in itertools.zip_longest(*work):
        pass

    for row in range(0, size, CHUNK):
        rows = slice(row, row + CHUNK)
        sums = {}

        def add(key, value):
            sums[key] = sums[key] + value if key in sums else value

        for view in range(views):
            beyond, place = row_mask(view, row)
            halves = []
            for part in range(2):
                cols = slice(part * half, (part + 1) * half)
                even_cols, odd_cols = g[view, 0, rows, cols], g[view, 1, rows, cols]
                halves.append((even_cols + odd_cols, even_cols - odd_cols))
            for block in range(2):
                cols = slice(block * LANES, (block + 1) * LANES)
                beside = col_mask(view, block)
                b_re, b_im = halves[0][block], halves[1][block]
                p_re, p_im = placed[view, 0, rows, cols], placed[view, 1, rows, cols]
                for part, value in enumerate((p_re * b_re + p_im * b_im, p_re * b_im - p_im * b_re)):
                    if beyond is not None:
                        outer, value = jnp.where(beyond, value, zero), jnp.where(beyond, zero, value)
                        add(("corner", part), jnp.where(beside, outer, zero))
                        add(("row", part, block), jnp.where(beside, zero, outer))
                    add(("col", part), jnp.where(beside, value, zero))
                    add(("core", part, block), jnp.where(beside, zero, value))
        for part in range(2):
            cols_m[part, rows] = sums["col", part]
            if place is not None:
                corner_m[part, place : place + CHUNK] = sums["corner", part]
            for block in range(2):
                cols = slice(block * LANES, (block + 1) * LANES)
                g_core[part, rows, cols] = sums["core", part, block]
                if place is not None:
                    rows_m[part, place : place + CHUNK, cols] = sums["row", part, block]

    def packed(channel, re, im):
        to_right = jnp.where(low_lanes, re, swap_halves(im))
        to_left = jnp.where(low_lanes, swap_halves(im), re)
        return jnp.where(sends_right(channel), to_right, to_left)

    for part in range(2):
        bottom, top = rows_m[part, :m], rows_m[part, m:]
        g_a[part] = jnp.where(lower, bottom, top)
        g_b[part] = jnp.where(lower, top, bottom)
    bottom = (corner_m[0, :m], corner_m[1, :m])
    top = (corner_m[0, m:], corner_m[1, m:])
    for number, channel in enumerate(chans):
        for row in range(0, size, CHUNK):
            rows = slice(row, row + CHUNK)
            g_x[number][rows] = packed(channel, cols_m[0, rows], cols_m[1, rows])
        below, above = packed(channel, *bottom), packed(channel, *top)
        g_ka[number][...] = jnp.where(lower, below, above)
        g_kb[number][...] = jnp.where(lower, above, below)


def views_call(chans, offsets, counts, core, placed, amplitude, tables, a_in, b_in, x_in, ka_in, kb_in):
    views, size = placed.shape[0], core.shape[1]
    count = len(chans)
    vmem = pl.BlockSpec(memory_space=pltpu.VMEM)
    shapes = [(2, size, size), (2, MARGIN, size), (2, MARGIN, size)]
    shapes += [(size, LANES)] * count + [(MARGIN, LANES)] * (2 * count)
    full = pltpu.VMEM((views, 2, size, size), F32)
    tall = pltpu.VMEM((views, 2, 2 * size, size), BF16)
    wide = pltpu.VMEM((views, 2, size, 2 * size), BF16)
    outs = pl.pallas_call(
        functools.partial(views_kernel, chans),
        out_shape=[jax.ShapeDtypeStruct(shape, F32) for shape in shapes],
        in_specs=[
            pl.BlockSpec(memory_space=pltpu.HBM),
            pl.BlockSpec(memory_space=pltpu.SMEM),
            *[vmem] * (7 + 3 * count),
        ],
        out_specs=[vmem] * len(shapes),
        scratch_shapes=[
            pltpu.SMEM(offsets.shape, jnp.int32),
            pltpu.SemaphoreType.DMA((1,)),
            pltpu.VMEM((2, size, LANES), F32),
            pltpu.VMEM((2, 2 * MARGIN, size), F32),
            pltpu.VMEM((2, 2 * MARGIN, LANES), F32),
            wide, full, tall, full, tall, full, wide, full,
        ],
        compiler_params=pltpu.CompilerParams(vmem_limit_bytes=40 * 1024 * 1024),
    )(offsets, counts, core, placed, amplitude, b_in, *x_in, *kb_in, *ka_in, a_in, *tables)
    return (*outs[:3], outs[3 : 3 + count], outs[3 + count : 3 + 2 * count], outs[3 + 2 * count :])


def finish_kernel(chans, object_ref, g_core, b_in, *rest):
    count = len(chans)
    x_in, kb_in, ka_in = rest[:count], rest[count : 2 * count], rest[2 * count : 3 * count]
    a_in, out = rest[3 * count :]
    size = object_ref.shape[1]
    lower = lower_partner()
    a_rows = pl.ds(pl.multiple_of(jnp.where(lower, size - MARGIN, 0), MARGIN), MARGIN)
    b_rows = pl.ds(pl.multiple_of(jnp.where(lower, 0, size - MARGIN), MARGIN), MARGIN)
    columns = []
    for channel in chans:
        right = takes_right(channel)
        mine = lane_ids() // (LANES // 2) == jnp.where(right, 1, 0)
        block = pl.multiple_of(jnp.where(right, size - LANES, 0), LANES)
        columns.append((mine, pl.ds(block, LANES)))

    def take(place, value):
        out[place] -= step_size * value

    def take_packed(rows, column, block):
        mine, lanes = column
        take((0, rows, lanes), jnp.where(mine, block, 0.0))
        take((1, rows, lanes), jnp.where(mine, swap_halves(block), 0.0))

    for part in range(2):
        out[part] = object_ref[part] - step_size * g_core[part]
        take((part, a_rows), a_in[part])
    for number, column in enumerate(columns):
        take_packed(slice(None), column, x_in[number][...])
        take_packed(a_rows, column, ka_in[number][...])

    @pl.when(b_partner())
    def _():
        for part in range(2):
            take((part, b_rows), b_in[part])
        for number, column in enumerate(columns):
            take_packed(b_rows, column, kb_in[number][...])


def finish_call(chans, object_field, g_core, a_in, b_in, x_in, ka_in, kb_in):
    vmem = pl.BlockSpec(memory_space=pltpu.VMEM)
    return pl.pallas_call(
        functools.partial(finish_kernel, chans),
        out_shape=jax.ShapeDtypeStruct(object_field.shape, F32),
        in_specs=[vmem] * (4 + 3 * len(chans)),
        out_specs=vmem,
        compiler_params=pltpu.CompilerParams(vmem_limit_bytes=6 * 1024 * 1024),
    )(object_field, g_core, b_in, *x_in, *kb_in, *ka_in, a_in)


def per_device(object_field, probe_field, intensity, view_offsets, view_counts):
    size = object_field.shape[1]
    mesh_rows, mesh_cols = lax.axis_size("row"), lax.axis_size("col")
    chans = channels(mesh_cols)
    tables = dft_tables(size)
    a_pairs, b_pairs = row_pairs(mesh_rows, 0), row_pairs(mesh_rows, 1)
    spare = spare_route(b_pairs, mesh_rows, mesh_cols)

    def over_rows(block, pairs, extra):
        route = [(i * mesh_cols + k, j * mesh_cols + k) for i, j in pairs for k in range(mesh_cols)]
        return lax.ppermute(block, ("row", "col"), route + extra)

    def across(block, pairs, extra, channel):
        route = [(i * mesh_cols + k, j * mesh_cols + l) for i, j in pairs for k, l in channel[0]]
        return lax.ppermute(block, ("row", "col"), route + (extra if mesh_cols == 2 else []))

    def exchange(a_send, b_send, x_send, ka_send, kb_send):
        x_in = [lax.ppermute(block, "col", channel[0]) for block, channel in zip(x_send, chans)]
        b_in = over_rows(b_send, b_pairs, spare)
        kb_in = [across(block, b_pairs, spare, channel) for block, channel in zip(kb_send, chans)]
        ka_in = [across(block, a_pairs, [], channel) for block, channel in zip(ka_send, chans)]
        a_in = over_rows(a_send, a_pairs, [])
        return a_in, b_in, x_in, ka_in, kb_in

    packs = pack_call(object_field, chans)
    offsets, probe, measured = (
        pltpu.with_memory_space_constraint(array, pltpu.HBM)
        for array in (jnp.swapaxes(view_offsets, 2, 3), probe_field, intensity)
    )
    margins = exchange(packs[0], packs[1], packs[2::3], packs[3::3], packs[4::3])
    placed, amplitude = prepare_call(offsets, view_counts, probe, measured)
    g_core, *sends = views_call(
        chans, offsets, view_counts, object_field, placed, amplitude, tables, *margins
    )
    return finish_call(chans, object_field, g_core, *exchange(*sends))


def solution(mesh):
    in_specs = (
        P(None, "row", "col"),
        P(),
        P("row", "col", None, None, None),
        P("row", "col", None, None),
        P("row", "col"),
    )
    out_specs = P(None, "row", "col")
    return jax.shard_map(
        per_device, mesh=mesh, in_specs=in_specs, out_specs=out_specs, check_vma=False
    )
```

```python
import functools
import itertools
import math

import jax
import jax.numpy as jnp
import ml_dtypes
import numpy as np
from jax import lax
from jax.experimental import pallas as pl
from jax.experimental.pallas import tpu as pltpu
from jax.sharding import PartitionSpec as P

MARGIN = 64
LANES = 128
CHUNK = 64
STAGGER = 4

smooth_eps = 0.1
step_size = 0.2

F32 = jnp.float32
BF16 = jnp.bfloat16


def dft_tables(length):
    half = length // 2
    counter = np.arange(half)
    factor = 1.0 / math.sqrt(length)
    product = np.outer(counter, counter)
    even = np.exp(-2j * np.pi * (product % half) / half) * factor
    odd = np.exp(-2j * np.pi * ((2 * product + counter[:, None]) % length) / length) * factor

    def as_real(table):
        return np.block([[table.real, table.imag], [-table.imag, table.real]])

    def parts(table):
        high = table.astype(ml_dtypes.bfloat16)
        low = (table - high.astype(np.float64)).astype(ml_dtypes.bfloat16)
        return high, low

    even, odd = as_real(even), as_real(odd)
    by_right = [np.concatenate(parts(t), 0) for t in (even, odd, even.T, odd.T)]
    by_left = [np.concatenate(parts(t), 1) for t in (even.T, odd.T, even, odd)]
    return np.stack(by_right), np.stack(by_left)


def channels(mesh_cols):
    if mesh_cols == 1:
        return []
    if mesh_cols == 2:
        return [([(0, 1), (1, 0)], None, None)]
    forward = [(i, i + 1) for i in range(mesh_cols - 1)]
    return [(forward, True, False), ([(j, i) for i, j in forward], False, True)]


def row_pairs(count, first):
    pairs = [(i, i + 1) for i in range(first, count - 1, 2)]
    return pairs + [(j, i) for i, j in pairs]


def spare_route(pairs, mesh_rows, mesh_cols):
    rows = [i for i in range(mesh_rows) if i not in dict(pairs)]
    if mesh_cols % 2:
        return []
    return [(i * mesh_cols + k, i * mesh_cols + (k ^ 1)) for i in rows for k in range(mesh_cols)]


def b_partner():
    row = lax.axis_index("row")
    return jnp.where(lower_partner(), row > 0, row < lax.axis_size("row") - 1)


def sends_right(channel):
    return lax.axis_index("col") == 0 if channel[1] is None else channel[1]


def takes_right(channel):
    return lax.axis_index("col") == 0 if channel[2] is None else channel[2]


def lower_partner():
    return lax.rem(lax.axis_index("row"), 2) == 0


def lane_ids():
    return lax.broadcasted_iota(jnp.int32, (1, LANES), 1)


def half_lanes(right):
    low = lane_ids() < LANES // 2
    if isinstance(right, bool):
        return low if right else ~low
    return lane_ids() // (LANES // 2) == jnp.where(right, 0, 1)


def split(value):
    high = value.astype(BF16)
    return high, (value - high.astype(F32)).astype(BF16)


def dot(first, second):
    return jnp.dot(first, second, preferred_element_type=F32)


def swap_halves(block):
    return pltpu.roll(block, LANES // 2, 1)


def fetch(pairs, sems):
    copies = [pltpu.make_async_copy(source, target, sems.at[i]) for i, (source, target) in enumerate(pairs)]
    for copy in copies:
        copy.start()
    return copies


def pack_kernel(chans, object_ref, a_ref, b_ref, *edge_refs):
    size = object_ref.shape[1]
    top, bottom = pl.ds(0, MARGIN), pl.ds(size - MARGIN, MARGIN)
    lower = lower_partner()
    for part in range(2):
        head, tail = object_ref[part, top, :], object_ref[part, bottom, :]
        a_ref[part] = jnp.where(lower, tail, head)
        b_ref[part] = jnp.where(lower, head, tail)
    for number, channel in enumerate(chans):
        right = sends_right(channel)
        x_ref, ka_ref, kb_ref = edge_refs[3 * number : 3 * number + 3]
        low = lane_ids() < LANES // 2
        for start in range(0, size, CHUNK):
            rows = slice(start, start + CHUNK)
            left_edge = jnp.where(
                low, object_ref[0, rows, :LANES], swap_halves(object_ref[1, rows, :LANES])
            )
            right_edge = jnp.where(
                low,
                swap_halves(object_ref[1, rows, size - LANES :]),
                object_ref[0, rows, size - LANES :],
            )
            x_ref[rows] = jnp.where(right, right_edge, left_edge)
        ka_ref[...] = jnp.where(lower, x_ref[size - MARGIN :], x_ref[:MARGIN])
        kb_ref[...] = jnp.where(lower, x_ref[:MARGIN], x_ref[size - MARGIN :])


def pack_call(object_field, chans):
    size = object_field.shape[1]
    shapes = [(2, MARGIN, size)] * 2 + [(size, LANES), (MARGIN, LANES), (MARGIN, LANES)] * len(chans)
    vmem = pl.BlockSpec(memory_space=pltpu.VMEM)
    return pl.pallas_call(
        functools.partial(pack_kernel, chans),
        out_shape=[jax.ShapeDtypeStruct(shape, F32) for shape in shapes],
        in_specs=[vmem],
        out_specs=[vmem] * len(shapes),
        compiler_params=pltpu.CompilerParams(vmem_limit_bytes=4 * 1024 * 1024),
    )(object_field)


def prepare_kernel(
    offsets_in, counts, probe, intensity, placed, amplitude, offsets, doubled, measured, sems
):
    views, size = measured.shape[0], probe.shape[1]
    half = size // 2
    copies = fetch(
        [(offsets_in, offsets)]
        + [(probe, doubled.at[:, pl.ds(size * i, size)]) for i in range(2)]
        + [(intensity.at[0, 0, view], measured.at[view]) for view in range(views)],
        sems,
    )
    source = lax.broadcasted_iota(jnp.int32, (size, size), 0)
    target = lax.broadcasted_iota(jnp.int32, (size, size), 1)
    order = (target == (source % 2) * half + source // 2).astype(F32).astype(BF16)
    sublane = lax.broadcasted_iota(jnp.int32, (1, 8, 1), 1)
    for copy in copies[:3]:
        copy.wait()
    for view in range(views):
        shift_row = lax.rem(offsets[0, 0, 0, view] - MARGIN + size, size)
        shift_col = lax.rem(offsets[0, 0, 1, view] - MARGIN + size, size)
        start = lax.rem(size - shift_row, size)
        whole = pl.multiple_of((start // 8) * 8, 8)
        rest = start - whole
        for part in range(2):
            for row in range(0, size, CHUNK):
                block = doubled[part, pl.ds(whole + row, CHUNK + 8), :]
                block = pltpu.roll(block, shift_col, 1).reshape(CHUNK // 8 + 1, 8, size)
                block = pltpu.roll(block, lax.rem(8 - rest, 8), 1)
                block = jnp.where(sublane < 8 - rest, block[:-1], block[1:])
                placed[view, part, row : row + CHUNK] = block.reshape(CHUNK, size)
    for view in range(views):
        copies[3 + view].wait()
        valid = (view < counts[0, 0]).astype(F32)
        power = measured[view] + smooth_eps
        high, low = split(power * lax.rsqrt(power) * valid)
        ordered = dot(high, order) + dot(low, order)
        amplitude[view, 0] = ordered[:, :half]
        amplitude[view, 1] = ordered[:, half:]


def prepare_call(offsets, counts, probe, intensity):
    views, size = intensity.shape[2], probe.shape[1]
    vmem, hbm = pl.BlockSpec(memory_space=pltpu.VMEM), pl.BlockSpec(memory_space=pltpu.HBM)
    return pl.pallas_call(
        prepare_kernel,
        out_shape=[
            jax.ShapeDtypeStruct((views, 2, size, size), F32),
            jax.ShapeDtypeStruct((views, 2, size, size // 2), F32),
        ],
        in_specs=[hbm, pl.BlockSpec(memory_space=pltpu.SMEM), hbm, hbm],
        out_specs=[vmem] * 2,
        scratch_shapes=[
            pltpu.SMEM(offsets.shape, jnp.int32),
            pltpu.VMEM((2, 2 * size, size), F32),
            pltpu.VMEM((views, size, size), F32),
            pltpu.SemaphoreType.DMA((3 + views,)),
        ],
        compiler_params=pltpu.CompilerParams(vmem_limit_bytes=16 * 1024 * 1024),
        cost_estimate=pl.CostEstimate(flops=10**9, bytes_accessed=10**5, transcendentals=0),
    )(offsets, counts, probe, intensity)


def views_kernel(chans, offsets_in, counts, core, placed, amplitude, *rest):
    count = len(chans)
    x_in, b_in, rest = rest[:count], rest[count], rest[count + 1 :]
    kb_in, ka_in = rest[:count], rest[count : 2 * count]
    a_in, right, left, *rest = rest[2 * count :]
    g_core, g_a, g_b = rest[:3]
    g_x, g_ka = rest[3 : 3 + count], rest[3 + count : 3 + 2 * count]
    g_kb = rest[3 + 2 * count : 3 + 3 * count]
    offsets, sem, cols_m, rows_m, corner_m, s1, y, s2, z, s3, u, s4, g = rest[3 + 3 * count :]
    (offsets_copy,) = fetch([(offsets_in, offsets)], sem)
    views, size = placed.shape[0], core.shape[1]
    half, m = size // 2, MARGIN
    lower, partner = lower_partner(), b_partner()
    low_lanes = lane_ids() < LANES // 2
    zero = jnp.zeros((CHUNK, LANES), F32)

    def unpack(blocks):
        re = im = None
        for channel, block in zip(chans, blocks):
            mine = half_lanes(takes_right(channel))
            re = jnp.where(mine, block, 0.0 if re is None else re)
            im = jnp.where(mine, swap_halves(block), 0.0 if im is None else im)
        return (re, im) if blocks else (jnp.zeros((MARGIN, LANES), F32),) * 2

    for row in range(0, size, CHUNK):
        rows = slice(row, row + CHUNK)
        cols_m[0, rows], cols_m[1, rows] = unpack([ref[rows] for ref in x_in]) if chans else (zero, zero)
    corner_a = unpack([ref[...] for ref in ka_in])
    corner_b = [jnp.where(partner, part, 0.0) for part in unpack([ref[...] for ref in kb_in])]
    for part in range(2):
        a_rows, b_rows = a_in[part], jnp.where(partner, b_in[part], 0.0)
        rows_m[part, :m] = jnp.where(lower, a_rows, b_rows)
        rows_m[part, m:] = jnp.where(lower, b_rows, a_rows)
        corner_m[part, :m] = jnp.where(lower, corner_a[part], corner_b[part])
        corner_m[part, m:] = jnp.where(lower, corner_b[part], corner_a[part])

    offsets_copy.wait()

    def by_right(lhs, t):
        out = dot(lhs[:, :size], right[t, :size]) + dot(lhs[:, size:], right[t, :size])
        return out + dot(lhs[:, :size], right[t, size:])

    def by_left(t, rhs):
        out = dot(left[t, :, :size], rhs[:size]) + dot(left[t, :, :size], rhs[size:])
        return out + dot(left[t, :, size:], rhs[:size])

    def put_below(ref, row, col, value):
        high, low = split(value)
        rows, cols = value.shape
        ref[row : row + rows, col : col + cols] = high
        ref[size + row : size + row + rows, col : col + cols] = low

    def put_beside(ref, row, col, value):
        high, low = split(value)
        rows, cols = value.shape
        ref[row : row + rows, col : col + cols] = high
        ref[row : row + rows, size + col : size + col + cols] = low

    def row_mask(view, row):
        ids = row + lax.broadcasted_iota(jnp.int32, (CHUNK, LANES), 0)
        if row < m:
            return ids < offsets[0, 0, 0, view] - m, row
        if row >= size - m:
            return ids >= size - m + offsets[0, 0, 0, view], row - size + 2 * m
        return None, None

    def col_mask(view, block):
        if block == 0:
            return lane_ids() < offsets[0, 0, 1, view] - m
        return lane_ids() >= m + offsets[0, 0, 1, view]

    def patch(view, row, block):
        cols = slice(block * LANES, (block + 1) * LANES)
        rows = slice(row, row + CHUNK)
        beside = col_mask(view, block)
        beyond, place = row_mask(view, row)
        found = []
        for part in range(2):
            value = jnp.where(beside, cols_m[part, rows], core[part, rows, cols])
            if beyond is not None:
                there = slice(place, place + CHUNK)
                outer = jnp.where(beside, corner_m[part, there], rows_m[part, there, cols])
                value = jnp.where(beyond, outer, value)
            found.append(value)
        return found

    def steps(view):
        for row in range(0, size, CHUNK):
            rows = slice(row, row + CHUNK)
            waves = []
            for block in range(2):
                cols = slice(block * LANES, (block + 1) * LANES)
                o_re, o_im = patch(view, row, block)
                p_re, p_im = placed[view, 0, rows, cols], placed[view, 1, rows, cols]
                waves.append((p_re * o_re - p_im * o_im, p_re * o_im + p_im * o_re))
            for part in range(2):
                put_beside(s1.at[view, 0], row, part * half, waves[0][part] + waves[1][part])
                put_beside(s1.at[view, 1], row, part * half, waves[0][part] - waves[1][part])
            yield
        for odd in range(2):
            y[view, odd] = by_right(s1.at[view, odd], odd)
            yield
        for odd in range(2):
            for row in range(0, half, CHUNK):
                for part in range(2):
                    cols = slice(part * half, (part + 1) * half)
                    above = y[view, odd, row : row + CHUNK, cols]
                    below = y[view, odd, half + row : half + row + CHUNK, cols]
                    put_below(s2.at[view, 0], part * half + row, odd * half, above + below)
                    put_below(s2.at[view, 1], part * half + row, odd * half, above - below)
                yield
        for odd in range(2):
            z[view, odd] = by_left(odd, s2.at[view, odd])
            yield
        valid = (view < counts[0, 0]).astype(F32)
        for odd in range(2):
            for row in range(0, half, CHUNK):
                re, im = z[view, odd, row : row + CHUNK], z[view, odd, half + row : half + row + CHUNK]
                taken = pl.ds(2 * row + odd, CHUNK, stride=2)
                wanted = jnp.concatenate([amplitude[view, 0, taken], amplitude[view, 1, taken]], 1)
                scaling = valid - wanted * lax.rsqrt(re * re + im * im + smooth_eps)
                put_below(s3.at[view, odd], row, 0, re * scaling)
                put_below(s3.at[view, odd], half + row, 0, im * scaling)
                yield
        for odd in range(2):
            u[view, odd] = by_left(2 + odd, s3.at[view, odd])
            yield
        for row in range(0, half, CHUNK):
            for part in range(2):
                rows = slice(part * half + row, part * half + row + CHUNK)
                even_rows, odd_rows = u[view, 0, rows], u[view, 1, rows]
                for value, place in ((even_rows + odd_rows, row), (even_rows - odd_rows, half + row)):
                    put_beside(s4.at[view, 0], place, part * half, value[:, :half])
                    put_beside(s4.at[view, 1], place, part * half, value[:, half:])
                yield
        for odd in range(2):
            g[view, odd] = by_right(s4.at[view, odd], 2 + odd)
            yield

    work = [steps(view) for view in range(views)]
    for view in range(views):
        for _ in range(view * STAGGER):
            work[view] = itertools.chain([None], work[view])
    for _ in itertools.zip_longest(*work):
        pass

    for row in range(0, size, CHUNK):
        rows = slice(row, row + CHUNK)
        sums = {}

        def add(key, value):
            sums[key] = sums[key] + value if key in sums else value

        for view in range(views):
            beyond, place = row_mask(view, row)
            halves = []
            for part in range(2):
                cols = slice(part * half, (part + 1) * half)
                even_cols, odd_cols = g[view, 0, rows, cols], g[view, 1, rows, cols]
                halves.append((even_cols + odd_cols, even_cols - odd_cols))
            for block in range(2):
                cols = slice(block * LANES, (block + 1) * LANES)
                beside = col_mask(view, block)
                b_re, b_im = halves[0][block], halves[1][block]
                p_re, p_im = placed[view, 0, rows, cols], placed[view, 1, rows, cols]
                for part, value in enumerate((p_re * b_re + p_im * b_im, p_re * b_im - p_im * b_re)):
                    if beyond is not None:
                        outer, value = jnp.where(beyond, value, zero), jnp.where(beyond, zero, value)
                        add(("corner", part), jnp.where(beside, outer, zero))
                        add(("row", part, block), jnp.where(beside, zero, outer))
                    add(("col", part), jnp.where(beside, value, zero))
                    add(("core", part, block), jnp.where(beside, zero, value))
        for part in range(2):
            cols_m[part, rows] = sums["col", part]
            if place is not None:
                corner_m[part, place : place + CHUNK] = sums["corner", part]
            for block in range(2):
                cols = slice(block * LANES, (block + 1) * LANES)
                g_core[part, rows, cols] = sums["core", part, block]
                if place is not None:
                    rows_m[part, place : place + CHUNK, cols] = sums["row", part, block]

    def packed(channel, re, im):
        to_right = jnp.where(low_lanes, re, swap_halves(im))
        to_left = jnp.where(low_lanes, swap_halves(im), re)
        return jnp.where(sends_right(channel), to_right, to_left)

    for part in range(2):
        bottom, top = rows_m[part, :m], rows_m[part, m:]
        g_a[part] = jnp.where(lower, bottom, top)
        g_b[part] = jnp.where(lower, top, bottom)
    bottom = (corner_m[0, :m], corner_m[1, :m])
    top = (corner_m[0, m:], corner_m[1, m:])
    for number, channel in enumerate(chans):
        for row in range(0, size, CHUNK):
            rows = slice(row, row + CHUNK)
            g_x[number][rows] = packed(channel, cols_m[0, rows], cols_m[1, rows])
        below, above = packed(channel, *bottom), packed(channel, *top)
        g_ka[number][...] = jnp.where(lower, below, above)
        g_kb[number][...] = jnp.where(lower, above, below)


def views_call(chans, offsets, counts, core, placed, amplitude, tables, a_in, b_in, x_in, ka_in, kb_in):
    views, size = placed.shape[0], core.shape[1]
    count = len(chans)
    vmem = pl.BlockSpec(memory_space=pltpu.VMEM)
    shapes = [(2, size, size), (2, MARGIN, size), (2, MARGIN, size)]
    shapes += [(size, LANES)] * count + [(MARGIN, LANES)] * (2 * count)
    full = pltpu.VMEM((views, 2, size, size), F32)
    tall = pltpu.VMEM((views, 2, 2 * size, size), BF16)
    wide = pltpu.VMEM((views, 2, size, 2 * size), BF16)
    outs = pl.pallas_call(
        functools.partial(views_kernel, chans),
        out_shape=[jax.ShapeDtypeStruct(shape, F32) for shape in shapes],
        in_specs=[
            pl.BlockSpec(memory_space=pltpu.HBM),
            pl.BlockSpec(memory_space=pltpu.SMEM),
            *[vmem] * (7 + 3 * count),
        ],
        out_specs=[vmem] * len(shapes),
        scratch_shapes=[
            pltpu.SMEM(offsets.shape, jnp.int32),
            pltpu.SemaphoreType.DMA((1,)),
            pltpu.VMEM((2, size, LANES), F32),
            pltpu.VMEM((2, 2 * MARGIN, size), F32),
            pltpu.VMEM((2, 2 * MARGIN, LANES), F32),
            wide, full, tall, full, tall, full, wide, full,
        ],
        compiler_params=pltpu.CompilerParams(vmem_limit_bytes=40 * 1024 * 1024),
    )(offsets, counts, core, placed, amplitude, *x_in, b_in, *kb_in, *ka_in, a_in, *tables)
    return (*outs[:3], outs[3 : 3 + count], outs[3 + count : 3 + 2 * count], outs[3 + 2 * count :])


def finish_kernel(chans, object_ref, g_core, *rest):
    count = len(chans)
    x_in, b_in, rest = rest[:count], rest[count], rest[count + 1 :]
    kb_in, ka_in = rest[:count], rest[count : 2 * count]
    a_in, out = rest[2 * count :]
    size = object_ref.shape[1]
    lower = lower_partner()
    a_rows = pl.ds(pl.multiple_of(jnp.where(lower, size - MARGIN, 0), MARGIN), MARGIN)
    b_rows = pl.ds(pl.multiple_of(jnp.where(lower, 0, size - MARGIN), MARGIN), MARGIN)
    columns = []
    for channel in chans:
        right = takes_right(channel)
        mine = lane_ids() // (LANES // 2) == jnp.where(right, 1, 0)
        block = pl.multiple_of(jnp.where(right, size - LANES, 0), LANES)
        columns.append((mine, pl.ds(block, LANES)))

    def take(place, value):
        out[place] -= step_size * value

    def take_packed(rows, column, block):
        mine, lanes = column
        take((0, rows, lanes), jnp.where(mine, block, 0.0))
        take((1, rows, lanes), jnp.where(mine, swap_halves(block), 0.0))

    for part in range(2):
        out[part] = object_ref[part] - step_size * g_core[part]
        take((part, a_rows), a_in[part])
    for number, column in enumerate(columns):
        take_packed(slice(None), column, x_in[number][...])
        take_packed(a_rows, column, ka_in[number][...])

    @pl.when(b_partner())
    def _():
        for part in range(2):
            take((part, b_rows), b_in[part])
        for number, column in enumerate(columns):
            take_packed(b_rows, column, kb_in[number][...])


def finish_call(chans, object_field, g_core, a_in, b_in, x_in, ka_in, kb_in):
    vmem = pl.BlockSpec(memory_space=pltpu.VMEM)
    return pl.pallas_call(
        functools.partial(finish_kernel, chans),
        out_shape=jax.ShapeDtypeStruct(object_field.shape, F32),
        in_specs=[vmem] * (4 + 3 * len(chans)),
        out_specs=vmem,
        compiler_params=pltpu.CompilerParams(vmem_limit_bytes=6 * 1024 * 1024),
    )(object_field, g_core, *x_in, b_in, *kb_in, *ka_in, a_in)


def per_device(object_field, probe_field, intensity, view_offsets, view_counts):
    size = object_field.shape[1]
    mesh_rows, mesh_cols = lax.axis_size("row"), lax.axis_size("col")
    chans = channels(mesh_cols)
    tables = dft_tables(size)
    a_pairs, b_pairs = row_pairs(mesh_rows, 0), row_pairs(mesh_rows, 1)
    spare = spare_route(b_pairs, mesh_rows, mesh_cols)

    def over_rows(block, pairs, extra):
        route = [(i * mesh_cols + k, j * mesh_cols + k) for i, j in pairs for k in range(mesh_cols)]
        return lax.ppermute(block, ("row", "col"), route + extra)

    def across(block, pairs, extra, channel):
        route = [(i * mesh_cols + k, j * mesh_cols + l) for i, j in pairs for k, l in channel[0]]
        return lax.ppermute(block, ("row", "col"), route + (extra if mesh_cols == 2 else []))

    def exchange(a_send, b_send, x_send, ka_send, kb_send):
        x_in = [lax.ppermute(block, "col", channel[0]) for block, channel in zip(x_send, chans)]
        b_in = over_rows(b_send, b_pairs, spare)
        kb_in = [across(block, b_pairs, spare, channel) for block, channel in zip(kb_send, chans)]
        ka_in = [across(block, a_pairs, [], channel) for block, channel in zip(ka_send, chans)]
        a_in = over_rows(a_send, a_pairs, [])
        return a_in, b_in, x_in, ka_in, kb_in

    packs = pack_call(object_field, chans)
    offsets, probe, measured = (
        pltpu.with_memory_space_constraint(array, pltpu.HBM)
        for array in (jnp.swapaxes(view_offsets, 2, 3), probe_field, intensity)
    )
    margins = exchange(packs[0], packs[1], packs[2::3], packs[3::3], packs[4::3])
    placed, amplitude = prepare_call(offsets, view_counts, probe, measured)
    g_core, *sends = views_call(
        chans, offsets, view_counts, object_field, placed, amplitude, tables, *margins
    )
    return finish_call(chans, object_field, g_core, *exchange(*sends))


def solution(mesh):
    in_specs = (
        P(None, "row", "col"),
        P(),
        P("row", "col", None, None, None),
        P("row", "col", None, None),
        P("row", "col"),
    )
    out_specs = P(None, "row", "col")
    return jax.shard_map(
        per_device, mesh=mesh, in_specs=in_specs, out_specs=out_specs, check_vma=False
    )
```

```python
import functools
import itertools
import math

import jax
import jax.numpy as jnp
import ml_dtypes
import numpy as np
from jax import lax
from jax.experimental import pallas as pl
from jax.experimental.pallas import tpu as pltpu
from jax.sharding import PartitionSpec as P

MARGIN = 64
LANES = 128
CHUNK = 64
STAGGER = 4

smooth_eps = 0.1
step_size = 0.2

F32 = jnp.float32
BF16 = jnp.bfloat16


def dft_tables(length):
    half = length // 2
    counter = np.arange(half)
    factor = 1.0 / math.sqrt(length)
    product = np.outer(counter, counter)
    even = np.exp(-2j * np.pi * (product % half) / half) * factor
    odd = np.exp(-2j * np.pi * ((2 * product + counter[:, None]) % length) / length) * factor

    def as_real(table):
        return np.block([[table.real, table.imag], [-table.imag, table.real]])

    def parts(table):
        high = table.astype(ml_dtypes.bfloat16)
        low = (table - high.astype(np.float64)).astype(ml_dtypes.bfloat16)
        return high, low

    even, odd = as_real(even), as_real(odd)
    by_right = [np.concatenate(parts(t), 0) for t in (even, odd, even.T, odd.T)]
    by_left = [np.concatenate(parts(t), 1) for t in (even.T, odd.T, even, odd)]
    return np.stack(by_right), np.stack(by_left)


def channels(mesh_cols):
    if mesh_cols == 1:
        return []
    if mesh_cols == 2:
        return [([(0, 1), (1, 0)], None, None)]
    forward = [(i, i + 1) for i in range(mesh_cols - 1)]
    return [(forward, True, False), ([(j, i) for i, j in forward], False, True)]


def row_pairs(count, first):
    pairs = [(i, i + 1) for i in range(first, count - 1, 2)]
    return pairs + [(j, i) for i, j in pairs]


def spare_route(pairs, mesh_rows, mesh_cols):
    rows = [i for i in range(mesh_rows) if i not in dict(pairs)]
    if mesh_cols % 2:
        return []
    return [(i * mesh_cols + k, i * mesh_cols + (k ^ 1)) for i in rows for k in range(mesh_cols)]


def b_partner():
    row = lax.axis_index("row")
    return jnp.where(lower_partner(), row > 0, row < lax.axis_size("row") - 1)


def sends_right(channel):
    return lax.axis_index("col") == 0 if channel[1] is None else channel[1]


def takes_right(channel):
    return lax.axis_index("col") == 0 if channel[2] is None else channel[2]


def lower_partner():
    return lax.rem(lax.axis_index("row"), 2) == 0


def lane_ids():
    return lax.broadcasted_iota(jnp.int32, (1, LANES), 1)


def half_lanes(right):
    low = lane_ids() < LANES // 2
    if isinstance(right, bool):
        return low if right else ~low
    return lane_ids() // (LANES // 2) == jnp.where(right, 0, 1)


def split(value):
    high = value.astype(BF16)
    return high, (value - high.astype(F32)).astype(BF16)


def dot(first, second):
    return jnp.dot(first, second, preferred_element_type=F32)


def swap_halves(block):
    return pltpu.roll(block, LANES // 2, 1)


def fetch(pairs, sems):
    copies = [pltpu.make_async_copy(source, target, sems.at[i]) for i, (source, target) in enumerate(pairs)]
    for copy in copies:
        copy.start()
    return copies


def pack_kernel(chans, object_ref, a_ref, b_ref, *edge_refs):
    size = object_ref.shape[1]
    top, bottom = pl.ds(0, MARGIN), pl.ds(size - MARGIN, MARGIN)
    lower = lower_partner()
    for part in range(2):
        head, tail = object_ref[part, top, :], object_ref[part, bottom, :]
        a_ref[part] = jnp.where(lower, tail, head)
        b_ref[part] = jnp.where(lower, head, tail)
    for number, channel in enumerate(chans):
        right = sends_right(channel)
        x_ref, ka_ref, kb_ref = edge_refs[3 * number : 3 * number + 3]
        low = lane_ids() < LANES // 2
        for start in range(0, size, CHUNK):
            rows = slice(start, start + CHUNK)
            left_edge = jnp.where(
                low, object_ref[0, rows, :LANES], swap_halves(object_ref[1, rows, :LANES])
            )
            right_edge = jnp.where(
                low,
                swap_halves(object_ref[1, rows, size - LANES :]),
                object_ref[0, rows, size - LANES :],
            )
            x_ref[rows] = jnp.where(right, right_edge, left_edge)
        ka_ref[...] = jnp.where(lower, x_ref[size - MARGIN :], x_ref[:MARGIN])
        kb_ref[...] = jnp.where(lower, x_ref[:MARGIN], x_ref[size - MARGIN :])


def pack_call(object_field, chans):
    size = object_field.shape[1]
    shapes = [(2, MARGIN, size)] * 2 + [(size, LANES), (MARGIN, LANES), (MARGIN, LANES)] * len(chans)
    vmem = pl.BlockSpec(memory_space=pltpu.VMEM)
    return pl.pallas_call(
        functools.partial(pack_kernel, chans),
        out_shape=[jax.ShapeDtypeStruct(shape, F32) for shape in shapes],
        in_specs=[vmem],
        out_specs=[vmem] * len(shapes),
        compiler_params=pltpu.CompilerParams(vmem_limit_bytes=4 * 1024 * 1024),
    )(object_field)


def prepare_kernel(offsets_in, probe, placed, offsets, doubled, sems):
    views, size = placed.shape[0], probe.shape[1]
    copies = fetch(
        [(offsets_in, offsets)] + [(probe, doubled.at[:, pl.ds(size * i, size)]) for i in range(2)], sems
    )
    sublane = lax.broadcasted_iota(jnp.int32, (1, 8, 1), 1)
    for copy in copies:
        copy.wait()
    for view in range(views):
        shift_row = lax.rem(offsets[0, 0, 0, view] - MARGIN + size, size)
        shift_col = lax.rem(offsets[0, 0, 1, view] - MARGIN + size, size)
        start = lax.rem(size - shift_row, size)
        whole = pl.multiple_of((start // 8) * 8, 8)
        rest = start - whole
        for part in range(2):
            for row in range(0, size, CHUNK):
                block = doubled[part, pl.ds(whole + row, CHUNK + 8), :]
                block = pltpu.roll(block, shift_col, 1).reshape(CHUNK // 8 + 1, 8, size)
                block = pltpu.roll(block, lax.rem(8 - rest, 8), 1)
                block = jnp.where(sublane < 8 - rest, block[:-1], block[1:])
                placed[view, part, row : row + CHUNK] = block.reshape(CHUNK, size)


def prepare_call(offsets, probe):
    views, size = offsets.shape[3], probe.shape[1]
    vmem, hbm = pl.BlockSpec(memory_space=pltpu.VMEM), pl.BlockSpec(memory_space=pltpu.HBM)
    return pl.pallas_call(
        prepare_kernel,
        out_shape=jax.ShapeDtypeStruct((views, 2, size, size), F32),
        in_specs=[hbm, hbm],
        out_specs=vmem,
        scratch_shapes=[
            pltpu.SMEM(offsets.shape, jnp.int32),
            pltpu.VMEM((2, 2 * size, size), F32),
            pltpu.SemaphoreType.DMA((3,)),
        ],
        compiler_params=pltpu.CompilerParams(vmem_limit_bytes=16 * 1024 * 1024),
        cost_estimate=pl.CostEstimate(flops=10**9, bytes_accessed=10**5, transcendentals=0),
    )(offsets, probe)


def views_kernel(chans, offsets_in, counts, core, placed, intensity, *rest):
    count = len(chans)
    x_in, b_in, rest = rest[:count], rest[count], rest[count + 1 :]
    kb_in, ka_in = rest[:count], rest[count : 2 * count]
    a_in, right, left, *rest = rest[2 * count :]
    g_core, g_a, g_b = rest[:3]
    g_x, g_ka = rest[3 : 3 + count], rest[3 + count : 3 + 2 * count]
    g_kb = rest[3 + 2 * count : 3 + 3 * count]
    offsets, sem, amplitude, cols_m, rows_m, corner_m, s1, y, s2, z, s3, u, s4, g = rest[3 + 3 * count :]
    (offsets_copy,) = fetch([(offsets_in, offsets)], sem)
    views, size = placed.shape[0], core.shape[1]
    half, m = size // 2, MARGIN
    lower, partner = lower_partner(), b_partner()
    low_lanes = lane_ids() < LANES // 2
    zero = jnp.zeros((CHUNK, LANES), F32)

    def unpack(blocks):
        re = im = None
        for channel, block in zip(chans, blocks):
            mine = half_lanes(takes_right(channel))
            re = jnp.where(mine, block, 0.0 if re is None else re)
            im = jnp.where(mine, swap_halves(block), 0.0 if im is None else im)
        return (re, im) if blocks else (jnp.zeros((MARGIN, LANES), F32),) * 2

    for row in range(0, size, CHUNK):
        rows = slice(row, row + CHUNK)
        cols_m[0, rows], cols_m[1, rows] = unpack([ref[rows] for ref in x_in]) if chans else (zero, zero)
    corner_a = unpack([ref[...] for ref in ka_in])
    corner_b = [jnp.where(partner, part, 0.0) for part in unpack([ref[...] for ref in kb_in])]
    for part in range(2):
        a_rows, b_rows = a_in[part], jnp.where(partner, b_in[part], 0.0)
        rows_m[part, :m] = jnp.where(lower, a_rows, b_rows)
        rows_m[part, m:] = jnp.where(lower, b_rows, a_rows)
        corner_m[part, :m] = jnp.where(lower, corner_a[part], corner_b[part])
        corner_m[part, m:] = jnp.where(lower, corner_b[part], corner_a[part])

    offsets_copy.wait()

    def by_right(lhs, t):
        out = dot(lhs[:, :size], right[t, :size]) + dot(lhs[:, size:], right[t, :size])
        return out + dot(lhs[:, :size], right[t, size:])

    def by_left(t, rhs):
        out = dot(left[t, :, :size], rhs[:size]) + dot(left[t, :, :size], rhs[size:])
        return out + dot(left[t, :, size:], rhs[:size])

    def put_below(ref, row, col, value):
        high, low = split(value)
        rows, cols = value.shape
        ref[row : row + rows, col : col + cols] = high
        ref[size + row : size + row + rows, col : col + cols] = low

    def put_beside(ref, row, col, value):
        high, low = split(value)
        rows, cols = value.shape
        ref[row : row + rows, col : col + cols] = high
        ref[row : row + rows, size + col : size + col + cols] = low

    def row_mask(view, row):
        ids = row + lax.broadcasted_iota(jnp.int32, (CHUNK, LANES), 0)
        if row < m:
            return ids < offsets[0, 0, 0, view] - m, row
        if row >= size - m:
            return ids >= size - m + offsets[0, 0, 0, view], row - size + 2 * m
        return None, None

    def col_mask(view, block):
        if block == 0:
            return lane_ids() < offsets[0, 0, 1, view] - m
        return lane_ids() >= m + offsets[0, 0, 1, view]

    def patch(view, row, block):
        cols = slice(block * LANES, (block + 1) * LANES)
        rows = slice(row, row + CHUNK)
        beside = col_mask(view, block)
        beyond, place = row_mask(view, row)
        found = []
        for part in range(2):
            value = jnp.where(beside, cols_m[part, rows], core[part, rows, cols])
            if beyond is not None:
                there = slice(place, place + CHUNK)
                outer = jnp.where(beside, corner_m[part, there], rows_m[part, there, cols])
                value = jnp.where(beyond, outer, value)
            found.append(value)
        return found

    def steps(view):
        for row in range(0, size, CHUNK):
            rows = slice(row, row + CHUNK)
            waves = []
            for block in range(2):
                cols = slice(block * LANES, (block + 1) * LANES)
                o_re, o_im = patch(view, row, block)
                p_re, p_im = placed[view, 0, rows, cols], placed[view, 1, rows, cols]
                waves.append((p_re * o_re - p_im * o_im, p_re * o_im + p_im * o_re))
            for part in range(2):
                put_beside(s1.at[view, 0], row, part * half, waves[0][part] + waves[1][part])
                put_beside(s1.at[view, 1], row, part * half, waves[0][part] - waves[1][part])
            yield
        for odd in range(2):
            y[view, odd] = by_right(s1.at[view, odd], odd)
            yield
        for odd in range(2):
            for row in range(0, half, CHUNK):
                for part in range(2):
                    cols = slice(part * half, (part + 1) * half)
                    above = y[view, odd, row : row + CHUNK, cols]
                    below = y[view, odd, half + row : half + row + CHUNK, cols]
                    put_below(s2.at[view, 0], part * half + row, odd * half, above + below)
                    put_below(s2.at[view, 1], part * half + row, odd * half, above - below)
                yield
        valid = (view < counts[0, 0]).astype(F32)
        for row in range(0, size, CHUNK):
            rows = slice(row, row + CHUNK)
            lanes = lax.broadcasted_iota(jnp.int32, (CHUNK, LANES), 1)
            wanted = []
            for block in range(2):
                power = intensity[0, 0, view, rows, block * LANES : (block + 1) * LANES] + smooth_eps
                wanted.append(power * lax.rsqrt(power) * valid)
            for odd in range(2):
                taken = lax.rem(2 * lanes + odd, LANES)
                ordered = [jnp.take_along_axis(block, taken, axis=1) for block in wanted]
                amplitude[view, odd, rows] = jnp.where(lanes < LANES // 2, *ordered)
        yield
        for odd in range(2):
            z[view, odd] = by_left(odd, s2.at[view, odd])
            yield
        for odd in range(2):
            for row in range(0, half, CHUNK):
                re, im = z[view, odd, row : row + CHUNK], z[view, odd, half + row : half + row + CHUNK]
                taken = pl.ds(2 * row + odd, CHUNK, stride=2)
                wanted = jnp.concatenate([amplitude[view, 0, taken], amplitude[view, 1, taken]], 1)
                scaling = valid - wanted * lax.rsqrt(re * re + im * im + smooth_eps)
                put_below(s3.at[view, odd], row, 0, re * scaling)
                put_below(s3.at[view, odd], half + row, 0, im * scaling)
                yield
        for odd in range(2):
            u[view, odd] = by_left(2 + odd, s3.at[view, odd])
            yield
        for row in range(0, half, CHUNK):
            for part in range(2):
                rows = slice(part * half + row, part * half + row + CHUNK)
                even_rows, odd_rows = u[view, 0, rows], u[view, 1, rows]
                for value, place in ((even_rows + odd_rows, row), (even_rows - odd_rows, half + row)):
                    put_beside(s4.at[view, 0], place, part * half, value[:, :half])
                    put_beside(s4.at[view, 1], place, part * half, value[:, half:])
                yield
        for odd in range(2):
            g[view, odd] = by_right(s4.at[view, odd], 2 + odd)
            yield

    work = [steps(view) for view in range(views)]
    for view in range(views):
        for _ in range(view * STAGGER):
            work[view] = itertools.chain([None], work[view])
    for _ in itertools.zip_longest(*work):
        pass

    for row in range(0, size, CHUNK):
        rows = slice(row, row + CHUNK)
        sums = {}

        def add(key, value):
            sums[key] = sums[key] + value if key in sums else value

        for view in range(views):
            beyond, place = row_mask(view, row)
            halves = []
            for part in range(2):
                cols = slice(part * half, (part + 1) * half)
                even_cols, odd_cols = g[view, 0, rows, cols], g[view, 1, rows, cols]
                halves.append((even_cols + odd_cols, even_cols - odd_cols))
            for block in range(2):
                cols = slice(block * LANES, (block + 1) * LANES)
                beside = col_mask(view, block)
                b_re, b_im = halves[0][block], halves[1][block]
                p_re, p_im = placed[view, 0, rows, cols], placed[view, 1, rows, cols]
                for part, value in enumerate((p_re * b_re + p_im * b_im, p_re * b_im - p_im * b_re)):
                    if beyond is not None:
                        outer, value = jnp.where(beyond, value, zero), jnp.where(beyond, zero, value)
                        add(("corner", part), jnp.where(beside, outer, zero))
                        add(("row", part, block), jnp.where(beside, zero, outer))
                    add(("col", part), jnp.where(beside, value, zero))
                    add(("core", part, block), jnp.where(beside, zero, value))
        for part in range(2):
            cols_m[part, rows] = sums["col", part]
            if place is not None:
                corner_m[part, place : place + CHUNK] = sums["corner", part]
            for block in range(2):
                cols = slice(block * LANES, (block + 1) * LANES)
                g_core[part, rows, cols] = sums["core", part, block]
                if place is not None:
                    rows_m[part, place : place + CHUNK, cols] = sums["row", part, block]

    def packed(channel, re, im):
        to_right = jnp.where(low_lanes, re, swap_halves(im))
        to_left = jnp.where(low_lanes, swap_halves(im), re)
        return jnp.where(sends_right(channel), to_right, to_left)

    for part in range(2):
        bottom, top = rows_m[part, :m], rows_m[part, m:]
        g_a[part] = jnp.where(lower, bottom, top)
        g_b[part] = jnp.where(lower, top, bottom)
    bottom = (corner_m[0, :m], corner_m[1, :m])
    top = (corner_m[0, m:], corner_m[1, m:])
    for number, channel in enumerate(chans):
        for row in range(0, size, CHUNK):
            rows = slice(row, row + CHUNK)
            g_x[number][rows] = packed(channel, cols_m[0, rows], cols_m[1, rows])
        below, above = packed(channel, *bottom), packed(channel, *top)
        g_ka[number][...] = jnp.where(lower, below, above)
        g_kb[number][...] = jnp.where(lower, above, below)


def views_call(chans, offsets, counts, core, placed, intensity, tables, a_in, b_in, x_in, ka_in, kb_in):
    views, size = placed.shape[0], core.shape[1]
    count = len(chans)
    vmem = pl.BlockSpec(memory_space=pltpu.VMEM)
    shapes = [(2, size, size), (2, MARGIN, size), (2, MARGIN, size)]
    shapes += [(size, LANES)] * count + [(MARGIN, LANES)] * (2 * count)
    full = pltpu.VMEM((views, 2, size, size), F32)
    tall = pltpu.VMEM((views, 2, 2 * size, size), BF16)
    wide = pltpu.VMEM((views, 2, size, 2 * size), BF16)
    outs = pl.pallas_call(
        functools.partial(views_kernel, chans),
        out_shape=[jax.ShapeDtypeStruct(shape, F32) for shape in shapes],
        in_specs=[
            pl.BlockSpec(memory_space=pltpu.HBM),
            pl.BlockSpec(memory_space=pltpu.SMEM),
            *[vmem] * (7 + 3 * count),
        ],
        out_specs=[vmem] * len(shapes),
        scratch_shapes=[
            pltpu.SMEM(offsets.shape, jnp.int32),
            pltpu.SemaphoreType.DMA((1,)),
            pltpu.VMEM((views, 2, size, size // 2), F32),
            pltpu.VMEM((2, size, LANES), F32),
            pltpu.VMEM((2, 2 * MARGIN, size), F32),
            pltpu.VMEM((2, 2 * MARGIN, LANES), F32),
            wide, full, tall, full, tall, full, wide, full,
        ],
        compiler_params=pltpu.CompilerParams(vmem_limit_bytes=40 * 1024 * 1024),
    )(offsets, counts, core, placed, intensity, *x_in, b_in, *kb_in, *ka_in, a_in, *tables)
    return (*outs[:3], outs[3 : 3 + count], outs[3 + count : 3 + 2 * count], outs[3 + 2 * count :])


def finish_kernel(chans, object_ref, g_core, *rest):
    count = len(chans)
    x_in, b_in, rest = rest[:count], rest[count], rest[count + 1 :]
    kb_in, ka_in = rest[:count], rest[count : 2 * count]
    a_in, out = rest[2 * count :]
    size = object_ref.shape[1]
    lower = lower_partner()
    a_rows = pl.ds(pl.multiple_of(jnp.where(lower, size - MARGIN, 0), MARGIN), MARGIN)
    b_rows = pl.ds(pl.multiple_of(jnp.where(lower, 0, size - MARGIN), MARGIN), MARGIN)
    columns = []
    for channel in chans:
        right = takes_right(channel)
        mine = lane_ids() // (LANES // 2) == jnp.where(right, 1, 0)
        block = pl.multiple_of(jnp.where(right, size - LANES, 0), LANES)
        columns.append((mine, pl.ds(block, LANES)))

    def take(place, value):
        out[place] -= step_size * value

    def take_packed(rows, column, block):
        mine, lanes = column
        take((0, rows, lanes), jnp.where(mine, block, 0.0))
        take((1, rows, lanes), jnp.where(mine, swap_halves(block), 0.0))

    for part in range(2):
        out[part] = object_ref[part] - step_size * g_core[part]
        take((part, a_rows), a_in[part])
    for number, column in enumerate(columns):
        take_packed(slice(None), column, x_in[number][...])
        take_packed(a_rows, column, ka_in[number][...])

    @pl.when(b_partner())
    def _():
        for part in range(2):
            take((part, b_rows), b_in[part])
        for number, column in enumerate(columns):
            take_packed(b_rows, column, kb_in[number][...])


def finish_call(chans, object_field, g_core, a_in, b_in, x_in, ka_in, kb_in):
    vmem = pl.BlockSpec(memory_space=pltpu.VMEM)
    return pl.pallas_call(
        functools.partial(finish_kernel, chans),
        out_shape=jax.ShapeDtypeStruct(object_field.shape, F32),
        in_specs=[vmem] * (4 + 3 * len(chans)),
        out_specs=vmem,
        compiler_params=pltpu.CompilerParams(vmem_limit_bytes=6 * 1024 * 1024),
    )(object_field, g_core, *x_in, b_in, *kb_in, *ka_in, a_in)


def per_device(object_field, probe_field, intensity, view_offsets, view_counts):
    size = object_field.shape[1]
    mesh_rows, mesh_cols = lax.axis_size("row"), lax.axis_size("col")
    chans = channels(mesh_cols)
    tables = dft_tables(size)
    a_pairs, b_pairs = row_pairs(mesh_rows, 0), row_pairs(mesh_rows, 1)
    spare = spare_route(b_pairs, mesh_rows, mesh_cols)

    def over_rows(block, pairs, extra):
        route = [(i * mesh_cols + k, j * mesh_cols + k) for i, j in pairs for k in range(mesh_cols)]
        return lax.ppermute(block, ("row", "col"), route + extra)

    def across(block, pairs, extra, channel):
        route = [(i * mesh_cols + k, j * mesh_cols + l) for i, j in pairs for k, l in channel[0]]
        return lax.ppermute(block, ("row", "col"), route + (extra if mesh_cols == 2 else []))

    def exchange(a_send, b_send, x_send, ka_send, kb_send):
        x_in = [lax.ppermute(block, "col", channel[0]) for block, channel in zip(x_send, chans)]
        b_in = over_rows(b_send, b_pairs, spare)
        kb_in = [across(block, b_pairs, spare, channel) for block, channel in zip(kb_send, chans)]
        ka_in = [across(block, a_pairs, [], channel) for block, channel in zip(ka_send, chans)]
        a_in = over_rows(a_send, a_pairs, [])
        return a_in, b_in, x_in, ka_in, kb_in

    packs = pack_call(object_field, chans)
    offsets, probe = (
        pltpu.with_memory_space_constraint(array, pltpu.HBM)
        for array in (jnp.swapaxes(view_offsets, 2, 3), probe_field)
    )
    margins = exchange(packs[0], packs[1], packs[2::3], packs[3::3], packs[4::3])
    placed = prepare_call(offsets, probe)
    g_core, *sends = views_call(
        chans, offsets, view_counts, object_field, placed, intensity, tables, *margins
    )
    return finish_call(chans, object_field, g_core, *exchange(*sends))


def solution(mesh):
    in_specs = (
        P(None, "row", "col"),
        P(),
        P("row", "col", None, None, None),
        P("row", "col", None, None),
        P("row", "col"),
    )
    out_specs = P(None, "row", "col")
    return jax.shard_map(
        per_device, mesh=mesh, in_specs=in_specs, out_specs=out_specs, check_vma=False
    )
```

```python
import functools
import itertools
import math

import jax
import jax.numpy as jnp
import ml_dtypes
import numpy as np
from jax import lax
from jax.experimental import pallas as pl
from jax.experimental.pallas import tpu as pltpu
from jax.sharding import PartitionSpec as P

MARGIN = 64
LANES = 128
CHUNK = 64
STAGGER = 4

smooth_eps = 0.1
step_size = 0.2

F32 = jnp.float32
BF16 = jnp.bfloat16


def dft_tables(length):
    half = length // 2
    counter = np.arange(half)
    factor = 1.0 / math.sqrt(length)
    product = np.outer(counter, counter)
    even = np.exp(-2j * np.pi * (product % half) / half) * factor
    odd = np.exp(-2j * np.pi * ((2 * product + counter[:, None]) % length) / length) * factor

    def as_real(table):
        return np.block([[table.real, table.imag], [-table.imag, table.real]])

    def parts(table):
        high = table.astype(ml_dtypes.bfloat16)
        low = (table - high.astype(np.float64)).astype(ml_dtypes.bfloat16)
        return high, low

    even, odd = as_real(even), as_real(odd)
    by_right = [np.concatenate(parts(t), 0) for t in (even, odd, even.T, odd.T)]
    by_left = [np.concatenate(parts(t), 1) for t in (even.T, odd.T, even, odd)]
    return np.stack(by_right), np.stack(by_left)


def channels(mesh_cols):
    if mesh_cols == 1:
        return []
    if mesh_cols == 2:
        return [([(0, 1), (1, 0)], None, None)]
    forward = [(i, i + 1) for i in range(mesh_cols - 1)]
    return [(forward, True, False), ([(j, i) for i, j in forward], False, True)]


def row_pairs(count, first):
    pairs = [(i, i + 1) for i in range(first, count - 1, 2)]
    return pairs + [(j, i) for i, j in pairs]


def spare_route(pairs, mesh_rows, mesh_cols):
    rows = [i for i in range(mesh_rows) if i not in dict(pairs)]
    if mesh_cols % 2:
        return []
    return [(i * mesh_cols + k, i * mesh_cols + (k ^ 1)) for i in rows for k in range(mesh_cols)]


def b_partner():
    row = lax.axis_index("row")
    return jnp.where(lower_partner(), row > 0, row < lax.axis_size("row") - 1)


def sends_right(channel):
    return lax.axis_index("col") == 0 if channel[1] is None else channel[1]


def takes_right(channel):
    return lax.axis_index("col") == 0 if channel[2] is None else channel[2]


def lower_partner():
    return lax.rem(lax.axis_index("row"), 2) == 0


def lane_ids():
    return lax.broadcasted_iota(jnp.int32, (1, LANES), 1)


def half_lanes(right):
    low = lane_ids() < LANES // 2
    if isinstance(right, bool):
        return low if right else ~low
    return lane_ids() // (LANES // 2) == jnp.where(right, 0, 1)


def split(value):
    high = value.astype(BF16)
    return high, (value - high.astype(F32)).astype(BF16)


def dot(first, second):
    return jnp.dot(first, second, preferred_element_type=F32)


def swap_halves(block):
    return pltpu.roll(block, LANES // 2, 1)


def fetch(pairs, sems):
    copies = [pltpu.make_async_copy(source, target, sems.at[i]) for i, (source, target) in enumerate(pairs)]
    for copy in copies:
        copy.start()
    return copies


def pack_kernel(chans, counts, object_ref, a_ref, b_ref, *edge_refs):
    size = object_ref.shape[1]
    top, bottom = pl.ds(0, MARGIN), pl.ds(size - MARGIN, MARGIN)
    lower = lower_partner()
    for part in range(2):
        head, tail = object_ref[part, top, :], object_ref[part, bottom, :]
        a_ref[part] = jnp.where(lower, tail, head)
        b_ref[part] = jnp.where(lower, head, tail)
    for number, channel in enumerate(chans):
        right = sends_right(channel)
        x_ref, ka_ref, kb_ref = edge_refs[3 * number : 3 * number + 3]
        low = lane_ids() < LANES // 2
        for start in range(0, size, CHUNK):
            rows = slice(start, start + CHUNK)
            left_edge = jnp.where(
                low, object_ref[0, rows, :LANES], swap_halves(object_ref[1, rows, :LANES])
            )
            right_edge = jnp.where(
                low,
                swap_halves(object_ref[1, rows, size - LANES :]),
                object_ref[0, rows, size - LANES :],
            )
            x_ref[rows] = jnp.where(right, right_edge, left_edge)
        ka_ref[...] = jnp.where(lower, x_ref[size - MARGIN :], x_ref[:MARGIN])
        kb_ref[...] = jnp.where(lower, x_ref[:MARGIN], x_ref[size - MARGIN :])


def pack_call(counts, object_field, chans):
    size = object_field.shape[1]
    shapes = [(2, MARGIN, size)] * 2 + [(size, LANES), (MARGIN, LANES), (MARGIN, LANES)] * len(chans)
    vmem = pl.BlockSpec(memory_space=pltpu.VMEM)
    return pl.pallas_call(
        functools.partial(pack_kernel, chans),
        out_shape=[jax.ShapeDtypeStruct(shape, F32) for shape in shapes],
        in_specs=[pl.BlockSpec(memory_space=pltpu.SMEM), vmem],
        out_specs=[vmem] * len(shapes),
        compiler_params=pltpu.CompilerParams(vmem_limit_bytes=4 * 1024 * 1024),
    )(counts, object_field)


def prepare_kernel(offsets_in, probe, placed, offsets, doubled, sems):
    views, size = placed.shape[0], probe.shape[1]
    copies = fetch(
        [(offsets_in, offsets)] + [(probe, doubled.at[:, pl.ds(size * i, size)]) for i in range(2)], sems
    )
    sublane = lax.broadcasted_iota(jnp.int32, (1, 8, 1), 1)
    for copy in copies:
        copy.wait()
    for view in range(views):
        shift_row = lax.rem(offsets[0, 0, 0, view] - MARGIN + size, size)
        shift_col = lax.rem(offsets[0, 0, 1, view] - MARGIN + size, size)
        start = lax.rem(size - shift_row, size)
        whole = pl.multiple_of((start // 8) * 8, 8)
        rest = start - whole
        for part in range(2):
            for row in range(0, size, CHUNK):
                block = doubled[part, pl.ds(whole + row, CHUNK + 8), :]
                block = pltpu.roll(block, shift_col, 1).reshape(CHUNK // 8 + 1, 8, size)
                block = pltpu.roll(block, lax.rem(8 - rest, 8), 1)
                block = jnp.where(sublane < 8 - rest, block[:-1], block[1:])
                placed[view, part, row : row + CHUNK] = block.reshape(CHUNK, size)


def prepare_call(offsets, probe):
    views, size = offsets.shape[3], probe.shape[1]
    vmem, hbm = pl.BlockSpec(memory_space=pltpu.VMEM), pl.BlockSpec(memory_space=pltpu.HBM)
    return pl.pallas_call(
        prepare_kernel,
        out_shape=jax.ShapeDtypeStruct((views, 2, size, size), F32),
        in_specs=[hbm, hbm],
        out_specs=vmem,
        scratch_shapes=[
            pltpu.SMEM(offsets.shape, jnp.int32),
            pltpu.VMEM((2, 2 * size, size), F32),
            pltpu.SemaphoreType.DMA((3,)),
        ],
        compiler_params=pltpu.CompilerParams(vmem_limit_bytes=16 * 1024 * 1024),
        cost_estimate=pl.CostEstimate(flops=10**9, bytes_accessed=10**5, transcendentals=0),
    )(offsets, probe)


def a_corner(size, number):
    return slice(2 * size + number * LANES, 2 * size + (number + 1) * LANES)


def views_kernel(chans, offsets_in, counts, core, placed, intensity, *rest):
    count = len(chans)
    x_in, b_in, rest = rest[:count], rest[count], rest[count + 1 :]
    kb_in, ka_in = rest[:count], rest[count : 2 * count]
    a_in, right, left, *rest = rest[2 * count :]
    base, g_a, g_b = rest[:3]
    g_x, g_kb = rest[3 : 3 + count], rest[3 + count : 3 + 2 * count]
    offsets, sem, amplitude, cols_m, rows_m, corner_m, s1, y, s2, z, s3, u, s4, g = rest[3 + 2 * count :]
    (offsets_copy,) = fetch([(offsets_in, offsets)], sem)
    views, size = placed.shape[0], core.shape[1]
    half, m = size // 2, MARGIN
    lower, partner = lower_partner(), b_partner()
    low_lanes = lane_ids() < LANES // 2
    zero = jnp.zeros((CHUNK, LANES), F32)

    def unpack(blocks):
        re = im = None
        for channel, block in zip(chans, blocks):
            mine = half_lanes(takes_right(channel))
            re = jnp.where(mine, block, 0.0 if re is None else re)
            im = jnp.where(mine, swap_halves(block), 0.0 if im is None else im)
        return (re, im) if blocks else (jnp.zeros((MARGIN, LANES), F32),) * 2

    for row in range(0, size, CHUNK):
        rows = slice(row, row + CHUNK)
        cols_m[0, rows], cols_m[1, rows] = unpack([ref[rows] for ref in x_in]) if chans else (zero, zero)
    corner_a = unpack([ref[...] for ref in ka_in])
    corner_b = [jnp.where(partner, part, 0.0) for part in unpack([ref[...] for ref in kb_in])]
    for part in range(2):
        a_rows, b_rows = a_in[part], jnp.where(partner, b_in[part], 0.0)
        rows_m[part, :m] = jnp.where(lower, a_rows, b_rows)
        rows_m[part, m:] = jnp.where(lower, b_rows, a_rows)
        corner_m[part, :m] = jnp.where(lower, corner_a[part], corner_b[part])
        corner_m[part, m:] = jnp.where(lower, corner_b[part], corner_a[part])

    offsets_copy.wait()

    def by_right(lhs, t):
        out = dot(lhs[:, :size], right[t, :size]) + dot(lhs[:, size:], right[t, :size])
        return out + dot(lhs[:, :size], right[t, size:])

    def by_left(t, rhs):
        out = dot(left[t, :, :size], rhs[:size]) + dot(left[t, :, :size], rhs[size:])
        return out + dot(left[t, :, size:], rhs[:size])

    def put_below(ref, row, col, value):
        high, low = split(value)
        rows, cols = value.shape
        ref[row : row + rows, col : col + cols] = high
        ref[size + row : size + row + rows, col : col + cols] = low

    def put_beside(ref, row, col, value):
        high, low = split(value)
        rows, cols = value.shape
        ref[row : row + rows, col : col + cols] = high
        ref[row : row + rows, size + col : size + col + cols] = low

    def row_mask(view, row):
        ids = row + lax.broadcasted_iota(jnp.int32, (CHUNK, LANES), 0)
        if row < m:
            return ids < offsets[0, 0, 0, view] - m, row
        if row >= size - m:
            return ids >= size - m + offsets[0, 0, 0, view], row - size + 2 * m
        return None, None

    def col_mask(view, block):
        if block == 0:
            return lane_ids() < offsets[0, 0, 1, view] - m
        return lane_ids() >= m + offsets[0, 0, 1, view]

    def patch(view, row, block):
        cols = slice(block * LANES, (block + 1) * LANES)
        rows = slice(row, row + CHUNK)
        beside = col_mask(view, block)
        beyond, place = row_mask(view, row)
        found = []
        for part in range(2):
            value = jnp.where(beside, cols_m[part, rows], core[part, rows, cols])
            if beyond is not None:
                there = slice(place, place + CHUNK)
                outer = jnp.where(beside, corner_m[part, there], rows_m[part, there, cols])
                value = jnp.where(beyond, outer, value)
            found.append(value)
        return found

    def steps(view):
        for row in range(0, size, CHUNK):
            rows = slice(row, row + CHUNK)
            waves = []
            for block in range(2):
                cols = slice(block * LANES, (block + 1) * LANES)
                o_re, o_im = patch(view, row, block)
                p_re, p_im = placed[view, 0, rows, cols], placed[view, 1, rows, cols]
                waves.append((p_re * o_re - p_im * o_im, p_re * o_im + p_im * o_re))
            for part in range(2):
                put_beside(s1.at[view, 0], row, part * half, waves[0][part] + waves[1][part])
                put_beside(s1.at[view, 1], row, part * half, waves[0][part] - waves[1][part])
            yield
        for odd in range(2):
            y[view, odd] = by_right(s1.at[view, odd], odd)
            yield
        for odd in range(2):
            for row in range(0, half, CHUNK):
                for part in range(2):
                    cols = slice(part * half, (part + 1) * half)
                    above = y[view, odd, row : row + CHUNK, cols]
                    below = y[view, odd, half + row : half + row + CHUNK, cols]
                    put_below(s2.at[view, 0], part * half + row, odd * half, above + below)
                    put_below(s2.at[view, 1], part * half + row, odd * half, above - below)
                yield
        valid = (view < counts[0, 0]).astype(F32)
        for row in range(0, size, CHUNK):
            rows = slice(row, row + CHUNK)
            lanes = lax.broadcasted_iota(jnp.int32, (CHUNK, LANES), 1)
            wanted = []
            for block in range(2):
                power = intensity[0, 0, view, rows, block * LANES : (block + 1) * LANES] + smooth_eps
                wanted.append(power * lax.rsqrt(power) * valid)
            for odd in range(2):
                taken = lax.rem(2 * lanes + odd, LANES)
                ordered = [jnp.take_along_axis(block, taken, axis=1) for block in wanted]
                amplitude[view, odd, rows] = jnp.where(lanes < LANES // 2, *ordered)
        yield
        for odd in range(2):
            z[view, odd] = by_left(odd, s2.at[view, odd])
            yield
        for odd in range(2):
            for row in range(0, half, CHUNK):
                re, im = z[view, odd, row : row + CHUNK], z[view, odd, half + row : half + row + CHUNK]
                taken = pl.ds(2 * row + odd, CHUNK, stride=2)
                wanted = jnp.concatenate([amplitude[view, 0, taken], amplitude[view, 1, taken]], 1)
                scaling = valid - wanted * lax.rsqrt(re * re + im * im + smooth_eps)
                put_below(s3.at[view, odd], row, 0, re * scaling)
                put_below(s3.at[view, odd], half + row, 0, im * scaling)
                yield
        for odd in range(2):
            u[view, odd] = by_left(2 + odd, s3.at[view, odd])
            yield
        for row in range(0, half, CHUNK):
            for part in range(2):
                rows = slice(part * half + row, part * half + row + CHUNK)
                even_rows, odd_rows = u[view, 0, rows], u[view, 1, rows]
                for value, place in ((even_rows + odd_rows, row), (even_rows - odd_rows, half + row)):
                    put_beside(s4.at[view, 0], place, part * half, value[:, :half])
                    put_beside(s4.at[view, 1], place, part * half, value[:, half:])
                yield
        for odd in range(2):
            g[view, odd] = by_right(s4.at[view, odd], 2 + odd)
            yield

    work = [steps(view) for view in range(views)]
    for view in range(views):
        for _ in range(view * STAGGER):
            work[view] = itertools.chain([None], work[view])
    for _ in itertools.zip_longest(*work):
        pass

    for row in range(0, size, CHUNK):
        rows = slice(row, row + CHUNK)
        sums = {}

        def add(key, value):
            sums[key] = sums[key] + value if key in sums else value

        for view in range(views):
            beyond, place = row_mask(view, row)
            halves = []
            for part in range(2):
                cols = slice(part * half, (part + 1) * half)
                even_cols, odd_cols = g[view, 0, rows, cols], g[view, 1, rows, cols]
                halves.append((even_cols + odd_cols, even_cols - odd_cols))
            for block in range(2):
                cols = slice(block * LANES, (block + 1) * LANES)
                beside = col_mask(view, block)
                b_re, b_im = halves[0][block], halves[1][block]
                p_re, p_im = placed[view, 0, rows, cols], placed[view, 1, rows, cols]
                for part, value in enumerate((p_re * b_re + p_im * b_im, p_re * b_im - p_im * b_re)):
                    if beyond is not None:
                        outer, value = jnp.where(beyond, value, zero), jnp.where(beyond, zero, value)
                        add(("corner", part), jnp.where(beside, outer, zero))
                        add(("row", part, block), jnp.where(beside, zero, outer))
                    add(("col", part), jnp.where(beside, value, zero))
                    add(("core", part, block), jnp.where(beside, zero, value))
        for part in range(2):
            cols_m[part, rows] = sums["col", part]
            if place is not None:
                corner_m[part, place : place + CHUNK] = sums["corner", part]
            for block in range(2):
                cols = slice(block * LANES, (block + 1) * LANES)
                base[part, rows, cols] = core[part, rows, cols] - step_size * sums["core", part, block]
                if place is not None:
                    rows_m[part, place : place + CHUNK, cols] = sums["row", part, block]

    def packed(channel, re, im):
        to_right = jnp.where(low_lanes, re, swap_halves(im))
        to_left = jnp.where(low_lanes, swap_halves(im), re)
        return jnp.where(sends_right(channel), to_right, to_left)

    for part in range(2):
        bottom, top = rows_m[part, :m], rows_m[part, m:]
        g_a[:, part * size : (part + 1) * size] = jnp.where(lower, bottom, top)
        g_b[part] = jnp.where(lower, top, bottom)
    bottom = (corner_m[0, :m], corner_m[1, :m])
    top = (corner_m[0, m:], corner_m[1, m:])
    for number, channel in enumerate(chans):
        for row in range(0, size, CHUNK):
            rows = slice(row, row + CHUNK)
            g_x[number][rows] = packed(channel, cols_m[0, rows], cols_m[1, rows])
        below, above = packed(channel, *bottom), packed(channel, *top)
        g_a[:, a_corner(size, number)] = jnp.where(lower, below, above)
        g_kb[number][...] = jnp.where(lower, above, below)


def views_call(chans, offsets, counts, core, placed, intensity, tables, a_in, b_in, x_in, ka_in, kb_in):
    views, size = placed.shape[0], core.shape[1]
    count = len(chans)
    vmem = pl.BlockSpec(memory_space=pltpu.VMEM)
    shapes = [(2, size, size), (MARGIN, 2 * size + count * LANES), (2, MARGIN, size)]
    shapes += [(size, LANES)] * count + [(MARGIN, LANES)] * count
    full = pltpu.VMEM((views, 2, size, size), F32)
    tall = pltpu.VMEM((views, 2, 2 * size, size), BF16)
    wide = pltpu.VMEM((views, 2, size, 2 * size), BF16)
    outs = pl.pallas_call(
        functools.partial(views_kernel, chans),
        out_shape=[jax.ShapeDtypeStruct(shape, F32) for shape in shapes],
        in_specs=[
            pl.BlockSpec(memory_space=pltpu.HBM),
            pl.BlockSpec(memory_space=pltpu.SMEM),
            *[vmem] * (7 + 3 * count),
        ],
        out_specs=[vmem] * len(shapes),
        scratch_shapes=[
            pltpu.SMEM(offsets.shape, jnp.int32),
            pltpu.SemaphoreType.DMA((1,)),
            pltpu.VMEM((views, 2, size, size // 2), F32),
            pltpu.VMEM((2, size, LANES), F32),
            pltpu.VMEM((2, 2 * MARGIN, size), F32),
            pltpu.VMEM((2, 2 * MARGIN, LANES), F32),
            wide, full, tall, full, tall, full, wide, full,
        ],
        compiler_params=pltpu.CompilerParams(vmem_limit_bytes=40 * 1024 * 1024),
    )(offsets, counts, core, placed, intensity, *x_in, b_in, *kb_in, *ka_in, a_in, *tables)
    return (*outs[:3], outs[3 : 3 + count], outs[3 + count :])


def merge_kernel(number, a_in, block, out):
    size = block.shape[0]
    lower = lower_partner()
    corner = a_in[:, a_corner(size, number)]
    out[...] = block[...]
    rows = pl.ds(pl.multiple_of(jnp.where(lower, size - MARGIN, 0), MARGIN), MARGIN)
    out[rows] += corner


def merge_call(number, a_in, block):
    vmem = pl.BlockSpec(memory_space=pltpu.VMEM)
    return pl.pallas_call(
        functools.partial(merge_kernel, number),
        out_shape=jax.ShapeDtypeStruct(block.shape, F32),
        in_specs=[vmem] * 2,
        out_specs=vmem,
        compiler_params=pltpu.CompilerParams(vmem_limit_bytes=2 * 1024 * 1024),
    )(a_in, block)


def finish_kernel(chans, base, *rest):
    count = len(chans)
    x_in, b_in, kb_in = rest[:count], rest[count], rest[count + 1 : 2 * count + 1]
    a_in, out, whole, sems = rest[2 * count + 1 :]
    size = base.shape[1]
    lower, partner = lower_partner(), b_partner()
    columns = []
    for channel in chans:
        right = takes_right(channel)
        mine = lane_ids() // (LANES // 2) == jnp.where(right, 1, 0)
        columns.append((mine, pl.ds(pl.multiple_of(jnp.where(right, size - LANES, 0), LANES), LANES)))

    def take_packed(part, rows, column, block):
        mine, lanes = column
        block = block if part == 0 else swap_halves(block)
        whole[part, rows, lanes] -= step_size * jnp.where(mine, block, 0.0)

    copies = []
    middle = range(MARGIN, size - MARGIN, MARGIN)
    for start in (*middle, 0, size - MARGIN):
        rows = slice(start, start + MARGIN)
        for part in range(2):
            whole[part, rows] = base[part, rows]
            for number, column in enumerate(columns):
                take_packed(part, rows, column, x_in[number][rows])
            if start not in middle:
                by_a = ~lower if start == 0 else lower

                @pl.when(by_a)
                def _():
                    whole[part, rows] -= step_size * a_in[:, part * size : (part + 1) * size]

                @pl.when(~by_a & partner)
                def _():
                    whole[part, rows] -= step_size * b_in[part]
                    for number, column in enumerate(columns):
                        take_packed(part, rows, column, kb_in[number][...])

            copy = pltpu.make_async_copy(
                whole.at[part, rows], out.at[part, rows], sems.at[part, start // MARGIN]
            )
            copy.start()
            copies.append(copy)
    for copy in copies:
        copy.wait()


def finish_call(chans, base, a_in, b_in, x_in, kb_in):
    vmem = pl.BlockSpec(memory_space=pltpu.VMEM)
    return pl.pallas_call(
        functools.partial(finish_kernel, chans),
        out_shape=jax.ShapeDtypeStruct(base.shape, F32),
        in_specs=[vmem] * (3 + 2 * len(chans)),
        out_specs=pl.BlockSpec(memory_space=pltpu.HBM),
        scratch_shapes=[
            pltpu.VMEM(base.shape, F32),
            pltpu.SemaphoreType.DMA((2, base.shape[1] // MARGIN)),
        ],
        compiler_params=pltpu.CompilerParams(vmem_limit_bytes=6 * 1024 * 1024),
    )(base, *x_in, b_in, *kb_in, a_in)


def per_device(object_field, probe_field, intensity, view_offsets, view_counts):
    size = object_field.shape[1]
    mesh_rows, mesh_cols = lax.axis_size("row"), lax.axis_size("col")
    chans = channels(mesh_cols)
    tables = dft_tables(size)
    a_pairs, b_pairs = row_pairs(mesh_rows, 0), row_pairs(mesh_rows, 1)
    spare = spare_route(b_pairs, mesh_rows, mesh_cols)

    def over_rows(block, pairs, extra):
        route = [(i * mesh_cols + k, j * mesh_cols + k) for i, j in pairs for k in range(mesh_cols)]
        return lax.ppermute(block, ("row", "col"), route + extra)

    def across(block, pairs, extra, channel):
        route = [(i * mesh_cols + k, j * mesh_cols + l) for i, j in pairs for k, l in channel[0]]
        return lax.ppermute(block, ("row", "col"), route + (extra if mesh_cols == 2 else []))

    def swap_x(block, channel):
        return lax.ppermute(block, "col", channel[0])

    packs = pack_call(view_counts, object_field, chans)
    x_in = [swap_x(block, channel) for block, channel in zip(packs[2::3], chans)]
    b_in = over_rows(packs[1], b_pairs, spare)
    kb_in = [across(block, b_pairs, spare, channel) for block, channel in zip(packs[4::3], chans)]
    ka_in = [across(block, a_pairs, [], channel) for block, channel in zip(packs[3::3], chans)]
    a_in = over_rows(packs[0], a_pairs, [])
    offsets, probe = (
        pltpu.with_memory_space_constraint(array, pltpu.HBM)
        for array in (jnp.swapaxes(view_offsets, 2, 3), probe_field)
    )
    placed = prepare_call(offsets, probe)
    base, g_a, g_b, g_x, g_kb = views_call(
        chans, offsets, view_counts, object_field, placed, intensity, tables,
        a_in, b_in, x_in, ka_in, kb_in,
    )
    a_in = over_rows(g_a, a_pairs, [])
    b_in = over_rows(g_b, b_pairs, spare)
    g_x = [merge_call(number, a_in, block) for number, block in enumerate(g_x)]
    x_in = [swap_x(block, channel) for block, channel in zip(g_x, chans)]
    kb_in = [across(block, b_pairs, spare, channel) for block, channel in zip(g_kb, chans)]
    return finish_call(chans, base, a_in, b_in, x_in, kb_in)


def solution(mesh):
    in_specs = (
        P(None, "row", "col"),
        P(),
        P("row", "col", None, None, None),
        P("row", "col", None, None),
        P("row", "col"),
    )
    out_specs = P(None, "row", "col")
    return jax.shard_map(
        per_device, mesh=mesh, in_specs=in_specs, out_specs=out_specs, check_vma=False
    )
```

```python
import functools
import itertools
import math

import jax
import jax.numpy as jnp
import ml_dtypes
import numpy as np
from jax import lax
from jax.experimental import pallas as pl
from jax.experimental.pallas import tpu as pltpu
from jax.sharding import PartitionSpec as P

MARGIN = 64
LANES = 128
CHUNK = 64
STAGGER = 4

smooth_eps = 0.1
step_size = 0.2

F32 = jnp.float32
BF16 = jnp.bfloat16


def dft_tables(length):
    half = length // 2
    counter = np.arange(half)
    factor = 1.0 / math.sqrt(length)
    product = np.outer(counter, counter)
    even = np.exp(-2j * np.pi * (product % half) / half) * factor
    odd = np.exp(-2j * np.pi * ((2 * product + counter[:, None]) % length) / length) * factor

    def as_real(table):
        return np.block([[table.real, table.imag], [-table.imag, table.real]])

    def parts(table):
        high = table.astype(ml_dtypes.bfloat16)
        low = (table - high.astype(np.float64)).astype(ml_dtypes.bfloat16)
        return high, low

    even, odd = as_real(even), as_real(odd)
    by_right = [np.concatenate(parts(t), 0) for t in (even, odd, even.T, odd.T)]
    by_left = [np.concatenate(parts(t), 1) for t in (even.T, odd.T, even, odd)]
    return np.stack(by_right), np.stack(by_left)


def channels(mesh_cols):
    if mesh_cols == 1:
        return []
    if mesh_cols == 2:
        return [([(0, 1), (1, 0)], None, None)]
    forward = [(i, i + 1) for i in range(mesh_cols - 1)]
    return [(forward, True, False), ([(j, i) for i, j in forward], False, True)]


def row_pairs(count, first):
    pairs = [(i, i + 1) for i in range(first, count - 1, 2)]
    return pairs + [(j, i) for i, j in pairs]


def spare_route(pairs, mesh_rows, mesh_cols):
    rows = [i for i in range(mesh_rows) if i not in dict(pairs)]
    if mesh_cols % 2:
        return []
    return [(i * mesh_cols + k, i * mesh_cols + (k ^ 1)) for i in rows for k in range(mesh_cols)]


def b_partner():
    row = lax.axis_index("row")
    return jnp.where(lower_partner(), row > 0, row < lax.axis_size("row") - 1)


def sends_right(channel):
    return lax.axis_index("col") == 0 if channel[1] is None else channel[1]


def takes_right(channel):
    return lax.axis_index("col") == 0 if channel[2] is None else channel[2]


def lower_partner():
    return lax.rem(lax.axis_index("row"), 2) == 0


def lane_ids():
    return lax.broadcasted_iota(jnp.int32, (1, LANES), 1)


def half_lanes(right):
    low = lane_ids() < LANES // 2
    if isinstance(right, bool):
        return low if right else ~low
    return lane_ids() // (LANES // 2) == jnp.where(right, 0, 1)


def split(value):
    high = value.astype(BF16)
    return high, (value - high.astype(F32)).astype(BF16)


def dot(first, second):
    return jnp.dot(first, second, preferred_element_type=F32)


def swap_halves(block):
    return pltpu.roll(block, LANES // 2, 1)


def fetch(pairs, sems):
    copies = [pltpu.make_async_copy(source, target, sems.at[i]) for i, (source, target) in enumerate(pairs)]
    for copy in copies:
        copy.start()
    return copies


def pack_kernel(chans, object_ref, a_ref, b_ref, *edge_refs):
    size = object_ref.shape[1]
    top, bottom = pl.ds(0, MARGIN), pl.ds(size - MARGIN, MARGIN)
    lower = lower_partner()
    for part in range(2):
        head, tail = object_ref[part, top, :], object_ref[part, bottom, :]
        a_ref[part] = jnp.where(lower, tail, head)
        b_ref[part] = jnp.where(lower, head, tail)
    for number, channel in enumerate(chans):
        right = sends_right(channel)
        x_ref, ka_ref, kb_ref = edge_refs[3 * number : 3 * number + 3]
        low = lane_ids() < LANES // 2
        for start in range(0, size, CHUNK):
            rows = slice(start, start + CHUNK)
            left_edge = jnp.where(
                low, object_ref[0, rows, :LANES], swap_halves(object_ref[1, rows, :LANES])
            )
            right_edge = jnp.where(
                low,
                swap_halves(object_ref[1, rows, size - LANES :]),
                object_ref[0, rows, size - LANES :],
            )
            x_ref[rows] = jnp.where(right, right_edge, left_edge)
        ka_ref[...] = jnp.where(lower, x_ref[size - MARGIN :], x_ref[:MARGIN])
        kb_ref[...] = jnp.where(lower, x_ref[:MARGIN], x_ref[size - MARGIN :])


def pack_call(object_field, chans):
    size = object_field.shape[1]
    shapes = [(2, MARGIN, size)] * 2 + [(size, LANES), (MARGIN, LANES), (MARGIN, LANES)] * len(chans)
    vmem = pl.BlockSpec(memory_space=pltpu.VMEM)
    return pl.pallas_call(
        functools.partial(pack_kernel, chans),
        out_shape=[jax.ShapeDtypeStruct(shape, F32) for shape in shapes],
        in_specs=[vmem],
        out_specs=[vmem] * len(shapes),
        compiler_params=pltpu.CompilerParams(vmem_limit_bytes=4 * 1024 * 1024),
    )(object_field)


def prepare_kernel(offsets_in, probe, placed, offsets, doubled, sems):
    views, size = placed.shape[0], probe.shape[1]
    copies = fetch(
        [(offsets_in, offsets)] + [(probe, doubled.at[:, pl.ds(size * i, size)]) for i in range(2)], sems
    )
    sublane = lax.broadcasted_iota(jnp.int32, (1, 8, 1), 1)
    for copy in copies:
        copy.wait()
    for view in range(views):
        shift_row = lax.rem(offsets[0, 0, 0, view] - MARGIN + size, size)
        shift_col = lax.rem(offsets[0, 0, 1, view] - MARGIN + size, size)
        start = lax.rem(size - shift_row, size)
        whole = pl.multiple_of((start // 8) * 8, 8)
        rest = start - whole
        for part in range(2):
            for row in range(0, size, CHUNK):
                block = doubled[part, pl.ds(whole + row, CHUNK + 8), :]
                block = pltpu.roll(block, shift_col, 1).reshape(CHUNK // 8 + 1, 8, size)
                block = pltpu.roll(block, lax.rem(8 - rest, 8), 1)
                block = jnp.where(sublane < 8 - rest, block[:-1], block[1:])
                placed[view, part, row : row + CHUNK] = block.reshape(CHUNK, size)


def prepare_call(offsets, probe):
    views, size = offsets.shape[3], probe.shape[1]
    vmem, hbm = pl.BlockSpec(memory_space=pltpu.VMEM), pl.BlockSpec(memory_space=pltpu.HBM)
    return pl.pallas_call(
        prepare_kernel,
        out_shape=jax.ShapeDtypeStruct((views, 2, size, size), F32),
        in_specs=[hbm, hbm],
        out_specs=vmem,
        scratch_shapes=[
            pltpu.SMEM(offsets.shape, jnp.int32),
            pltpu.VMEM((2, 2 * size, size), F32),
            pltpu.SemaphoreType.DMA((3,)),
        ],
        compiler_params=pltpu.CompilerParams(vmem_limit_bytes=16 * 1024 * 1024),
        cost_estimate=pl.CostEstimate(flops=10**9, bytes_accessed=10**5, transcendentals=0),
    )(offsets, probe)


def views_kernel(chans, offsets_in, counts, core, placed, intensity, *rest):
    count = len(chans)
    x_in, b_in, rest = rest[:count], rest[count], rest[count + 1 :]
    kb_in, ka_in = rest[:count], rest[count : 2 * count]
    a_in, right, left, *rest = rest[2 * count :]
    base, g_a, g_b = rest[:3]
    g_x, g_kb = rest[3 : 3 + count], rest[3 + count : 3 + 2 * count]
    offsets, sem, amplitude, cols_m, rows_m, corner_m, s1, y, s2, z, s3, u, s4, g = rest[3 + 2 * count :]
    (offsets_copy,) = fetch([(offsets_in, offsets)], sem)
    views, size = placed.shape[0], core.shape[1]
    half, m = size // 2, MARGIN
    lower, partner = lower_partner(), b_partner()
    low_lanes = lane_ids() < LANES // 2
    zero = jnp.zeros((CHUNK, LANES), F32)

    def unpack(blocks):
        re = im = None
        for channel, block in zip(chans, blocks):
            mine = half_lanes(takes_right(channel))
            re = jnp.where(mine, block, 0.0 if re is None else re)
            im = jnp.where(mine, swap_halves(block), 0.0 if im is None else im)
        return (re, im) if blocks else (jnp.zeros((MARGIN, LANES), F32),) * 2

    for row in range(0, size, CHUNK):
        rows = slice(row, row + CHUNK)
        cols_m[0, rows], cols_m[1, rows] = unpack([ref[rows] for ref in x_in]) if chans else (zero, zero)
    corner_a = unpack([ref[...] for ref in ka_in])
    corner_b = [jnp.where(partner, part, 0.0) for part in unpack([ref[...] for ref in kb_in])]
    for part in range(2):
        a_rows, b_rows = a_in[part], jnp.where(partner, b_in[part], 0.0)
        rows_m[part, :m] = jnp.where(lower, a_rows, b_rows)
        rows_m[part, m:] = jnp.where(lower, b_rows, a_rows)
        corner_m[part, :m] = jnp.where(lower, corner_a[part], corner_b[part])
        corner_m[part, m:] = jnp.where(lower, corner_b[part], corner_a[part])

    offsets_copy.wait()

    def by_right(lhs, t):
        out = dot(lhs[:, :size], right[t, :size]) + dot(lhs[:, size:], right[t, :size])
        return out + dot(lhs[:, :size], right[t, size:])

    def by_left(t, rhs):
        out = dot(left[t, :, :size], rhs[:size]) + dot(left[t, :, :size], rhs[size:])
        return out + dot(left[t, :, size:], rhs[:size])

    def put_below(ref, row, col, value):
        high, low = split(value)
        rows, cols = value.shape
        ref[row : row + rows, col : col + cols] = high
        ref[size + row : size + row + rows, col : col + cols] = low

    def put_beside(ref, row, col, value):
        high, low = split(value)
        rows, cols = value.shape
        ref[row : row + rows, col : col + cols] = high
        ref[row : row + rows, size + col : size + col + cols] = low

    def row_mask(view, row):
        ids = row + lax.broadcasted_iota(jnp.int32, (CHUNK, LANES), 0)
        if row < m:
            return ids < offsets[0, 0, 0, view] - m, row
        if row >= size - m:
            return ids >= size - m + offsets[0, 0, 0, view], row - size + 2 * m
        return None, None

    def col_mask(view, block):
        if block == 0:
            return lane_ids() < offsets[0, 0, 1, view] - m
        return lane_ids() >= m + offsets[0, 0, 1, view]

    def patch(view, row, block):
        cols = slice(block * LANES, (block + 1) * LANES)
        rows = slice(row, row + CHUNK)
        beside = col_mask(view, block)
        beyond, place = row_mask(view, row)
        found = []
        for part in range(2):
            value = jnp.where(beside, cols_m[part, rows], core[part, rows, cols])
            if beyond is not None:
                there = slice(place, place + CHUNK)
                outer = jnp.where(beside, corner_m[part, there], rows_m[part, there, cols])
                value = jnp.where(beyond, outer, value)
            found.append(value)
        return found

    def steps(view):
        for row in range(0, size, CHUNK):
            rows = slice(row, row + CHUNK)
            waves = []
            for block in range(2):
                cols = slice(block * LANES, (block + 1) * LANES)
                o_re, o_im = patch(view, row, block)
                p_re, p_im = placed[view, 0, rows, cols], placed[view, 1, rows, cols]
                waves.append((p_re * o_re - p_im * o_im, p_re * o_im + p_im * o_re))
            for part in range(2):
                put_beside(s1.at[view, 0], row, part * half, waves[0][part] + waves[1][part])
                put_beside(s1.at[view, 1], row, part * half, waves[0][part] - waves[1][part])
            yield
        for odd in range(2):
            y[view, odd] = by_right(s1.at[view, odd], odd)
            yield
        for odd in range(2):
            for row in range(0, half, CHUNK):
                for part in range(2):
                    cols = slice(part * half, (part + 1) * half)
                    above = y[view, odd, row : row + CHUNK, cols]
                    below = y[view, odd, half + row : half + row + CHUNK, cols]
                    put_below(s2.at[view, 0], part * half + row, odd * half, above + below)
                    put_below(s2.at[view, 1], part * half + row, odd * half, above - below)
                yield
        valid = (view < counts[0, 0]).astype(F32)
        for row in range(0, size, CHUNK):
            rows = slice(row, row + CHUNK)
            lanes = lax.broadcasted_iota(jnp.int32, (CHUNK, LANES), 1)
            wanted = []
            for block in range(2):
                power = intensity[0, 0, view, rows, block * LANES : (block + 1) * LANES] + smooth_eps
                wanted.append(power * lax.rsqrt(power) * valid)
            for odd in range(2):
                taken = lax.rem(2 * lanes + odd, LANES)
                ordered = [jnp.take_along_axis(block, taken, axis=1) for block in wanted]
                amplitude[view, odd, rows] = jnp.where(lanes < LANES // 2, *ordered)
        yield
        for odd in range(2):
            z[view, odd] = by_left(odd, s2.at[view, odd])
            yield
        for odd in range(2):
            for row in range(0, half, CHUNK):
                re, im = z[view, odd, row : row + CHUNK], z[view, odd, half + row : half + row + CHUNK]
                taken = pl.ds(2 * row + odd, CHUNK, stride=2)
                wanted = jnp.concatenate([amplitude[view, 0, taken], amplitude[view, 1, taken]], 1)
                scaling = valid - wanted * lax.rsqrt(re * re + im * im + smooth_eps)
                put_below(s3.at[view, odd], row, 0, re * scaling)
                put_below(s3.at[view, odd], half + row, 0, im * scaling)
                yield
        for odd in range(2):
            u[view, odd] = by_left(2 + odd, s3.at[view, odd])
            yield
        for row in range(0, half, CHUNK):
            for part in range(2):
                rows = slice(part * half + row, part * half + row + CHUNK)
                even_rows, odd_rows = u[view, 0, rows], u[view, 1, rows]
                for value, place in ((even_rows + odd_rows, row), (even_rows - odd_rows, half + row)):
                    put_beside(s4.at[view, 0], place, part * half, value[:, :half])
                    put_beside(s4.at[view, 1], place, part * half, value[:, half:])
                yield
        for odd in range(2):
            g[view, odd] = by_right(s4.at[view, odd], 2 + odd)
            yield

    work = [steps(view) for view in range(views)]
    for view in range(views):
        for _ in range(view * STAGGER):
            work[view] = itertools.chain([None], work[view])
    for _ in itertools.zip_longest(*work):
        pass

    for row in range(0, size, CHUNK):
        rows = slice(row, row + CHUNK)
        sums = {}

        def add(key, value):
            sums[key] = sums[key] + value if key in sums else value

        for view in range(views):
            beyond, place = row_mask(view, row)
            halves = []
            for part in range(2):
                cols = slice(part * half, (part + 1) * half)
                even_cols, odd_cols = g[view, 0, rows, cols], g[view, 1, rows, cols]
                halves.append((even_cols + odd_cols, even_cols - odd_cols))
            for block in range(2):
                cols = slice(block * LANES, (block + 1) * LANES)
                beside = col_mask(view, block)
                b_re, b_im = halves[0][block], halves[1][block]
                p_re, p_im = placed[view, 0, rows, cols], placed[view, 1, rows, cols]
                for part, value in enumerate((p_re * b_re + p_im * b_im, p_re * b_im - p_im * b_re)):
                    if beyond is not None:
                        outer, value = jnp.where(beyond, value, zero), jnp.where(beyond, zero, value)
                        add(("corner", part), jnp.where(beside, outer, zero))
                        add(("row", part, block), jnp.where(beside, zero, outer))
                    add(("col", part), jnp.where(beside, value, zero))
                    add(("core", part, block), jnp.where(beside, zero, value))
        for part in range(2):
            cols_m[part, rows] = sums["col", part]
            if place is not None:
                corner_m[part, place : place + CHUNK] = sums["corner", part]
            for block in range(2):
                cols = slice(block * LANES, (block + 1) * LANES)
                base[part, rows, cols] = core[part, rows, cols] - step_size * sums["core", part, block]
                if place is not None:
                    rows_m[part, place : place + CHUNK, cols] = sums["row", part, block]

    def packed(channel, re, im):
        to_right = jnp.where(low_lanes, re, swap_halves(im))
        to_left = jnp.where(low_lanes, swap_halves(im), re)
        return jnp.where(sends_right(channel), to_right, to_left)

    for part in range(2):
        bottom, top = rows_m[part, :m], rows_m[part, m:]
        g_a[part] = jnp.where(lower, bottom, top)
        g_b[part] = jnp.where(lower, top, bottom)
    bottom = (corner_m[0, :m], corner_m[1, :m])
    top = (corner_m[0, m:], corner_m[1, m:])
    for number, channel in enumerate(chans):
        for row in range(0, size, CHUNK):
            rows = slice(row, row + CHUNK)
            g_x[number][rows] = packed(channel, cols_m[0, rows], cols_m[1, rows])
        below, above = packed(channel, *bottom), packed(channel, *top)
        g_x[number][size:] = jnp.where(lower, below, above)
        g_kb[number][...] = jnp.where(lower, above, below)


def views_call(chans, offsets, counts, core, placed, intensity, tables, a_in, b_in, x_in, ka_in, kb_in):
    views, size = placed.shape[0], core.shape[1]
    count = len(chans)
    vmem = pl.BlockSpec(memory_space=pltpu.VMEM)
    shapes = [(2, size, size), (2, MARGIN, size), (2, MARGIN, size)]
    shapes += [(size + MARGIN, LANES)] * count + [(MARGIN, LANES)] * count
    full = pltpu.VMEM((views, 2, size, size), F32)
    tall = pltpu.VMEM((views, 2, 2 * size, size), BF16)
    wide = pltpu.VMEM((views, 2, size, 2 * size), BF16)
    outs = pl.pallas_call(
        functools.partial(views_kernel, chans),
        out_shape=[jax.ShapeDtypeStruct(shape, F32) for shape in shapes],
        in_specs=[
            pl.BlockSpec(memory_space=pltpu.HBM),
            pl.BlockSpec(memory_space=pltpu.SMEM),
            *[vmem] * (7 + 3 * count),
        ],
        out_specs=[vmem] * len(shapes),
        scratch_shapes=[
            pltpu.SMEM(offsets.shape, jnp.int32),
            pltpu.SemaphoreType.DMA((1,)),
            pltpu.VMEM((views, 2, size, size // 2), F32),
            pltpu.VMEM((2, size, LANES), F32),
            pltpu.VMEM((2, 2 * MARGIN, size), F32),
            pltpu.VMEM((2, 2 * MARGIN, LANES), F32),
            wide, full, tall, full, tall, full, wide, full,
        ],
        compiler_params=pltpu.CompilerParams(vmem_limit_bytes=40 * 1024 * 1024),
    )(offsets, counts, core, placed, intensity, *x_in, b_in, *kb_in, *ka_in, a_in, *tables)
    return (*outs[:3], outs[3 : 3 + count], outs[3 + count :])


def finish_kernel(chans, base, *rest):
    count = len(chans)
    x_in, b_in, rest = rest[:count], rest[count], rest[count + 1 :]
    kb_in, ka_in = rest[:count], rest[count : 2 * count]
    a_in, out, whole, sems = rest[2 * count :]
    size = base.shape[1]
    lower, partner = lower_partner(), b_partner()
    columns = []
    for channel in chans:
        right = takes_right(channel)
        mine = lane_ids() // (LANES // 2) == jnp.where(right, 1, 0)
        columns.append((mine, pl.ds(pl.multiple_of(jnp.where(right, size - LANES, 0), LANES), LANES)))

    def take_packed(part, rows, column, block):
        mine, lanes = column
        block = block if part == 0 else swap_halves(block)
        whole[part, rows, lanes] -= step_size * jnp.where(mine, block, 0.0)

    copies = []
    middle = range(MARGIN, size - MARGIN, MARGIN)
    for start in (*middle, 0, size - MARGIN):
        rows = slice(start, start + MARGIN)
        for part in range(2):
            whole[part, rows] = base[part, rows]
            for number, column in enumerate(columns):
                take_packed(part, rows, column, x_in[number][rows])
            if start not in middle:
                by_a = ~lower if start == 0 else lower

                @pl.when(by_a)
                def _():
                    whole[part, rows] -= step_size * a_in[part]
                    for number, column in enumerate(columns):
                        take_packed(part, rows, column, ka_in[number][...])

                @pl.when(~by_a & partner)
                def _():
                    whole[part, rows] -= step_size * b_in[part]
                    for number, column in enumerate(columns):
                        take_packed(part, rows, column, kb_in[number][...])

            copy = pltpu.make_async_copy(
                whole.at[part, rows], out.at[part, rows], sems.at[part, start // MARGIN]
            )
            copy.start()
            copies.append(copy)
    for copy in copies:
        copy.wait()


def finish_call(chans, base, a_in, b_in, x_in, ka_in, kb_in):
    vmem = pl.BlockSpec(memory_space=pltpu.VMEM)
    return pl.pallas_call(
        functools.partial(finish_kernel, chans),
        out_shape=jax.ShapeDtypeStruct(base.shape, F32),
        in_specs=[vmem] * (3 + 3 * len(chans)),
        out_specs=pl.BlockSpec(memory_space=pltpu.HBM),
        scratch_shapes=[
            pltpu.VMEM(base.shape, F32),
            pltpu.SemaphoreType.DMA((2, base.shape[1] // MARGIN)),
        ],
        compiler_params=pltpu.CompilerParams(vmem_limit_bytes=6 * 1024 * 1024),
    )(base, *x_in, b_in, *kb_in, *ka_in, a_in)


def per_device(object_field, probe_field, intensity, view_offsets, view_counts):
    size = object_field.shape[1]
    mesh_rows, mesh_cols = lax.axis_size("row"), lax.axis_size("col")
    chans = channels(mesh_cols)
    tables = dft_tables(size)
    a_pairs, b_pairs = row_pairs(mesh_rows, 0), row_pairs(mesh_rows, 1)
    spare = spare_route(b_pairs, mesh_rows, mesh_cols)

    def over_rows(block, pairs, extra):
        route = [(i * mesh_cols + k, j * mesh_cols + k) for i, j in pairs for k in range(mesh_cols)]
        return lax.ppermute(block, ("row", "col"), route + extra)

    def across(block, pairs, extra, channel):
        route = [(i * mesh_cols + k, j * mesh_cols + l) for i, j in pairs for k, l in channel[0]]
        return lax.ppermute(block, ("row", "col"), route + (extra if mesh_cols == 2 else []))

    def swap_x(block, channel):
        return lax.ppermute(block, "col", channel[0])

    packs = pack_call(object_field, chans)
    x_in = [swap_x(block, channel) for block, channel in zip(packs[2::3], chans)]
    b_in = over_rows(packs[1], b_pairs, spare)
    kb_in = [across(block, b_pairs, spare, channel) for block, channel in zip(packs[4::3], chans)]
    ka_in = [across(block, a_pairs, [], channel) for block, channel in zip(packs[3::3], chans)]
    a_in = over_rows(packs[0], a_pairs, [])
    offsets, probe = (
        pltpu.with_memory_space_constraint(array, pltpu.HBM)
        for array in (jnp.swapaxes(view_offsets, 2, 3), probe_field)
    )
    placed = prepare_call(offsets, probe)
    base, g_a, g_b, g_x, g_kb = views_call(
        chans, offsets, view_counts, object_field, placed, intensity, tables,
        a_in, b_in, x_in, ka_in, kb_in,
    )
    x_in = [swap_x(block, channel) for block, channel in zip(g_x, chans)]
    b_in = over_rows(g_b, b_pairs, spare)
    kb_in = [across(block, b_pairs, spare, channel) for block, channel in zip(g_kb, chans)]
    ka_in = [over_rows(block[size:], a_pairs, []) for block in x_in]
    a_in = over_rows(g_a, a_pairs, [])
    return finish_call(chans, base, a_in, b_in, x_in, ka_in, kb_in)


def solution(mesh):
    in_specs = (
        P(None, "row", "col"),
        P(),
        P("row", "col", None, None, None),
        P("row", "col", None, None),
        P("row", "col"),
    )
    out_specs = P(None, "row", "col")
    return jax.shard_map(
        per_device, mesh=mesh, in_specs=in_specs, out_specs=out_specs, check_vma=False
    )
```

```python
import functools
import itertools
import math

import jax
import jax.numpy as jnp
import ml_dtypes
import numpy as np
from jax import lax
from jax.experimental import pallas as pl
from jax.experimental.pallas import tpu as pltpu
from jax.sharding import PartitionSpec as P

MARGIN = 64
LANES = 128
CHUNK = 64
STAGGER = 4

smooth_eps = 0.1
step_size = 0.2

F32 = jnp.float32
BF16 = jnp.bfloat16


def dft_tables(length):
    half = length // 2
    counter = np.arange(half)
    factor = 1.0 / math.sqrt(length)
    product = np.outer(counter, counter)
    even = np.exp(-2j * np.pi * (product % half) / half) * factor
    odd = np.exp(-2j * np.pi * ((2 * product + counter[:, None]) % length) / length) * factor

    def as_real(table):
        return np.block([[table.real, table.imag], [-table.imag, table.real]])

    def parts(table):
        high = table.astype(ml_dtypes.bfloat16)
        low = (table - high.astype(np.float64)).astype(ml_dtypes.bfloat16)
        return high, low

    even, odd = as_real(even), as_real(odd)
    by_right = [np.concatenate(parts(t), 0) for t in (even, odd, even.T, odd.T)]
    by_left = [np.concatenate(parts(t), 1) for t in (even.T, odd.T, even, odd)]
    return np.stack(by_right), np.stack(by_left)


def channels(mesh_cols):
    if mesh_cols == 1:
        return []
    if mesh_cols == 2:
        return [([(0, 1), (1, 0)], None, None)]
    forward = [(i, i + 1) for i in range(mesh_cols - 1)]
    return [(forward, True, False), ([(j, i) for i, j in forward], False, True)]


def row_pairs(count, first):
    pairs = [(i, i + 1) for i in range(first, count - 1, 2)]
    return pairs + [(j, i) for i, j in pairs]


def spare_route(pairs, mesh_rows, mesh_cols):
    rows = [i for i in range(mesh_rows) if i not in dict(pairs)]
    if mesh_cols % 2:
        return []
    return [(i * mesh_cols + k, i * mesh_cols + (k ^ 1)) for i in rows for k in range(mesh_cols)]


def b_partner():
    row = lax.axis_index("row")
    return jnp.where(lower_partner(), row > 0, row < lax.axis_size("row") - 1)


def sends_right(channel):
    return lax.axis_index("col") == 0 if channel[1] is None else channel[1]


def takes_right(channel):
    return lax.axis_index("col") == 0 if channel[2] is None else channel[2]


def lower_partner():
    return lax.rem(lax.axis_index("row"), 2) == 0


def lane_ids():
    return lax.broadcasted_iota(jnp.int32, (1, LANES), 1)


def half_lanes(right):
    low = lane_ids() < LANES // 2
    if isinstance(right, bool):
        return low if right else ~low
    return lane_ids() // (LANES // 2) == jnp.where(right, 0, 1)


def split(value):
    high = value.astype(BF16)
    return high, (value - high.astype(F32)).astype(BF16)


def dot(first, second):
    return jnp.dot(first, second, preferred_element_type=F32)


def swap_halves(block):
    return pltpu.roll(block, LANES // 2, 1)


def fetch(pairs, sems):
    copies = [pltpu.make_async_copy(source, target, sems.at[i]) for i, (source, target) in enumerate(pairs)]
    for copy in copies:
        copy.start()
    return copies


def pack_kernel(chans, object_ref, *rest):
    count = len(chans)
    a_ref, b_ref, *edge_refs = rest[: 2 + 3 * count]
    head, tail, sides, sems = rest[2 + 3 * count :]
    size = object_ref.shape[1]
    inner = size - 2 * MARGIN
    low = lane_ids() < LANES // 2
    lower = lower_partner()
    pairs = [(object_ref.at[:, pl.ds(0, MARGIN)], head), (object_ref.at[:, pl.ds(size - MARGIN, MARGIN)], tail)]
    starts = []
    for number, channel in enumerate(chans):
        starts.append(pl.multiple_of(jnp.where(sends_right(channel), size - LANES, 0), LANES))
        block = object_ref.at[:, pl.ds(MARGIN, inner), pl.ds(starts[-1], LANES)]
        pairs.append((block, sides.at[number]))
    copies = fetch(pairs, sems)
    copies[0].wait()
    copies[1].wait()
    for part in range(2):
        a_ref[part] = jnp.where(lower, tail[part], head[part])
        b_ref[part] = jnp.where(lower, head[part], tail[part])
    for number, channel in enumerate(chans):
        right = sends_right(channel)
        x_ref, ka_ref, kb_ref = edge_refs[3 * number : 3 * number + 3]

        def packed(re, im):
            return jnp.where(
                right, jnp.where(low, swap_halves(im), re), jnp.where(low, re, swap_halves(im))
            )

        lanes = pl.ds(starts[number], LANES)
        upper = packed(head[0, :, lanes], head[1, :, lanes])
        under = packed(tail[0, :, lanes], tail[1, :, lanes])
        x_ref[:MARGIN], x_ref[size - MARGIN :] = upper, under
        ka_ref[...] = jnp.where(lower, under, upper)
        kb_ref[...] = jnp.where(lower, upper, under)
        copies[2 + number].wait()
        x_ref[MARGIN : size - MARGIN] = packed(sides[number, 0], sides[number, 1])


def pack_call(object_field, chans):
    size = object_field.shape[1]
    count = len(chans)
    shapes = [(2, MARGIN, size)] * 2 + [(size, LANES), (MARGIN, LANES), (MARGIN, LANES)] * count
    vmem = pl.BlockSpec(memory_space=pltpu.VMEM)
    return pl.pallas_call(
        functools.partial(pack_kernel, chans),
        out_shape=[jax.ShapeDtypeStruct(shape, F32) for shape in shapes],
        in_specs=[pl.BlockSpec(memory_space=pltpu.HBM)],
        out_specs=[vmem] * len(shapes),
        scratch_shapes=[
            pltpu.VMEM((2, MARGIN, size), F32),
            pltpu.VMEM((2, MARGIN, size), F32),
            pltpu.VMEM((max(count, 1), 2, size - 2 * MARGIN, LANES), F32),
            pltpu.SemaphoreType.DMA((2 + count,)),
        ],
        compiler_params=pltpu.CompilerParams(vmem_limit_bytes=4 * 1024 * 1024),
    )(pltpu.with_memory_space_constraint(object_field, pltpu.HBM))


def prepare_kernel(offsets_in, probe, placed, spots, offsets, doubled, sems):
    views, size = placed.shape[0], probe.shape[1]
    copies = fetch(
        [(offsets_in, offsets)] + [(probe, doubled.at[:, pl.ds(size * i, size)]) for i in range(2)], sems
    )
    sublane = lax.broadcasted_iota(jnp.int32, (1, 8, 1), 1)
    for copy in copies:
        copy.wait()
    for view in range(views):
        for axis in range(2):
            spots[view, axis] = jnp.full(spots.shape[2:], offsets[0, 0, axis, view], jnp.int32)
        shift_row = lax.rem(offsets[0, 0, 0, view] - MARGIN + size, size)
        shift_col = lax.rem(offsets[0, 0, 1, view] - MARGIN + size, size)
        start = lax.rem(size - shift_row, size)
        whole = pl.multiple_of((start // 8) * 8, 8)
        rest = start - whole
        for part in range(2):
            for row in range(0, size, CHUNK):
                block = doubled[part, pl.ds(whole + row, CHUNK + 8), :]
                block = pltpu.roll(block, shift_col, 1).reshape(CHUNK // 8 + 1, 8, size)
                block = pltpu.roll(block, lax.rem(8 - rest, 8), 1)
                block = jnp.where(sublane < 8 - rest, block[:-1], block[1:])
                placed[view, part, row : row + CHUNK] = block.reshape(CHUNK, size)


def prepare_call(offsets, probe):
    views, size = offsets.shape[3], probe.shape[1]
    vmem, hbm = pl.BlockSpec(memory_space=pltpu.VMEM), pl.BlockSpec(memory_space=pltpu.HBM)
    return pl.pallas_call(
        prepare_kernel,
        out_shape=[
            jax.ShapeDtypeStruct((views, 2, size, size), F32),
            jax.ShapeDtypeStruct((views, 2, 8, LANES), jnp.int32),
        ],
        in_specs=[hbm, hbm],
        out_specs=[vmem, vmem],
        scratch_shapes=[
            pltpu.SMEM(offsets.shape, jnp.int32),
            pltpu.VMEM((2, 2 * size, size), F32),
            pltpu.SemaphoreType.DMA((3,)),
        ],
        compiler_params=pltpu.CompilerParams(vmem_limit_bytes=16 * 1024 * 1024),
        cost_estimate=pl.CostEstimate(flops=10**9, bytes_accessed=10**5, transcendentals=0),
    )(offsets, probe)


def views_kernel(chans, spots, counts, core, placed, intensity, *rest):
    count = len(chans)
    x_in, b_in, rest = rest[:count], rest[count], rest[count + 1 :]
    kb_in, ka_in = rest[:count], rest[count : 2 * count]
    a_in, right, left, *rest = rest[2 * count :]
    g_core, g_a, g_b = rest[:3]
    g_x, g_ka = rest[3 : 3 + count], rest[3 + count : 3 + 2 * count]
    g_kb = rest[3 + 2 * count : 3 + 3 * count]
    amplitude, cols_m, rows_m, corner_m, s1, y, s2, z, s3, u, s4, g = rest[3 + 3 * count :]
    views, size = placed.shape[0], core.shape[1]
    half, m = size // 2, MARGIN
    lower, partner = lower_partner(), b_partner()
    low_lanes = lane_ids() < LANES // 2
    zero = jnp.zeros((CHUNK, LANES), F32)

    def unpack(blocks):
        re = im = None
        for channel, block in zip(chans, blocks):
            mine = half_lanes(takes_right(channel))
            re = jnp.where(mine, block, 0.0 if re is None else re)
            im = jnp.where(mine, swap_halves(block), 0.0 if im is None else im)
        return (re, im) if blocks else (jnp.zeros((MARGIN, LANES), F32),) * 2

    for row in range(0, size, CHUNK):
        rows = slice(row, row + CHUNK)
        cols_m[0, rows], cols_m[1, rows] = unpack([ref[rows] for ref in x_in]) if chans else (zero, zero)
    corner_a = unpack([ref[...] for ref in ka_in])
    corner_b = [jnp.where(partner, part, 0.0) for part in unpack([ref[...] for ref in kb_in])]
    for part in range(2):
        a_rows, b_rows = a_in[part], jnp.where(partner, b_in[part], 0.0)
        rows_m[part, :m] = jnp.where(lower, a_rows, b_rows)
        rows_m[part, m:] = jnp.where(lower, b_rows, a_rows)
        corner_m[part, :m] = jnp.where(lower, corner_a[part], corner_b[part])
        corner_m[part, m:] = jnp.where(lower, corner_b[part], corner_a[part])

    def by_right(lhs, t):
        out = dot(lhs[:, :size], right[t, :size]) + dot(lhs[:, size:], right[t, :size])
        return out + dot(lhs[:, :size], right[t, size:])

    def by_left(t, rhs):
        out = dot(left[t, :, :size], rhs[:size]) + dot(left[t, :, :size], rhs[size:])
        return out + dot(left[t, :, size:], rhs[:size])

    def put_below(ref, row, col, value):
        high, low = split(value)
        rows, cols = value.shape
        ref[row : row + rows, col : col + cols] = high
        ref[size + row : size + row + rows, col : col + cols] = low

    def put_beside(ref, row, col, value):
        high, low = split(value)
        rows, cols = value.shape
        ref[row : row + rows, col : col + cols] = high
        ref[row : row + rows, size + col : size + col + cols] = low

    def row_mask(view, row):
        ids = row + lax.broadcasted_iota(jnp.int32, (CHUNK, LANES), 0)
        if row < m:
            return ids < spots[view, 0, :1] - m, row
        if row >= size - m:
            return ids >= size - m + spots[view, 0, :1], row - size + 2 * m
        return None, None

    def col_mask(view, block):
        if block == 0:
            return lane_ids() < spots[view, 1, :1] - m
        return lane_ids() >= m + spots[view, 1, :1]

    def patch(view, row, block):
        cols = slice(block * LANES, (block + 1) * LANES)
        rows = slice(row, row + CHUNK)
        beside = col_mask(view, block)
        beyond, place = row_mask(view, row)
        found = []
        for part in range(2):
            value = jnp.where(beside, cols_m[part, rows], core[part, rows, cols])
            if beyond is not None:
                there = slice(place, place + CHUNK)
                outer = jnp.where(beside, corner_m[part, there], rows_m[part, there, cols])
                value = jnp.where(beyond, outer, value)
            found.append(value)
        return found

    def steps(view):
        for row in range(0, size, CHUNK):
            rows = slice(row, row + CHUNK)
            waves = []
            for block in range(2):
                cols = slice(block * LANES, (block + 1) * LANES)
                o_re, o_im = patch(view, row, block)
                p_re, p_im = placed[view, 0, rows, cols], placed[view, 1, rows, cols]
                waves.append((p_re * o_re - p_im * o_im, p_re * o_im + p_im * o_re))
            for part in range(2):
                put_beside(s1.at[view, 0], row, part * half, waves[0][part] + waves[1][part])
                put_beside(s1.at[view, 1], row, part * half, waves[0][part] - waves[1][part])
            yield
        for odd in range(2):
            y[view, odd] = by_right(s1.at[view, odd], odd)
            yield
        for odd in range(2):
            for row in range(0, half, CHUNK):
                for part in range(2):
                    cols = slice(part * half, (part + 1) * half)
                    above = y[view, odd, row : row + CHUNK, cols]
                    below = y[view, odd, half + row : half + row + CHUNK, cols]
                    put_below(s2.at[view, 0], part * half + row, odd * half, above + below)
                    put_below(s2.at[view, 1], part * half + row, odd * half, above - below)
                yield
        valid = (view < counts[0, 0]).astype(F32)
        for row in range(0, size, CHUNK):
            rows = slice(row, row + CHUNK)
            lanes = lax.broadcasted_iota(jnp.int32, (CHUNK, LANES), 1)
            wanted = []
            for block in range(2):
                power = intensity[0, 0, view, rows, block * LANES : (block + 1) * LANES] + smooth_eps
                wanted.append(power * lax.rsqrt(power) * valid)
            for odd in range(2):
                taken = lax.rem(2 * lanes + odd, LANES)
                ordered = [jnp.take_along_axis(block, taken, axis=1) for block in wanted]
                amplitude[view, odd, rows] = jnp.where(lanes < LANES // 2, *ordered)
        yield
        for odd in range(2):
            z[view, odd] = by_left(odd, s2.at[view, odd])
            yield
        for odd in range(2):
            for row in range(0, half, CHUNK):
                re, im = z[view, odd, row : row + CHUNK], z[view, odd, half + row : half + row + CHUNK]
                taken = pl.ds(2 * row + odd, CHUNK, stride=2)
                wanted = jnp.concatenate([amplitude[view, 0, taken], amplitude[view, 1, taken]], 1)
                scaling = valid - wanted * lax.rsqrt(re * re + im * im + smooth_eps)
                put_below(s3.at[view, odd], row, 0, re * scaling)
                put_below(s3.at[view, odd], half + row, 0, im * scaling)
                yield
        for odd in range(2):
            u[view, odd] = by_left(2 + odd, s3.at[view, odd])
            yield
        for row in range(0, half, CHUNK):
            for part in range(2):
                rows = slice(part * half + row, part * half + row + CHUNK)
                even_rows, odd_rows = u[view, 0, rows], u[view, 1, rows]
                for value, place in ((even_rows + odd_rows, row), (even_rows - odd_rows, half + row)):
                    put_beside(s4.at[view, 0], place, part * half, value[:, :half])
                    put_beside(s4.at[view, 1], place, part * half, value[:, half:])
                yield
        for odd in range(2):
            g[view, odd] = by_right(s4.at[view, odd], 2 + odd)
            yield

    work = [steps(view) for view in range(views)]
    for view in range(views):
        for _ in range(view * STAGGER):
            work[view] = itertools.chain([None], work[view])
    for _ in itertools.zip_longest(*work):
        pass

    for row in range(0, size, CHUNK):
        rows = slice(row, row + CHUNK)
        sums = {}

        def add(key, value):
            sums[key] = sums[key] + value if key in sums else value

        for view in range(views):
            beyond, place = row_mask(view, row)
            halves = []
            for part in range(2):
                cols = slice(part * half, (part + 1) * half)
                even_cols, odd_cols = g[view, 0, rows, cols], g[view, 1, rows, cols]
                halves.append((even_cols + odd_cols, even_cols - odd_cols))
            for block in range(2):
                cols = slice(block * LANES, (block + 1) * LANES)
                beside = col_mask(view, block)
                b_re, b_im = halves[0][block], halves[1][block]
                p_re, p_im = placed[view, 0, rows, cols], placed[view, 1, rows, cols]
                for part, value in enumerate((p_re * b_re + p_im * b_im, p_re * b_im - p_im * b_re)):
                    if beyond is not None:
                        outer, value = jnp.where(beyond, value, zero), jnp.where(beyond, zero, value)
                        add(("corner", part), jnp.where(beside, outer, zero))
                        add(("row", part, block), jnp.where(beside, zero, outer))
                    add(("col", part), jnp.where(beside, value, zero))
                    add(("core", part, block), jnp.where(beside, zero, value))
        for part in range(2):
            cols_m[part, rows] = sums["col", part]
            if place is not None:
                corner_m[part, place : place + CHUNK] = sums["corner", part]
            for block in range(2):
                cols = slice(block * LANES, (block + 1) * LANES)
                g_core[part, rows, cols] = sums["core", part, block]
                if place is not None:
                    rows_m[part, place : place + CHUNK, cols] = sums["row", part, block]

    def packed(channel, re, im):
        to_right = jnp.where(low_lanes, re, swap_halves(im))
        to_left = jnp.where(low_lanes, swap_halves(im), re)
        return jnp.where(sends_right(channel), to_right, to_left)

    for part in range(2):
        bottom, top = rows_m[part, :m], rows_m[part, m:]
        g_a[part] = jnp.where(lower, bottom, top)
        g_b[part] = jnp.where(lower, top, bottom)
    bottom = (corner_m[0, :m], corner_m[1, :m])
    top = (corner_m[0, m:], corner_m[1, m:])
    for number, channel in enumerate(chans):
        for row in range(0, size, CHUNK):
            rows = slice(row, row + CHUNK)
            g_x[number][rows] = packed(channel, cols_m[0, rows], cols_m[1, rows])
        below, above = packed(channel, *bottom), packed(channel, *top)
        g_ka[number][...] = jnp.where(lower, below, above)
        g_kb[number][...] = jnp.where(lower, above, below)


def views_call(chans, spots, counts, core, placed, intensity, tables, a_in, b_in, x_in, ka_in, kb_in):
    views, size = placed.shape[0], core.shape[1]
    count = len(chans)
    vmem = pl.BlockSpec(memory_space=pltpu.VMEM)
    shapes = [(2, size, size), (2, MARGIN, size), (2, MARGIN, size)]
    shapes += [(size, LANES)] * count + [(MARGIN, LANES)] * (2 * count)
    full = pltpu.VMEM((views, 2, size, size), F32)
    tall = pltpu.VMEM((views, 2, 2 * size, size), BF16)
    wide = pltpu.VMEM((views, 2, size, 2 * size), BF16)
    outs = pl.pallas_call(
        functools.partial(views_kernel, chans),
        out_shape=[jax.ShapeDtypeStruct(shape, F32) for shape in shapes],
        in_specs=[
            vmem,
            pl.BlockSpec(memory_space=pltpu.SMEM),
            *[vmem] * (7 + 3 * count),
        ],
        out_specs=[vmem] * len(shapes),
        scratch_shapes=[
            pltpu.VMEM((views, 2, size, size // 2), F32),
            pltpu.VMEM((2, size, LANES), F32),
            pltpu.VMEM((2, 2 * MARGIN, size), F32),
            pltpu.VMEM((2, 2 * MARGIN, LANES), F32),
            wide, full, tall, full, tall, full, wide, full,
        ],
        compiler_params=pltpu.CompilerParams(vmem_limit_bytes=40 * 1024 * 1024),
    )(spots, counts, core, placed, intensity, *x_in, b_in, *kb_in, *ka_in, a_in, *tables)
    return (*outs[:3], outs[3 : 3 + count], outs[3 + count : 3 + 2 * count], outs[3 + 2 * count :])


def finish_kernel(chans, object_ref, g_core, *rest):
    count = len(chans)
    x_in, b_in, rest = rest[:count], rest[count], rest[count + 1 :]
    kb_in, ka_in = rest[:count], rest[count : 2 * count]
    a_in, out = rest[2 * count :]
    size = object_ref.shape[1]
    lower = lower_partner()
    a_rows = pl.ds(pl.multiple_of(jnp.where(lower, size - MARGIN, 0), MARGIN), MARGIN)
    b_rows = pl.ds(pl.multiple_of(jnp.where(lower, 0, size - MARGIN), MARGIN), MARGIN)
    columns = []
    for channel in chans:
        right = takes_right(channel)
        mine = lane_ids() // (LANES // 2) == jnp.where(right, 1, 0)
        block = pl.multiple_of(jnp.where(right, size - LANES, 0), LANES)
        columns.append((mine, pl.ds(block, LANES)))

    def take(place, value):
        out[place] -= step_size * value

    def take_packed(rows, column, block):
        mine, lanes = column
        take((0, rows, lanes), jnp.where(mine, block, 0.0))
        take((1, rows, lanes), jnp.where(mine, swap_halves(block), 0.0))

    for part in range(2):
        out[part] = object_ref[part] - step_size * g_core[part]
        take((part, a_rows), a_in[part])
    for number, column in enumerate(columns):
        take_packed(slice(None), column, x_in[number][...])
        take_packed(a_rows, column, ka_in[number][...])

    @pl.when(b_partner())
    def _():
        for part in range(2):
            take((part, b_rows), b_in[part])
        for number, column in enumerate(columns):
            take_packed(b_rows, column, kb_in[number][...])


def finish_call(chans, object_field, g_core, a_in, b_in, x_in, ka_in, kb_in):
    vmem = pl.BlockSpec(memory_space=pltpu.VMEM)
    return pl.pallas_call(
        functools.partial(finish_kernel, chans),
        out_shape=jax.ShapeDtypeStruct(object_field.shape, F32),
        in_specs=[vmem] * (4 + 3 * len(chans)),
        out_specs=vmem,
        compiler_params=pltpu.CompilerParams(vmem_limit_bytes=6 * 1024 * 1024),
    )(object_field, g_core, *x_in, b_in, *kb_in, *ka_in, a_in)


def per_device(object_field, probe_field, intensity, view_offsets, view_counts):
    size = object_field.shape[1]
    mesh_rows, mesh_cols = lax.axis_size("row"), lax.axis_size("col")
    chans = channels(mesh_cols)
    tables = dft_tables(size)
    a_pairs, b_pairs = row_pairs(mesh_rows, 0), row_pairs(mesh_rows, 1)
    spare = spare_route(b_pairs, mesh_rows, mesh_cols)

    def over_rows(block, pairs, extra):
        route = [(i * mesh_cols + k, j * mesh_cols + k) for i, j in pairs for k in range(mesh_cols)]
        return lax.ppermute(block, ("row", "col"), route + extra)

    def across(block, pairs, extra, channel):
        route = [(i * mesh_cols + k, j * mesh_cols + l) for i, j in pairs for k, l in channel[0]]
        return lax.ppermute(block, ("row", "col"), route + (extra if mesh_cols == 2 else []))

    def exchange(a_send, b_send, x_send, ka_send, kb_send):
        x_in = [lax.ppermute(block, "col", channel[0]) for block, channel in zip(x_send, chans)]
        b_in = over_rows(b_send, b_pairs, spare)
        kb_in = [across(block, b_pairs, spare, channel) for block, channel in zip(kb_send, chans)]
        ka_in = [across(block, a_pairs, [], channel) for block, channel in zip(ka_send, chans)]
        a_in = over_rows(a_send, a_pairs, [])
        return a_in, b_in, x_in, ka_in, kb_in

    packs = pack_call(object_field, chans)
    offsets, probe = (
        pltpu.with_memory_space_constraint(array, pltpu.HBM)
        for array in (jnp.swapaxes(view_offsets, 2, 3), probe_field)
    )
    margins = exchange(packs[0], packs[1], packs[2::3], packs[3::3], packs[4::3])
    placed, spots = prepare_call(offsets, probe)
    g_core, *sends = views_call(
        chans, spots, view_counts, object_field, placed, intensity, tables, *margins
    )
    return finish_call(chans, object_field, g_core, *exchange(*sends))


def solution(mesh):
    in_specs = (
        P(None, "row", "col"),
        P(),
        P("row", "col", None, None, None),
        P("row", "col", None, None),
        P("row", "col"),
    )
    out_specs = P(None, "row", "col")
    return jax.shard_map(
        per_device, mesh=mesh, in_specs=in_specs, out_specs=out_specs, check_vma=False
    )
```

```python
import functools
import itertools
import math

import jax
import jax.numpy as jnp
import ml_dtypes
import numpy as np
from jax import lax
from jax.experimental import pallas as pl
from jax.experimental.pallas import tpu as pltpu
from jax.sharding import PartitionSpec as P

MARGIN = 64
LANES = 128
CHUNK = 64
STAGGER = 2

smooth_eps = 0.1
step_size = 0.2

F32 = jnp.float32
BF16 = jnp.bfloat16


def dft_tables(length):
    half = length // 2
    counter = np.arange(half)
    factor = 1.0 / math.sqrt(length)
    product = np.outer(counter, counter)
    even = np.exp(-2j * np.pi * (product % half) / half) * factor
    odd = np.exp(-2j * np.pi * ((2 * product + counter[:, None]) % length) / length) * factor

    def as_real(table):
        return np.block([[table.real, table.imag], [-table.imag, table.real]])

    def parts(table):
        high = table.astype(ml_dtypes.bfloat16)
        low = (table - high.astype(np.float64)).astype(ml_dtypes.bfloat16)
        return high, low

    even, odd = as_real(even), as_real(odd)
    by_right = [np.concatenate(parts(t), 0) for t in (even, odd, even.T, odd.T)]
    by_left = [np.concatenate(parts(t), 0) for t in (even.T, odd.T, even, odd)]
    return np.stack(by_right), np.stack(by_left)


def channels(mesh_cols):
    if mesh_cols == 1:
        return []
    if mesh_cols == 2:
        return [([(0, 1), (1, 0)], None, None)]
    forward = [(i, i + 1) for i in range(mesh_cols - 1)]
    return [(forward, True, False), ([(j, i) for i, j in forward], False, True)]


def row_pairs(count, first):
    pairs = [(i, i + 1) for i in range(first, count - 1, 2)]
    return pairs + [(j, i) for i, j in pairs]


def spare_route(pairs, mesh_rows, mesh_cols):
    rows = [i for i in range(mesh_rows) if i not in dict(pairs)]
    if mesh_cols % 2:
        return []
    return [(i * mesh_cols + k, i * mesh_cols + (k ^ 1)) for i in rows for k in range(mesh_cols)]


def b_partner():
    row = lax.axis_index("row")
    return jnp.where(lower_partner(), row > 0, row < lax.axis_size("row") - 1)


def sends_right(channel):
    return lax.axis_index("col") == 0 if channel[1] is None else channel[1]


def takes_right(channel):
    return lax.axis_index("col") == 0 if channel[2] is None else channel[2]


def lower_partner():
    return lax.rem(lax.axis_index("row"), 2) == 0


def lane_ids():
    return lax.broadcasted_iota(jnp.int32, (1, LANES), 1)


def half_lanes(right):
    low = lane_ids() < LANES // 2
    if isinstance(right, bool):
        return low if right else ~low
    return lane_ids() // (LANES // 2) == jnp.where(right, 0, 1)


def split(value):
    high = value.astype(BF16)
    return high, (value - high.astype(F32)).astype(BF16)


def dot(first, second):
    return jnp.dot(first, second, preferred_element_type=F32)


def swap_halves(block):
    return pltpu.roll(block, LANES // 2, 1)


def fetch(pairs, sems):
    copies = [pltpu.make_async_copy(source, target, sems.at[i]) for i, (source, target) in enumerate(pairs)]
    for copy in copies:
        copy.start()
    return copies


def pack_kernel(chans, object_ref, a_ref, b_ref, *edge_refs):
    size = object_ref.shape[1]
    top, bottom = pl.ds(0, MARGIN), pl.ds(size - MARGIN, MARGIN)
    lower = lower_partner()
    for part in range(2):
        head, tail = object_ref[part, top, :], object_ref[part, bottom, :]
        a_ref[part] = jnp.where(lower, tail, head)
        b_ref[part] = jnp.where(lower, head, tail)
    for number, channel in enumerate(chans):
        right = sends_right(channel)
        x_ref, ka_ref, kb_ref = edge_refs[3 * number : 3 * number + 3]
        low = lane_ids() < LANES // 2
        for start in range(0, size, CHUNK):
            rows = slice(start, start + CHUNK)
            left_edge = jnp.where(
                low, object_ref[0, rows, :LANES], swap_halves(object_ref[1, rows, :LANES])
            )
            right_edge = jnp.where(
                low,
                swap_halves(object_ref[1, rows, size - LANES :]),
                object_ref[0, rows, size - LANES :],
            )
            x_ref[rows] = jnp.where(right, right_edge, left_edge)
        ka_ref[...] = jnp.where(lower, x_ref[size - MARGIN :], x_ref[:MARGIN])
        kb_ref[...] = jnp.where(lower, x_ref[:MARGIN], x_ref[size - MARGIN :])


def pack_call(object_field, chans):
    size = object_field.shape[1]
    shapes = [(2, MARGIN, size)] * 2 + [(size, LANES), (MARGIN, LANES), (MARGIN, LANES)] * len(chans)
    vmem = pl.BlockSpec(memory_space=pltpu.VMEM)
    return pl.pallas_call(
        functools.partial(pack_kernel, chans),
        out_shape=[jax.ShapeDtypeStruct(shape, F32) for shape in shapes],
        in_specs=[vmem],
        out_specs=[vmem] * len(shapes),
        compiler_params=pltpu.CompilerParams(vmem_limit_bytes=4 * 1024 * 1024),
    )(object_field)


def prepare_kernel(offsets_in, probe, placed, spots, offsets, doubled, sems):
    views, size = placed.shape[0], probe.shape[1]
    copies = fetch(
        [(offsets_in, offsets)] + [(probe, doubled.at[:, pl.ds(size * i, size)]) for i in range(2)], sems
    )
    sublane = lax.broadcasted_iota(jnp.int32, (1, 8, 1), 1)
    for copy in copies:
        copy.wait()
    for view in range(views):
        for axis in range(2):
            spots[view, axis] = jnp.full(spots.shape[2:], offsets[0, 0, axis, view], jnp.int32)
        shift_row = lax.rem(offsets[0, 0, 0, view] - MARGIN + size, size)
        shift_col = lax.rem(offsets[0, 0, 1, view] - MARGIN + size, size)
        start = lax.rem(size - shift_row, size)
        whole = pl.multiple_of((start // 8) * 8, 8)
        rest = start - whole
        for part in range(2):
            for row in range(0, size, CHUNK):
                block = doubled[part, pl.ds(whole + row, CHUNK + 8), :]
                block = pltpu.roll(block, shift_col, 1).reshape(CHUNK // 8 + 1, 8, size)
                block = pltpu.roll(block, lax.rem(8 - rest, 8), 1)
                block = jnp.where(sublane < 8 - rest, block[:-1], block[1:])
                placed[view, part, row : row + CHUNK] = block.reshape(CHUNK, size)


def prepare_call(offsets, probe):
    views, size = offsets.shape[3], probe.shape[1]
    vmem, hbm = pl.BlockSpec(memory_space=pltpu.VMEM), pl.BlockSpec(memory_space=pltpu.HBM)
    return pl.pallas_call(
        prepare_kernel,
        out_shape=[
            jax.ShapeDtypeStruct((views, 2, size, size), F32),
            jax.ShapeDtypeStruct((views, 2, 8, LANES), jnp.int32),
        ],
        in_specs=[hbm, hbm],
        out_specs=[vmem, vmem],
        scratch_shapes=[
            pltpu.SMEM(offsets.shape, jnp.int32),
            pltpu.VMEM((2, 2 * size, size), F32),
            pltpu.SemaphoreType.DMA((3,)),
        ],
        compiler_params=pltpu.CompilerParams(vmem_limit_bytes=16 * 1024 * 1024),
        cost_estimate=pl.CostEstimate(flops=10**9, bytes_accessed=10**5, transcendentals=0),
    )(offsets, probe)


def views_kernel(chans, spots, counts, core, placed, intensity, *rest):
    count = len(chans)
    x_in, b_in, rest = rest[:count], rest[count], rest[count + 1 :]
    kb_in, ka_in = rest[:count], rest[count : 2 * count]
    a_in, right, left, *rest = rest[2 * count :]
    g_core, g_a, g_b = rest[:3]
    g_x, g_ka = rest[3 : 3 + count], rest[3 + count : 3 + 2 * count]
    g_kb = rest[3 + 2 * count : 3 + 3 * count]
    amplitude, cols_m, rows_m, corner_m, s1, y, s2, z, s3, u, s4, g = rest[3 + 3 * count :]
    views, size = placed.shape[0], core.shape[1]
    half, m = size // 2, MARGIN
    lower, partner = lower_partner(), b_partner()
    low_lanes = lane_ids() < LANES // 2
    zero = jnp.zeros((CHUNK, LANES), F32)

    def unpack(blocks):
        re = im = None
        for channel, block in zip(chans, blocks):
            mine = half_lanes(takes_right(channel))
            re = jnp.where(mine, block, 0.0 if re is None else re)
            im = jnp.where(mine, swap_halves(block), 0.0 if im is None else im)
        return (re, im) if blocks else (jnp.zeros((MARGIN, LANES), F32),) * 2

    for row in range(0, size, CHUNK):
        rows = slice(row, row + CHUNK)
        cols_m[0, rows], cols_m[1, rows] = unpack([ref[rows] for ref in x_in]) if chans else (zero, zero)
    corner_a = unpack([ref[...] for ref in ka_in])
    corner_b = [jnp.where(partner, part, 0.0) for part in unpack([ref[...] for ref in kb_in])]
    for part in range(2):
        a_rows, b_rows = a_in[part], jnp.where(partner, b_in[part], 0.0)
        rows_m[part, :m] = jnp.where(lower, a_rows, b_rows)
        rows_m[part, m:] = jnp.where(lower, b_rows, a_rows)
        corner_m[part, :m] = jnp.where(lower, corner_a[part], corner_b[part])
        corner_m[part, m:] = jnp.where(lower, corner_b[part], corner_a[part])

    def by_right(lhs, t):
        both = dot(lhs[...], right[t, :size])
        return both[:size] + both[size:] + dot(lhs[:size], right[t, size:])

    def by_left(t, rhs):
        both = dot(left[t], rhs[:size])
        return both[:size] + both[size:] + dot(left[t, :size], rhs[size:])

    def put(ref, row, col, value):
        high, low = split(value)
        rows, cols = value.shape
        ref[row : row + rows, col : col + cols] = high
        ref[size + row : size + row + rows, col : col + cols] = low

    def row_mask(view, row):
        ids = row + lax.broadcasted_iota(jnp.int32, (CHUNK, LANES), 0)
        if row < m:
            return ids < spots[view, 0, :1] - m, row
        if row >= size - m:
            return ids >= size - m + spots[view, 0, :1], row - size + 2 * m
        return None, None

    def col_mask(view, block):
        if block == 0:
            return lane_ids() < spots[view, 1, :1] - m
        return lane_ids() >= m + spots[view, 1, :1]

    def patch(view, row, block):
        cols = slice(block * LANES, (block + 1) * LANES)
        rows = slice(row, row + CHUNK)
        beside = col_mask(view, block)
        beyond, place = row_mask(view, row)
        found = []
        for part in range(2):
            value = jnp.where(beside, cols_m[part, rows], core[part, rows, cols])
            if beyond is not None:
                there = slice(place, place + CHUNK)
                outer = jnp.where(beside, corner_m[part, there], rows_m[part, there, cols])
                value = jnp.where(beyond, outer, value)
            found.append(value)
        return found

    def steps(view):
        for row in range(0, size, CHUNK):
            rows = slice(row, row + CHUNK)
            waves = []
            for block in range(2):
                cols = slice(block * LANES, (block + 1) * LANES)
                o_re, o_im = patch(view, row, block)
                p_re, p_im = placed[view, 0, rows, cols], placed[view, 1, rows, cols]
                waves.append((p_re * o_re - p_im * o_im, p_re * o_im + p_im * o_re))
            for part in range(2):
                put(s1.at[view, 0], row, part * half, waves[0][part] + waves[1][part])
                put(s1.at[view, 1], row, part * half, waves[0][part] - waves[1][part])
            yield
        for odd in range(2):
            y[view, odd] = by_right(s1.at[view, odd], odd)
            yield
        for odd in range(2):
            for row in range(0, half, CHUNK):
                for part in range(2):
                    cols = slice(part * half, (part + 1) * half)
                    above = y[view, odd, row : row + CHUNK, cols]
                    below = y[view, odd, half + row : half + row + CHUNK, cols]
                    put(s2.at[view, 0], part * half + row, odd * half, above + below)
                    put(s2.at[view, 1], part * half + row, odd * half, above - below)
                yield
        valid = (view < counts[0, 0]).astype(F32)
        for row in range(0, size, CHUNK):
            rows = slice(row, row + CHUNK)
            lanes = lax.broadcasted_iota(jnp.int32, (CHUNK, LANES), 1)
            wanted = []
            for block in range(2):
                power = intensity[0, 0, view, rows, block * LANES : (block + 1) * LANES] + smooth_eps
                wanted.append(power * lax.rsqrt(power) * valid)
            for odd in range(2):
                taken = lax.rem(2 * lanes + odd, LANES)
                ordered = [jnp.take_along_axis(block, taken, axis=1) for block in wanted]
                amplitude[view, odd, rows] = jnp.where(lanes < LANES // 2, *ordered)
        yield
        for odd in range(2):
            z[view, odd] = by_left(odd, s2.at[view, odd])
            yield
        for odd in range(2):
            for row in range(0, half, CHUNK):
                re, im = z[view, odd, row : row + CHUNK], z[view, odd, half + row : half + row + CHUNK]
                taken = pl.ds(2 * row + odd, CHUNK, stride=2)
                wanted = jnp.concatenate([amplitude[view, 0, taken], amplitude[view, 1, taken]], 1)
                scaling = valid - wanted * lax.rsqrt(re * re + im * im + smooth_eps)
                put(s3.at[view, odd], row, 0, re * scaling)
                put(s3.at[view, odd], half + row, 0, im * scaling)
                yield
        for odd in range(2):
            u[view, odd] = by_left(2 + odd, s3.at[view, odd])
            yield
        for row in range(0, half, CHUNK):
            for part in range(2):
                rows = slice(part * half + row, part * half + row + CHUNK)
                even_rows, odd_rows = u[view, 0, rows], u[view, 1, rows]
                for value, place in ((even_rows + odd_rows, row), (even_rows - odd_rows, half + row)):
                    put(s4.at[view, 0], place, part * half, value[:, :half])
                    put(s4.at[view, 1], place, part * half, value[:, half:])
                yield
        for odd in range(2):
            g[view, odd] = by_right(s4.at[view, odd], 2 + odd)
            yield

    work = [steps(view) for view in range(views)]
    for view in range(views):
        for _ in range(view * STAGGER):
            work[view] = itertools.chain([None], work[view])
    for _ in itertools.zip_longest(*work):
        pass

    for row in range(0, size, CHUNK):
        rows = slice(row, row + CHUNK)
        sums = {}

        def add(key, value):
            sums[key] = sums[key] + value if key in sums else value

        for view in range(views):
            beyond, place = row_mask(view, row)
            halves = []
            for part in range(2):
                cols = slice(part * half, (part + 1) * half)
                even_cols, odd_cols = g[view, 0, rows, cols], g[view, 1, rows, cols]
                halves.append((even_cols + odd_cols, even_cols - odd_cols))
            for block in range(2):
                cols = slice(block * LANES, (block + 1) * LANES)
                beside = col_mask(view, block)
                b_re, b_im = halves[0][block], halves[1][block]
                p_re, p_im = placed[view, 0, rows, cols], placed[view, 1, rows, cols]
                for part, value in enumerate((p_re * b_re + p_im * b_im, p_re * b_im - p_im * b_re)):
                    if beyond is not None:
                        outer, value = jnp.where(beyond, value, zero), jnp.where(beyond, zero, value)
                        add(("corner", part), jnp.where(beside, outer, zero))
                        add(("row", part, block), jnp.where(beside, zero, outer))
                    add(("col", part), jnp.where(beside, value, zero))
                    add(("core", part, block), jnp.where(beside, zero, value))
        for part in range(2):
            cols_m[part, rows] = sums["col", part]
            if place is not None:
                corner_m[part, place : place + CHUNK] = sums["corner", part]
            for block in range(2):
                cols = slice(block * LANES, (block + 1) * LANES)
                g_core[part, rows, cols] = sums["core", part, block]
                if place is not None:
                    rows_m[part, place : place + CHUNK, cols] = sums["row", part, block]

    def packed(channel, re, im):
        to_right = jnp.where(low_lanes, re, swap_halves(im))
        to_left = jnp.where(low_lanes, swap_halves(im), re)
        return jnp.where(sends_right(channel), to_right, to_left)

    for part in range(2):
        bottom, top = rows_m[part, :m], rows_m[part, m:]
        g_a[part] = jnp.where(lower, bottom, top)
        g_b[part] = jnp.where(lower, top, bottom)
    bottom = (corner_m[0, :m], corner_m[1, :m])
    top = (corner_m[0, m:], corner_m[1, m:])
    for number, channel in enumerate(chans):
        for row in range(0, size, CHUNK):
            rows = slice(row, row + CHUNK)
            g_x[number][rows] = packed(channel, cols_m[0, rows], cols_m[1, rows])
        below, above = packed(channel, *bottom), packed(channel, *top)
        g_ka[number][...] = jnp.where(lower, below, above)
        g_kb[number][...] = jnp.where(lower, above, below)


def views_call(chans, spots, counts, core, placed, intensity, tables, a_in, b_in, x_in, ka_in, kb_in):
    views, size = placed.shape[0], core.shape[1]
    count = len(chans)
    vmem = pl.BlockSpec(memory_space=pltpu.VMEM)
    shapes = [(2, size, size), (2, MARGIN, size), (2, MARGIN, size)]
    shapes += [(size, LANES)] * count + [(MARGIN, LANES)] * (2 * count)
    full = pltpu.VMEM((views, 2, size, size), F32)
    tall = pltpu.VMEM((views, 2, 2 * size, size), BF16)
    outs = pl.pallas_call(
        functools.partial(views_kernel, chans),
        out_shape=[jax.ShapeDtypeStruct(shape, F32) for shape in shapes],
        in_specs=[
            vmem,
            pl.BlockSpec(memory_space=pltpu.SMEM),
            *[vmem] * (7 + 3 * count),
        ],
        out_specs=[vmem] * len(shapes),
        scratch_shapes=[
            pltpu.VMEM((views, 2, size, size // 2), F32),
            pltpu.VMEM((2, size, LANES), F32),
            pltpu.VMEM((2, 2 * MARGIN, size), F32),
            pltpu.VMEM((2, 2 * MARGIN, LANES), F32),
            *[tall, full] * 4,
        ],
        compiler_params=pltpu.CompilerParams(vmem_limit_bytes=40 * 1024 * 1024),
    )(spots, counts, core, placed, intensity, *x_in, b_in, *kb_in, *ka_in, a_in, *tables)
    return (*outs[:3], outs[3 : 3 + count], outs[3 + count : 3 + 2 * count], outs[3 + 2 * count :])


def finish_kernel(chans, object_ref, g_core, *rest):
    count = len(chans)
    x_in, b_in, rest = rest[:count], rest[count], rest[count + 1 :]
    kb_in, ka_in = rest[:count], rest[count : 2 * count]
    a_in, out = rest[2 * count :]
    size = object_ref.shape[1]
    lower = lower_partner()
    a_rows = pl.ds(pl.multiple_of(jnp.where(lower, size - MARGIN, 0), MARGIN), MARGIN)
    b_rows = pl.ds(pl.multiple_of(jnp.where(lower, 0, size - MARGIN), MARGIN), MARGIN)
    columns = []
    for channel in chans:
        right = takes_right(channel)
        mine = lane_ids() // (LANES // 2) == jnp.where(right, 1, 0)
        block = pl.multiple_of(jnp.where(right, size - LANES, 0), LANES)
        columns.append((mine, pl.ds(block, LANES)))

    def take(place, value):
        out[place] -= step_size * value

    def take_packed(rows, column, block):
        mine, lanes = column
        take((0, rows, lanes), jnp.where(mine, block, 0.0))
        take((1, rows, lanes), jnp.where(mine, swap_halves(block), 0.0))

    for part in range(2):
        out[part] = object_ref[part] - step_size * g_core[part]
        take((part, a_rows), a_in[part])
    for number, column in enumerate(columns):
        take_packed(slice(None), column, x_in[number][...])
        take_packed(a_rows, column, ka_in[number][...])

    @pl.when(b_partner())
    def _():
        for part in range(2):
            take((part, b_rows), b_in[part])
        for number, column in enumerate(columns):
            take_packed(b_rows, column, kb_in[number][...])


def finish_call(chans, object_field, g_core, a_in, b_in, x_in, ka_in, kb_in):
    vmem = pl.BlockSpec(memory_space=pltpu.VMEM)
    return pl.pallas_call(
        functools.partial(finish_kernel, chans),
        out_shape=jax.ShapeDtypeStruct(object_field.shape, F32),
        in_specs=[vmem] * (4 + 3 * len(chans)),
        out_specs=vmem,
        compiler_params=pltpu.CompilerParams(vmem_limit_bytes=6 * 1024 * 1024),
    )(object_field, g_core, *x_in, b_in, *kb_in, *ka_in, a_in)


def per_device(object_field, probe_field, intensity, view_offsets, view_counts):
    size = object_field.shape[1]
    mesh_rows, mesh_cols = lax.axis_size("row"), lax.axis_size("col")
    chans = channels(mesh_cols)
    tables = dft_tables(size)
    a_pairs, b_pairs = row_pairs(mesh_rows, 0), row_pairs(mesh_rows, 1)
    spare = spare_route(b_pairs, mesh_rows, mesh_cols)

    def over_rows(block, pairs, extra):
        route = [(i * mesh_cols + k, j * mesh_cols + k) for i, j in pairs for k in range(mesh_cols)]
        return lax.ppermute(block, ("row", "col"), route + extra)

    def across(block, pairs, extra, channel):
        route = [(i * mesh_cols + k, j * mesh_cols + l) for i, j in pairs for k, l in channel[0]]
        return lax.ppermute(block, ("row", "col"), route + (extra if mesh_cols == 2 else []))

    def exchange(a_send, b_send, x_send, ka_send, kb_send):
        x_in = [lax.ppermute(block, "col", channel[0]) for block, channel in zip(x_send, chans)]
        b_in = over_rows(b_send, b_pairs, spare)
        kb_in = [across(block, b_pairs, spare, channel) for block, channel in zip(kb_send, chans)]
        ka_in = [across(block, a_pairs, [], channel) for block, channel in zip(ka_send, chans)]
        a_in = over_rows(a_send, a_pairs, [])
        return a_in, b_in, x_in, ka_in, kb_in

    packs = pack_call(object_field, chans)
    offsets, probe = (
        pltpu.with_memory_space_constraint(array, pltpu.HBM)
        for array in (jnp.swapaxes(view_offsets, 2, 3), probe_field)
    )
    margins = exchange(packs[0], packs[1], packs[2::3], packs[3::3], packs[4::3])
    placed, spots = prepare_call(offsets, probe)
    g_core, *sends = views_call(
        chans, spots, view_counts, object_field, placed, intensity, tables, *margins
    )
    return finish_call(chans, object_field, g_core, *exchange(*sends))


def solution(mesh):
    in_specs = (
        P(None, "row", "col"),
        P(),
        P("row", "col", None, None, None),
        P("row", "col", None, None),
        P("row", "col"),
    )
    out_specs = P(None, "row", "col")
    return jax.shard_map(
        per_device, mesh=mesh, in_specs=in_specs, out_specs=out_specs, check_vma=False
    )
```

```python
import functools
import itertools
import math

import jax
import jax.numpy as jnp
import ml_dtypes
import numpy as np
from jax import lax
from jax.experimental import pallas as pl
from jax.experimental.pallas import tpu as pltpu
from jax.sharding import PartitionSpec as P

MARGIN = 64
LANES = 128
CHUNK = 64
STAGGER = 2

smooth_eps = 0.1
step_size = 0.2

F32 = jnp.float32
BF16 = jnp.bfloat16


def dft_tables(length):
    half = length // 2
    counter = np.arange(half)
    factor = 1.0 / math.sqrt(length)
    product = np.outer(counter, counter)
    even = np.exp(-2j * np.pi * (product % half) / half) * factor
    odd = np.exp(-2j * np.pi * ((2 * product + counter[:, None]) % length) / length) * factor

    def as_real(table):
        return np.block([[table.real, table.imag], [-table.imag, table.real]])

    def parts(table):
        high = table.astype(ml_dtypes.bfloat16)
        low = (table - high.astype(np.float64)).astype(ml_dtypes.bfloat16)
        return high, low

    even, odd = as_real(even), as_real(odd)
    by_right = [np.concatenate(parts(t), 0) for t in (even, odd, even.T, odd.T)]
    by_left = [np.concatenate(parts(t), 0) for t in (even.T, odd.T, even, odd)]
    return np.stack(by_right), np.stack(by_left)


def channels(mesh_cols):
    if mesh_cols == 1:
        return []
    if mesh_cols == 2:
        return [([(0, 1), (1, 0)], None, None)]
    forward = [(i, i + 1) for i in range(mesh_cols - 1)]
    return [(forward, True, False), ([(j, i) for i, j in forward], False, True)]


def row_pairs(count, first):
    pairs = [(i, i + 1) for i in range(first, count - 1, 2)]
    return pairs + [(j, i) for i, j in pairs]


def spare_route(pairs, mesh_rows, mesh_cols):
    rows = [i for i in range(mesh_rows) if i not in dict(pairs)]
    if mesh_cols % 2:
        return []
    return [(i * mesh_cols + k, i * mesh_cols + (k ^ 1)) for i in rows for k in range(mesh_cols)]


def b_partner():
    row = lax.axis_index("row")
    return jnp.where(lower_partner(), row > 0, row < lax.axis_size("row") - 1)


def sends_right(channel):
    return lax.axis_index("col") == 0 if channel[1] is None else channel[1]


def takes_right(channel):
    return lax.axis_index("col") == 0 if channel[2] is None else channel[2]


def lower_partner():
    return lax.rem(lax.axis_index("row"), 2) == 0


def lane_ids():
    return lax.broadcasted_iota(jnp.int32, (1, LANES), 1)


def half_lanes(right):
    low = lane_ids() < LANES // 2
    if isinstance(right, bool):
        return low if right else ~low
    return lane_ids() // (LANES // 2) == jnp.where(right, 0, 1)


def split(value):
    high = value.astype(BF16)
    return high, (value - high.astype(F32)).astype(BF16)


def dot(first, second):
    return jnp.dot(first, second, preferred_element_type=F32)


def swap_halves(block):
    return pltpu.roll(block, LANES // 2, 1)


def fetch(pairs, sems):
    copies = [pltpu.make_async_copy(source, target, sems.at[i]) for i, (source, target) in enumerate(pairs)]
    for copy in copies:
        copy.start()
    return copies


def pack_kernel(chans, object_ref, a_ref, b_ref, *edge_refs):
    size = object_ref.shape[1]
    top, bottom = pl.ds(0, MARGIN), pl.ds(size - MARGIN, MARGIN)
    lower = lower_partner()
    for part in range(2):
        head, tail = object_ref[part, top, :], object_ref[part, bottom, :]
        a_ref[part] = jnp.where(lower, tail, head)
        b_ref[part] = jnp.where(lower, head, tail)
    for number, channel in enumerate(chans):
        right = sends_right(channel)
        x_ref, ka_ref, kb_ref = edge_refs[3 * number : 3 * number + 3]
        low = lane_ids() < LANES // 2
        for start in range(0, size, CHUNK):
            rows = slice(start, start + CHUNK)
            left_edge = jnp.where(
                low, object_ref[0, rows, :LANES], swap_halves(object_ref[1, rows, :LANES])
            )
            right_edge = jnp.where(
                low,
                swap_halves(object_ref[1, rows, size - LANES :]),
                object_ref[0, rows, size - LANES :],
            )
            x_ref[rows] = jnp.where(right, right_edge, left_edge)
        ka_ref[...] = jnp.where(lower, x_ref[size - MARGIN :], x_ref[:MARGIN])
        kb_ref[...] = jnp.where(lower, x_ref[:MARGIN], x_ref[size - MARGIN :])


def pack_call(object_field, chans):
    size = object_field.shape[1]
    shapes = [(2, MARGIN, size)] * 2 + [(size, LANES), (MARGIN, LANES), (MARGIN, LANES)] * len(chans)
    vmem = pl.BlockSpec(memory_space=pltpu.VMEM)
    return pl.pallas_call(
        functools.partial(pack_kernel, chans),
        out_shape=[jax.ShapeDtypeStruct(shape, F32) for shape in shapes],
        in_specs=[vmem],
        out_specs=[vmem] * len(shapes),
        compiler_params=pltpu.CompilerParams(vmem_limit_bytes=4 * 1024 * 1024),
    )(object_field)


def prepare_kernel(offsets_in, probe, placed, spots, offsets, doubled, sems):
    views, size = placed.shape[0], probe.shape[1]
    copies = fetch(
        [(offsets_in, offsets)] + [(probe, doubled.at[:, pl.ds(size * i, size)]) for i in range(2)], sems
    )
    sublane = lax.broadcasted_iota(jnp.int32, (1, 8, 1), 1)
    for copy in copies:
        copy.wait()
    for view in range(views):
        for axis in range(2):
            spots[view, axis] = jnp.full(spots.shape[2:], offsets[0, 0, axis, view], jnp.int32)
        shift_row = lax.rem(offsets[0, 0, 0, view] - MARGIN + size, size)
        shift_col = lax.rem(offsets[0, 0, 1, view] - MARGIN + size, size)
        start = lax.rem(size - shift_row, size)
        whole = pl.multiple_of((start // 8) * 8, 8)
        rest = start - whole
        for part in range(2):
            for row in range(0, size, CHUNK):
                block = doubled[part, pl.ds(whole + row, CHUNK + 8), :]
                block = pltpu.roll(block, shift_col, 1).reshape(CHUNK // 8 + 1, 8, size)
                block = pltpu.roll(block, lax.rem(8 - rest, 8), 1)
                block = jnp.where(sublane < 8 - rest, block[:-1], block[1:])
                placed[view, part, row : row + CHUNK] = block.reshape(CHUNK, size)


def prepare_call(offsets, probe):
    views, size = offsets.shape[3], probe.shape[1]
    vmem, hbm = pl.BlockSpec(memory_space=pltpu.VMEM), pl.BlockSpec(memory_space=pltpu.HBM)
    return pl.pallas_call(
        prepare_kernel,
        out_shape=[
            jax.ShapeDtypeStruct((views, 2, size, size), F32),
            jax.ShapeDtypeStruct((views, 2, 8, LANES), jnp.int32),
        ],
        in_specs=[hbm, hbm],
        out_specs=[vmem, vmem],
        scratch_shapes=[
            pltpu.SMEM(offsets.shape, jnp.int32),
            pltpu.VMEM((2, 2 * size, size), F32),
            pltpu.SemaphoreType.DMA((3,)),
        ],
        compiler_params=pltpu.CompilerParams(vmem_limit_bytes=16 * 1024 * 1024),
        cost_estimate=pl.CostEstimate(flops=10**9, bytes_accessed=10**5, transcendentals=0),
    )(offsets, probe)


def views_kernel(chans, spots, counts, core, placed, intensity, *rest):
    count = len(chans)
    a_in, *rest = rest
    x_in, b_in, rest = rest[:count], rest[count], rest[count + 1 :]
    kb_in, ka_in = rest[:count], rest[count : 2 * count]
    right, left, *rest = rest[2 * count :]
    g_core, g_a, g_b = rest[:3]
    g_x, g_ka = rest[3 : 3 + count], rest[3 + count : 3 + 2 * count]
    g_kb = rest[3 + 2 * count : 3 + 3 * count]
    amplitude, cols_m, rows_m, corner_m, s1, y, s2, z, s3, u, s4, g = rest[3 + 3 * count :]
    views, size = placed.shape[0], core.shape[1]
    half, m = size // 2, MARGIN
    lower, partner = lower_partner(), b_partner()
    low_lanes = lane_ids() < LANES // 2
    zero = jnp.zeros((CHUNK, LANES), F32)

    def unpack(blocks):
        re = im = None
        for channel, block in zip(chans, blocks):
            mine = half_lanes(takes_right(channel))
            re = jnp.where(mine, block, 0.0 if re is None else re)
            im = jnp.where(mine, swap_halves(block), 0.0 if im is None else im)
        return (re, im) if blocks else (jnp.zeros((MARGIN, LANES), F32),) * 2

    for row in range(0, size, CHUNK):
        rows = slice(row, row + CHUNK)
        cols_m[0, rows], cols_m[1, rows] = unpack([ref[rows] for ref in x_in]) if chans else (zero, zero)
    corner_a = unpack([ref[...] for ref in ka_in])
    corner_b = [jnp.where(partner, part, 0.0) for part in unpack([ref[...] for ref in kb_in])]
    for part in range(2):
        a_rows, b_rows = a_in[part], jnp.where(partner, b_in[part], 0.0)
        rows_m[part, :m] = jnp.where(lower, a_rows, b_rows)
        rows_m[part, m:] = jnp.where(lower, b_rows, a_rows)
        corner_m[part, :m] = jnp.where(lower, corner_a[part], corner_b[part])
        corner_m[part, m:] = jnp.where(lower, corner_b[part], corner_a[part])

    def by_right(lhs, t):
        both = dot(lhs[...], right[t, :size])
        return both[:size] + both[size:] + dot(lhs[:size], right[t, size:])

    def by_left(t, rhs):
        both = dot(left[t], rhs[:size])
        return both[:size] + both[size:] + dot(left[t, :size], rhs[size:])

    def put(ref, row, col, value):
        high, low = split(value)
        rows, cols = value.shape
        ref[row : row + rows, col : col + cols] = high
        ref[size + row : size + row + rows, col : col + cols] = low

    def row_mask(view, row):
        ids = row + lax.broadcasted_iota(jnp.int32, (CHUNK, LANES), 0)
        if row < m:
            return ids < spots[view, 0, :1] - m, row
        if row >= size - m:
            return ids >= size - m + spots[view, 0, :1], row - size + 2 * m
        return None, None

    def col_mask(view, block):
        if block == 0:
            return lane_ids() < spots[view, 1, :1] - m
        return lane_ids() >= m + spots[view, 1, :1]

    def patch(view, row, block):
        cols = slice(block * LANES, (block + 1) * LANES)
        rows = slice(row, row + CHUNK)
        beside = col_mask(view, block)
        beyond, place = row_mask(view, row)
        found = []
        for part in range(2):
            value = jnp.where(beside, cols_m[part, rows], core[part, rows, cols])
            if beyond is not None:
                there = slice(place, place + CHUNK)
                outer = jnp.where(beside, corner_m[part, there], rows_m[part, there, cols])
                value = jnp.where(beyond, outer, value)
            found.append(value)
        return found

    def steps(view):
        for row in range(0, size, CHUNK):
            rows = slice(row, row + CHUNK)
            waves = []
            for block in range(2):
                cols = slice(block * LANES, (block + 1) * LANES)
                o_re, o_im = patch(view, row, block)
                p_re, p_im = placed[view, 0, rows, cols], placed[view, 1, rows, cols]
                waves.append((p_re * o_re - p_im * o_im, p_re * o_im + p_im * o_re))
            for part in range(2):
                put(s1.at[view, 0], row, part * half, waves[0][part] + waves[1][part])
                put(s1.at[view, 1], row, part * half, waves[0][part] - waves[1][part])
            yield
        for odd in range(2):
            y[view, odd] = by_right(s1.at[view, odd], odd)
            yield
        for odd in range(2):
            for row in range(0, half, CHUNK):
                for part in range(2):
                    cols = slice(part * half, (part + 1) * half)
                    above = y[view, odd, row : row + CHUNK, cols]
                    below = y[view, odd, half + row : half + row + CHUNK, cols]
                    put(s2.at[view, 0], part * half + row, odd * half, above + below)
                    put(s2.at[view, 1], part * half + row, odd * half, above - below)
                yield
        valid = (view < counts[0, 0]).astype(F32)
        for row in range(0, size, CHUNK):
            rows = slice(row, row + CHUNK)
            lanes = lax.broadcasted_iota(jnp.int32, (CHUNK, LANES), 1)
            wanted = []
            for block in range(2):
                power = intensity[0, 0, view, rows, block * LANES : (block + 1) * LANES] + smooth_eps
                wanted.append(power * lax.rsqrt(power) * valid)
            for odd in range(2):
                taken = lax.rem(2 * lanes + odd, LANES)
                ordered = [jnp.take_along_axis(block, taken, axis=1) for block in wanted]
                amplitude[view, odd, rows] = jnp.where(lanes < LANES // 2, *ordered)
        yield
        for odd in range(2):
            z[view, odd] = by_left(odd, s2.at[view, odd])
            yield
        for odd in range(2):
            for row in range(0, half, CHUNK):
                re, im = z[view, odd, row : row + CHUNK], z[view, odd, half + row : half + row + CHUNK]
                taken = pl.ds(2 * row + odd, CHUNK, stride=2)
                wanted = jnp.concatenate([amplitude[view, 0, taken], amplitude[view, 1, taken]], 1)
                scaling = valid - wanted * lax.rsqrt(re * re + im * im + smooth_eps)
                put(s3.at[view, odd], row, 0, re * scaling)
                put(s3.at[view, odd], half + row, 0, im * scaling)
                yield
        for odd in range(2):
            u[view, odd] = by_left(2 + odd, s3.at[view, odd])
            yield
        for row in range(0, half, CHUNK):
            for part in range(2):
                rows = slice(part * half + row, part * half + row + CHUNK)
                even_rows, odd_rows = u[view, 0, rows], u[view, 1, rows]
                for value, place in ((even_rows + odd_rows, row), (even_rows - odd_rows, half + row)):
                    put(s4.at[view, 0], place, part * half, value[:, :half])
                    put(s4.at[view, 1], place, part * half, value[:, half:])
                yield
        for odd in range(2):
            g[view, odd] = by_right(s4.at[view, odd], 2 + odd)
            yield

    work = [steps(view) for view in range(views)]
    for view in range(views):
        for _ in range(view * STAGGER):
            work[view] = itertools.chain([None], work[view])
    for _ in itertools.zip_longest(*work):
        pass

    for row in range(0, size, CHUNK):
        rows = slice(row, row + CHUNK)
        sums = {}

        def add(key, value):
            sums[key] = sums[key] + value if key in sums else value

        for view in range(views):
            beyond, place = row_mask(view, row)
            halves = []
            for part in range(2):
                cols = slice(part * half, (part + 1) * half)
                even_cols, odd_cols = g[view, 0, rows, cols], g[view, 1, rows, cols]
                halves.append((even_cols + odd_cols, even_cols - odd_cols))
            for block in range(2):
                cols = slice(block * LANES, (block + 1) * LANES)
                beside = col_mask(view, block)
                b_re, b_im = halves[0][block], halves[1][block]
                p_re, p_im = placed[view, 0, rows, cols], placed[view, 1, rows, cols]
                for part, value in enumerate((p_re * b_re + p_im * b_im, p_re * b_im - p_im * b_re)):
                    if beyond is not None:
                        outer, value = jnp.where(beyond, value, zero), jnp.where(beyond, zero, value)
                        add(("corner", part), jnp.where(beside, outer, zero))
                        add(("row", part, block), jnp.where(beside, zero, outer))
                    add(("col", part), jnp.where(beside, value, zero))
                    add(("core", part, block), jnp.where(beside, zero, value))
        for part in range(2):
            cols_m[part, rows] = sums["col", part]
            if place is not None:
                corner_m[part, place : place + CHUNK] = sums["corner", part]
            for block in range(2):
                cols = slice(block * LANES, (block + 1) * LANES)
                g_core[part, rows, cols] = sums["core", part, block]
                if place is not None:
                    rows_m[part, place : place + CHUNK, cols] = sums["row", part, block]

    def packed(channel, re, im):
        to_right = jnp.where(low_lanes, re, swap_halves(im))
        to_left = jnp.where(low_lanes, swap_halves(im), re)
        return jnp.where(sends_right(channel), to_right, to_left)

    for part in range(2):
        bottom, top = rows_m[part, :m], rows_m[part, m:]
        g_a[part] = jnp.where(lower, bottom, top)
        g_b[part] = jnp.where(lower, top, bottom)
    bottom = (corner_m[0, :m], corner_m[1, :m])
    top = (corner_m[0, m:], corner_m[1, m:])
    for number, channel in enumerate(chans):
        for row in range(0, size, CHUNK):
            rows = slice(row, row + CHUNK)
            g_x[number][rows] = packed(channel, cols_m[0, rows], cols_m[1, rows])
        below, above = packed(channel, *bottom), packed(channel, *top)
        g_ka[number][...] = jnp.where(lower, below, above)
        g_kb[number][...] = jnp.where(lower, above, below)


def views_call(chans, spots, counts, core, placed, intensity, tables, a_in, b_in, x_in, ka_in, kb_in):
    views, size = placed.shape[0], core.shape[1]
    count = len(chans)
    vmem = pl.BlockSpec(memory_space=pltpu.VMEM)
    shapes = [(2, size, size), (2, MARGIN, size), (2, MARGIN, size)]
    shapes += [(size, LANES)] * count + [(MARGIN, LANES)] * (2 * count)
    full = pltpu.VMEM((views, 2, size, size), F32)
    tall = pltpu.VMEM((views, 2, 2 * size, size), BF16)
    outs = pl.pallas_call(
        functools.partial(views_kernel, chans),
        out_shape=[jax.ShapeDtypeStruct(shape, F32) for shape in shapes],
        in_specs=[
            vmem,
            pl.BlockSpec(memory_space=pltpu.SMEM),
            *[vmem] * (7 + 3 * count),
        ],
        out_specs=[vmem] * len(shapes),
        scratch_shapes=[
            pltpu.VMEM((views, 2, size, size // 2), F32),
            pltpu.VMEM((2, size, LANES), F32),
            pltpu.VMEM((2, 2 * MARGIN, size), F32),
            pltpu.VMEM((2, 2 * MARGIN, LANES), F32),
            *[tall, full] * 4,
        ],
        compiler_params=pltpu.CompilerParams(vmem_limit_bytes=40 * 1024 * 1024),
    )(spots, counts, core, placed, intensity, a_in, *x_in, b_in, *kb_in, *ka_in, *tables)
    return (*outs[:3], outs[3 : 3 + count], outs[3 + count : 3 + 2 * count], outs[3 + 2 * count :])


def finish_kernel(chans, object_ref, g_core, *rest):
    count = len(chans)
    a_in, *rest = rest
    x_in, b_in, rest = rest[:count], rest[count], rest[count + 1 :]
    kb_in, ka_in, out = rest[:count], rest[count : 2 * count], rest[-1]
    size = object_ref.shape[1]
    lower = lower_partner()
    a_rows = pl.ds(pl.multiple_of(jnp.where(lower, size - MARGIN, 0), MARGIN), MARGIN)
    b_rows = pl.ds(pl.multiple_of(jnp.where(lower, 0, size - MARGIN), MARGIN), MARGIN)
    columns = []
    for channel in chans:
        right = takes_right(channel)
        mine = lane_ids() // (LANES // 2) == jnp.where(right, 1, 0)
        block = pl.multiple_of(jnp.where(right, size - LANES, 0), LANES)
        columns.append((mine, pl.ds(block, LANES)))

    def take(place, value):
        out[place] -= step_size * value

    def take_packed(rows, column, block):
        mine, lanes = column
        take((0, rows, lanes), jnp.where(mine, block, 0.0))
        take((1, rows, lanes), jnp.where(mine, swap_halves(block), 0.0))

    for part in range(2):
        out[part] = object_ref[part] - step_size * g_core[part]
        take((part, a_rows), a_in[part])
    for number, column in enumerate(columns):
        take_packed(slice(None), column, x_in[number][...])
        take_packed(a_rows, column, ka_in[number][...])

    @pl.when(b_partner())
    def _():
        for part in range(2):
            take((part, b_rows), b_in[part])
        for number, column in enumerate(columns):
            take_packed(b_rows, column, kb_in[number][...])


def finish_call(chans, object_field, g_core, a_in, b_in, x_in, ka_in, kb_in):
    vmem = pl.BlockSpec(memory_space=pltpu.VMEM)
    return pl.pallas_call(
        functools.partial(finish_kernel, chans),
        out_shape=jax.ShapeDtypeStruct(object_field.shape, F32),
        in_specs=[vmem] * (4 + 3 * len(chans)),
        out_specs=vmem,
        compiler_params=pltpu.CompilerParams(vmem_limit_bytes=6 * 1024 * 1024),
    )(object_field, g_core, a_in, *x_in, b_in, *kb_in, *ka_in)


def per_device(object_field, probe_field, intensity, view_offsets, view_counts):
    size = object_field.shape[1]
    mesh_rows, mesh_cols = lax.axis_size("row"), lax.axis_size("col")
    chans = channels(mesh_cols)
    tables = dft_tables(size)
    a_pairs, b_pairs = row_pairs(mesh_rows, 0), row_pairs(mesh_rows, 1)
    spare = spare_route(b_pairs, mesh_rows, mesh_cols)

    def over_rows(block, pairs, extra):
        route = [(i * mesh_cols + k, j * mesh_cols + k) for i, j in pairs for k in range(mesh_cols)]
        return lax.ppermute(block, ("row", "col"), route + extra)

    def across(block, pairs, extra, channel):
        route = [(i * mesh_cols + k, j * mesh_cols + l) for i, j in pairs for k, l in channel[0]]
        return lax.ppermute(block, ("row", "col"), route + (extra if mesh_cols == 2 else []))

    def exchange(a_send, b_send, x_send, ka_send, kb_send):
        x_in = [lax.ppermute(block, "col", channel[0]) for block, channel in zip(x_send, chans)]
        b_in = over_rows(b_send, b_pairs, spare)
        kb_in = [across(block, b_pairs, spare, channel) for block, channel in zip(kb_send, chans)]
        ka_in = [across(block, a_pairs, [], channel) for block, channel in zip(ka_send, chans)]
        a_in = over_rows(a_send, a_pairs, [])
        return a_in, b_in, x_in, ka_in, kb_in

    packs = pack_call(object_field, chans)
    offsets, probe = (
        pltpu.with_memory_space_constraint(array, pltpu.HBM)
        for array in (jnp.swapaxes(view_offsets, 2, 3), probe_field)
    )
    margins = exchange(packs[0], packs[1], packs[2::3], packs[3::3], packs[4::3])
    placed, spots = prepare_call(offsets, probe)
    g_core, *sends = views_call(
        chans, spots, view_counts, object_field, placed, intensity, tables, *margins
    )
    return finish_call(chans, object_field, g_core, *exchange(*sends))


def solution(mesh):
    in_specs = (
        P(None, "row", "col"),
        P(),
        P("row", "col", None, None, None),
        P("row", "col", None, None),
        P("row", "col"),
    )
    out_specs = P(None, "row", "col")
    return jax.shard_map(
        per_device, mesh=mesh, in_specs=in_specs, out_specs=out_specs, check_vma=False
    )
```

```python
import functools
import itertools
import math

import jax
import jax.numpy as jnp
import ml_dtypes
import numpy as np
from jax import lax
from jax.experimental import pallas as pl
from jax.experimental.pallas import tpu as pltpu
from jax.sharding import PartitionSpec as P

MARGIN = 64
LANES = 128
CHUNK = 64
STAGGER = 2

smooth_eps = 0.1
step_size = 0.2

F32 = jnp.float32
BF16 = jnp.bfloat16


def dft_tables(length):
    half = length // 2
    counter = np.arange(half)
    factor = 1.0 / math.sqrt(length)
    product = np.outer(counter, counter)
    even = np.exp(-2j * np.pi * (product % half) / half) * factor
    odd = np.exp(-2j * np.pi * ((2 * product + counter[:, None]) % length) / length) * factor

    def as_real(table):
        return np.block([[table.real, table.imag], [-table.imag, table.real]])

    def parts(table):
        high = table.astype(ml_dtypes.bfloat16)
        low = (table - high.astype(np.float64)).astype(ml_dtypes.bfloat16)
        return high, low

    even, odd = as_real(even), as_real(odd)
    by_right = [np.concatenate(parts(t), 0) for t in (even, odd, even.T, odd.T)]
    by_left = [np.concatenate(parts(t), 0) for t in (even.T, odd.T, even, odd)]
    return np.stack(by_right), np.stack(by_left)


def channels(mesh_cols):
    if mesh_cols == 1:
        return []
    if mesh_cols == 2:
        return [([(0, 1), (1, 0)], None, None)]
    forward = [(i, i + 1) for i in range(mesh_cols - 1)]
    return [(forward, True, False), ([(j, i) for i, j in forward], False, True)]


def row_pairs(count, first):
    pairs = [(i, i + 1) for i in range(first, count - 1, 2)]
    return pairs + [(j, i) for i, j in pairs]


def spare_route(pairs, mesh_rows, mesh_cols):
    rows = [i for i in range(mesh_rows) if i not in dict(pairs)]
    if mesh_cols % 2:
        return []
    return [(i * mesh_cols + k, i * mesh_cols + (k ^ 1)) for i in rows for k in range(mesh_cols)]


def b_partner():
    row = lax.axis_index("row")
    return jnp.where(lower_partner(), row > 0, row < lax.axis_size("row") - 1)


def sends_right(channel):
    return lax.axis_index("col") == 0 if channel[1] is None else channel[1]


def takes_right(channel):
    return lax.axis_index("col") == 0 if channel[2] is None else channel[2]


def lower_partner():
    return lax.rem(lax.axis_index("row"), 2) == 0


def lane_ids():
    return lax.broadcasted_iota(jnp.int32, (1, LANES), 1)


def half_lanes(right):
    low = lane_ids() < LANES // 2
    if isinstance(right, bool):
        return low if right else ~low
    return lane_ids() // (LANES // 2) == jnp.where(right, 0, 1)


def split(value):
    high = value.astype(BF16)
    return high, (value - high.astype(F32)).astype(BF16)


def dot(first, second):
    return jnp.dot(first, second, preferred_element_type=F32)


def swap_halves(block):
    return pltpu.roll(block, LANES // 2, 1)


def fetch(pairs, sems):
    copies = [pltpu.make_async_copy(source, target, sems.at[i]) for i, (source, target) in enumerate(pairs)]
    for copy in copies:
        copy.start()
    return copies


def pack_kernel(chans, object_ref, a_ref, b_ref, *edge_refs):
    size = object_ref.shape[1]
    top, bottom = pl.ds(0, MARGIN), pl.ds(size - MARGIN, MARGIN)
    lower = lower_partner()
    for part in range(2):
        head, tail = object_ref[part, top, :], object_ref[part, bottom, :]
        a_ref[part] = jnp.where(lower, tail, head)
        b_ref[part] = jnp.where(lower, head, tail)
    for number, channel in enumerate(chans):
        right = sends_right(channel)
        x_ref, ka_ref, kb_ref = edge_refs[3 * number : 3 * number + 3]
        low = lane_ids() < LANES // 2
        for start in range(0, size, CHUNK):
            rows = slice(start, start + CHUNK)
            left_edge = jnp.where(
                low, object_ref[0, rows, :LANES], swap_halves(object_ref[1, rows, :LANES])
            )
            right_edge = jnp.where(
                low,
                swap_halves(object_ref[1, rows, size - LANES :]),
                object_ref[0, rows, size - LANES :],
            )
            x_ref[rows] = jnp.where(right, right_edge, left_edge)
        ka_ref[...] = jnp.where(lower, x_ref[size - MARGIN :], x_ref[:MARGIN])
        kb_ref[...] = jnp.where(lower, x_ref[:MARGIN], x_ref[size - MARGIN :])


def pack_call(object_field, chans):
    size = object_field.shape[1]
    shapes = [(2, MARGIN, size)] * 2 + [(size, LANES), (MARGIN, LANES), (MARGIN, LANES)] * len(chans)
    vmem = pl.BlockSpec(memory_space=pltpu.VMEM)
    return pl.pallas_call(
        functools.partial(pack_kernel, chans),
        out_shape=[jax.ShapeDtypeStruct(shape, F32) for shape in shapes],
        in_specs=[vmem],
        out_specs=[vmem] * len(shapes),
        compiler_params=pltpu.CompilerParams(vmem_limit_bytes=4 * 1024 * 1024),
    )(object_field)


def prepare_kernel(offsets_in, probe, placed, spots, offsets, doubled, sems):
    views, size = placed.shape[0], probe.shape[1]
    copies = fetch(
        [(offsets_in, offsets)] + [(probe, doubled.at[:, pl.ds(size * i, size)]) for i in range(2)], sems
    )
    sublane = lax.broadcasted_iota(jnp.int32, (1, 8, 1), 1)
    for copy in copies:
        copy.wait()
    for view in range(views):
        for axis in range(2):
            spots[view, axis] = jnp.full(spots.shape[2:], offsets[0, 0, axis, view], jnp.int32)
        shift_row = lax.rem(offsets[0, 0, 0, view] - MARGIN + size, size)
        shift_col = lax.rem(offsets[0, 0, 1, view] - MARGIN + size, size)
        start = lax.rem(size - shift_row, size)
        whole = pl.multiple_of((start // 8) * 8, 8)
        rest = start - whole
        for part in range(2):
            for row in range(0, size, CHUNK):
                block = doubled[part, pl.ds(whole + row, CHUNK + 8), :]
                block = pltpu.roll(block, shift_col, 1).reshape(CHUNK // 8 + 1, 8, size)
                block = pltpu.roll(block, lax.rem(8 - rest, 8), 1)
                block = jnp.where(sublane < 8 - rest, block[:-1], block[1:])
                placed[view, part, row : row + CHUNK] = block.reshape(CHUNK, size)


def prepare_call(offsets, probe):
    views, size = offsets.shape[3], probe.shape[1]
    vmem, hbm = pl.BlockSpec(memory_space=pltpu.VMEM), pl.BlockSpec(memory_space=pltpu.HBM)
    return pl.pallas_call(
        prepare_kernel,
        out_shape=[
            jax.ShapeDtypeStruct((views, 2, size, size), F32),
            jax.ShapeDtypeStruct((views, 2, 8, LANES), jnp.int32),
        ],
        in_specs=[hbm, hbm],
        out_specs=[vmem, vmem],
        scratch_shapes=[
            pltpu.SMEM(offsets.shape, jnp.int32),
            pltpu.VMEM((2, 2 * size, size), F32),
            pltpu.SemaphoreType.DMA((3,)),
        ],
        compiler_params=pltpu.CompilerParams(vmem_limit_bytes=16 * 1024 * 1024),
        cost_estimate=pl.CostEstimate(flops=10**9, bytes_accessed=10**5, transcendentals=0),
    )(offsets, probe)


def views_kernel(chans, spots, counts, core, placed, intensity, *rest):
    count = len(chans)
    a_in, *rest = rest
    x_in, b_in, rest = rest[:count], rest[count], rest[count + 1 :]
    kb_in, ka_in = rest[:count], rest[count : 2 * count]
    right, left, *rest = rest[2 * count :]
    g_core, g_a, g_b = rest[:3]
    g_x, g_ka = rest[3 : 3 + count], rest[3 + count : 3 + 2 * count]
    g_kb = rest[3 + 2 * count : 3 + 3 * count]
    amplitude, cols_m, rows_m, corner_m, s1, y, s2, z, s3, u, s4, g = rest[3 + 3 * count :]
    views, size = placed.shape[0], core.shape[1]
    half, m = size // 2, MARGIN
    lower, partner = lower_partner(), b_partner()
    low_lanes = lane_ids() < LANES // 2
    zero = jnp.zeros((CHUNK, LANES), F32)

    def unpack(blocks):
        re = im = None
        for channel, block in zip(chans, blocks):
            mine = half_lanes(takes_right(channel))
            re = jnp.where(mine, block, 0.0 if re is None else re)
            im = jnp.where(mine, swap_halves(block), 0.0 if im is None else im)
        return (re, im) if blocks else (jnp.zeros((MARGIN, LANES), F32),) * 2

    for row in range(0, size, CHUNK):
        rows = slice(row, row + CHUNK)
        cols_m[0, rows], cols_m[1, rows] = unpack([ref[rows] for ref in x_in]) if chans else (zero, zero)
    corner_a = unpack([ref[...] for ref in ka_in])
    corner_b = [jnp.where(partner, part, 0.0) for part in unpack([ref[...] for ref in kb_in])]
    for part in range(2):
        a_rows, b_rows = a_in[part], jnp.where(partner, b_in[part], 0.0)
        rows_m[part, :m] = jnp.where(lower, a_rows, b_rows)
        rows_m[part, m:] = jnp.where(lower, b_rows, a_rows)
        corner_m[part, :m] = jnp.where(lower, corner_a[part], corner_b[part])
        corner_m[part, m:] = jnp.where(lower, corner_b[part], corner_a[part])

    def by_right(lhs, t):
        both = dot(lhs[...], right[t, :size])
        return both[:size] + both[size:] + dot(lhs[:size], right[t, size:])

    def by_left(t, rhs):
        both = dot(left[t], rhs[:size])
        return both[:size] + both[size:] + dot(left[t, :size], rhs[size:])

    def put(ref, row, col, value):
        high, low = split(value)
        rows, cols = value.shape
        ref[row : row + rows, col : col + cols] = high
        ref[size + row : size + row + rows, col : col + cols] = low

    def row_mask(view, row):
        ids = row + lax.broadcasted_iota(jnp.int32, (CHUNK, LANES), 0)
        if row < m:
            return ids < spots[view, 0, :1] - m, row
        if row >= size - m:
            return ids >= size - m + spots[view, 0, :1], row - size + 2 * m
        return None, None

    def col_mask(view, block):
        if block == 0:
            return lane_ids() < spots[view, 1, :1] - m
        return lane_ids() >= m + spots[view, 1, :1]

    def patch(view, row, block):
        cols = slice(block * LANES, (block + 1) * LANES)
        rows = slice(row, row + CHUNK)
        beside = col_mask(view, block)
        beyond, place = row_mask(view, row)
        found = []
        for part in range(2):
            value = jnp.where(beside, cols_m[part, rows], core[part, rows, cols])
            if beyond is not None:
                there = slice(place, place + CHUNK)
                outer = jnp.where(beside, corner_m[part, there], rows_m[part, there, cols])
                value = jnp.where(beyond, outer, value)
            found.append(value)
        return found

    def steps(view):
        for row in range(0, size, CHUNK):
            rows = slice(row, row + CHUNK)
            waves = []
            for block in range(2):
                cols = slice(block * LANES, (block + 1) * LANES)
                o_re, o_im = patch(view, row, block)
                p_re, p_im = placed[view, 0, rows, cols], placed[view, 1, rows, cols]
                waves.append((p_re * o_re - p_im * o_im, p_re * o_im + p_im * o_re))
            for part in range(2):
                put(s1.at[view, 0], row, part * half, waves[0][part] + waves[1][part])
                put(s1.at[view, 1], row, part * half, waves[0][part] - waves[1][part])
            yield
        for odd in range(2):
            y[view, odd] = by_right(s1.at[view, odd], odd)
            yield
        for odd in range(2):
            for row in range(0, half, CHUNK):
                for part in range(2):
                    cols = slice(part * half, (part + 1) * half)
                    above = y[view, odd, row : row + CHUNK, cols]
                    below = y[view, odd, half + row : half + row + CHUNK, cols]
                    put(s2.at[view, 0], part * half + row, odd * half, above + below)
                    put(s2.at[view, 1], part * half + row, odd * half, above - below)
                yield
        valid = (view < counts[0, 0]).astype(F32)
        for row in range(0, size, CHUNK):
            rows = slice(row, row + CHUNK)
            lanes = lax.broadcasted_iota(jnp.int32, (CHUNK, LANES), 1)
            wanted = []
            for block in range(2):
                power = intensity[0, 0, view, rows, block * LANES : (block + 1) * LANES] + smooth_eps
                wanted.append(power * lax.rsqrt(power) * valid)
            for odd in range(2):
                taken = lax.rem(2 * lanes + odd, LANES)
                ordered = [jnp.take_along_axis(block, taken, axis=1) for block in wanted]
                amplitude[view, odd, rows] = jnp.where(lanes < LANES // 2, *ordered)
        yield
        for odd in range(2):
            z[view, odd] = by_left(odd, s2.at[view, odd])
            yield
        for odd in range(2):
            for row in range(0, half, CHUNK):
                re, im = z[view, odd, row : row + CHUNK], z[view, odd, half + row : half + row + CHUNK]
                taken = pl.ds(2 * row + odd, CHUNK, stride=2)
                wanted = jnp.concatenate([amplitude[view, 0, taken], amplitude[view, 1, taken]], 1)
                scaling = valid - wanted * lax.rsqrt(re * re + im * im + smooth_eps)
                put(s3.at[view, odd], row, 0, re * scaling)
                put(s3.at[view, odd], half + row, 0, im * scaling)
                yield
        for odd in range(2):
            u[view, odd] = by_left(2 + odd, s3.at[view, odd])
            yield
        for row in range(0, half, CHUNK):
            for part in range(2):
                rows = slice(part * half + row, part * half + row + CHUNK)
                even_rows, odd_rows = u[view, 0, rows], u[view, 1, rows]
                for value, place in ((even_rows + odd_rows, row), (even_rows - odd_rows, half + row)):
                    put(s4.at[view, 0], place, part * half, value[:, :half])
                    put(s4.at[view, 1], place, part * half, value[:, half:])
                yield
        for odd in range(2):
            g[view, odd] = by_right(s4.at[view, odd], 2 + odd)
            yield

    work = [steps(view) for view in range(views)]
    for view in range(views):
        for _ in range(view * STAGGER):
            work[view] = itertools.chain([None], work[view])
    for _ in itertools.zip_longest(*work):
        pass

    for row in range(0, size, CHUNK):
        rows = slice(row, row + CHUNK)
        sums = {}

        def add(key, value):
            sums[key] = sums[key] + value if key in sums else value

        for view in range(views):
            beyond, place = row_mask(view, row)
            halves = []
            for part in range(2):
                cols = slice(part * half, (part + 1) * half)
                even_cols, odd_cols = g[view, 0, rows, cols], g[view, 1, rows, cols]
                halves.append((even_cols + odd_cols, even_cols - odd_cols))
            for block in range(2):
                cols = slice(block * LANES, (block + 1) * LANES)
                beside = col_mask(view, block)
                b_re, b_im = halves[0][block], halves[1][block]
                p_re, p_im = placed[view, 0, rows, cols], placed[view, 1, rows, cols]
                for part, value in enumerate((p_re * b_re + p_im * b_im, p_re * b_im - p_im * b_re)):
                    if beyond is not None:
                        outer, value = jnp.where(beyond, value, zero), jnp.where(beyond, zero, value)
                        add(("corner", part), jnp.where(beside, outer, zero))
                        add(("row", part, block), jnp.where(beside, zero, outer))
                    add(("col", part), jnp.where(beside, value, zero))
                    add(("core", part, block), jnp.where(beside, zero, value))
        for part in range(2):
            cols_m[part, rows] = sums["col", part]
            if place is not None:
                corner_m[part, place : place + CHUNK] = sums["corner", part]
            for block in range(2):
                cols = slice(block * LANES, (block + 1) * LANES)
                g_core[part, rows, cols] = sums["core", part, block]
                if place is not None:
                    rows_m[part, place : place + CHUNK, cols] = sums["row", part, block]

    def packed(channel, re, im):
        to_right = jnp.where(low_lanes, re, swap_halves(im))
        to_left = jnp.where(low_lanes, swap_halves(im), re)
        return jnp.where(sends_right(channel), to_right, to_left)

    for part in range(2):
        bottom, top = rows_m[part, :m], rows_m[part, m:]
        g_a[part] = jnp.where(lower, bottom, top)
        g_b[part] = jnp.where(lower, top, bottom)
    bottom = (corner_m[0, :m], corner_m[1, :m])
    top = (corner_m[0, m:], corner_m[1, m:])
    for number, channel in enumerate(chans):
        for row in range(0, size, CHUNK):
            rows = slice(row, row + CHUNK)
            g_x[number][rows] = packed(channel, cols_m[0, rows], cols_m[1, rows])
        below, above = packed(channel, *bottom), packed(channel, *top)
        g_ka[number][...] = jnp.where(lower, below, above)
        g_kb[number][...] = jnp.where(lower, above, below)


def views_call(chans, spots, counts, core, placed, intensity, tables, a_in, b_in, x_in, ka_in, kb_in):
    views, size = placed.shape[0], core.shape[1]
    count = len(chans)
    vmem = pl.BlockSpec(memory_space=pltpu.VMEM)
    shapes = [(2, size, size), (2, MARGIN, size), (2, MARGIN, size)]
    shapes += [(size, LANES)] * count + [(MARGIN, LANES)] * (2 * count)
    full = pltpu.VMEM((views, 2, size, size), F32)
    tall = pltpu.VMEM((views, 2, 2 * size, size), BF16)
    outs = pl.pallas_call(
        functools.partial(views_kernel, chans),
        out_shape=[jax.ShapeDtypeStruct(shape, F32) for shape in shapes],
        in_specs=[
            vmem,
            pl.BlockSpec(memory_space=pltpu.SMEM),
            *[vmem] * (7 + 3 * count),
        ],
        out_specs=[vmem] * len(shapes),
        scratch_shapes=[
            pltpu.VMEM((views, 2, size, size // 2), F32),
            pltpu.VMEM((2, size, LANES), F32),
            pltpu.VMEM((2, 2 * MARGIN, size), F32),
            pltpu.VMEM((2, 2 * MARGIN, LANES), F32),
            *[tall, full] * 4,
        ],
        compiler_params=pltpu.CompilerParams(vmem_limit_bytes=40 * 1024 * 1024),
    )(spots, counts, core, placed, intensity, a_in, *x_in, b_in, *kb_in, *ka_in, *tables)
    return (*outs[:3], outs[3 : 3 + count], outs[3 + count : 3 + 2 * count], outs[3 + 2 * count :])


def finish_kernel(chans, object_ref, g_core, *rest):
    count = len(chans)
    a_in, *rest = rest
    x_in, b_in, rest = rest[:count], rest[count], rest[count + 1 :]
    kb_in, ka_in, out = rest[:count], rest[count : 2 * count], rest[-1]
    size = object_ref.shape[1]
    lower = lower_partner()
    a_rows = pl.ds(pl.multiple_of(jnp.where(lower, size - MARGIN, 0), MARGIN), MARGIN)
    b_rows = pl.ds(pl.multiple_of(jnp.where(lower, 0, size - MARGIN), MARGIN), MARGIN)
    columns = []
    for channel in chans:
        right = takes_right(channel)
        mine = lane_ids() // (LANES // 2) == jnp.where(right, 1, 0)
        block = pl.multiple_of(jnp.where(right, size - LANES, 0), LANES)
        columns.append((mine, pl.ds(block, LANES)))

    def take(place, value):
        out[place] -= step_size * value

    def take_packed(rows, column, block):
        mine, lanes = column
        take((0, rows, lanes), jnp.where(mine, block, 0.0))
        take((1, rows, lanes), jnp.where(mine, swap_halves(block), 0.0))

    for part in range(2):
        out[part] = object_ref[part] - step_size * g_core[part]
        take((part, a_rows), a_in[part])
    for number, column in enumerate(columns):
        take_packed(slice(None), column, x_in[number][...])
        take_packed(a_rows, column, ka_in[number][...])

    @pl.when(b_partner())
    def _():
        for part in range(2):
            take((part, b_rows), b_in[part])
        for number, column in enumerate(columns):
            take_packed(b_rows, column, kb_in[number][...])


def finish_call(chans, object_field, g_core, a_in, b_in, x_in, ka_in, kb_in):
    vmem = pl.BlockSpec(memory_space=pltpu.VMEM)
    return pl.pallas_call(
        functools.partial(finish_kernel, chans),
        out_shape=jax.ShapeDtypeStruct(object_field.shape, F32),
        in_specs=[vmem] * (4 + 3 * len(chans)),
        out_specs=vmem,
        compiler_params=pltpu.CompilerParams(vmem_limit_bytes=6 * 1024 * 1024),
    )(object_field, g_core, a_in, *x_in, b_in, *kb_in, *ka_in)


def per_device(object_field, probe_field, intensity, view_offsets, view_counts):
    size = object_field.shape[1]
    mesh_rows, mesh_cols = lax.axis_size("row"), lax.axis_size("col")
    chans = channels(mesh_cols)
    tables = dft_tables(size)
    a_pairs, b_pairs = row_pairs(mesh_rows, 0), row_pairs(mesh_rows, 1)
    spare = spare_route(b_pairs, mesh_rows, mesh_cols)
    alone = [i for i in range(mesh_rows) if i not in dict(b_pairs)]
    ends = list(zip(alone, alone[::-1])) if len(alone) == 2 else []

    def over_rows(block, pairs, extra):
        route = [(i * mesh_cols + k, j * mesh_cols + k) for i, j in pairs for k in range(mesh_cols)]
        return lax.ppermute(block, ("row", "col"), route + extra)

    def across(block, pairs, extra, channel):
        route = [(i * mesh_cols + k, j * mesh_cols + l) for i, j in pairs for k, l in channel[0]]
        return lax.ppermute(block, ("row", "col"), route + (extra if mesh_cols == 2 else []))

    def exchange(a_send, b_send, x_send, ka_send, kb_send):
        x_in = [lax.ppermute(block, "col", channel[0]) for block, channel in zip(x_send, chans)]
        b_in = over_rows(b_send, b_pairs + ends, [])
        kb_in = [across(block, b_pairs, spare, channel) for block, channel in zip(kb_send, chans)]
        ka_in = [across(block, a_pairs, [], channel) for block, channel in zip(ka_send, chans)]
        a_in = over_rows(a_send, a_pairs, [])
        return a_in, b_in, x_in, ka_in, kb_in

    packs = pack_call(object_field, chans)
    offsets, probe = (
        pltpu.with_memory_space_constraint(array, pltpu.HBM)
        for array in (jnp.swapaxes(view_offsets, 2, 3), probe_field)
    )
    margins = exchange(packs[0], packs[1], packs[2::3], packs[3::3], packs[4::3])
    placed, spots = prepare_call(offsets, probe)
    g_core, *sends = views_call(
        chans, spots, view_counts, object_field, placed, intensity, tables, *margins
    )
    return finish_call(chans, object_field, g_core, *exchange(*sends))


def solution(mesh):
    in_specs = (
        P(None, "row", "col"),
        P(),
        P("row", "col", None, None, None),
        P("row", "col", None, None),
        P("row", "col"),
    )
    out_specs = P(None, "row", "col")
    return jax.shard_map(
        per_device, mesh=mesh, in_specs=in_specs, out_specs=out_specs, check_vma=False
    )
```

```python
import functools
import itertools
import math

import jax
import jax.numpy as jnp
import ml_dtypes
import numpy as np
from jax import lax
from jax.experimental import pallas as pl
from jax.experimental.pallas import tpu as pltpu
from jax.sharding import PartitionSpec as P

MARGIN = 64
LANES = 128
CHUNK = 64
STAGGER = 2

smooth_eps = 0.1
step_size = 0.2

F32 = jnp.float32
BF16 = jnp.bfloat16


def dft_tables(length):
    half = length // 2
    counter = np.arange(half)
    factor = 1.0 / math.sqrt(length)
    product = np.outer(counter, counter)
    even = np.exp(-2j * np.pi * (product % half) / half) * factor
    odd = np.exp(-2j * np.pi * ((2 * product + counter[:, None]) % length) / length) * factor

    def as_real(table):
        return np.block([[table.real, table.imag], [-table.imag, table.real]])

    def parts(table):
        high = table.astype(ml_dtypes.bfloat16)
        low = (table - high.astype(np.float64)).astype(ml_dtypes.bfloat16)
        return high, low

    even, odd = as_real(even), as_real(odd)
    by_right = [np.concatenate(parts(t), 0) for t in (even, odd, even.T, odd.T)]
    by_left = [np.concatenate(parts(t), 0) for t in (even.T, odd.T, even, odd)]
    return np.stack(by_right), np.stack(by_left)


def channels(mesh_cols):
    if mesh_cols == 1:
        return []
    if mesh_cols == 2:
        return [([(0, 1), (1, 0)], None, None)]
    forward = [(i, i + 1) for i in range(mesh_cols - 1)]
    return [(forward, True, False), ([(j, i) for i, j in forward], False, True)]


def row_pairs(count, first):
    pairs = [(i, i + 1) for i in range(first, count - 1, 2)]
    return pairs + [(j, i) for i, j in pairs]


def spare_route(pairs, mesh_rows, mesh_cols):
    rows = [i for i in range(mesh_rows) if i not in dict(pairs)]
    if mesh_cols % 2:
        return []
    return [(i * mesh_cols + k, i * mesh_cols + (k ^ 1)) for i in rows for k in range(mesh_cols)]


def b_partner():
    row = lax.axis_index("row")
    return jnp.where(lower_partner(), row > 0, row < lax.axis_size("row") - 1)


def sends_right(channel):
    return lax.axis_index("col") == 0 if channel[1] is None else channel[1]


def takes_right(channel):
    return lax.axis_index("col") == 0 if channel[2] is None else channel[2]


def lower_partner():
    return lax.rem(lax.axis_index("row"), 2) == 0


def lane_ids():
    return lax.broadcasted_iota(jnp.int32, (1, LANES), 1)


def half_lanes(right):
    low = lane_ids() < LANES // 2
    if isinstance(right, bool):
        return low if right else ~low
    return lane_ids() // (LANES // 2) == jnp.where(right, 0, 1)


def split(value):
    high = value.astype(BF16)
    return high, (value - high.astype(F32)).astype(BF16)


def dot(first, second):
    return jnp.dot(first, second, preferred_element_type=F32)


def swap_halves(block):
    return pltpu.roll(block, LANES // 2, 1)


def fetch(pairs, sems):
    copies = [pltpu.make_async_copy(source, target, sems.at[i]) for i, (source, target) in enumerate(pairs)]
    for copy in copies:
        copy.start()
    return copies


def pack_kernel(chans, object_ref, a_ref, b_ref, *edge_refs):
    size = object_ref.shape[1]
    top, bottom = pl.ds(0, MARGIN), pl.ds(size - MARGIN, MARGIN)
    lower = lower_partner()
    for part in range(2):
        head, tail = object_ref[part, top, :], object_ref[part, bottom, :]
        a_ref[part] = jnp.where(lower, tail, head)
        b_ref[part] = jnp.where(lower, head, tail)
    for number, channel in enumerate(chans):
        right = sends_right(channel)
        x_ref, ka_ref, kb_ref = edge_refs[3 * number : 3 * number + 3]
        low = lane_ids() < LANES // 2
        for start in range(0, size, CHUNK):
            rows = slice(start, start + CHUNK)
            left_edge = jnp.where(
                low, object_ref[0, rows, :LANES], swap_halves(object_ref[1, rows, :LANES])
            )
            right_edge = jnp.where(
                low,
                swap_halves(object_ref[1, rows, size - LANES :]),
                object_ref[0, rows, size - LANES :],
            )
            x_ref[rows] = jnp.where(right, right_edge, left_edge)
        ka_ref[...] = jnp.where(lower, x_ref[size - MARGIN :], x_ref[:MARGIN])
        kb_ref[...] = jnp.where(lower, x_ref[:MARGIN], x_ref[size - MARGIN :])


def pack_call(object_field, chans):
    size = object_field.shape[1]
    shapes = [(2, MARGIN, size)] * 2 + [(size, LANES), (MARGIN, LANES), (MARGIN, LANES)] * len(chans)
    vmem = pl.BlockSpec(memory_space=pltpu.VMEM)
    return pl.pallas_call(
        functools.partial(pack_kernel, chans),
        out_shape=[jax.ShapeDtypeStruct(shape, F32) for shape in shapes],
        in_specs=[vmem],
        out_specs=[vmem] * len(shapes),
        compiler_params=pltpu.CompilerParams(vmem_limit_bytes=4 * 1024 * 1024),
    )(object_field)


def prepare_kernel(offsets_in, probe, placed, spots, offsets, doubled, sems):
    views, size = placed.shape[0], probe.shape[1]
    copies = fetch(
        [(offsets_in, offsets)] + [(probe, doubled.at[:, pl.ds(size * i, size)]) for i in range(2)], sems
    )
    sublane = lax.broadcasted_iota(jnp.int32, (1, 8, 1), 1)
    for copy in copies:
        copy.wait()
    for view in range(views):
        for axis in range(2):
            spots[view, axis] = jnp.full(spots.shape[2:], offsets[0, 0, axis, view], jnp.int32)
        shift_row = lax.rem(offsets[0, 0, 0, view] - MARGIN + size, size)
        shift_col = lax.rem(offsets[0, 0, 1, view] - MARGIN + size, size)
        start = lax.rem(size - shift_row, size)
        whole = pl.multiple_of((start // 8) * 8, 8)
        rest = start - whole
        for part in range(2):
            for row in range(0, size, CHUNK):
                block = doubled[part, pl.ds(whole + row, CHUNK + 8), :]
                block = pltpu.roll(block, shift_col, 1).reshape(CHUNK // 8 + 1, 8, size)
                block = pltpu.roll(block, lax.rem(8 - rest, 8), 1)
                block = jnp.where(sublane < 8 - rest, block[:-1], block[1:])
                placed[view, part, row : row + CHUNK] = block.reshape(CHUNK, size)


def prepare_call(offsets, probe):
    views, size = offsets.shape[3], probe.shape[1]
    vmem, hbm = pl.BlockSpec(memory_space=pltpu.VMEM), pl.BlockSpec(memory_space=pltpu.HBM)
    return pl.pallas_call(
        prepare_kernel,
        out_shape=[
            jax.ShapeDtypeStruct((views, 2, size, size), F32),
            jax.ShapeDtypeStruct((views, 2, 8, LANES), jnp.int32),
        ],
        in_specs=[hbm, hbm],
        out_specs=[vmem, vmem],
        scratch_shapes=[
            pltpu.SMEM(offsets.shape, jnp.int32),
            pltpu.VMEM((2, 2 * size, size), F32),
            pltpu.SemaphoreType.DMA((3,)),
        ],
        compiler_params=pltpu.CompilerParams(vmem_limit_bytes=16 * 1024 * 1024),
        cost_estimate=pl.CostEstimate(flops=10**9, bytes_accessed=10**5, transcendentals=0),
    )(offsets, probe)


def views_kernel(chans, spots, counts, core, placed, intensity, *rest):
    count = len(chans)
    x_in, (a_in, b_in), rest = rest[:count], rest[count : count + 2], rest[count + 2 :]
    kb_in, ka_in = rest[:count], rest[count : 2 * count]
    right, left, *rest = rest[2 * count :]
    g_core, g_a, g_b = rest[:3]
    g_x, g_ka = rest[3 : 3 + count], rest[3 + count : 3 + 2 * count]
    g_kb = rest[3 + 2 * count : 3 + 3 * count]
    amplitude, cols_m, rows_m, corner_m, s1, y, s2, z, s3, u, s4, g = rest[3 + 3 * count :]
    views, size = placed.shape[0], core.shape[1]
    half, m = size // 2, MARGIN
    lower, partner = lower_partner(), b_partner()
    low_lanes = lane_ids() < LANES // 2
    zero = jnp.zeros((CHUNK, LANES), F32)

    def unpack(blocks):
        re = im = None
        for channel, block in zip(chans, blocks):
            mine = half_lanes(takes_right(channel))
            re = jnp.where(mine, block, 0.0 if re is None else re)
            im = jnp.where(mine, swap_halves(block), 0.0 if im is None else im)
        return (re, im) if blocks else (jnp.zeros((MARGIN, LANES), F32),) * 2

    for row in range(0, size, CHUNK):
        rows = slice(row, row + CHUNK)
        cols_m[0, rows], cols_m[1, rows] = unpack([ref[rows] for ref in x_in]) if chans else (zero, zero)
    corner_a = unpack([ref[...] for ref in ka_in])
    corner_b = [jnp.where(partner, part, 0.0) for part in unpack([ref[...] for ref in kb_in])]
    for part in range(2):
        a_rows, b_rows = a_in[part], jnp.where(partner, b_in[part], 0.0)
        rows_m[part, :m] = jnp.where(lower, a_rows, b_rows)
        rows_m[part, m:] = jnp.where(lower, b_rows, a_rows)
        corner_m[part, :m] = jnp.where(lower, corner_a[part], corner_b[part])
        corner_m[part, m:] = jnp.where(lower, corner_b[part], corner_a[part])

    def by_right(lhs, t):
        both = dot(lhs[...], right[t, :size])
        return both[:size] + both[size:] + dot(lhs[:size], right[t, size:])

    def by_left(t, rhs):
        both = dot(left[t], rhs[:size])
        return both[:size] + both[size:] + dot(left[t, :size], rhs[size:])

    def put(ref, row, col, value):
        high, low = split(value)
        rows, cols = value.shape
        ref[row : row + rows, col : col + cols] = high
        ref[size + row : size + row + rows, col : col + cols] = low

    def row_mask(view, row):
        ids = row + lax.broadcasted_iota(jnp.int32, (CHUNK, LANES), 0)
        if row < m:
            return ids < spots[view, 0, :1] - m, row
        if row >= size - m:
            return ids >= size - m + spots[view, 0, :1], row - size + 2 * m
        return None, None

    def col_mask(view, block):
        if block == 0:
            return lane_ids() < spots[view, 1, :1] - m
        return lane_ids() >= m + spots[view, 1, :1]

    def patch(view, row, block):
        cols = slice(block * LANES, (block + 1) * LANES)
        rows = slice(row, row + CHUNK)
        beside = col_mask(view, block)
        beyond, place = row_mask(view, row)
        found = []
        for part in range(2):
            value = jnp.where(beside, cols_m[part, rows], core[part, rows, cols])
            if beyond is not None:
                there = slice(place, place + CHUNK)
                outer = jnp.where(beside, corner_m[part, there], rows_m[part, there, cols])
                value = jnp.where(beyond, outer, value)
            found.append(value)
        return found

    def steps(view):
        for row in range(0, size, CHUNK):
            rows = slice(row, row + CHUNK)
            waves = []
            for block in range(2):
                cols = slice(block * LANES, (block + 1) * LANES)
                o_re, o_im = patch(view, row, block)
                p_re, p_im = placed[view, 0, rows, cols], placed[view, 1, rows, cols]
                waves.append((p_re * o_re - p_im * o_im, p_re * o_im + p_im * o_re))
            for part in range(2):
                put(s1.at[view, 0], row, part * half, waves[0][part] + waves[1][part])
                put(s1.at[view, 1], row, part * half, waves[0][part] - waves[1][part])
            yield
        for odd in range(2):
            y[view, odd] = by_right(s1.at[view, odd], odd)
            yield
        for odd in range(2):
            for row in range(0, half, CHUNK):
                for part in range(2):
                    cols = slice(part * half, (part + 1) * half)
                    above = y[view, odd, row : row + CHUNK, cols]
                    below = y[view, odd, half + row : half + row + CHUNK, cols]
                    put(s2.at[view, 0], part * half + row, odd * half, above + below)
                    put(s2.at[view, 1], part * half + row, odd * half, above - below)
                yield
        valid = (view < counts[0, 0]).astype(F32)
        for row in range(0, size, CHUNK):
            rows = slice(row, row + CHUNK)
            lanes = lax.broadcasted_iota(jnp.int32, (CHUNK, LANES), 1)
            wanted = []
            for block in range(2):
                power = intensity[0, 0, view, rows, block * LANES : (block + 1) * LANES] + smooth_eps
                wanted.append(power * lax.rsqrt(power) * valid)
            for odd in range(2):
                taken = lax.rem(2 * lanes + odd, LANES)
                ordered = [jnp.take_along_axis(block, taken, axis=1) for block in wanted]
                amplitude[view, odd, rows] = jnp.where(lanes < LANES // 2, *ordered)
        yield
        for odd in range(2):
            z[view, odd] = by_left(odd, s2.at[view, odd])
            yield
        for odd in range(2):
            for row in range(0, half, CHUNK):
                re, im = z[view, odd, row : row + CHUNK], z[view, odd, half + row : half + row + CHUNK]
                taken = pl.ds(2 * row + odd, CHUNK, stride=2)
                wanted = jnp.concatenate([amplitude[view, 0, taken], amplitude[view, 1, taken]], 1)
                scaling = valid - wanted * lax.rsqrt(re * re + im * im + smooth_eps)
                put(s3.at[view, odd], row, 0, re * scaling)
                put(s3.at[view, odd], half + row, 0, im * scaling)
                yield
        for odd in range(2):
            u[view, odd] = by_left(2 + odd, s3.at[view, odd])
            yield
        for row in range(0, half, CHUNK):
            for part in range(2):
                rows = slice(part * half + row, part * half + row + CHUNK)
                even_rows, odd_rows = u[view, 0, rows], u[view, 1, rows]
                for value, place in ((even_rows + odd_rows, row), (even_rows - odd_rows, half + row)):
                    put(s4.at[view, 0], place, part * half, value[:, :half])
                    put(s4.at[view, 1], place, part * half, value[:, half:])
                yield
        for odd in range(2):
            g[view, odd] = by_right(s4.at[view, odd], 2 + odd)
            yield

    work = [steps(view) for view in range(views)]
    for view in range(views):
        for _ in range(view * STAGGER):
            work[view] = itertools.chain([None], work[view])
    for _ in itertools.zip_longest(*work):
        pass

    for row in range(0, size, CHUNK):
        rows = slice(row, row + CHUNK)
        sums = {}

        def add(key, value):
            sums[key] = sums[key] + value if key in sums else value

        for view in range(views):
            beyond, place = row_mask(view, row)
            halves = []
            for part in range(2):
                cols = slice(part * half, (part + 1) * half)
                even_cols, odd_cols = g[view, 0, rows, cols], g[view, 1, rows, cols]
                halves.append((even_cols + odd_cols, even_cols - odd_cols))
            for block in range(2):
                cols = slice(block * LANES, (block + 1) * LANES)
                beside = col_mask(view, block)
                b_re, b_im = halves[0][block], halves[1][block]
                p_re, p_im = placed[view, 0, rows, cols], placed[view, 1, rows, cols]
                for part, value in enumerate((p_re * b_re + p_im * b_im, p_re * b_im - p_im * b_re)):
                    if beyond is not None:
                        outer, value = jnp.where(beyond, value, zero), jnp.where(beyond, zero, value)
                        add(("corner", part), jnp.where(beside, outer, zero))
                        add(("row", part, block), jnp.where(beside, zero, outer))
                    add(("col", part), jnp.where(beside, value, zero))
                    add(("core", part, block), jnp.where(beside, zero, value))
        for part in range(2):
            cols_m[part, rows] = sums["col", part]
            if place is not None:
                corner_m[part, place : place + CHUNK] = sums["corner", part]
            for block in range(2):
                cols = slice(block * LANES, (block + 1) * LANES)
                g_core[part, rows, cols] = sums["core", part, block]
                if place is not None:
                    rows_m[part, place : place + CHUNK, cols] = sums["row", part, block]

    def packed(channel, re, im):
        to_right = jnp.where(low_lanes, re, swap_halves(im))
        to_left = jnp.where(low_lanes, swap_halves(im), re)
        return jnp.where(sends_right(channel), to_right, to_left)

    for part in range(2):
        bottom, top = rows_m[part, :m], rows_m[part, m:]
        g_a[part] = jnp.where(lower, bottom, top)
        g_b[part] = jnp.where(lower, top, bottom)
    bottom = (corner_m[0, :m], corner_m[1, :m])
    top = (corner_m[0, m:], corner_m[1, m:])
    for number, channel in enumerate(chans):
        for row in range(0, size, CHUNK):
            rows = slice(row, row + CHUNK)
            g_x[number][rows] = packed(channel, cols_m[0, rows], cols_m[1, rows])
        below, above = packed(channel, *bottom), packed(channel, *top)
        g_ka[number][...] = jnp.where(lower, below, above)
        g_kb[number][...] = jnp.where(lower, above, below)


def views_call(chans, spots, counts, core, placed, intensity, tables, a_in, b_in, x_in, ka_in, kb_in):
    views, size = placed.shape[0], core.shape[1]
    count = len(chans)
    vmem = pl.BlockSpec(memory_space=pltpu.VMEM)
    shapes = [(2, size, size), (2, MARGIN, size), (2, MARGIN, size)]
    shapes += [(size, LANES)] * count + [(MARGIN, LANES)] * (2 * count)
    full = pltpu.VMEM((views, 2, size, size), F32)
    tall = pltpu.VMEM((views, 2, 2 * size, size), BF16)
    outs = pl.pallas_call(
        functools.partial(views_kernel, chans),
        out_shape=[jax.ShapeDtypeStruct(shape, F32) for shape in shapes],
        in_specs=[
            vmem,
            pl.BlockSpec(memory_space=pltpu.SMEM),
            *[vmem] * (7 + 3 * count),
        ],
        out_specs=[vmem] * len(shapes),
        scratch_shapes=[
            pltpu.VMEM((views, 2, size, size // 2), F32),
            pltpu.VMEM((2, size, LANES), F32),
            pltpu.VMEM((2, 2 * MARGIN, size), F32),
            pltpu.VMEM((2, 2 * MARGIN, LANES), F32),
            *[tall, full] * 4,
        ],
        compiler_params=pltpu.CompilerParams(vmem_limit_bytes=40 * 1024 * 1024),
    )(spots, counts, core, placed, intensity, *x_in, a_in, b_in, *kb_in, *ka_in, *tables)
    return (*outs[:3], outs[3 : 3 + count], outs[3 + count : 3 + 2 * count], outs[3 + 2 * count :])


def finish_kernel(chans, object_ref, g_core, *rest):
    count = len(chans)
    x_in, (a_in, b_in), rest = rest[:count], rest[count : count + 2], rest[count + 2 :]
    kb_in, ka_in, out = rest[:count], rest[count : 2 * count], rest[-1]
    size = object_ref.shape[1]
    lower = lower_partner()
    a_rows = pl.ds(pl.multiple_of(jnp.where(lower, size - MARGIN, 0), MARGIN), MARGIN)
    b_rows = pl.ds(pl.multiple_of(jnp.where(lower, 0, size - MARGIN), MARGIN), MARGIN)
    columns = []
    for channel in chans:
        right = takes_right(channel)
        mine = lane_ids() // (LANES // 2) == jnp.where(right, 1, 0)
        block = pl.multiple_of(jnp.where(right, size - LANES, 0), LANES)
        columns.append((mine, pl.ds(block, LANES)))

    def take(place, value):
        out[place] -= step_size * value

    def take_packed(rows, column, block):
        mine, lanes = column
        take((0, rows, lanes), jnp.where(mine, block, 0.0))
        take((1, rows, lanes), jnp.where(mine, swap_halves(block), 0.0))

    for part in range(2):
        out[part] = object_ref[part] - step_size * g_core[part]
        take((part, a_rows), a_in[part])
    for number, column in enumerate(columns):
        take_packed(slice(None), column, x_in[number][...])
        take_packed(a_rows, column, ka_in[number][...])

    @pl.when(b_partner())
    def _():
        for part in range(2):
            take((part, b_rows), b_in[part])
        for number, column in enumerate(columns):
            take_packed(b_rows, column, kb_in[number][...])


def finish_call(chans, object_field, g_core, a_in, b_in, x_in, ka_in, kb_in):
    vmem = pl.BlockSpec(memory_space=pltpu.VMEM)
    return pl.pallas_call(
        functools.partial(finish_kernel, chans),
        out_shape=jax.ShapeDtypeStruct(object_field.shape, F32),
        in_specs=[vmem] * (4 + 3 * len(chans)),
        out_specs=vmem,
        compiler_params=pltpu.CompilerParams(vmem_limit_bytes=6 * 1024 * 1024),
    )(object_field, g_core, *x_in, a_in, b_in, *kb_in, *ka_in)


def per_device(object_field, probe_field, intensity, view_offsets, view_counts):
    size = object_field.shape[1]
    mesh_rows, mesh_cols = lax.axis_size("row"), lax.axis_size("col")
    chans = channels(mesh_cols)
    tables = dft_tables(size)
    a_pairs, b_pairs = row_pairs(mesh_rows, 0), row_pairs(mesh_rows, 1)
    spare = spare_route(b_pairs, mesh_rows, mesh_cols)

    def over_rows(block, pairs, extra):
        route = [(i * mesh_cols + k, j * mesh_cols + k) for i, j in pairs for k in range(mesh_cols)]
        return lax.ppermute(block, ("row", "col"), route + extra)

    def across(block, pairs, extra, channel):
        route = [(i * mesh_cols + k, j * mesh_cols + l) for i, j in pairs for k, l in channel[0]]
        return lax.ppermute(block, ("row", "col"), route + (extra if mesh_cols == 2 else []))

    def exchange(a_send, b_send, x_send, ka_send, kb_send):
        x_in = [lax.ppermute(block, "col", channel[0]) for block, channel in zip(x_send, chans)]
        b_in = over_rows(b_send, b_pairs, spare)
        kb_in = [across(block, b_pairs, spare, channel) for block, channel in zip(kb_send, chans)]
        ka_in = [across(block, a_pairs, [], channel) for block, channel in zip(ka_send, chans)]
        a_in = over_rows(a_send, a_pairs, [])
        return a_in, b_in, x_in, ka_in, kb_in

    packs = pack_call(object_field, chans)
    offsets, probe = (
        pltpu.with_memory_space_constraint(array, pltpu.HBM)
        for array in (jnp.swapaxes(view_offsets, 2, 3), probe_field)
    )
    margins = exchange(packs[0], packs[1], packs[2::3], packs[3::3], packs[4::3])
    placed, spots = prepare_call(offsets, probe)
    g_core, *sends = views_call(
        chans, spots, view_counts, object_field, placed, intensity, tables, *margins
    )
    return finish_call(chans, object_field, g_core, *exchange(*sends))


def solution(mesh):
    in_specs = (
        P(None, "row", "col"),
        P(),
        P("row", "col", None, None, None),
        P("row", "col", None, None),
        P("row", "col"),
    )
    out_specs = P(None, "row", "col")
    return jax.shard_map(
        per_device, mesh=mesh, in_specs=in_specs, out_specs=out_specs, check_vma=False
    )
```

```python
import functools
import itertools
import math

import jax
import jax.numpy as jnp
import ml_dtypes
import numpy as np
from jax import lax
from jax.experimental import pallas as pl
from jax.experimental.pallas import tpu as pltpu
from jax.sharding import PartitionSpec as P

MARGIN = 64
LANES = 128
CHUNK = 64
STAGGER = 2

smooth_eps = 0.1
step_size = 0.2

F32 = jnp.float32
BF16 = jnp.bfloat16


def dft_tables(length):
    half = length // 2
    counter = np.arange(half)
    factor = 1.0 / math.sqrt(length)
    product = np.outer(counter, counter)
    even = np.exp(-2j * np.pi * (product % half) / half) * factor
    odd = np.exp(-2j * np.pi * ((2 * product + counter[:, None]) % length) / length) * factor

    def as_real(table):
        return np.block([[table.real, table.imag], [-table.imag, table.real]])

    def parts(table):
        high = table.astype(ml_dtypes.bfloat16)
        low = (table - high.astype(np.float64)).astype(ml_dtypes.bfloat16)
        return high, low

    even, odd = as_real(even), as_real(odd)
    by_right = [np.concatenate(parts(t), 0) for t in (even, odd, even.T, odd.T)]
    by_left = [np.concatenate(parts(t), 0) for t in (even.T, odd.T, even, odd)]
    return np.stack(by_right), np.stack(by_left)


def channels(mesh_cols):
    if mesh_cols == 1:
        return []
    if mesh_cols == 2:
        return [([(0, 1), (1, 0)], None, None)]
    forward = [(i, i + 1) for i in range(mesh_cols - 1)]
    return [(forward, True, False), ([(j, i) for i, j in forward], False, True)]


def row_pairs(count, first):
    pairs = [(i, i + 1) for i in range(first, count - 1, 2)]
    return pairs + [(j, i) for i, j in pairs]


def spare_route(pairs, mesh_rows, mesh_cols):
    rows = [i for i in range(mesh_rows) if i not in dict(pairs)]
    if mesh_cols % 2:
        return []
    return [(i * mesh_cols + k, i * mesh_cols + (k ^ 1)) for i in rows for k in range(mesh_cols)]


def b_partner():
    row = lax.axis_index("row")
    return jnp.where(lower_partner(), row > 0, row < lax.axis_size("row") - 1)


def sends_right(channel):
    return lax.axis_index("col") == 0 if channel[1] is None else channel[1]


def takes_right(channel):
    return lax.axis_index("col") == 0 if channel[2] is None else channel[2]


def lower_partner():
    return lax.rem(lax.axis_index("row"), 2) == 0


def lane_ids():
    return lax.broadcasted_iota(jnp.int32, (1, LANES), 1)


def half_lanes(right):
    low = lane_ids() < LANES // 2
    if isinstance(right, bool):
        return low if right else ~low
    return lane_ids() // (LANES // 2) == jnp.where(right, 0, 1)


def split(value):
    high = value.astype(BF16)
    return high, (value - high.astype(F32)).astype(BF16)


def dot(first, second):
    return jnp.dot(first, second, preferred_element_type=F32)


def swap_halves(block):
    return pltpu.roll(block, LANES // 2, 1)


def fetch(pairs, sems):
    copies = [pltpu.make_async_copy(source, target, sems.at[i]) for i, (source, target) in enumerate(pairs)]
    for copy in copies:
        copy.start()
    return copies


def pack_kernel(chans, object_ref, a_ref, b_ref, *edge_refs):
    size = object_ref.shape[1]
    top, bottom = pl.ds(0, MARGIN), pl.ds(size - MARGIN, MARGIN)
    lower = lower_partner()
    for part in range(2):
        head, tail = object_ref[part, top, :], object_ref[part, bottom, :]
        a_ref[part] = jnp.where(lower, tail, head)
        b_ref[part] = jnp.where(lower, head, tail)
    for number, channel in enumerate(chans):
        right = sends_right(channel)
        x_ref, kb_ref = edge_refs[2 * number : 2 * number + 2]
        low = lane_ids() < LANES // 2
        for start in range(0, size, CHUNK):
            rows = slice(start, start + CHUNK)
            left_edge = jnp.where(
                low, object_ref[0, rows, :LANES], swap_halves(object_ref[1, rows, :LANES])
            )
            right_edge = jnp.where(
                low,
                swap_halves(object_ref[1, rows, size - LANES :]),
                object_ref[0, rows, size - LANES :],
            )
            x_ref[rows] = jnp.where(right, right_edge, left_edge)
        kb_ref[...] = jnp.where(lower, x_ref[:MARGIN], x_ref[size - MARGIN :])


def pack_call(object_field, chans):
    size = object_field.shape[1]
    shapes = [(2, MARGIN, size)] * 2 + [(size, LANES), (MARGIN, LANES)] * len(chans)
    vmem = pl.BlockSpec(memory_space=pltpu.VMEM)
    return pl.pallas_call(
        functools.partial(pack_kernel, chans),
        out_shape=[jax.ShapeDtypeStruct(shape, F32) for shape in shapes],
        in_specs=[vmem],
        out_specs=[vmem] * len(shapes),
        compiler_params=pltpu.CompilerParams(vmem_limit_bytes=4 * 1024 * 1024),
    )(object_field)


def prepare_kernel(offsets_in, probe, placed, spots, offsets, doubled, sems):
    views, size = placed.shape[0], probe.shape[1]
    copies = fetch(
        [(offsets_in, offsets)]
        + [(probe.at[part], doubled.at[part, pl.ds(0, size)]) for part in range(2)],
        sems,
    )
    sublane = lax.broadcasted_iota(jnp.int32, (1, 8, 1), 1)
    copies[0].wait()
    for part in range(2):
        copies[1 + part].wait()
        doubled[part, size:] = doubled[part, :size]
        for view in range(views):
            shift_row = lax.rem(offsets[0, 0, 0, view] - MARGIN + size, size)
            shift_col = lax.rem(offsets[0, 0, 1, view] - MARGIN + size, size)
            start = lax.rem(size - shift_row, size)
            whole = pl.multiple_of((start // 8) * 8, 8)
            rest = start - whole
            for row in range(0, size, CHUNK):
                block = doubled[part, pl.ds(whole + row, CHUNK + 8), :]
                block = pltpu.roll(block, shift_col, 1).reshape(CHUNK // 8 + 1, 8, size)
                block = pltpu.roll(block, lax.rem(8 - rest, 8), 1)
                block = jnp.where(sublane < 8 - rest, block[:-1], block[1:])
                placed[view, part, row : row + CHUNK] = block.reshape(CHUNK, size)
    for view in range(views):
        for axis in range(2):
            spots[view, axis] = jnp.full(spots.shape[2:], offsets[0, 0, axis, view], jnp.int32)


def prepare_call(offsets, probe):
    views, size = offsets.shape[3], probe.shape[1]
    vmem, hbm = pl.BlockSpec(memory_space=pltpu.VMEM), pl.BlockSpec(memory_space=pltpu.HBM)
    return pl.pallas_call(
        prepare_kernel,
        out_shape=[
            jax.ShapeDtypeStruct((views, 2, size, size), F32),
            jax.ShapeDtypeStruct((views, 2, 8, LANES), jnp.int32),
        ],
        in_specs=[hbm, hbm],
        out_specs=[vmem, vmem],
        scratch_shapes=[
            pltpu.SMEM(offsets.shape, jnp.int32),
            pltpu.VMEM((2, 2 * size, size), F32),
            pltpu.SemaphoreType.DMA((3,)),
        ],
        compiler_params=pltpu.CompilerParams(vmem_limit_bytes=16 * 1024 * 1024),
        cost_estimate=pl.CostEstimate(flops=10**9, bytes_accessed=10**5, transcendentals=0),
    )(offsets, probe)


def edge_kernel(block, spots, out):
    out[...] = jnp.where(lower_partner(), block[block.shape[0] - MARGIN :], block[:MARGIN])


def edge_call(block, spots):
    vmem = pl.BlockSpec(memory_space=pltpu.VMEM)
    return pl.pallas_call(
        edge_kernel,
        out_shape=jax.ShapeDtypeStruct((MARGIN, LANES), F32),
        in_specs=[vmem, vmem],
        out_specs=vmem,
        compiler_params=pltpu.CompilerParams(vmem_limit_bytes=2 * 1024 * 1024),
    )(block, spots)


def views_kernel(chans, spots, counts, core, placed, intensity, *rest):
    count = len(chans)
    x_in, (a_in, b_in), rest = rest[:count], rest[count : count + 2], rest[count + 2 :]
    kb_in, ka_in = rest[:count], rest[count : 2 * count]
    right, left, *rest = rest[2 * count :]
    g_core, g_a, g_b = rest[:3]
    g_x, g_ka = rest[3 : 3 + count], rest[3 + count : 3 + 2 * count]
    g_kb = rest[3 + 2 * count : 3 + 3 * count]
    amplitude, cols_m, rows_m, corner_m, s1, y, s2, z, s3, u, s4, g = rest[3 + 3 * count :]
    views, size = placed.shape[0], core.shape[1]
    half, m = size // 2, MARGIN
    lower, partner = lower_partner(), b_partner()
    low_lanes = lane_ids() < LANES // 2
    zero = jnp.zeros((CHUNK, LANES), F32)

    def unpack(blocks):
        re = im = None
        for channel, block in zip(chans, blocks):
            mine = half_lanes(takes_right(channel))
            re = jnp.where(mine, block, 0.0 if re is None else re)
            im = jnp.where(mine, swap_halves(block), 0.0 if im is None else im)
        return (re, im) if blocks else (jnp.zeros((MARGIN, LANES), F32),) * 2

    for row in range(0, size, CHUNK):
        rows = slice(row, row + CHUNK)
        cols_m[0, rows], cols_m[1, rows] = unpack([ref[rows] for ref in x_in]) if chans else (zero, zero)
    corner_a = unpack([ref[...] for ref in ka_in])
    corner_b = [jnp.where(partner, part, 0.0) for part in unpack([ref[...] for ref in kb_in])]
    for part in range(2):
        a_rows, b_rows = a_in[part], jnp.where(partner, b_in[part], 0.0)
        rows_m[part, :m] = jnp.where(lower, a_rows, b_rows)
        rows_m[part, m:] = jnp.where(lower, b_rows, a_rows)
        corner_m[part, :m] = jnp.where(lower, corner_a[part], corner_b[part])
        corner_m[part, m:] = jnp.where(lower, corner_b[part], corner_a[part])

    def by_right(lhs, t):
        both = dot(lhs[...], right[t, :size])
        return both[:size] + both[size:] + dot(lhs[:size], right[t, size:])

    def by_left(t, rhs):
        both = dot(left[t], rhs[:size])
        return both[:size] + both[size:] + dot(left[t, :size], rhs[size:])

    def put(ref, row, col, value):
        high, low = split(value)
        rows, cols = value.shape
        ref[row : row + rows, col : col + cols] = high
        ref[size + row : size + row + rows, col : col + cols] = low

    def row_mask(view, row):
        ids = row + lax.broadcasted_iota(jnp.int32, (CHUNK, LANES), 0)
        if row < m:
            return ids < spots[view, 0, :1] - m, row
        if row >= size - m:
            return ids >= size - m + spots[view, 0, :1], row - size + 2 * m
        return None, None

    def col_mask(view, block):
        if block == 0:
            return lane_ids() < spots[view, 1, :1] - m
        return lane_ids() >= m + spots[view, 1, :1]

    def patch(view, row, block):
        cols = slice(block * LANES, (block + 1) * LANES)
        rows = slice(row, row + CHUNK)
        beside = col_mask(view, block)
        beyond, place = row_mask(view, row)
        found = []
        for part in range(2):
            value = jnp.where(beside, cols_m[part, rows], core[part, rows, cols])
            if beyond is not None:
                there = slice(place, place + CHUNK)
                outer = jnp.where(beside, corner_m[part, there], rows_m[part, there, cols])
                value = jnp.where(beyond, outer, value)
            found.append(value)
        return found

    def steps(view):
        for row in range(0, size, CHUNK):
            rows = slice(row, row + CHUNK)
            waves = []
            for block in range(2):
                cols = slice(block * LANES, (block + 1) * LANES)
                o_re, o_im = patch(view, row, block)
                p_re, p_im = placed[view, 0, rows, cols], placed[view, 1, rows, cols]
                waves.append((p_re * o_re - p_im * o_im, p_re * o_im + p_im * o_re))
            for part in range(2):
                put(s1.at[view, 0], row, part * half, waves[0][part] + waves[1][part])
                put(s1.at[view, 1], row, part * half, waves[0][part] - waves[1][part])
            yield
        for odd in range(2):
            y[view, odd] = by_right(s1.at[view, odd], odd)
            yield
        for odd in range(2):
            for row in range(0, half, CHUNK):
                for part in range(2):
                    cols = slice(part * half, (part + 1) * half)
                    above = y[view, odd, row : row + CHUNK, cols]
                    below = y[view, odd, half + row : half + row + CHUNK, cols]
                    put(s2.at[view, 0], part * half + row, odd * half, above + below)
                    put(s2.at[view, 1], part * half + row, odd * half, above - below)
                yield
        valid = (view < counts[0, 0]).astype(F32)
        for row in range(0, size, CHUNK):
            rows = slice(row, row + CHUNK)
            lanes = lax.broadcasted_iota(jnp.int32, (CHUNK, LANES), 1)
            wanted = []
            for block in range(2):
                power = intensity[0, 0, view, rows, block * LANES : (block + 1) * LANES] + smooth_eps
                wanted.append(power * lax.rsqrt(power) * valid)
            for odd in range(2):
                taken = lax.rem(2 * lanes + odd, LANES)
                ordered = [jnp.take_along_axis(block, taken, axis=1) for block in wanted]
                amplitude[view, odd, rows] = jnp.where(lanes < LANES // 2, *ordered)
        yield
        for odd in range(2):
            z[view, odd] = by_left(odd, s2.at[view, odd])
            yield
        for odd in range(2):
            for row in range(0, half, CHUNK):
                re, im = z[view, odd, row : row + CHUNK], z[view, odd, half + row : half + row + CHUNK]
                taken = pl.ds(2 * row + odd, CHUNK, stride=2)
                wanted = jnp.concatenate([amplitude[view, 0, taken], amplitude[view, 1, taken]], 1)
                scaling = valid - wanted * lax.rsqrt(re * re + im * im + smooth_eps)
                put(s3.at[view, odd], row, 0, re * scaling)
                put(s3.at[view, odd], half + row, 0, im * scaling)
                yield
        for odd in range(2):
            u[view, odd] = by_left(2 + odd, s3.at[view, odd])
            yield
        for row in range(0, half, CHUNK):
            for part in range(2):
                rows = slice(part * half + row, part * half + row + CHUNK)
                even_rows, odd_rows = u[view, 0, rows], u[view, 1, rows]
                for value, place in ((even_rows + odd_rows, row), (even_rows - odd_rows, half + row)):
                    put(s4.at[view, 0], place, part * half, value[:, :half])
                    put(s4.at[view, 1], place, part * half, value[:, half:])
                yield
        for odd in range(2):
            g[view, odd] = by_right(s4.at[view, odd], 2 + odd)
            yield

    work = [steps(view) for view in range(views)]
    for view in range(views):
        for _ in range(view * STAGGER):
            work[view] = itertools.chain([None], work[view])
    for _ in itertools.zip_longest(*work):
        pass

    for row in range(0, size, CHUNK):
        rows = slice(row, row + CHUNK)
        sums = {}

        def add(key, value):
            sums[key] = sums[key] + value if key in sums else value

        for view in range(views):
            beyond, place = row_mask(view, row)
            halves = []
            for part in range(2):
                cols = slice(part * half, (part + 1) * half)
                even_cols, odd_cols = g[view, 0, rows, cols], g[view, 1, rows, cols]
                halves.append((even_cols + odd_cols, even_cols - odd_cols))
            for block in range(2):
                cols = slice(block * LANES, (block + 1) * LANES)
                beside = col_mask(view, block)
                b_re, b_im = halves[0][block], halves[1][block]
                p_re, p_im = placed[view, 0, rows, cols], placed[view, 1, rows, cols]
                for part, value in enumerate((p_re * b_re + p_im * b_im, p_re * b_im - p_im * b_re)):
                    if beyond is not None:
                        outer, value = jnp.where(beyond, value, zero), jnp.where(beyond, zero, value)
                        add(("corner", part), jnp.where(beside, outer, zero))
                        add(("row", part, block), jnp.where(beside, zero, outer))
                    add(("col", part), jnp.where(beside, value, zero))
                    add(("core", part, block), jnp.where(beside, zero, value))
        for part in range(2):
            cols_m[part, rows] = sums["col", part]
            if place is not None:
                corner_m[part, place : place + CHUNK] = sums["corner", part]
            for block in range(2):
                cols = slice(block * LANES, (block + 1) * LANES)
                g_core[part, rows, cols] = sums["core", part, block]
                if place is not None:
                    rows_m[part, place : place + CHUNK, cols] = sums["row", part, block]

    def packed(channel, re, im):
        to_right = jnp.where(low_lanes, re, swap_halves(im))
        to_left = jnp.where(low_lanes, swap_halves(im), re)
        return jnp.where(sends_right(channel), to_right, to_left)

    for part in range(2):
        bottom, top = rows_m[part, :m], rows_m[part, m:]
        g_a[part] = jnp.where(lower, bottom, top)
        g_b[part] = jnp.where(lower, top, bottom)
    bottom = (corner_m[0, :m], corner_m[1, :m])
    top = (corner_m[0, m:], corner_m[1, m:])
    for number, channel in enumerate(chans):
        for row in range(0, size, CHUNK):
            rows = slice(row, row + CHUNK)
            g_x[number][rows] = packed(channel, cols_m[0, rows], cols_m[1, rows])
        below, above = packed(channel, *bottom), packed(channel, *top)
        g_ka[number][...] = jnp.where(lower, below, above)
        g_kb[number][...] = jnp.where(lower, above, below)


def views_call(chans, spots, counts, core, placed, intensity, tables, a_in, b_in, x_in, ka_in, kb_in):
    views, size = placed.shape[0], core.shape[1]
    count = len(chans)
    vmem = pl.BlockSpec(memory_space=pltpu.VMEM)
    shapes = [(2, size, size), (2, MARGIN, size), (2, MARGIN, size)]
    shapes += [(size, LANES)] * count + [(MARGIN, LANES)] * (2 * count)
    full = pltpu.VMEM((views, 2, size, size), F32)
    tall = pltpu.VMEM((views, 2, 2 * size, size), BF16)
    outs = pl.pallas_call(
        functools.partial(views_kernel, chans),
        out_shape=[jax.ShapeDtypeStruct(shape, F32) for shape in shapes],
        in_specs=[
            vmem,
            pl.BlockSpec(memory_space=pltpu.SMEM),
            *[vmem] * (7 + 3 * count),
        ],
        out_specs=[vmem] * len(shapes),
        scratch_shapes=[
            pltpu.VMEM((views, 2, size, size // 2), F32),
            pltpu.VMEM((2, size, LANES), F32),
            pltpu.VMEM((2, 2 * MARGIN, size), F32),
            pltpu.VMEM((2, 2 * MARGIN, LANES), F32),
            *[tall, full] * 4,
        ],
        compiler_params=pltpu.CompilerParams(vmem_limit_bytes=40 * 1024 * 1024),
    )(spots, counts, core, placed, intensity, *x_in, a_in, b_in, *kb_in, *ka_in, *tables)
    return (*outs[:3], outs[3 : 3 + count], outs[3 + count : 3 + 2 * count], outs[3 + 2 * count :])


def finish_kernel(chans, object_ref, g_core, *rest):
    count = len(chans)
    x_in, (a_in, b_in), rest = rest[:count], rest[count : count + 2], rest[count + 2 :]
    kb_in, ka_in, out = rest[:count], rest[count : 2 * count], rest[-1]
    size = object_ref.shape[1]
    lower = lower_partner()
    a_rows = pl.ds(pl.multiple_of(jnp.where(lower, size - MARGIN, 0), MARGIN), MARGIN)
    b_rows = pl.ds(pl.multiple_of(jnp.where(lower, 0, size - MARGIN), MARGIN), MARGIN)
    columns = []
    for channel in chans:
        right = takes_right(channel)
        mine = lane_ids() // (LANES // 2) == jnp.where(right, 1, 0)
        block = pl.multiple_of(jnp.where(right, size - LANES, 0), LANES)
        columns.append((mine, pl.ds(block, LANES)))

    def take(place, value):
        out[place] -= step_size * value

    def take_packed(rows, column, block):
        mine, lanes = column
        take((0, rows, lanes), jnp.where(mine, block, 0.0))
        take((1, rows, lanes), jnp.where(mine, swap_halves(block), 0.0))

    for part in range(2):
        out[part] = object_ref[part] - step_size * g_core[part]
        take((part, a_rows), a_in[part])
    for number, column in enumerate(columns):
        take_packed(slice(None), column, x_in[number][...])
        take_packed(a_rows, column, ka_in[number][...])

    @pl.when(b_partner())
    def _():
        for part in range(2):
            take((part, b_rows), b_in[part])
        for number, column in enumerate(columns):
            take_packed(b_rows, column, kb_in[number][...])


def finish_call(chans, object_field, g_core, a_in, b_in, x_in, ka_in, kb_in):
    vmem = pl.BlockSpec(memory_space=pltpu.VMEM)
    return pl.pallas_call(
        functools.partial(finish_kernel, chans),
        out_shape=jax.ShapeDtypeStruct(object_field.shape, F32),
        in_specs=[vmem] * (4 + 3 * len(chans)),
        out_specs=vmem,
        compiler_params=pltpu.CompilerParams(vmem_limit_bytes=6 * 1024 * 1024),
    )(object_field, g_core, *x_in, a_in, b_in, *kb_in, *ka_in)


def per_device(object_field, probe_field, intensity, view_offsets, view_counts):
    size = object_field.shape[1]
    mesh_rows, mesh_cols = lax.axis_size("row"), lax.axis_size("col")
    chans = channels(mesh_cols)
    tables = dft_tables(size)
    a_pairs, b_pairs = row_pairs(mesh_rows, 0), row_pairs(mesh_rows, 1)
    spare = spare_route(b_pairs, mesh_rows, mesh_cols)

    def over_rows(block, pairs, extra):
        route = [(i * mesh_cols + k, j * mesh_cols + k) for i, j in pairs for k in range(mesh_cols)]
        return lax.ppermute(block, ("row", "col"), route + extra)

    def across(block, pairs, extra, channel):
        route = [(i * mesh_cols + k, j * mesh_cols + l) for i, j in pairs for k, l in channel[0]]
        return lax.ppermute(block, ("row", "col"), route + (extra if mesh_cols == 2 else []))

    def exchange(a_send, b_send, x_send, kb_send):
        x_in = [lax.ppermute(block, "col", channel[0]) for block, channel in zip(x_send, chans)]
        a_in = over_rows(a_send, a_pairs, [])
        b_in = over_rows(b_send, b_pairs, spare)
        kb_in = [across(block, b_pairs, spare, channel) for block, channel in zip(kb_send, chans)]
        return a_in, b_in, x_in, kb_in

    packs = pack_call(object_field, chans)
    a_in, b_in, x_in, kb_in = exchange(packs[0], packs[1], packs[2::2], packs[3::2])
    offsets, probe = (
        pltpu.with_memory_space_constraint(array, pltpu.HBM)
        for array in (jnp.swapaxes(view_offsets, 2, 3), probe_field)
    )
    placed, spots = prepare_call(offsets, probe)
    ka_in = [over_rows(edge_call(block, spots), a_pairs, []) for block in x_in]
    g_core, g_a, g_b, g_x, g_ka, g_kb = views_call(
        chans, spots, view_counts, object_field, placed, intensity, tables,
        a_in, b_in, x_in, ka_in, kb_in,
    )
    a_in, b_in, x_in, kb_in = exchange(g_a, g_b, g_x, g_kb)
    ka_in = [across(block, a_pairs, [], channel) for block, channel in zip(g_ka, chans)]
    return finish_call(chans, object_field, g_core, a_in, b_in, x_in, ka_in, kb_in)


def solution(mesh):
    in_specs = (
        P(None, "row", "col"),
        P(),
        P("row", "col", None, None, None),
        P("row", "col", None, None),
        P("row", "col"),
    )
    out_specs = P(None, "row", "col")
    return jax.shard_map(
        per_device, mesh=mesh, in_specs=in_specs, out_specs=out_specs, check_vma=False
    )
```

```python
import functools
import itertools
import math

import jax
import jax.numpy as jnp
import ml_dtypes
import numpy as np
from jax import lax
from jax.experimental import pallas as pl
from jax.experimental.pallas import tpu as pltpu
from jax.sharding import PartitionSpec as P

MARGIN = 64
LANES = 128
CHUNK = MARGIN
STAGGER = 2

smooth_eps = 0.1
step_size = 0.2

F32 = jnp.float32
BF16 = jnp.bfloat16


def dft_tables(length):
    half = length // 2
    counter = np.arange(half)
    factor = 1.0 / math.sqrt(length)
    product = np.outer(counter, counter)
    even = np.exp(-2j * np.pi * (product % half) / half) * factor
    odd = np.exp(-2j * np.pi * ((2 * product + counter[:, None]) % length) / length) * factor

    def as_real(table):
        return np.block([[table.real, table.imag], [-table.imag, table.real]])

    def parts(table):
        high = table.astype(ml_dtypes.bfloat16)
        low = (table - high.astype(np.float64)).astype(ml_dtypes.bfloat16)
        return high, low

    even, odd = as_real(even), as_real(odd)
    by_right = [np.concatenate(parts(t), 0) for t in (even, odd, even.T, odd.T)]
    by_left = [np.concatenate(parts(t), 0) for t in (even.T, odd.T, even, odd)]
    return np.stack(by_right), np.stack(by_left)


def channels(mesh_cols):
    if mesh_cols == 1:
        return []
    if mesh_cols == 2:
        return [([(0, 1), (1, 0)], None, None)]
    forward = [(i, i + 1) for i in range(mesh_cols - 1)]
    return [(forward, True, False), ([(j, i) for i, j in forward], False, True)]


def row_pairs(count, first):
    pairs = [(i, i + 1) for i in range(first, count - 1, 2)]
    return pairs + [(j, i) for i, j in pairs]


def spare_route(pairs, mesh_rows, mesh_cols):
    rows = [i for i in range(mesh_rows) if i not in dict(pairs)]
    if mesh_cols % 2:
        return []
    return [(i * mesh_cols + k, i * mesh_cols + (k ^ 1)) for i in rows for k in range(mesh_cols)]


def b_partner():
    row = lax.axis_index("row")
    return jnp.where(lower_partner(), row > 0, row < lax.axis_size("row") - 1)


def sends_right(channel):
    return lax.axis_index("col") == 0 if channel[1] is None else channel[1]


def takes_right(channel):
    return lax.axis_index("col") == 0 if channel[2] is None else channel[2]


def lower_partner():
    return lax.rem(lax.axis_index("row"), 2) == 0


def lane_ids():
    return lax.broadcasted_iota(jnp.int32, (1, LANES), 1)


def half_lanes(right):
    low = lane_ids() < LANES // 2
    if isinstance(right, bool):
        return low if right else ~low
    return lane_ids() // (LANES // 2) == jnp.where(right, 0, 1)


def split(value):
    high = value.astype(BF16)
    return high, (value - high.astype(F32)).astype(BF16)


def dot(first, second):
    return jnp.dot(first, second, preferred_element_type=F32)


def swap_halves(block):
    return pltpu.roll(block, LANES // 2, 1)


def fetch(pairs, sems):
    copies = [pltpu.make_async_copy(source, target, sems.at[i]) for i, (source, target) in enumerate(pairs)]
    for copy in copies:
        copy.start()
    return copies


def pack_kernel(chans, object_ref, a_ref, b_ref, *edge_refs):
    size = object_ref.shape[1]
    top, bottom = pl.ds(0, MARGIN), pl.ds(size - MARGIN, MARGIN)
    lower = lower_partner()
    for part in range(2):
        head, tail = object_ref[part, top, :], object_ref[part, bottom, :]
        a_ref[part] = jnp.where(lower, tail, head)
        b_ref[part] = jnp.where(lower, head, tail)
    for number, channel in enumerate(chans):
        right = sends_right(channel)
        x_ref, kb_ref = edge_refs[2 * number : 2 * number + 2]
        low = lane_ids() < LANES // 2
        for start in range(0, size, CHUNK):
            rows = slice(start, start + CHUNK)
            left_edge = jnp.where(
                low, object_ref[0, rows, :LANES], swap_halves(object_ref[1, rows, :LANES])
            )
            right_edge = jnp.where(
                low,
                swap_halves(object_ref[1, rows, size - LANES :]),
                object_ref[0, rows, size - LANES :],
            )
            x_ref[rows] = jnp.where(right, right_edge, left_edge)
        kb_ref[...] = jnp.where(lower, x_ref[:MARGIN], x_ref[size - MARGIN :])


def pack_call(object_field, chans):
    size = object_field.shape[1]
    shapes = [(2, MARGIN, size)] * 2 + [(size, LANES), (MARGIN, LANES)] * len(chans)
    vmem = pl.BlockSpec(memory_space=pltpu.VMEM)
    return pl.pallas_call(
        functools.partial(pack_kernel, chans),
        out_shape=[jax.ShapeDtypeStruct(shape, F32) for shape in shapes],
        in_specs=[vmem],
        out_specs=[vmem] * len(shapes),
        compiler_params=pltpu.CompilerParams(vmem_limit_bytes=4 * 1024 * 1024),
    )(object_field)


def prepare_kernel(offsets_in, probe, placed, spots, offsets, doubled, sems):
    views, size = placed.shape[0], probe.shape[1]
    copies = fetch(
        [(offsets_in, offsets)]
        + [(probe.at[part], doubled.at[part, pl.ds(0, size)]) for part in range(2)],
        sems,
    )
    sublane = lax.broadcasted_iota(jnp.int32, (1, 8, 1), 1)
    copies[0].wait()
    for part in range(2):
        copies[1 + part].wait()
        doubled[part, size:] = doubled[part, :size]
        for view in range(views):
            shift_row = lax.rem(offsets[0, 0, 0, view] - MARGIN + size, size)
            shift_col = lax.rem(offsets[0, 0, 1, view] - MARGIN + size, size)
            start = lax.rem(size - shift_row, size)
            whole = pl.multiple_of((start // 8) * 8, 8)
            rest = start - whole
            for row in range(0, size, CHUNK):
                block = doubled[part, pl.ds(whole + row, CHUNK + 8), :]
                block = pltpu.roll(block, shift_col, 1).reshape(CHUNK // 8 + 1, 8, size)
                block = pltpu.roll(block, lax.rem(8 - rest, 8), 1)
                block = jnp.where(sublane < 8 - rest, block[:-1], block[1:])
                placed[view, part, row : row + CHUNK] = block.reshape(CHUNK, size)
    for view in range(views):
        for axis in range(2):
            spots[view, axis] = jnp.full(spots.shape[2:], offsets[0, 0, axis, view], jnp.int32)


def prepare_call(offsets, probe):
    views, size = offsets.shape[3], probe.shape[1]
    vmem, hbm = pl.BlockSpec(memory_space=pltpu.VMEM), pl.BlockSpec(memory_space=pltpu.HBM)
    return pl.pallas_call(
        prepare_kernel,
        out_shape=[
            jax.ShapeDtypeStruct((views, 2, size, size), F32),
            jax.ShapeDtypeStruct((views, 2, 8, LANES), jnp.int32),
        ],
        in_specs=[hbm, hbm],
        out_specs=[vmem, vmem],
        scratch_shapes=[
            pltpu.SMEM(offsets.shape, jnp.int32),
            pltpu.VMEM((2, 2 * size, size), F32),
            pltpu.SemaphoreType.DMA((3,)),
        ],
        compiler_params=pltpu.CompilerParams(vmem_limit_bytes=16 * 1024 * 1024),
        cost_estimate=pl.CostEstimate(flops=10**9, bytes_accessed=10**5, transcendentals=0),
    )(offsets, probe)


def edge_kernel(block, spots, out):
    out[...] = jnp.where(lower_partner(), block[block.shape[0] - MARGIN :], block[:MARGIN])


def edge_call(block, spots):
    vmem = pl.BlockSpec(memory_space=pltpu.VMEM)
    return pl.pallas_call(
        edge_kernel,
        out_shape=jax.ShapeDtypeStruct((MARGIN, LANES), F32),
        in_specs=[vmem, vmem],
        out_specs=vmem,
        compiler_params=pltpu.CompilerParams(vmem_limit_bytes=2 * 1024 * 1024),
    )(block, spots)


def unpack(chans, blocks):
    re = im = jnp.zeros((MARGIN, LANES), F32)
    for channel, block in zip(chans, blocks):
        mine = half_lanes(takes_right(channel))
        re, im = jnp.where(mine, block, re), jnp.where(mine, swap_halves(block), im)
    return re, im


def col_mask(spots, view, block):
    if block == 0:
        return lane_ids() < spots[view, 1, :1] - MARGIN
    return lane_ids() >= MARGIN + spots[view, 1, :1]


def put(ref, row, col, value):
    high, low = split(value)
    count, (rows, cols) = ref.shape[0] // 2, value.shape
    ref[row : row + rows, col : col + cols] = high
    ref[count + row : count + row + rows, col : col + cols] = low


def by_right(lhs, right, t):
    count, size = lhs.shape[0] // 2, lhs.shape[1]
    both = dot(lhs[...], right[t, :size])
    return both[:count] + both[count:] + dot(lhs[:count], right[t, size:])


def put_waves(ref, placed, view, row, place, patch):
    rows = slice(row, row + CHUNK)
    waves = []
    for block in range(2):
        cols = slice(block * LANES, (block + 1) * LANES)
        o_re, o_im = patch(view, row, block)
        p_re, p_im = placed[view, 0, rows, cols], placed[view, 1, rows, cols]
        waves.append((p_re * o_re - p_im * o_im, p_re * o_im + p_im * o_re))
    for part in range(2):
        put(ref.at[0], place, part * LANES, waves[0][part] + waves[1][part])
        put(ref.at[1], place, part * LANES, waves[0][part] - waves[1][part])


def early_kernel(chans, spots, core, placed, right, _, *rest):
    x_in, out, cols_m, s1 = rest[: len(chans)], *rest[len(chans) :]
    views, size = placed.shape[0], core.shape[1]

    def patch(view, row, block):
        cols, rows = slice(block * LANES, (block + 1) * LANES), slice(row, row + CHUNK)
        beside = col_mask(spots, view, block)
        return [jnp.where(beside, cols_m[p, rows], core[p, rows, cols]) for p in range(2)]

    for row in range(CHUNK, size - CHUNK, CHUNK):
        rows = slice(row, row + CHUNK)
        cols_m[0, rows], cols_m[1, rows] = unpack(chans, [ref[rows] for ref in x_in])
    for view in range(views):
        for row in range(CHUNK, size - CHUNK, CHUNK):
            put_waves(s1.at[view], placed, view, row, row - CHUNK, patch)
        for odd in range(2):
            out[view, odd] = by_right(s1.at[view, odd], right, odd)


def early_call(chans, spots, core, placed, right, edge, x_in):
    views, size = placed.shape[0], core.shape[1]
    vmem = pl.BlockSpec(memory_space=pltpu.VMEM)
    return pl.pallas_call(
        functools.partial(early_kernel, chans),
        out_shape=jax.ShapeDtypeStruct((views, 2, size - 2 * CHUNK, size), F32),
        in_specs=[vmem] * (5 + len(chans)),
        out_specs=vmem,
        scratch_shapes=[
            pltpu.VMEM((2, size, LANES), F32),
            pltpu.VMEM((views, 2, 2 * (size - 2 * CHUNK), size), BF16),
        ],
        compiler_params=pltpu.CompilerParams(vmem_limit_bytes=8 * 1024 * 1024),
        cost_estimate=pl.CostEstimate(flops=10**8, bytes_accessed=10**4, transcendentals=0),
    )(spots, core, placed, right, edge, *x_in)


def views_kernel(chans, spots, counts, core, placed, inner, intensity, *rest):
    count = len(chans)
    x_in, (a_in, b_in), rest = rest[:count], rest[count : count + 2], rest[count + 2 :]
    kb_in, ka_in = rest[:count], rest[count : 2 * count]
    right, left, *rest = rest[2 * count :]
    g_core, g_a, g_b = rest[:3]
    g_x, g_ka = rest[3 : 3 + count], rest[3 + count : 3 + 2 * count]
    g_kb = rest[3 + 2 * count : 3 + 3 * count]
    amplitude, cols_m, rows_m, corner_m, s1, y, s2, z, s3, u, s4, g = rest[3 + 3 * count :]
    views, size = placed.shape[0], core.shape[1]
    half, m = size // 2, MARGIN
    lower, partner = lower_partner(), b_partner()
    low_lanes = lane_ids() < LANES // 2
    zero = jnp.zeros((CHUNK, LANES), F32)

    for row in (0, size - CHUNK):
        rows = slice(row, row + CHUNK)
        cols_m[0, rows], cols_m[1, rows] = unpack(chans, [ref[rows] for ref in x_in])
    corner_a = unpack(chans, [ref[...] for ref in ka_in])
    corner_b = [jnp.where(partner, part, 0.0) for part in unpack(chans, [ref[...] for ref in kb_in])]
    for part in range(2):
        a_rows, b_rows = a_in[part], jnp.where(partner, b_in[part], 0.0)
        rows_m[part, :m] = jnp.where(lower, a_rows, b_rows)
        rows_m[part, m:] = jnp.where(lower, b_rows, a_rows)
        corner_m[part, :m] = jnp.where(lower, corner_a[part], corner_b[part])
        corner_m[part, m:] = jnp.where(lower, corner_b[part], corner_a[part])

    def by_left(t, rhs):
        both = dot(left[t], rhs[:size])
        return both[:size] + both[size:] + dot(left[t, :size], rhs[size:])

    def row_mask(view, row):
        ids = row + lax.broadcasted_iota(jnp.int32, (CHUNK, LANES), 0)
        if row < m:
            return ids < spots[view, 0, :1] - m, row
        if row >= size - m:
            return ids >= size - m + spots[view, 0, :1], row - size + 2 * m
        return None, None

    def patch(view, row, block):
        cols = slice(block * LANES, (block + 1) * LANES)
        rows = slice(row, row + CHUNK)
        beside = col_mask(spots, view, block)
        beyond, place = row_mask(view, row)
        found = []
        for part in range(2):
            value = jnp.where(beside, cols_m[part, rows], core[part, rows, cols])
            if beyond is not None:
                there = slice(place, place + CHUNK)
                outer = jnp.where(beside, corner_m[part, there], rows_m[part, there, cols])
                value = jnp.where(beyond, outer, value)
            found.append(value)
        return found

    def first(view, odd, row, cols):
        if CHUNK <= row < size - CHUNK:
            return inner[view, odd, row - CHUNK : row, cols]
        place = 0 if row == 0 else CHUNK
        return y[view, odd, place : place + CHUNK, cols]

    def steps(view):
        for row in (0, size - CHUNK):
            put_waves(s1.at[view], placed, view, row, 0 if row == 0 else CHUNK, patch)
            yield
        for odd in range(2):
            y[view, odd] = by_right(s1.at[view, odd], right, odd)
            yield
        for odd in range(2):
            for row in range(0, half, CHUNK):
                for part in range(2):
                    cols = slice(part * half, (part + 1) * half)
                    above, below = first(view, odd, row, cols), first(view, odd, half + row, cols)
                    put(s2.at[view, 0], part * half + row, odd * half, above + below)
                    put(s2.at[view, 1], part * half + row, odd * half, above - below)
                yield
        valid = (view < counts[0, 0]).astype(F32)
        for row in range(0, size, CHUNK):
            rows = slice(row, row + CHUNK)
            lanes = lax.broadcasted_iota(jnp.int32, (CHUNK, LANES), 1)
            wanted = []
            for block in range(2):
                power = intensity[0, 0, view, rows, block * LANES : (block + 1) * LANES] + smooth_eps
                wanted.append(power * lax.rsqrt(power) * valid)
            for odd in range(2):
                taken = lax.rem(2 * lanes + odd, LANES)
                ordered = [jnp.take_along_axis(block, taken, axis=1) for block in wanted]
                amplitude[view, odd, rows] = jnp.where(lanes < LANES // 2, *ordered)
        yield
        for odd in range(2):
            z[view, odd] = by_left(odd, s2.at[view, odd])
            yield
        for odd in range(2):
            for row in range(0, half, CHUNK):
                re, im = z[view, odd, row : row + CHUNK], z[view, odd, half + row : half + row + CHUNK]
                taken = pl.ds(2 * row + odd, CHUNK, stride=2)
                wanted = jnp.concatenate([amplitude[view, 0, taken], amplitude[view, 1, taken]], 1)
                scaling = valid - wanted * lax.rsqrt(re * re + im * im + smooth_eps)
                put(s3.at[view, odd], row, 0, re * scaling)
                put(s3.at[view, odd], half + row, 0, im * scaling)
                yield
        for odd in range(2):
            u[view, odd] = by_left(2 + odd, s3.at[view, odd])
            yield
        for row in range(0, half, CHUNK):
            for part in range(2):
                rows = slice(part * half + row, part * half + row + CHUNK)
                even_rows, odd_rows = u[view, 0, rows], u[view, 1, rows]
                for value, place in ((even_rows + odd_rows, row), (even_rows - odd_rows, half + row)):
                    put(s4.at[view, 0], place, part * half, value[:, :half])
                    put(s4.at[view, 1], place, part * half, value[:, half:])
                yield
        for odd in range(2):
            g[view, odd] = by_right(s4.at[view, odd], right, 2 + odd)
            yield

    work = [steps(view) for view in range(views)]
    for view in range(views):
        for _ in range(view * STAGGER):
            work[view] = itertools.chain([None], work[view])
    for _ in itertools.zip_longest(*work):
        pass

    for row in range(0, size, CHUNK):
        rows = slice(row, row + CHUNK)
        sums = {}

        def add(key, value):
            sums[key] = sums[key] + value if key in sums else value

        for view in range(views):
            beyond, place = row_mask(view, row)
            halves = []
            for part in range(2):
                cols = slice(part * half, (part + 1) * half)
                even_cols, odd_cols = g[view, 0, rows, cols], g[view, 1, rows, cols]
                halves.append((even_cols + odd_cols, even_cols - odd_cols))
            for block in range(2):
                cols = slice(block * LANES, (block + 1) * LANES)
                beside = col_mask(spots, view, block)
                b_re, b_im = halves[0][block], halves[1][block]
                p_re, p_im = placed[view, 0, rows, cols], placed[view, 1, rows, cols]
                for part, value in enumerate((p_re * b_re + p_im * b_im, p_re * b_im - p_im * b_re)):
                    if beyond is not None:
                        outer, value = jnp.where(beyond, value, zero), jnp.where(beyond, zero, value)
                        add(("corner", part), jnp.where(beside, outer, zero))
                        add(("row", part, block), jnp.where(beside, zero, outer))
                    add(("col", part), jnp.where(beside, value, zero))
                    add(("core", part, block), jnp.where(beside, zero, value))
        for part in range(2):
            cols_m[part, rows] = sums["col", part]
            if place is not None:
                corner_m[part, place : place + CHUNK] = sums["corner", part]
            for block in range(2):
                cols = slice(block * LANES, (block + 1) * LANES)
                g_core[part, rows, cols] = sums["core", part, block]
                if place is not None:
                    rows_m[part, place : place + CHUNK, cols] = sums["row", part, block]

    def packed(channel, re, im):
        to_right = jnp.where(low_lanes, re, swap_halves(im))
        to_left = jnp.where(low_lanes, swap_halves(im), re)
        return jnp.where(sends_right(channel), to_right, to_left)

    for part in range(2):
        bottom, top = rows_m[part, :m], rows_m[part, m:]
        g_a[part] = jnp.where(lower, bottom, top)
        g_b[part] = jnp.where(lower, top, bottom)
    bottom = (corner_m[0, :m], corner_m[1, :m])
    top = (corner_m[0, m:], corner_m[1, m:])
    for number, channel in enumerate(chans):
        for row in range(0, size, CHUNK):
            rows = slice(row, row + CHUNK)
            g_x[number][rows] = packed(channel, cols_m[0, rows], cols_m[1, rows])
        below, above = packed(channel, *bottom), packed(channel, *top)
        g_ka[number][...] = jnp.where(lower, below, above)
        g_kb[number][...] = jnp.where(lower, above, below)


def views_call(chans, spots, counts, core, placed, inner, intensity, tables, a_in, b_in, x_in, ka_in, kb_in):
    views, size = placed.shape[0], core.shape[1]
    count = len(chans)
    vmem = pl.BlockSpec(memory_space=pltpu.VMEM)
    shapes = [(2, size, size), (2, MARGIN, size), (2, MARGIN, size)]
    shapes += [(size, LANES)] * count + [(MARGIN, LANES)] * (2 * count)
    full = pltpu.VMEM((views, 2, size, size), F32)
    tall = pltpu.VMEM((views, 2, 2 * size, size), BF16)
    outs = pl.pallas_call(
        functools.partial(views_kernel, chans),
        out_shape=[jax.ShapeDtypeStruct(shape, F32) for shape in shapes],
        in_specs=[
            vmem,
            pl.BlockSpec(memory_space=pltpu.SMEM),
            *[vmem] * (8 + 3 * count),
        ],
        out_specs=[vmem] * len(shapes),
        scratch_shapes=[
            pltpu.VMEM((views, 2, size, size // 2), F32),
            pltpu.VMEM((2, size, LANES), F32),
            pltpu.VMEM((2, 2 * MARGIN, size), F32),
            pltpu.VMEM((2, 2 * MARGIN, LANES), F32),
            pltpu.VMEM((views, 2, 4 * CHUNK, size), BF16),
            pltpu.VMEM((views, 2, 2 * CHUNK, size), F32),
            *[tall, full] * 3,
        ],
        compiler_params=pltpu.CompilerParams(vmem_limit_bytes=40 * 1024 * 1024),
    )(spots, counts, core, placed, inner, intensity, *x_in, a_in, b_in, *kb_in, *ka_in, *tables)
    return (*outs[:3], outs[3 : 3 + count], outs[3 + count : 3 + 2 * count], outs[3 + 2 * count :])


def finish_kernel(chans, object_ref, g_core, *rest):
    count = len(chans)
    x_in, (a_in, b_in), rest = rest[:count], rest[count : count + 2], rest[count + 2 :]
    kb_in, ka_in, out = rest[:count], rest[count : 2 * count], rest[-1]
    size = object_ref.shape[1]
    lower = lower_partner()
    a_rows = pl.ds(pl.multiple_of(jnp.where(lower, size - MARGIN, 0), MARGIN), MARGIN)
    b_rows = pl.ds(pl.multiple_of(jnp.where(lower, 0, size - MARGIN), MARGIN), MARGIN)
    columns = []
    for channel in chans:
        right = takes_right(channel)
        mine = lane_ids() // (LANES // 2) == jnp.where(right, 1, 0)
        block = pl.multiple_of(jnp.where(right, size - LANES, 0), LANES)
        columns.append((mine, pl.ds(block, LANES)))

    def take(place, value):
        out[place] -= step_size * value

    def take_packed(rows, column, block):
        mine, lanes = column
        take((0, rows, lanes), jnp.where(mine, block, 0.0))
        take((1, rows, lanes), jnp.where(mine, swap_halves(block), 0.0))

    for part in range(2):
        out[part] = object_ref[part] - step_size * g_core[part]
        take((part, a_rows), a_in[part])
    for number, column in enumerate(columns):
        take_packed(slice(None), column, x_in[number][...])
        take_packed(a_rows, column, ka_in[number][...])

    @pl.when(b_partner())
    def _():
        for part in range(2):
            take((part, b_rows), b_in[part])
        for number, column in enumerate(columns):
            take_packed(b_rows, column, kb_in[number][...])


def finish_call(chans, object_field, g_core, a_in, b_in, x_in, ka_in, kb_in):
    vmem = pl.BlockSpec(memory_space=pltpu.VMEM)
    return pl.pallas_call(
        functools.partial(finish_kernel, chans),
        out_shape=jax.ShapeDtypeStruct(object_field.shape, F32),
        in_specs=[vmem] * (4 + 3 * len(chans)),
        out_specs=vmem,
        compiler_params=pltpu.CompilerParams(vmem_limit_bytes=6 * 1024 * 1024),
    )(object_field, g_core, *x_in, a_in, b_in, *kb_in, *ka_in)


def per_device(object_field, probe_field, intensity, view_offsets, view_counts):
    size = object_field.shape[1]
    mesh_rows, mesh_cols = lax.axis_size("row"), lax.axis_size("col")
    chans = channels(mesh_cols)
    tables = dft_tables(size)
    a_pairs, b_pairs = row_pairs(mesh_rows, 0), row_pairs(mesh_rows, 1)
    spare = spare_route(b_pairs, mesh_rows, mesh_cols)

    def over_rows(block, pairs, extra):
        route = [(i * mesh_cols + k, j * mesh_cols + k) for i, j in pairs for k in range(mesh_cols)]
        return lax.ppermute(block, ("row", "col"), route + extra)

    def across(block, pairs, extra, channel):
        route = [(i * mesh_cols + k, j * mesh_cols + l) for i, j in pairs for k, l in channel[0]]
        return lax.ppermute(block, ("row", "col"), route + (extra if mesh_cols == 2 else []))

    def exchange(a_send, b_send, x_send, kb_send):
        x_in = [lax.ppermute(block, "col", channel[0]) for block, channel in zip(x_send, chans)]
        a_in = over_rows(a_send, a_pairs, [])
        b_in = over_rows(b_send, b_pairs, spare)
        kb_in = [across(block, b_pairs, spare, channel) for block, channel in zip(kb_send, chans)]
        return a_in, b_in, x_in, kb_in

    packs = pack_call(object_field, chans)
    a_in, b_in, x_in, kb_in = exchange(packs[0], packs[1], packs[2::2], packs[3::2])
    offsets, probe = (
        pltpu.with_memory_space_constraint(array, pltpu.HBM)
        for array in (jnp.swapaxes(view_offsets, 2, 3), probe_field)
    )
    placed, spots = prepare_call(offsets, probe)
    edges = [edge_call(block, spots) for block in x_in]
    ka_in = [over_rows(block, a_pairs, []) for block in edges]
    inner = early_call(
        chans, spots, object_field, placed, tables[0], edges[0] if edges else spots, x_in
    )
    g_core, g_a, g_b, g_x, g_ka, g_kb = views_call(
        chans, spots, view_counts, object_field, placed, inner, intensity, tables,
        a_in, b_in, x_in, ka_in, kb_in,
    )
    a_in, b_in, x_in, kb_in = exchange(g_a, g_b, g_x, g_kb)
    ka_in = [across(block, a_pairs, [], channel) for block, channel in zip(g_ka, chans)]
    return finish_call(chans, object_field, g_core, a_in, b_in, x_in, ka_in, kb_in)


def solution(mesh):
    in_specs = (
        P(None, "row", "col"),
        P(),
        P("row", "col", None, None, None),
        P("row", "col", None, None),
        P("row", "col"),
    )
    out_specs = P(None, "row", "col")
    return jax.shard_map(
        per_device, mesh=mesh, in_specs=in_specs, out_specs=out_specs, check_vma=False
    )
```

```python
import functools
import itertools
import math

import jax
import jax.numpy as jnp
import ml_dtypes
import numpy as np
from jax import lax
from jax.experimental import pallas as pl
from jax.experimental.pallas import tpu as pltpu
from jax.sharding import PartitionSpec as P

MARGIN = 64
LANES = 128
CHUNK = MARGIN
STAGGER = 2

smooth_eps = 0.1
step_size = 0.2

F32 = jnp.float32
BF16 = jnp.bfloat16


def dft_tables(length):
    half = length // 2
    counter = np.arange(half)
    factor = 1.0 / math.sqrt(length)
    product = np.outer(counter, counter)
    even = np.exp(-2j * np.pi * (product % half) / half) * factor
    odd = np.exp(-2j * np.pi * ((2 * product + counter[:, None]) % length) / length) * factor

    def as_real(table):
        return np.block([[table.real, table.imag], [-table.imag, table.real]])

    def parts(table):
        high = table.astype(ml_dtypes.bfloat16)
        low = (table - high.astype(np.float64)).astype(ml_dtypes.bfloat16)
        return high, low

    even, odd = as_real(even), as_real(odd)
    by_right = [np.concatenate(parts(t), 0) for t in (even, odd, even.T, odd.T)]
    by_left = [np.concatenate(parts(t), 0) for t in (even.T, odd.T, even, odd)]
    return np.stack(by_right), np.stack(by_left)


def channels(mesh_cols):
    if mesh_cols == 1:
        return []
    if mesh_cols == 2:
        return [([(0, 1), (1, 0)], None, None)]
    forward = [(i, i + 1) for i in range(mesh_cols - 1)]
    return [(forward, True, False), ([(j, i) for i, j in forward], False, True)]


def row_pairs(count, first):
    pairs = [(i, i + 1) for i in range(first, count - 1, 2)]
    return pairs + [(j, i) for i, j in pairs]


def spare_route(pairs, mesh_rows, mesh_cols):
    rows = [i for i in range(mesh_rows) if i not in dict(pairs)]
    if mesh_cols % 2:
        return []
    return [(i * mesh_cols + k, i * mesh_cols + (k ^ 1)) for i in rows for k in range(mesh_cols)]


def b_partner():
    row = lax.axis_index("row")
    return jnp.where(lower_partner(), row > 0, row < lax.axis_size("row") - 1)


def sends_right(channel):
    return lax.axis_index("col") == 0 if channel[1] is None else channel[1]


def takes_right(channel):
    return lax.axis_index("col") == 0 if channel[2] is None else channel[2]


def lower_partner():
    return lax.rem(lax.axis_index("row"), 2) == 0


def lane_ids():
    return lax.broadcasted_iota(jnp.int32, (1, LANES), 1)


def half_lanes(right):
    low = lane_ids() < LANES // 2
    if isinstance(right, bool):
        return low if right else ~low
    return lane_ids() // (LANES // 2) == jnp.where(right, 0, 1)


def split(value):
    high = value.astype(BF16)
    return high, (value - high.astype(F32)).astype(BF16)


def dot(first, second):
    return jnp.dot(first, second, preferred_element_type=F32)


def swap_halves(block):
    return pltpu.roll(block, LANES // 2, 1)


def fetch(pairs, sems):
    copies = [pltpu.make_async_copy(source, target, sems.at[i]) for i, (source, target) in enumerate(pairs)]
    for copy in copies:
        copy.start()
    return copies


def pack_kernel(chans, object_ref, a_ref, b_ref, *edge_refs):
    size = object_ref.shape[1]
    top, bottom = pl.ds(0, MARGIN), pl.ds(size - MARGIN, MARGIN)
    lower = lower_partner()
    for part in range(2):
        head, tail = object_ref[part, top, :], object_ref[part, bottom, :]
        a_ref[part] = jnp.where(lower, tail, head)
        b_ref[part] = jnp.where(lower, head, tail)
    for number, channel in enumerate(chans):
        right = sends_right(channel)
        x_ref, kb_ref = edge_refs[2 * number : 2 * number + 2]
        low = lane_ids() < LANES // 2
        for start in range(0, size, CHUNK):
            rows = slice(start, start + CHUNK)
            left_edge = jnp.where(
                low, object_ref[0, rows, :LANES], swap_halves(object_ref[1, rows, :LANES])
            )
            right_edge = jnp.where(
                low,
                swap_halves(object_ref[1, rows, size - LANES :]),
                object_ref[0, rows, size - LANES :],
            )
            x_ref[rows] = jnp.where(right, right_edge, left_edge)
        kb_ref[...] = jnp.where(lower, x_ref[:MARGIN], x_ref[size - MARGIN :])


def pack_call(object_field, chans):
    size = object_field.shape[1]
    shapes = [(2, MARGIN, size)] * 2 + [(size, LANES), (MARGIN, LANES)] * len(chans)
    vmem = pl.BlockSpec(memory_space=pltpu.VMEM)
    return pl.pallas_call(
        functools.partial(pack_kernel, chans),
        out_shape=[jax.ShapeDtypeStruct(shape, F32) for shape in shapes],
        in_specs=[vmem],
        out_specs=[vmem] * len(shapes),
        compiler_params=pltpu.CompilerParams(vmem_limit_bytes=4 * 1024 * 1024),
    )(object_field)


def prepare_kernel(offsets_in, probe, placed, spots, offsets, doubled, sems):
    views, size = placed.shape[0], probe.shape[1]
    copies = fetch(
        [(offsets_in, offsets)]
        + [(probe.at[part], doubled.at[part, pl.ds(0, size)]) for part in range(2)],
        sems,
    )
    sublane = lax.broadcasted_iota(jnp.int32, (1, 8, 1), 1)
    copies[0].wait()
    for part in range(2):
        copies[1 + part].wait()
        doubled[part, size:] = doubled[part, :size]
        for view in range(views):
            shift_row = lax.rem(offsets[0, 0, 0, view] - MARGIN + size, size)
            shift_col = lax.rem(offsets[0, 0, 1, view] - MARGIN + size, size)
            start = lax.rem(size - shift_row, size)
            whole = pl.multiple_of((start // 8) * 8, 8)
            rest = start - whole
            for row in range(0, size, CHUNK):
                block = doubled[part, pl.ds(whole + row, CHUNK + 8), :]
                block = pltpu.roll(block, shift_col, 1).reshape(CHUNK // 8 + 1, 8, size)
                block = pltpu.roll(block, lax.rem(8 - rest, 8), 1)
                block = jnp.where(sublane < 8 - rest, block[:-1], block[1:])
                placed[view, part, row : row + CHUNK] = block.reshape(CHUNK, size)
    for view in range(views):
        for axis in range(2):
            spots[view, axis] = jnp.full(spots.shape[2:], offsets[0, 0, axis, view], jnp.int32)


def prepare_call(offsets, probe):
    views, size = offsets.shape[3], probe.shape[1]
    vmem, hbm = pl.BlockSpec(memory_space=pltpu.VMEM), pl.BlockSpec(memory_space=pltpu.HBM)
    return pl.pallas_call(
        prepare_kernel,
        out_shape=[
            jax.ShapeDtypeStruct((views, 2, size, size), F32),
            jax.ShapeDtypeStruct((views, 2, 8, LANES), jnp.int32),
        ],
        in_specs=[hbm, hbm],
        out_specs=[vmem, vmem],
        scratch_shapes=[
            pltpu.SMEM(offsets.shape, jnp.int32),
            pltpu.VMEM((2, 2 * size, size), F32),
            pltpu.SemaphoreType.DMA((3,)),
        ],
        compiler_params=pltpu.CompilerParams(vmem_limit_bytes=16 * 1024 * 1024),
        cost_estimate=pl.CostEstimate(flops=10**9, bytes_accessed=10**5, transcendentals=0),
    )(offsets, probe)


def edge_kernel(block, spots, out):
    out[...] = jnp.where(lower_partner(), block[block.shape[0] - MARGIN :], block[:MARGIN])


def edge_call(block, spots):
    vmem = pl.BlockSpec(memory_space=pltpu.VMEM)
    return pl.pallas_call(
        edge_kernel,
        out_shape=jax.ShapeDtypeStruct((MARGIN, LANES), F32),
        in_specs=[vmem, vmem],
        out_specs=vmem,
        compiler_params=pltpu.CompilerParams(vmem_limit_bytes=2 * 1024 * 1024),
    )(block, spots)


def unpack(chans, blocks):
    re = im = jnp.zeros((MARGIN, LANES), F32)
    for channel, block in zip(chans, blocks):
        mine = half_lanes(takes_right(channel))
        re, im = jnp.where(mine, block, re), jnp.where(mine, swap_halves(block), im)
    return re, im


def col_mask(spots, view, block):
    if block == 0:
        return lane_ids() < spots[view, 1, :1] - MARGIN
    return lane_ids() >= MARGIN + spots[view, 1, :1]


def put(ref, row, col, value):
    high, low = split(value)
    count, (rows, cols) = ref.shape[0] // 2, value.shape
    ref[row : row + rows, col : col + cols] = high
    ref[count + row : count + row + rows, col : col + cols] = low


def by_right(lhs, right, t):
    count, size = lhs.shape[0] // 2, lhs.shape[1]
    both = dot(lhs[...], right[t, :size])
    return both[:count] + both[count:] + dot(lhs[:count], right[t, size:])


def put_waves(ref, placed, view, row, place, patch):
    rows = slice(row, row + CHUNK)
    waves = []
    for block in range(2):
        cols = slice(block * LANES, (block + 1) * LANES)
        o_re, o_im = patch(view, row, block)
        p_re, p_im = placed[view, 0, rows, cols], placed[view, 1, rows, cols]
        waves.append((p_re * o_re - p_im * o_im, p_re * o_im + p_im * o_re))
    for part in range(2):
        put(ref.at[0], place, part * LANES, waves[0][part] + waves[1][part])
        put(ref.at[1], place, part * LANES, waves[0][part] - waves[1][part])


def early_kernel(chans, spots, core, placed, right, *rest):
    rest = rest[3:]
    x_in, out, cols_m, s1 = rest[: len(chans)], *rest[len(chans) :]
    views, size = placed.shape[0], core.shape[1]

    def patch(view, row, block):
        cols, rows = slice(block * LANES, (block + 1) * LANES), slice(row, row + CHUNK)
        beside = col_mask(spots, view, block)
        return [jnp.where(beside, cols_m[p, rows], core[p, rows, cols]) for p in range(2)]

    for row in range(CHUNK, size - CHUNK, CHUNK):
        rows = slice(row, row + CHUNK)
        cols_m[0, rows], cols_m[1, rows] = unpack(chans, [ref[rows] for ref in x_in])
    for view in range(views):
        for row in range(CHUNK, size - CHUNK, CHUNK):
            put_waves(s1.at[view], placed, view, row, row - CHUNK, patch)
        for odd in range(2):
            out[view, odd] = by_right(s1.at[view, odd], right, odd)


def early_call(chans, spots, core, placed, right, unused, x_in):
    views, size = placed.shape[0], core.shape[1]
    vmem = pl.BlockSpec(memory_space=pltpu.VMEM)
    return pl.pallas_call(
        functools.partial(early_kernel, chans),
        out_shape=jax.ShapeDtypeStruct((views, 2, size - 2 * CHUNK, size), F32),
        in_specs=[vmem] * (7 + len(chans)),
        out_specs=vmem,
        scratch_shapes=[
            pltpu.VMEM((2, size, LANES), F32),
            pltpu.VMEM((views, 2, 2 * (size - 2 * CHUNK), size), BF16),
        ],
        compiler_params=pltpu.CompilerParams(vmem_limit_bytes=8 * 1024 * 1024),
        cost_estimate=pl.CostEstimate(flops=10**8, bytes_accessed=10**4, transcendentals=0),
    )(spots, core, placed, right, *unused, *x_in)


def views_kernel(chans, spots, counts, core, placed, inner, intensity, *rest):
    count = len(chans)
    x_in, (a_in, b_in), rest = rest[:count], rest[count : count + 2], rest[count + 2 :]
    kb_in, ka_in = rest[:count], rest[count : 2 * count]
    right, left, *rest = rest[2 * count :]
    g_core, g_a, g_b = rest[:3]
    g_x, g_ka = rest[3 : 3 + count], rest[3 + count : 3 + 2 * count]
    g_kb = rest[3 + 2 * count : 3 + 3 * count]
    amplitude, cols_m, rows_m, corner_m, s1, y, s2, z, s3, u, s4, g = rest[3 + 3 * count :]
    views, size = placed.shape[0], core.shape[1]
    half, m = size // 2, MARGIN
    lower, partner = lower_partner(), b_partner()
    low_lanes = lane_ids() < LANES // 2
    zero = jnp.zeros((CHUNK, LANES), F32)

    for row in (0, size - CHUNK):
        rows = slice(row, row + CHUNK)
        cols_m[0, rows], cols_m[1, rows] = unpack(chans, [ref[rows] for ref in x_in])
    corner_a = unpack(chans, [ref[...] for ref in ka_in])
    corner_b = [jnp.where(partner, part, 0.0) for part in unpack(chans, [ref[...] for ref in kb_in])]
    for part in range(2):
        a_rows, b_rows = a_in[part], jnp.where(partner, b_in[part], 0.0)
        rows_m[part, :m] = jnp.where(lower, a_rows, b_rows)
        rows_m[part, m:] = jnp.where(lower, b_rows, a_rows)
        corner_m[part, :m] = jnp.where(lower, corner_a[part], corner_b[part])
        corner_m[part, m:] = jnp.where(lower, corner_b[part], corner_a[part])

    def by_left(t, rhs):
        both = dot(left[t], rhs[:size])
        return both[:size] + both[size:] + dot(left[t, :size], rhs[size:])

    def row_mask(view, row):
        ids = row + lax.broadcasted_iota(jnp.int32, (CHUNK, LANES), 0)
        if row < m:
            return ids < spots[view, 0, :1] - m, row
        if row >= size - m:
            return ids >= size - m + spots[view, 0, :1], row - size + 2 * m
        return None, None

    def patch(view, row, block):
        cols = slice(block * LANES, (block + 1) * LANES)
        rows = slice(row, row + CHUNK)
        beside = col_mask(spots, view, block)
        beyond, place = row_mask(view, row)
        found = []
        for part in range(2):
            value = jnp.where(beside, cols_m[part, rows], core[part, rows, cols])
            if beyond is not None:
                there = slice(place, place + CHUNK)
                outer = jnp.where(beside, corner_m[part, there], rows_m[part, there, cols])
                value = jnp.where(beyond, outer, value)
            found.append(value)
        return found

    def first(view, odd, row, cols):
        if CHUNK <= row < size - CHUNK:
            return inner[view, odd, row - CHUNK : row, cols]
        place = 0 if row == 0 else CHUNK
        return y[view, odd, place : place + CHUNK, cols]

    def steps(view):
        for row in (0, size - CHUNK):
            put_waves(s1.at[view], placed, view, row, 0 if row == 0 else CHUNK, patch)
            yield
        for odd in range(2):
            y[view, odd] = by_right(s1.at[view, odd], right, odd)
            yield
        for odd in range(2):
            for row in range(0, half, CHUNK):
                for part in range(2):
                    cols = slice(part * half, (part + 1) * half)
                    above, below = first(view, odd, row, cols), first(view, odd, half + row, cols)
                    put(s2.at[view, 0], part * half + row, odd * half, above + below)
                    put(s2.at[view, 1], part * half + row, odd * half, above - below)
                yield
        valid = (view < counts[0, 0]).astype(F32)
        for row in range(0, size, CHUNK):
            rows = slice(row, row + CHUNK)
            lanes = lax.broadcasted_iota(jnp.int32, (CHUNK, LANES), 1)
            wanted = []
            for block in range(2):
                power = intensity[0, 0, view, rows, block * LANES : (block + 1) * LANES] + smooth_eps
                wanted.append(power * lax.rsqrt(power) * valid)
            for odd in range(2):
                taken = lax.rem(2 * lanes + odd, LANES)
                ordered = [jnp.take_along_axis(block, taken, axis=1) for block in wanted]
                amplitude[view, odd, rows] = jnp.where(lanes < LANES // 2, *ordered)
        yield
        for odd in range(2):
            z[view, odd] = by_left(odd, s2.at[view, odd])
            yield
        for odd in range(2):
            for row in range(0, half, CHUNK):
                re, im = z[view, odd, row : row + CHUNK], z[view, odd, half + row : half + row + CHUNK]
                taken = pl.ds(2 * row + odd, CHUNK, stride=2)
                wanted = jnp.concatenate([amplitude[view, 0, taken], amplitude[view, 1, taken]], 1)
                scaling = valid - wanted * lax.rsqrt(re * re + im * im + smooth_eps)
                put(s3.at[view, odd], row, 0, re * scaling)
                put(s3.at[view, odd], half + row, 0, im * scaling)
                yield
        for odd in range(2):
            u[view, odd] = by_left(2 + odd, s3.at[view, odd])
            yield
        for row in range(0, half, CHUNK):
            for part in range(2):
                rows = slice(part * half + row, part * half + row + CHUNK)
                even_rows, odd_rows = u[view, 0, rows], u[view, 1, rows]
                for value, place in ((even_rows + odd_rows, row), (even_rows - odd_rows, half + row)):
                    put(s4.at[view, 0], place, part * half, value[:, :half])
                    put(s4.at[view, 1], place, part * half, value[:, half:])
                yield
        for odd in range(2):
            g[view, odd] = by_right(s4.at[view, odd], right, 2 + odd)
            yield

    work = [steps(view) for view in range(views)]
    for view in range(views):
        for _ in range(view * STAGGER):
            work[view] = itertools.chain([None], work[view])
    for _ in itertools.zip_longest(*work):
        pass

    for row in range(0, size, CHUNK):
        rows = slice(row, row + CHUNK)
        sums = {}

        def add(key, value):
            sums[key] = sums[key] + value if key in sums else value

        for view in range(views):
            beyond, place = row_mask(view, row)
            halves = []
            for part in range(2):
                cols = slice(part * half, (part + 1) * half)
                even_cols, odd_cols = g[view, 0, rows, cols], g[view, 1, rows, cols]
                halves.append((even_cols + odd_cols, even_cols - odd_cols))
            for block in range(2):
                cols = slice(block * LANES, (block + 1) * LANES)
                beside = col_mask(spots, view, block)
                b_re, b_im = halves[0][block], halves[1][block]
                p_re, p_im = placed[view, 0, rows, cols], placed[view, 1, rows, cols]
                for part, value in enumerate((p_re * b_re + p_im * b_im, p_re * b_im - p_im * b_re)):
                    if beyond is not None:
                        outer, value = jnp.where(beyond, value, zero), jnp.where(beyond, zero, value)
                        add(("corner", part), jnp.where(beside, outer, zero))
                        add(("row", part, block), jnp.where(beside, zero, outer))
                    add(("col", part), jnp.where(beside, value, zero))
                    add(("core", part, block), jnp.where(beside, zero, value))
        for part in range(2):
            cols_m[part, rows] = sums["col", part]
            if place is not None:
                corner_m[part, place : place + CHUNK] = sums["corner", part]
            for block in range(2):
                cols = slice(block * LANES, (block + 1) * LANES)
                g_core[part, rows, cols] = sums["core", part, block]
                if place is not None:
                    rows_m[part, place : place + CHUNK, cols] = sums["row", part, block]

    def packed(channel, re, im):
        to_right = jnp.where(low_lanes, re, swap_halves(im))
        to_left = jnp.where(low_lanes, swap_halves(im), re)
        return jnp.where(sends_right(channel), to_right, to_left)

    for part in range(2):
        bottom, top = rows_m[part, :m], rows_m[part, m:]
        g_a[part] = jnp.where(lower, bottom, top)
        g_b[part] = jnp.where(lower, top, bottom)
    bottom = (corner_m[0, :m], corner_m[1, :m])
    top = (corner_m[0, m:], corner_m[1, m:])
    for number, channel in enumerate(chans):
        for row in range(0, size, CHUNK):
            rows = slice(row, row + CHUNK)
            g_x[number][rows] = packed(channel, cols_m[0, rows], cols_m[1, rows])
        below, above = packed(channel, *bottom), packed(channel, *top)
        g_ka[number][...] = jnp.where(lower, below, above)
        g_kb[number][...] = jnp.where(lower, above, below)


def views_call(chans, spots, counts, core, placed, inner, intensity, tables, a_in, b_in, x_in, ka_in, kb_in):
    views, size = placed.shape[0], core.shape[1]
    count = len(chans)
    vmem = pl.BlockSpec(memory_space=pltpu.VMEM)
    shapes = [(2, size, size), (2, MARGIN, size), (2, MARGIN, size)]
    shapes += [(size, LANES)] * count + [(MARGIN, LANES)] * (2 * count)
    full = pltpu.VMEM((views, 2, size, size), F32)
    tall = pltpu.VMEM((views, 2, 2 * size, size), BF16)
    outs = pl.pallas_call(
        functools.partial(views_kernel, chans),
        out_shape=[jax.ShapeDtypeStruct(shape, F32) for shape in shapes],
        in_specs=[
            vmem,
            pl.BlockSpec(memory_space=pltpu.SMEM),
            *[vmem] * (8 + 3 * count),
        ],
        out_specs=[vmem] * len(shapes),
        scratch_shapes=[
            pltpu.VMEM((views, 2, size, size // 2), F32),
            pltpu.VMEM((2, size, LANES), F32),
            pltpu.VMEM((2, 2 * MARGIN, size), F32),
            pltpu.VMEM((2, 2 * MARGIN, LANES), F32),
            pltpu.VMEM((views, 2, 4 * CHUNK, size), BF16),
            pltpu.VMEM((views, 2, 2 * CHUNK, size), F32),
            *[tall, full] * 3,
        ],
        compiler_params=pltpu.CompilerParams(vmem_limit_bytes=40 * 1024 * 1024),
    )(spots, counts, core, placed, inner, intensity, *x_in, a_in, b_in, *kb_in, *ka_in, *tables)
    return (*outs[:3], outs[3 : 3 + count], outs[3 + count : 3 + 2 * count], outs[3 + 2 * count :])


def finish_kernel(chans, object_ref, g_core, *rest):
    count = len(chans)
    x_in, (a_in, b_in), rest = rest[:count], rest[count : count + 2], rest[count + 2 :]
    kb_in, ka_in, out = rest[:count], rest[count : 2 * count], rest[-1]
    size = object_ref.shape[1]
    lower = lower_partner()
    a_rows = pl.ds(pl.multiple_of(jnp.where(lower, size - MARGIN, 0), MARGIN), MARGIN)
    b_rows = pl.ds(pl.multiple_of(jnp.where(lower, 0, size - MARGIN), MARGIN), MARGIN)
    columns = []
    for channel in chans:
        right = takes_right(channel)
        mine = lane_ids() // (LANES // 2) == jnp.where(right, 1, 0)
        block = pl.multiple_of(jnp.where(right, size - LANES, 0), LANES)
        columns.append((mine, pl.ds(block, LANES)))

    def take(place, value):
        out[place] -= step_size * value

    def take_packed(rows, column, block):
        mine, lanes = column
        take((0, rows, lanes), jnp.where(mine, block, 0.0))
        take((1, rows, lanes), jnp.where(mine, swap_halves(block), 0.0))

    for part in range(2):
        out[part] = object_ref[part] - step_size * g_core[part]
        take((part, a_rows), a_in[part])
    for number, column in enumerate(columns):
        take_packed(slice(None), column, x_in[number][...])
        take_packed(a_rows, column, ka_in[number][...])

    @pl.when(b_partner())
    def _():
        for part in range(2):
            take((part, b_rows), b_in[part])
        for number, column in enumerate(columns):
            take_packed(b_rows, column, kb_in[number][...])


def finish_call(chans, object_field, g_core, a_in, b_in, x_in, ka_in, kb_in):
    vmem = pl.BlockSpec(memory_space=pltpu.VMEM)
    return pl.pallas_call(
        functools.partial(finish_kernel, chans),
        out_shape=jax.ShapeDtypeStruct(object_field.shape, F32),
        in_specs=[vmem] * (4 + 3 * len(chans)),
        out_specs=vmem,
        compiler_params=pltpu.CompilerParams(vmem_limit_bytes=6 * 1024 * 1024),
    )(object_field, g_core, *x_in, a_in, b_in, *kb_in, *ka_in)


def per_device(object_field, probe_field, intensity, view_offsets, view_counts):
    size = object_field.shape[1]
    mesh_rows, mesh_cols = lax.axis_size("row"), lax.axis_size("col")
    chans = channels(mesh_cols)
    tables = dft_tables(size)
    a_pairs, b_pairs = row_pairs(mesh_rows, 0), row_pairs(mesh_rows, 1)
    spare = spare_route(b_pairs, mesh_rows, mesh_cols)

    def over_rows(block, pairs, extra):
        route = [(i * mesh_cols + k, j * mesh_cols + k) for i, j in pairs for k in range(mesh_cols)]
        return lax.ppermute(block, ("row", "col"), route + extra)

    def across(block, pairs, extra, channel):
        route = [(i * mesh_cols + k, j * mesh_cols + l) for i, j in pairs for k, l in channel[0]]
        return lax.ppermute(block, ("row", "col"), route + (extra if mesh_cols == 2 else []))

    def exchange(a_send, b_send, x_send, kb_send):
        x_in = [lax.ppermute(block, "col", channel[0]) for block, channel in zip(x_send, chans)]
        a_in = over_rows(a_send, a_pairs, [])
        b_in = over_rows(b_send, b_pairs, spare)
        kb_in = [across(block, b_pairs, spare, channel) for block, channel in zip(kb_send, chans)]
        return a_in, b_in, x_in, kb_in

    packs = pack_call(object_field, chans)
    a_in, b_in, x_in, kb_in = exchange(packs[0], packs[1], packs[2::2], packs[3::2])
    offsets, probe = (
        pltpu.with_memory_space_constraint(array, pltpu.HBM)
        for array in (jnp.swapaxes(view_offsets, 2, 3), probe_field)
    )
    placed, spots = prepare_call(offsets, probe)
    edges = [edge_call(block, spots) for block in x_in]
    ka_in = [over_rows(block, a_pairs, []) for block in edges]
    unused = (edges[0] if edges else spots, tables[1], intensity)
    inner = early_call(chans, spots, object_field, placed, tables[0], unused, x_in)
    g_core, g_a, g_b, g_x, g_ka, g_kb = views_call(
        chans, spots, view_counts, object_field, placed, inner, intensity, tables,
        a_in, b_in, x_in, ka_in, kb_in,
    )
    a_in, b_in, x_in, kb_in = exchange(g_a, g_b, g_x, g_kb)
    ka_in = [across(block, a_pairs, [], channel) for block, channel in zip(g_ka, chans)]
    return finish_call(chans, object_field, g_core, a_in, b_in, x_in, ka_in, kb_in)


def solution(mesh):
    in_specs = (
        P(None, "row", "col"),
        P(),
        P("row", "col", None, None, None),
        P("row", "col", None, None),
        P("row", "col"),
    )
    out_specs = P(None, "row", "col")
    return jax.shard_map(
        per_device, mesh=mesh, in_specs=in_specs, out_specs=out_specs, check_vma=False
    )
```

```python
import functools
import itertools
import math

import jax
import jax.numpy as jnp
import ml_dtypes
import numpy as np
from jax import lax
from jax.experimental import pallas as pl
from jax.experimental.pallas import tpu as pltpu
from jax.sharding import PartitionSpec as P

MARGIN = 64
LANES = 128
CHUNK = MARGIN
STAGGER = 2

smooth_eps = 0.1
step_size = 0.2

F32 = jnp.float32
BF16 = jnp.bfloat16


def dft_tables(length):
    half = length // 2
    counter = np.arange(half)
    factor = 1.0 / math.sqrt(length)
    product = np.outer(counter, counter)
    even = np.exp(-2j * np.pi * (product % half) / half) * factor
    odd = np.exp(-2j * np.pi * ((2 * product + counter[:, None]) % length) / length) * factor

    def as_real(table):
        return np.block([[table.real, table.imag], [-table.imag, table.real]])

    def parts(table):
        high = table.astype(ml_dtypes.bfloat16)
        low = (table - high.astype(np.float64)).astype(ml_dtypes.bfloat16)
        return high, low

    even, odd = as_real(even), as_real(odd)
    by_right = [np.concatenate(parts(t), 0) for t in (even, odd, even.T, odd.T)]
    by_left = [np.concatenate(parts(t), 0) for t in (even.T, odd.T, even, odd)]
    return np.stack(by_right), np.stack(by_left)


def channels(mesh_cols):
    if mesh_cols == 1:
        return []
    if mesh_cols == 2:
        return [([(0, 1), (1, 0)], None, None)]
    forward = [(i, i + 1) for i in range(mesh_cols - 1)]
    return [(forward, True, False), ([(j, i) for i, j in forward], False, True)]


def row_pairs(count, first):
    pairs = [(i, i + 1) for i in range(first, count - 1, 2)]
    return pairs + [(j, i) for i, j in pairs]


def spare_route(pairs, mesh_rows, mesh_cols):
    rows = [i for i in range(mesh_rows) if i not in dict(pairs)]
    if mesh_cols % 2:
        return []
    return [(i * mesh_cols + k, i * mesh_cols + (k ^ 1)) for i in rows for k in range(mesh_cols)]


def b_partner():
    row = lax.axis_index("row")
    return jnp.where(lower_partner(), row > 0, row < lax.axis_size("row") - 1)


def sends_right(channel):
    return lax.axis_index("col") == 0 if channel[1] is None else channel[1]


def takes_right(channel):
    return lax.axis_index("col") == 0 if channel[2] is None else channel[2]


def lower_partner():
    return lax.rem(lax.axis_index("row"), 2) == 0


def lane_ids():
    return lax.broadcasted_iota(jnp.int32, (1, LANES), 1)


def half_lanes(right):
    low = lane_ids() < LANES // 2
    if isinstance(right, bool):
        return low if right else ~low
    return lane_ids() // (LANES // 2) == jnp.where(right, 0, 1)


def split(value):
    high = value.astype(BF16)
    return high, (value - high.astype(F32)).astype(BF16)


def dot(first, second):
    return jnp.dot(first, second, preferred_element_type=F32)


def swap_halves(block):
    return pltpu.roll(block, LANES // 2, 1)


def fetch(pairs, sems):
    copies = [pltpu.make_async_copy(source, target, sems.at[i]) for i, (source, target) in enumerate(pairs)]
    for copy in copies:
        copy.start()
    return copies


def pack_kernel(chans, object_ref, a_ref, b_ref, *edge_refs):
    size = object_ref.shape[1]
    top, bottom = pl.ds(0, MARGIN), pl.ds(size - MARGIN, MARGIN)
    lower = lower_partner()
    for part in range(2):
        head, tail = object_ref[part, top, :], object_ref[part, bottom, :]
        a_ref[part] = jnp.where(lower, tail, head)
        b_ref[part] = jnp.where(lower, head, tail)
    for number, channel in enumerate(chans):
        right = sends_right(channel)
        x_ref, kb_ref = edge_refs[2 * number : 2 * number + 2]
        low = lane_ids() < LANES // 2
        for start in range(0, size, CHUNK):
            rows = slice(start, start + CHUNK)
            left_edge = jnp.where(
                low, object_ref[0, rows, :LANES], swap_halves(object_ref[1, rows, :LANES])
            )
            right_edge = jnp.where(
                low,
                swap_halves(object_ref[1, rows, size - LANES :]),
                object_ref[0, rows, size - LANES :],
            )
            x_ref[rows] = jnp.where(right, right_edge, left_edge)
        kb_ref[...] = jnp.where(lower, x_ref[:MARGIN], x_ref[size - MARGIN :])


def pack_call(object_field, chans):
    size = object_field.shape[1]
    shapes = [(2, MARGIN, size)] * 2 + [(size, LANES), (MARGIN, LANES)] * len(chans)
    vmem = pl.BlockSpec(memory_space=pltpu.VMEM)
    return pl.pallas_call(
        functools.partial(pack_kernel, chans),
        out_shape=[jax.ShapeDtypeStruct(shape, F32) for shape in shapes],
        in_specs=[vmem],
        out_specs=[vmem] * len(shapes),
        compiler_params=pltpu.CompilerParams(vmem_limit_bytes=4 * 1024 * 1024),
    )(object_field)


def prepare_kernel(offsets_in, probe, placed, spots, offsets, doubled, sems):
    views, size = placed.shape[0], probe.shape[1]
    copies = fetch(
        [(offsets_in, offsets)]
        + [(probe.at[part], doubled.at[part, pl.ds(0, size)]) for part in range(2)],
        sems,
    )
    sublane = lax.broadcasted_iota(jnp.int32, (1, 8, 1), 1)
    copies[0].wait()
    for part in range(2):
        copies[1 + part].wait()
        doubled[part, size:] = doubled[part, :size]
        for view in range(views):
            shift_row = lax.rem(offsets[0, 0, 0, view] - MARGIN + size, size)
            shift_col = lax.rem(offsets[0, 0, 1, view] - MARGIN + size, size)
            start = lax.rem(size - shift_row, size)
            whole = pl.multiple_of((start // 8) * 8, 8)
            rest = start - whole
            for row in range(0, size, CHUNK):
                block = doubled[part, pl.ds(whole + row, CHUNK + 8), :]
                block = pltpu.roll(block, shift_col, 1).reshape(CHUNK // 8 + 1, 8, size)
                block = pltpu.roll(block, lax.rem(8 - rest, 8), 1)
                block = jnp.where(sublane < 8 - rest, block[:-1], block[1:])
                placed[view, part, row : row + CHUNK] = block.reshape(CHUNK, size)
    for view in range(views):
        for axis in range(2):
            spots[view, axis] = jnp.full(spots.shape[2:], offsets[0, 0, axis, view], jnp.int32)


def prepare_call(offsets, probe):
    views, size = offsets.shape[3], probe.shape[1]
    vmem, hbm = pl.BlockSpec(memory_space=pltpu.VMEM), pl.BlockSpec(memory_space=pltpu.HBM)
    return pl.pallas_call(
        prepare_kernel,
        out_shape=[
            jax.ShapeDtypeStruct((views, 2, size, size), F32),
            jax.ShapeDtypeStruct((views, 2, 8, LANES), jnp.int32),
        ],
        in_specs=[hbm, hbm],
        out_specs=[vmem, vmem],
        scratch_shapes=[
            pltpu.SMEM(offsets.shape, jnp.int32),
            pltpu.VMEM((2, 2 * size, size), F32),
            pltpu.SemaphoreType.DMA((3,)),
        ],
        compiler_params=pltpu.CompilerParams(vmem_limit_bytes=16 * 1024 * 1024),
        cost_estimate=pl.CostEstimate(flops=10**9, bytes_accessed=10**5, transcendentals=0),
    )(offsets, probe)


def edge_kernel(block, spots, out):
    out[...] = jnp.where(lower_partner(), block[block.shape[0] - MARGIN :], block[:MARGIN])


def edge_call(block, spots):
    vmem = pl.BlockSpec(memory_space=pltpu.VMEM)
    return pl.pallas_call(
        edge_kernel,
        out_shape=jax.ShapeDtypeStruct((MARGIN, LANES), F32),
        in_specs=[vmem, vmem],
        out_specs=vmem,
        compiler_params=pltpu.CompilerParams(vmem_limit_bytes=2 * 1024 * 1024),
    )(block, spots)


def unpack(chans, blocks):
    re = im = jnp.zeros((MARGIN, LANES), F32)
    for channel, block in zip(chans, blocks):
        mine = half_lanes(takes_right(channel))
        re, im = jnp.where(mine, block, re), jnp.where(mine, swap_halves(block), im)
    return re, im


def col_mask(spots, view, block):
    if block == 0:
        return lane_ids() < spots[view, 1, :1] - MARGIN
    return lane_ids() >= MARGIN + spots[view, 1, :1]


def put(ref, row, col, value):
    high, low = split(value)
    count, (rows, cols) = ref.shape[0] // 2, value.shape
    ref[row : row + rows, col : col + cols] = high
    ref[count + row : count + row + rows, col : col + cols] = low


def by_right(lhs, right, t):
    count, size = lhs.shape[0] // 2, lhs.shape[1]
    both = dot(lhs[...], right[t, :size])
    return both[:count] + both[count:] + dot(lhs[:count], right[t, size:])


def put_waves(ref, placed, view, row, place, patch):
    rows = slice(row, row + CHUNK)
    waves = []
    for block in range(2):
        cols = slice(block * LANES, (block + 1) * LANES)
        o_re, o_im = patch(view, row, block)
        p_re, p_im = placed[view, 0, rows, cols], placed[view, 1, rows, cols]
        waves.append((p_re * o_re - p_im * o_im, p_re * o_im + p_im * o_re))
    for part in range(2):
        put(ref.at[0], place, part * LANES, waves[0][part] + waves[1][part])
        put(ref.at[1], place, part * LANES, waves[0][part] - waves[1][part])


def early_kernel(chans, spots, core, placed, right, *rest):
    rest = rest[3:]
    x_in, out, cols_m, s1 = rest[: len(chans)], *rest[len(chans) :]
    views, size = placed.shape[0], core.shape[1]

    def patch(view, row, block):
        cols, rows = slice(block * LANES, (block + 1) * LANES), slice(row, row + CHUNK)
        beside = col_mask(spots, view, block)
        return [jnp.where(beside, cols_m[p, rows], core[p, rows, cols]) for p in range(2)]

    for row in range(CHUNK, size - CHUNK, CHUNK):
        rows = slice(row, row + CHUNK)
        cols_m[0, rows], cols_m[1, rows] = unpack(chans, [ref[rows] for ref in x_in])
    for view in range(views):
        for row in range(CHUNK, size - CHUNK, CHUNK):
            put_waves(s1.at[view], placed, view, row, row - CHUNK, patch)
        for odd in range(2):
            out[view, odd] = by_right(s1.at[view, odd], right, odd)


def early_call(chans, spots, core, placed, right, unused, x_in):
    views, size = placed.shape[0], core.shape[1]
    vmem = pl.BlockSpec(memory_space=pltpu.VMEM)
    return pl.pallas_call(
        functools.partial(early_kernel, chans),
        out_shape=jax.ShapeDtypeStruct((views, 2, size - 2 * CHUNK, size), F32),
        in_specs=[vmem] * (7 + len(chans)),
        out_specs=vmem,
        scratch_shapes=[
            pltpu.VMEM((2, size, LANES), F32),
            pltpu.VMEM((views, 2, 2 * (size - 2 * CHUNK), size), BF16),
        ],
        compiler_params=pltpu.CompilerParams(vmem_limit_bytes=8 * 1024 * 1024),
        cost_estimate=pl.CostEstimate(flops=10**8, bytes_accessed=10**4, transcendentals=0),
    )(spots, core, placed, right, *unused, *x_in)


def views_kernel(chans, spots, counts, core, placed, inner, intensity, *rest):
    count = len(chans)
    x_in, (a_in, b_in), rest = rest[:count], rest[count : count + 2], rest[count + 2 :]
    kb_in, ka_in = rest[:count], rest[count : 2 * count]
    right, left, *rest = rest[2 * count :]
    g_core, g_a, g_b = rest[:3]
    g_x, g_ka = rest[3 : 3 + count], rest[3 + count : 3 + 2 * count]
    g_kb = rest[3 + 2 * count : 3 + 3 * count]
    amplitude, cols_m, rows_m, corner_m, s1, y, s2, z, s3, u, s4, g = rest[3 + 3 * count :]
    views, size = placed.shape[0], core.shape[1]
    half, m = size // 2, MARGIN
    lower, partner = lower_partner(), b_partner()
    low_lanes = lane_ids() < LANES // 2
    zero = jnp.zeros((CHUNK, LANES), F32)

    for row in (0, size - CHUNK):
        rows = slice(row, row + CHUNK)
        cols_m[0, rows], cols_m[1, rows] = unpack(chans, [ref[rows] for ref in x_in])
    corner_a = unpack(chans, [ref[...] for ref in ka_in])
    corner_b = [jnp.where(partner, part, 0.0) for part in unpack(chans, [ref[...] for ref in kb_in])]
    for part in range(2):
        a_rows, b_rows = a_in[part], jnp.where(partner, b_in[part], 0.0)
        rows_m[part, :m] = jnp.where(lower, a_rows, b_rows)
        rows_m[part, m:] = jnp.where(lower, b_rows, a_rows)
        corner_m[part, :m] = jnp.where(lower, corner_a[part], corner_b[part])
        corner_m[part, m:] = jnp.where(lower, corner_b[part], corner_a[part])

    def by_left(t, rhs):
        both = dot(left[t], rhs[:size])
        return both[:size] + both[size:] + dot(left[t, :size], rhs[size:])

    def row_mask(view, row):
        ids = row + lax.broadcasted_iota(jnp.int32, (CHUNK, LANES), 0)
        if row < m:
            return ids < spots[view, 0, :1] - m, row
        if row >= size - m:
            return ids >= size - m + spots[view, 0, :1], row - size + 2 * m
        return None, None

    def patch(view, row, block):
        cols = slice(block * LANES, (block + 1) * LANES)
        rows = slice(row, row + CHUNK)
        beside = col_mask(spots, view, block)
        beyond, place = row_mask(view, row)
        found = []
        for part in range(2):
            value = jnp.where(beside, cols_m[part, rows], core[part, rows, cols])
            if beyond is not None:
                there = slice(place, place + CHUNK)
                outer = jnp.where(beside, corner_m[part, there], rows_m[part, there, cols])
                value = jnp.where(beyond, outer, value)
            found.append(value)
        return found

    def first(view, odd, row, cols):
        if CHUNK <= row < size - CHUNK:
            return inner[view, odd, row - CHUNK : row, cols]
        place = 0 if row == 0 else CHUNK
        return y[view, odd, place : place + CHUNK, cols]

    def steps(view):
        for row in (0, size - CHUNK):
            put_waves(s1.at[view], placed, view, row, 0 if row == 0 else CHUNK, patch)
            yield
        for odd in range(2):
            y[view, odd] = by_right(s1.at[view, odd], right, odd)
            yield
        for odd in range(2):
            for row in range(0, half, CHUNK):
                for part in range(2):
                    cols = slice(part * half, (part + 1) * half)
                    above, below = first(view, odd, row, cols), first(view, odd, half + row, cols)
                    put(s2.at[view, 0], part * half + row, odd * half, above + below)
                    put(s2.at[view, 1], part * half + row, odd * half, above - below)
                yield
        valid = (view < counts[0, 0]).astype(F32)
        for row in range(0, size, CHUNK):
            rows = slice(row, row + CHUNK)
            lanes = lax.broadcasted_iota(jnp.int32, (CHUNK, LANES), 1)
            wanted = []
            for block in range(2):
                power = intensity[0, 0, view, rows, block * LANES : (block + 1) * LANES] + smooth_eps
                wanted.append(power * lax.rsqrt(power) * valid)
            for odd in range(2):
                taken = lax.rem(2 * lanes + odd, LANES)
                ordered = [jnp.take_along_axis(block, taken, axis=1) for block in wanted]
                amplitude[view, odd, rows] = jnp.where(lanes < LANES // 2, *ordered)
        yield
        for odd in range(2):
            z[view, odd] = by_left(odd, s2.at[view, odd])
            yield
        for odd in range(2):
            for row in range(0, half, CHUNK):
                re, im = z[view, odd, row : row + CHUNK], z[view, odd, half + row : half + row + CHUNK]
                taken = pl.ds(2 * row + odd, CHUNK, stride=2)
                wanted = jnp.concatenate([amplitude[view, 0, taken], amplitude[view, 1, taken]], 1)
                scaling = valid - wanted * lax.rsqrt(re * re + im * im + smooth_eps)
                put(s3.at[view, odd], row, 0, re * scaling)
                put(s3.at[view, odd], half + row, 0, im * scaling)
                yield
        for odd in range(2):
            u[view, odd] = by_left(2 + odd, s3.at[view, odd])
            yield
        for row in range(0, half, CHUNK):
            for part in range(2):
                rows = slice(part * half + row, part * half + row + CHUNK)
                even_rows, odd_rows = u[view, 0, rows], u[view, 1, rows]
                for value, place in ((even_rows + odd_rows, row), (even_rows - odd_rows, half + row)):
                    put(s4.at[view, 0], place, part * half, value[:, :half])
                    put(s4.at[view, 1], place, part * half, value[:, half:])
                yield
        for odd in range(2):
            g[view, odd] = by_right(s4.at[view, odd], right, 2 + odd)
            yield

    work = [steps(view) for view in range(views)]
    for view in range(views):
        for _ in range(view * STAGGER):
            work[view] = itertools.chain([None], work[view])
    for _ in itertools.zip_longest(*work):
        pass

    for row in range(0, size, CHUNK):
        rows = slice(row, row + CHUNK)
        sums = {}

        def add(key, value):
            sums[key] = sums[key] + value if key in sums else value

        for view in range(views):
            beyond, place = row_mask(view, row)
            halves = []
            for part in range(2):
                cols = slice(part * half, (part + 1) * half)
                even_cols, odd_cols = g[view, 0, rows, cols], g[view, 1, rows, cols]
                halves.append((even_cols + odd_cols, even_cols - odd_cols))
            for block in range(2):
                cols = slice(block * LANES, (block + 1) * LANES)
                beside = col_mask(spots, view, block)
                b_re, b_im = halves[0][block], halves[1][block]
                p_re, p_im = placed[view, 0, rows, cols], placed[view, 1, rows, cols]
                for part, value in enumerate((p_re * b_re + p_im * b_im, p_re * b_im - p_im * b_re)):
                    if beyond is not None:
                        outer, value = jnp.where(beyond, value, zero), jnp.where(beyond, zero, value)
                        add(("corner", part), jnp.where(beside, outer, zero))
                        add(("row", part, block), jnp.where(beside, zero, outer))
                    add(("col", part), jnp.where(beside, value, zero))
                    add(("core", part, block), jnp.where(beside, zero, value))
        for part in range(2):
            cols_m[part, rows] = sums["col", part]
            if place is not None:
                corner_m[part, place : place + CHUNK] = sums["corner", part]
            for block in range(2):
                cols = slice(block * LANES, (block + 1) * LANES)
                g_core[part, rows, cols] = sums["core", part, block]
                if place is not None:
                    rows_m[part, place : place + CHUNK, cols] = sums["row", part, block]

    def packed(channel, re, im):
        to_right = jnp.where(low_lanes, re, swap_halves(im))
        to_left = jnp.where(low_lanes, swap_halves(im), re)
        return jnp.where(sends_right(channel), to_right, to_left)

    for part in range(2):
        bottom, top = rows_m[part, :m], rows_m[part, m:]
        g_a[part] = jnp.where(lower, bottom, top)
        g_b[part] = jnp.where(lower, top, bottom)
    bottom = (corner_m[0, :m], corner_m[1, :m])
    top = (corner_m[0, m:], corner_m[1, m:])
    for number, channel in enumerate(chans):
        for row in range(0, size, CHUNK):
            rows = slice(row, row + CHUNK)
            g_x[number][rows] = packed(channel, cols_m[0, rows], cols_m[1, rows])
        below, above = packed(channel, *bottom), packed(channel, *top)
        g_ka[number][...] = jnp.where(lower, below, above)
        g_kb[number][...] = jnp.where(lower, above, below)


def views_call(chans, spots, counts, core, placed, inner, intensity, tables, a_in, b_in, x_in, ka_in, kb_in):
    views, size = placed.shape[0], core.shape[1]
    count = len(chans)
    vmem = pl.BlockSpec(memory_space=pltpu.VMEM)
    shapes = [(2, size, size), (2, MARGIN, size), (2, MARGIN, size)]
    shapes += [(size, LANES)] * count + [(MARGIN, LANES)] * (2 * count)
    full = pltpu.VMEM((views, 2, size, size), F32)
    tall = pltpu.VMEM((views, 2, 2 * size, size), BF16)
    outs = pl.pallas_call(
        functools.partial(views_kernel, chans),
        out_shape=[jax.ShapeDtypeStruct(shape, F32) for shape in shapes],
        in_specs=[
            vmem,
            pl.BlockSpec(memory_space=pltpu.SMEM),
            *[vmem] * (8 + 3 * count),
        ],
        out_specs=[vmem] * len(shapes),
        scratch_shapes=[
            pltpu.VMEM((views, 2, size, size // 2), F32),
            pltpu.VMEM((2, size, LANES), F32),
            pltpu.VMEM((2, 2 * MARGIN, size), F32),
            pltpu.VMEM((2, 2 * MARGIN, LANES), F32),
            pltpu.VMEM((views, 2, 4 * CHUNK, size), BF16),
            pltpu.VMEM((views, 2, 2 * CHUNK, size), F32),
            *[tall, full] * 3,
        ],
        compiler_params=pltpu.CompilerParams(vmem_limit_bytes=40 * 1024 * 1024),
    )(spots, counts, core, placed, inner, intensity, *x_in, a_in, b_in, *kb_in, *ka_in, *tables)
    return (*outs[:3], outs[3 : 3 + count], outs[3 + count : 3 + 2 * count], outs[3 + 2 * count :])


def finish_kernel(chans, object_ref, g_core, *rest):
    count = len(chans)
    x_in, (a_in, b_in), rest = rest[:count], rest[count : count + 2], rest[count + 2 :]
    ka_in, kb_in, out = rest[:count], rest[count : 2 * count], rest[-1]
    size = object_ref.shape[1]
    lower = lower_partner()
    a_rows = pl.ds(pl.multiple_of(jnp.where(lower, size - MARGIN, 0), MARGIN), MARGIN)
    b_rows = pl.ds(pl.multiple_of(jnp.where(lower, 0, size - MARGIN), MARGIN), MARGIN)
    columns = []
    for channel in chans:
        right = takes_right(channel)
        mine = lane_ids() // (LANES // 2) == jnp.where(right, 1, 0)
        block = pl.multiple_of(jnp.where(right, size - LANES, 0), LANES)
        columns.append((mine, pl.ds(block, LANES)))

    def take(place, value):
        out[place] -= step_size * value

    def take_packed(rows, column, block):
        mine, lanes = column
        take((0, rows, lanes), jnp.where(mine, block, 0.0))
        take((1, rows, lanes), jnp.where(mine, swap_halves(block), 0.0))

    for part in range(2):
        out[part] = object_ref[part] - step_size * g_core[part]
        take((part, a_rows), a_in[part])
    for number, column in enumerate(columns):
        take_packed(slice(None), column, x_in[number][...])
        take_packed(a_rows, column, ka_in[number][...])

    @pl.when(b_partner())
    def _():
        for part in range(2):
            take((part, b_rows), b_in[part])
        for number, column in enumerate(columns):
            take_packed(b_rows, column, kb_in[number][...])


def finish_call(chans, object_field, g_core, a_in, b_in, x_in, ka_in, kb_in):
    vmem = pl.BlockSpec(memory_space=pltpu.VMEM)
    return pl.pallas_call(
        functools.partial(finish_kernel, chans),
        out_shape=jax.ShapeDtypeStruct(object_field.shape, F32),
        in_specs=[vmem] * (4 + 3 * len(chans)),
        out_specs=vmem,
        compiler_params=pltpu.CompilerParams(vmem_limit_bytes=6 * 1024 * 1024),
    )(object_field, g_core, *x_in, a_in, b_in, *ka_in, *kb_in)


def per_device(object_field, probe_field, intensity, view_offsets, view_counts):
    size = object_field.shape[1]
    mesh_rows, mesh_cols = lax.axis_size("row"), lax.axis_size("col")
    chans = channels(mesh_cols)
    tables = dft_tables(size)
    a_pairs, b_pairs = row_pairs(mesh_rows, 0), row_pairs(mesh_rows, 1)
    spare = spare_route(b_pairs, mesh_rows, mesh_cols)

    def over_rows(block, pairs, extra):
        route = [(i * mesh_cols + k, j * mesh_cols + k) for i, j in pairs for k in range(mesh_cols)]
        return lax.ppermute(block, ("row", "col"), route + extra)

    def across(block, pairs, extra, channel):
        route = [(i * mesh_cols + k, j * mesh_cols + l) for i, j in pairs for k, l in channel[0]]
        return lax.ppermute(block, ("row", "col"), route + (extra if mesh_cols == 2 else []))

    def exchange(a_send, b_send, x_send, kb_send):
        x_in = [lax.ppermute(block, "col", channel[0]) for block, channel in zip(x_send, chans)]
        a_in = over_rows(a_send, a_pairs, [])
        b_in = over_rows(b_send, b_pairs, spare)
        kb_in = [across(block, b_pairs, spare, channel) for block, channel in zip(kb_send, chans)]
        return a_in, b_in, x_in, kb_in

    packs = pack_call(object_field, chans)
    a_in, b_in, x_in, kb_in = exchange(packs[0], packs[1], packs[2::2], packs[3::2])
    offsets, probe = (
        pltpu.with_memory_space_constraint(array, pltpu.HBM)
        for array in (jnp.swapaxes(view_offsets, 2, 3), probe_field)
    )
    placed, spots = prepare_call(offsets, probe)
    edges = [edge_call(block, spots) for block in x_in]
    ka_in = [over_rows(block, a_pairs, []) for block in edges]
    unused = (edges[0] if edges else spots, tables[1], intensity)
    inner = early_call(chans, spots, object_field, placed, tables[0], unused, x_in)
    g_core, g_a, g_b, g_x, g_ka, g_kb = views_call(
        chans, spots, view_counts, object_field, placed, inner, intensity, tables,
        a_in, b_in, x_in, ka_in, kb_in,
    )
    a_in, b_in, x_in, kb_in = exchange(g_a, g_b, g_x, g_kb)
    ka_in = [across(block, a_pairs, [], channel) for block, channel in zip(g_ka, chans)]
    return finish_call(chans, object_field, g_core, a_in, b_in, x_in, ka_in, kb_in)


def solution(mesh):
    in_specs = (
        P(None, "row", "col"),
        P(),
        P("row", "col", None, None, None),
        P("row", "col", None, None),
        P("row", "col"),
    )
    out_specs = P(None, "row", "col")
    return jax.shard_map(
        per_device, mesh=mesh, in_specs=in_specs, out_specs=out_specs, check_vma=False
    )
```
